32 devices in a mesh: batch: 4 (over x, core), ctx: 8 (over z, y).
Axes of the slice: x: 2, y: 2, z: 4, core: 2. Of those that a mesh axis runs over, the one named last changes fastest.
Arguments:
- hidden_in: bfloat16 [4096, 1536], P(('batch', 'ctx')), may hold values from -6 to 6
- positions: int32 [4096], P(('batch', 'ctx')), may hold values from 0 to 1023, as said below
- doc_ids: int32 [4096], P(('batch', 'ctx')), may hold values from 0 to 2, as said below
- attn_gain: bfloat16 [1536], P(('batch', 'ctx')), may hold values from 0.25 to 1.75
- q_weight: bfloat16 [1536, 1536], P(('batch', 'ctx')), may hold values from -0.15625 to 0.15625
- q_bias: bfloat16 [1536], P(('batch', 'ctx')), may hold values from -3 to 3
- k_weight: bfloat16 [1536, 256], P(('batch', 'ctx')), may hold values from -0.15625 to 0.15625
- k_bias: bfloat16 [256], P(('batch', 'ctx')), may hold values from -3 to 3
- v_weight: bfloat16 [1536, 256], P(('batch', 'ctx')), may hold values from -0.15625 to 0.15625
- v_bias: bfloat16 [256], P(('batch', 'ctx')), may hold values from -3 to 3
- o_weight: bfloat16 [1536, 1536], P(('batch', 'ctx')), may hold values from -1.25 to 1.25
- mlp_gain: bfloat16 [1536], P(('batch', 'ctx')), may hold values from 0.25 to 1.75
- gate_weight: bfloat16 [1536, 8960], P(('batch', 'ctx')), may hold values from -0.15625 to 0.15625
- up_weight: bfloat16 [1536, 8960], P(('batch', 'ctx')), may hold values from -0.15625 to 0.15625
- down_weight: bfloat16 [8960, 1536], P(('batch', 'ctx')), may hold values from -0.0625 to 0.0625
- out_grad: bfloat16 [4096, 1536], P(('batch', 'ctx')), may hold values from -6 to 6
Outputs:
- hidden_out: bfloat16 [4096, 1536], P(('batch', 'ctx'))
- hidden_grad: float32 [4096, 1536], P(('batch', 'ctx'))
- attn_gain_grad: float32 [1536], P(('batch', 'ctx'))
- q_weight_grad: float32 [1536, 1536], P(('batch', 'ctx'))
- q_bias_grad: float32 [1536], P(('batch', 'ctx'))
- k_weight_grad: float32 [1536, 256], P(('batch', 'ctx'))
- k_bias_grad: float32 [256], P(('batch', 'ctx'))
- v_weight_grad: float32 [1536, 256], P(('batch', 'ctx'))
- v_bias_grad: float32 [256], P(('batch', 'ctx'))
- o_weight_grad: float32 [1536, 1536], P(('batch', 'ctx'))
- mlp_gain_grad: float32 [1536], P(('batch', 'ctx'))
- gate_weight_grad: float32 [1536, 8960], P(('batch', 'ctx'))
- up_weight_grad: float32 [1536, 8960], P(('batch', 'ctx'))
- down_weight_grad: float32 [8960, 1536], P(('batch', 'ctx'))
The draws below stay inside these ranges and needn't reach their ends.
Inputs may be any that keep to these rules, and one draw needn't show every extreme that they name: Each device's 128 rows are 1 runs of 128 rows, run s holding tokens of sequence s of its batch index; within a batch index every position of each sequence is held exactly once. On ctx index c a run holds either positions c * 128 onward in order, or block c and then block 15 - c of 64 positions each, in order. `doc_ids`: never falls as the position within a sequence rises; each of a sequence's three documents holds 128 positions or more.
All inputs are finite; a program needn't handle non-finite values.
Results may differ from the reference program's by a relative error of at most 0.015.
Values may be sent and summed in bfloat16 or wider, within the bound.
A program may use at most 448 MiB of HBM per device.

```python
import math
import jax
import jax.numpy as jnp
from jax import lax

D = 1536
HEADS = 12
KV_HEADS = 2
HEAD_DIM = 128
FF = 8960
SEQ_DEV = 128
SEQS = 1
KVW = 256
LENGTH = 1024
TOKENS = 4096
N_BATCH = 4
N_CTX = 8


def layout_tables(key):
    ctx_count = LENGTH // SEQ_DEV
    batch_count = TOKENS // (LENGTH * SEQS)
    seq_count = batch_count * SEQS
    folded_order = jax.random.randint(jax.random.fold_in(key, 101), (seq_count,), 0, 2)
    first_cut = jax.random.randint(jax.random.fold_in(key, 102), (seq_count,), LENGTH // 8, LENGTH // 2)
    second_cut = jax.random.randint(jax.random.fold_in(key, 103), (seq_count,), LENGTH // 2 + LENGTH // 8, LENGTH - LENGTH // 8 + 1)
    shape_all = (batch_count, ctx_count, SEQS, SEQ_DEV)
    batch_index = lax.broadcasted_iota(jnp.int32, shape_all, 0)
    ctx_index = lax.broadcasted_iota(jnp.int32, shape_all, 1)
    seq_slot = lax.broadcasted_iota(jnp.int32, shape_all, 2)
    token_index = lax.broadcasted_iota(jnp.int32, shape_all, 3)
    half_len = SEQ_DEV // 2
    drawn_pos = ctx_index * SEQ_DEV + token_index
    folded_block = jnp.where(token_index < half_len, ctx_index, 2 * ctx_count - 1 - ctx_index)
    folded_pos = folded_block * half_len + token_index % half_len
    seq_index = batch_index * SEQS + seq_slot
    position_all = jnp.where(folded_order[seq_index] == 1, folded_pos, drawn_pos).astype(jnp.int32)
    documents = (position_all >= first_cut[seq_index]).astype(jnp.int32) + (position_all >= second_cut[seq_index]).astype(jnp.int32)
    return (position_all.reshape(-1), documents.reshape(-1))


def draw_positions(key, part):
    return layout_tables(key)[0]


def draw_doc_ids(key, part):
    return layout_tables(key)[1]


def with_spikes(drawn, key, source, target, blocks, factor):
    owner, partner = [(jnp.arange(drawn.shape[axis_at]) // (drawn.shape[axis_at] // blocks)).reshape([-1 if axis == axis_at else 1 for axis in range(drawn.ndim)]) for axis_at in (source, target)]
    chosen = jax.random.permutation(key, blocks)[partner]
    strong = (owner == chosen) | (owner == (partner + blocks // 2) % blocks)
    return jnp.where(strong, factor * drawn, drawn)


def block_scale(stream_key, extent, pieces, low, largest):
    factor_of, own = 1.0, jax.random.fold_in(stream_key, 6)
    for axis_at, parts in pieces:
        draws = jnp.exp(jax.random.uniform(jax.random.fold_in(own, axis_at), (parts,), jnp.float32, low / len(pieces), largest / len(pieces)))
        factor_of = factor_of * jnp.repeat(draws, extent[axis_at] // parts).reshape([-1 if axis == axis_at else 1 for axis in range(len(extent))])
    return factor_of


def noise(stream_key, extent, scale, limit, cuts=(), held_as=jnp.bfloat16):
    values = jax.random.normal(stream_key, extent, jnp.float32) * scale
    if len(cuts) > 0:
        values = block_scale(stream_key, extent, cuts, -0.22, 0.18) * values
    return jnp.clip(values, min=-limit, max=limit).astype(held_as)


def bell_draw_with(own_key, extent, scale, reach, shards, heavy, kind=jnp.bfloat16):
    entries = scale * jax.random.normal(own_key, extent, jnp.float32)
    if shards:
        entries = entries * block_scale(own_key, extent, shards, -0.22, 0.18)
    return jnp.clip(with_spikes(entries, jax.random.fold_in(own_key, 3), *heavy), -reach, reach).astype(kind)


def setup_inputs(seed: int = 0) -> dict:
    key_of = jax.random.split(jax.random.key(seed), 17)
    hidden_in = bell_draw_with(key_of[0], (TOKENS, D), 1.0, 6.0, ((0, 32),), (0, 1, 32, 2.75))
    positions = draw_positions(jax.random.fold_in(key_of[16], 71), 0)
    doc_ids = draw_doc_ids(jax.random.fold_in(key_of[16], 71), 0)
    attn_gain = jnp.clip(1.0 + 0.15 * jax.random.normal(key_of[3], (D,), jnp.float32), 0.25, 1.75).astype(jnp.bfloat16)
    q_weight = noise(key_of[4], (D, D), D ** -0.5, 0.15625, ((0, 32),))
    q_bias = noise(key_of[5], (D,), 0.5, 3.0, ((0, 32),))
    k_weight = noise(key_of[6], (D, KVW), D ** -0.5, 0.15625, ((0, 32),))
    k_bias = noise(key_of[7], (KVW,), 0.5, 3.0, ((0, 32),))
    v_weight = noise(key_of[8], (D, KVW), D ** -0.5, 0.15625, ((0, 32),))
    v_bias = noise(key_of[9], (KVW,), 0.5, 3.0, ((0, 32),))
    o_weight = noise(key_of[10], (D, D), (D // 64) ** -0.5, 1.25, ((0, 32),))
    mlp_gain = jnp.clip(1.0 + 0.15 * jax.random.normal(key_of[11], (D,), jnp.float32), 0.25, 1.75).astype(jnp.bfloat16)
    gate_weight = noise(key_of[12], (D, FF), D ** -0.5, 0.15625, ((0, 32),))
    up_weight = noise(key_of[13], (D, FF), D ** -0.5, 0.15625, ((0, 32),))
    down_weight = noise(key_of[14], (FF, D), FF ** -0.5, 0.0625, ((0, 32),))
    out_grad = noise(key_of[15], (TOKENS, D), 1.0, 6.0, ((0, 32),))
    return {"hidden_in": hidden_in, "positions": positions, "doc_ids": doc_ids, "attn_gain": attn_gain, "q_weight": q_weight, "q_bias": q_bias, "k_weight": k_weight, "k_bias": k_bias, "v_weight": v_weight, "v_bias": v_bias, "o_weight": o_weight, "mlp_gain": mlp_gain, "gate_weight": gate_weight, "up_weight": up_weight, "down_weight": down_weight, "out_grad": out_grad}


@jax.custom_vjp
def low(v):
    return lax.optimization_barrier(v.astype(jnp.bfloat16)).astype(jnp.float32)

@jax.custom_vjp
def low_back(v):
    return v

def low_keep(v):
    return (low(v), None)

def low_pass(kept, grad):
    return (grad,)

def back_keep(v):
    return (v, None)

def back_low(kept, grad):
    return (low(grad),)
low.defvjp(low_keep, low_pass)
low_back.defvjp(back_keep, back_low)
EPSILON = 1e-06
ROPE_BASE = 10000.0
MASKED = -1e+30

def rope_tables(positions):
    half_dim = HEAD_DIM // 2
    inverse_freq = jnp.exp(jnp.arange(half_dim, dtype=jnp.float32) * (-2.0 * math.log(ROPE_BASE) / HEAD_DIM))
    angles = positions.astype(jnp.float32)[:, None] * inverse_freq[None, :]
    angles = jnp.concatenate([angles, angles], axis=1)
    return (jnp.cos(angles), jnp.sin(angles))

def rotate(values, cosine, sine_table):
    half_dim = values.shape[-1] // 2
    turned = jnp.concatenate([-values[..., half_dim:], values[..., :half_dim]], axis=-1)
    return values * cosine[:, None, :] + turned * sine_table[:, None, :]

def product(lhs_matrix, rhs_matrix):
    return jnp.dot(lhs_matrix, rhs_matrix, precision=lax.Precision.HIGHEST, preferred_element_type=jnp.float32)

def rms_scale(values, gain_vector):
    return values * lax.rsqrt(lax.optimization_barrier(jnp.mean(values * values, axis=-1, keepdims=True)) + EPSILON) * gain_vector

def attend_block(query_part, query_pos, query_doc, key_rows, value_rows, key_pos, key_doc):
    scores = jnp.einsum('qjhd,kjd->jhqk', query_part, key_rows, precision=lax.Precision.HIGHEST) * HEAD_DIM ** (-0.5)
    allowed = (key_pos[None, :] <= query_pos[:, None]) & (key_doc[None, :] == query_doc[:, None])
    scores = low_back(jnp.where(allowed[None, None], scores, MASKED))
    attn_probs = low(jax.nn.softmax(scores, axis=-1))
    return jnp.einsum('jhqk,kjd->qjhd', attn_probs, value_rows, precision=lax.Precision.HIGHEST)

def layer_seq(params, hidden, seq_pos, seq_doc):
    gain_one, w_query, b_query, w_key, b_key, w_value, b_value, w_out, gain_two, w_gate, w_up, w_down = params
    groups = HEADS // KV_HEADS
    normed_one = low(rms_scale(hidden, gain_one))
    q_lin = low_back(product(normed_one, w_query) + b_query)
    k_lin = low_back(product(normed_one, w_key) + b_key)
    v_lin = low(low_back(product(normed_one, w_value) + b_value))
    cosine, sine_table = rope_tables(seq_pos)
    queries = low(rotate(q_lin.reshape(LENGTH, HEADS, HEAD_DIM), cosine, sine_table))
    key_rows = low(rotate(k_lin.reshape(LENGTH, KV_HEADS, HEAD_DIM), cosine, sine_table))
    value_rows = v_lin.reshape(LENGTH, KV_HEADS, HEAD_DIM)
    block_len = math.gcd(LENGTH, 512)
    blocks_count = LENGTH // block_len
    query_blocks = queries.reshape(blocks_count, block_len, KV_HEADS, groups, HEAD_DIM)

    def one_block(seq_item):
        return attend_block(seq_item[0], seq_item[1], seq_item[2], key_rows, value_rows, seq_pos, seq_doc)
    attn_out = lax.map(jax.checkpoint(one_block), (query_blocks, seq_pos.reshape(blocks_count, block_len), seq_doc.reshape(blocks_count, block_len)))
    attn_out = low(low_back(attn_out.reshape(LENGTH, D)))
    residual = hidden + low_back(product(attn_out, w_out))
    normed_two = low(rms_scale(residual, gain_two))
    gate_lin = low_back(product(normed_two, w_gate))
    up_lin = low_back(product(normed_two, w_up))
    mixed_rows = low(jax.nn.silu(gate_lin) * up_lin)
    return residual + low_back(product(mixed_rows, w_down))

def regroup(array):
    tail_shape = array.shape[1:]
    shaped = array.reshape((N_BATCH, N_CTX, SEQS, SEQ_DEV) + tail_shape)
    axes_order = (0, 2, 1, 3) + tuple(range(4, 4 + len(tail_shape)))
    return shaped.transpose(axes_order).reshape((N_BATCH * SEQS, LENGTH) + tail_shape)

def ungroup(array):
    tail_shape = array.shape[2:]
    shaped = array.reshape((N_BATCH, SEQS, N_CTX, SEQ_DEV) + tail_shape)
    axes_order = (0, 2, 1, 3) + tuple(range(4, 4 + len(tail_shape)))
    return shaped.transpose(axes_order).reshape((TOKENS,) + tail_shape)

def reference(hidden_in, positions, doc_ids, attn_gain, q_weight, q_bias, k_weight, k_bias, v_weight, v_bias, o_weight, mlp_gain, gate_weight, up_weight, down_weight, out_grad):
    params = tuple((tensor.astype(jnp.float32) for tensor in (attn_gain, q_weight, q_bias, k_weight, k_bias, v_weight, v_bias, o_weight, mlp_gain, gate_weight, up_weight, down_weight)))
    seq_pos = regroup(positions)
    seq_doc = regroup(doc_ids)

    def forward(hidden, weights):
        step_fn = jax.checkpoint(lambda seq_item: layer_seq(weights, seq_item[0], seq_item[1], seq_item[2]))
        return ungroup(lax.map(step_fn, (regroup(hidden), seq_pos, seq_doc)))
    output, pullback = jax.vjp(forward, hidden_in.astype(jnp.float32), params)
    hidden_grad, weight_grads = pullback(out_grad.astype(jnp.float32))
    return (output.astype(jnp.bfloat16), hidden_grad, weight_grads[0], weight_grads[1], weight_grads[2], weight_grads[3], weight_grads[4], weight_grads[5], weight_grads[6], weight_grads[7], weight_grads[8], weight_grads[9], weight_grads[10], weight_grads[11])
```

```python
import math

import jax
import jax.numpy as jnp
from jax import lax
from jax.sharding import PartitionSpec as P

HEADS = 12
KV_HEADS = 2
GROUPS = HEADS // KV_HEADS
HEAD_DIM = 128
KVW = KV_HEADS * HEAD_DIM
INV_ROOT = HEAD_DIM ** (-0.5)
EPSILON = 1e-06
ROPE_BASE = 10000.0
MASKED = -1e30
ALL = ("batch", "ctx")
F32 = jnp.float32
BF16 = jnp.bfloat16


def rope_tables(positions):
    half_dim = HEAD_DIM // 2
    inverse_freq = jnp.exp(
        jnp.arange(half_dim, dtype=F32) * (-2.0 * math.log(ROPE_BASE) / HEAD_DIM)
    )
    angles = positions.astype(F32)[:, None] * inverse_freq[None, :]
    angles = jnp.concatenate([angles, angles], axis=1)
    return (jnp.cos(angles), jnp.sin(angles))


def rotate(values, cosine, sine_table):
    half_dim = values.shape[-1] // 2
    turned = jnp.concatenate([-values[..., half_dim:], values[..., :half_dim]], axis=-1)
    return values * cosine[:, None, :] + turned * sine_table[:, None, :]


def rotate_back(grad_rows, cosine, sine_table):
    half_dim = grad_rows.shape[-1] // 2
    scaled = grad_rows * sine_table[:, None, :]
    turned = jnp.concatenate([scaled[..., half_dim:], -scaled[..., :half_dim]], axis=-1)
    return grad_rows * cosine[:, None, :] + turned


def norm_rows(values, gain_vector):
    factor = lax.rsqrt(jnp.mean(values * values, axis=-1, keepdims=True) + EPSILON)
    return (values * factor * gain_vector, factor)


def norm_back(values, factor, gain_vector, grad_rows):
    scaled = grad_rows * gain_vector
    gain_grad = jnp.sum(grad_rows * values * factor, axis=0)
    value_grad = factor * scaled - values * (factor * factor * factor) * jnp.mean(
        scaled * values, axis=-1, keepdims=True
    )
    return (value_grad, gain_grad)


def dot(lhs, rhs):
    return jnp.dot(lhs, rhs, preferred_element_type=F32)


def contract_rows(lhs, rhs):
    return lax.dot_general(lhs, rhs, (((0,), (0,)), ((), ())), preferred_element_type=F32)


def times_transposed(lhs, rhs):
    return lax.dot_general(lhs, rhs, (((1,), (1,)), ((), ())), preferred_element_type=F32)


def lanes(width):
    return -(-width // 128) * 128


def pack_columns(weight, n_batch, n_ctx):
    rows, width = weight.shape
    piece = width // (n_batch * n_ctx)
    own = n_batch * piece
    packed = weight.reshape(rows, n_batch, n_ctx, piece).transpose(2, 0, 1, 3)
    packed = packed.reshape(n_ctx, rows, own)
    return jnp.pad(packed, ((0, 0), (0, 0), (0, lanes(own) - own)))


def unpack_columns(packed, n_batch, width):
    n_ctx, rows, _ = packed.shape
    piece = width // (n_batch * n_ctx)
    packed = packed[:, :, : n_batch * piece].reshape(n_ctx, rows, n_batch, piece)
    return packed.transpose(1, 2, 0, 3).reshape(rows, width)


def heads_of(rows):
    count = rows.shape[0]
    shaped = rows.reshape(count, KV_HEADS, GROUPS, HEAD_DIM).transpose(1, 2, 0, 3)
    return shaped.reshape(KV_HEADS, GROUPS * count, HEAD_DIM)


def rows_of(heads):
    count = heads.shape[1] // GROUPS
    shaped = heads.reshape(KV_HEADS, GROUPS, count, HEAD_DIM).transpose(2, 0, 1, 3)
    return shaped.reshape(count, HEADS * HEAD_DIM)


def kv_heads_of(rows):
    return rows.reshape(rows.shape[0], KV_HEADS, HEAD_DIM).transpose(1, 0, 2)


def own_slice(vector):
    width = vector.shape[0] // lax.axis_size(ALL)
    return lax.dynamic_slice_in_dim(vector, lax.axis_index(ALL) * width, width)


def local(
    hidden_in,
    positions,
    doc_ids,
    attn_gain,
    q_weight,
    q_bias,
    k_weight,
    k_bias,
    v_weight,
    v_bias,
    o_weight,
    mlp_gain,
    gate_weight,
    up_weight,
    down_weight,
    out_grad,
):
    n_batch, n_ctx = lax.axis_size("batch"), lax.axis_size("ctx")
    n_all = n_batch * n_ctx
    count, width = hidden_in.shape
    hidden_ff = gate_weight.shape[1]

    vectors = lax.all_gather(
        jnp.concatenate([attn_gain, mlp_gain, q_bias, k_bias, v_bias]), ALL, axis=0
    ).astype(F32)
    edges, at = [], 0
    for part in (attn_gain, mlp_gain, q_bias, k_bias, v_bias):
        edges.append(vectors[:, at : at + part.shape[0]].reshape(-1))
        at += part.shape[0]
    gain_one, gain_two, b_query, b_key, b_value = edges
    attn_all = lax.all_gather(
        jnp.concatenate([q_weight, k_weight, v_weight, o_weight], axis=1), ALL, axis=0, tiled=True
    )
    qkv_width = width + 2 * KVW
    w_qkv, w_out = attn_all[:, :qkv_width], attn_all[:, qkv_width:]
    b_qkv = jnp.concatenate([b_query, b_key, b_value])
    packed = jnp.concatenate(
        [pack_columns(gate_weight, n_batch, n_ctx), pack_columns(up_weight, n_batch, n_ctx)], axis=2
    )
    half = packed.shape[2] // 2
    packed = lax.all_to_all(packed, "ctx", split_axis=0, concat_axis=0)
    w_gate_up = lax.all_gather(packed.reshape(-1, 2 * half), "batch", axis=0, tiled=True)
    w_down = lax.all_gather(down_weight, "batch", axis=0, tiled=True)
    own_ff = w_down.shape[0]
    w_down = jnp.pad(w_down, ((0, half - own_ff), (0, 0)))
    out_grad_all = lax.all_gather(out_grad, "ctx", axis=0, tiled=True)

    cosine, sine_table = rope_tables(positions)
    hidden_wide = hidden_in.astype(F32)
    normed_wide, factor_one = norm_rows(hidden_wide, gain_one)
    normed_one = normed_wide.astype(BF16)
    lin = dot(normed_one, w_qkv) + b_qkv
    turned = rotate(
        lin[:, : width + KVW].reshape(count, HEADS + KV_HEADS, HEAD_DIM), cosine, sine_table
    ).astype(BF16).reshape(count, width + KVW)
    query_heads = heads_of(turned[:, :width])
    key_value = jnp.concatenate([turned[:, width:], lin[:, width + KVW :].astype(BF16)], axis=1)
    key_value = lax.all_gather(key_value, "ctx", axis=0, tiled=True)
    places = lax.all_gather(jnp.stack([positions, doc_ids]), "ctx", axis=1, tiled=True)
    key_heads, value_heads = kv_heads_of(key_value[:, :KVW]), kv_heads_of(key_value[:, KVW:])
    allowed = (places[0][None, :] <= positions[:, None]) & (places[1][None, :] == doc_ids[:, None])
    allowed = jnp.tile(allowed, (GROUPS, 1))
    scores = jnp.einsum("jqd,jkd->jqk", query_heads, key_heads, preferred_element_type=F32)
    scores = jnp.where(allowed[None], scores * INV_ROOT, MASKED)
    probs = jax.nn.softmax(scores, axis=-1)
    attn_probs = probs.astype(BF16)
    attn_out = rows_of(
        jnp.einsum("jqk,jkd->jqd", attn_probs, value_heads, preferred_element_type=F32)
    ).astype(BF16)
    residual = hidden_wide + dot(attn_out, w_out)

    normed_mid, factor_two = norm_rows(residual, gain_two)
    normed_two = lax.all_gather(normed_mid.astype(BF16), "ctx", axis=0, tiled=True)
    gate_up = dot(normed_two, w_gate_up)
    gate_lin, up_lin = gate_up[:, :half], gate_up[:, half:]
    sigmoid_gate = jax.nn.sigmoid(gate_lin)
    mixed_rows = (gate_lin * sigmoid_gate * up_lin).astype(BF16)
    d_mixed = times_transposed(out_grad_all, w_down)
    d_gate = d_mixed * up_lin * sigmoid_gate * (1.0 + gate_lin * (1.0 - sigmoid_gate))
    d_up = d_mixed * (gate_lin * sigmoid_gate)
    d_gate_up = jnp.concatenate([d_gate.astype(BF16), d_up.astype(BF16)], axis=1)
    d_normed_two = lax.psum_scatter(
        times_transposed(d_gate_up, w_gate_up).astype(BF16), "ctx", scatter_dimension=0, tiled=True
    ).astype(F32)
    ff_out = lax.psum_scatter(
        dot(mixed_rows, w_down).astype(BF16), "ctx", scatter_dimension=0, tiled=True
    )
    hidden_out = (residual + ff_out.astype(F32)).astype(BF16)
    down_grad = contract_rows(mixed_rows, out_grad_all)[:own_ff].astype(BF16)
    down_grad = lax.psum_scatter(down_grad, "batch", scatter_dimension=0, tiled=True)
    gate_up_grad = contract_rows(normed_two, d_gate_up).astype(BF16)
    gate_up_grad = lax.psum_scatter(gate_up_grad, "batch", scatter_dimension=0, tiled=True)
    gate_up_grad = lax.all_to_all(
        gate_up_grad.reshape(n_ctx, -1, 2 * half), "ctx", split_axis=0, concat_axis=0
    ).astype(F32)
    gate_grad = unpack_columns(gate_up_grad[:, :, :half], n_batch, hidden_ff)
    up_grad = unpack_columns(gate_up_grad[:, :, half:], n_batch, hidden_ff)

    d_residual_norm, gain_two_grad = norm_back(residual, factor_two, gain_two, d_normed_two)
    d_residual = out_grad.astype(F32) + d_residual_norm
    d_branch = d_residual.astype(BF16)
    out_proj_grad = contract_rows(attn_out, d_branch)
    grad_heads = heads_of(times_transposed(d_branch, w_out).astype(BF16))
    d_probs = jnp.einsum("jqd,jkd->jqk", grad_heads, value_heads, preferred_element_type=F32)
    row_delta = jnp.sum(probs * d_probs, axis=-1, keepdims=True)
    d_scores = (probs * (d_probs - row_delta)).astype(BF16)
    d_queries = rows_of(
        jnp.einsum("jqk,jkd->jqd", d_scores, key_heads, preferred_element_type=F32) * INV_ROOT
    )
    d_keys = jnp.einsum("jqk,jqd->kjd", d_scores, query_heads, preferred_element_type=F32) * INV_ROOT
    d_values = jnp.einsum("jqk,jqd->kjd", attn_probs, grad_heads, preferred_element_type=F32)
    d_key_value = jnp.concatenate([d_keys.reshape(-1, KVW), d_values.reshape(-1, KVW)], axis=1)
    d_key_value = lax.psum_scatter(
        d_key_value.astype(BF16), "ctx", scatter_dimension=0, tiled=True
    ).astype(F32)
    d_turned = jnp.concatenate([d_queries, d_key_value[:, :KVW]], axis=1)
    d_turned = rotate_back(
        d_turned.reshape(count, HEADS + KV_HEADS, HEAD_DIM), cosine, sine_table
    ).reshape(count, width + KVW)
    d_lin = jnp.concatenate([d_turned, d_key_value[:, KVW:]], axis=1).astype(BF16)
    qkv_grad = contract_rows(normed_one, d_lin)
    bias_grad = jnp.sum(d_lin.astype(F32), axis=0)
    d_normed_one = times_transposed(d_lin, w_qkv)
    d_hidden_norm, gain_one_grad = norm_back(hidden_wide, factor_one, gain_one, d_normed_one)
    hidden_grad = d_residual + d_hidden_norm

    attn_grads = jnp.concatenate([qkv_grad.astype(BF16), out_proj_grad.astype(BF16)], axis=1)
    attn_grads = lax.psum_scatter(attn_grads, ALL, scatter_dimension=0, tiled=True).astype(F32)
    sums = lax.psum(jnp.concatenate([gain_one_grad, bias_grad, gain_two_grad]), ALL)
    at_key, at_value, at_out = width, width + KVW, width + 2 * KVW
    return (
        hidden_out,
        hidden_grad,
        own_slice(sums[:width]),
        attn_grads[:, :at_key],
        own_slice(sums[width : 2 * width]),
        attn_grads[:, at_key:at_value],
        own_slice(sums[2 * width : 2 * width + KVW]),
        attn_grads[:, at_value:at_out],
        own_slice(sums[2 * width + KVW : 2 * width + 2 * KVW]),
        attn_grads[:, at_out:],
        own_slice(sums[2 * width + 2 * KVW :]),
        gate_grad,
        up_grad,
        lax.convert_element_type(down_grad, F32),
    )


def solution(mesh):
    matrix, vector = P(ALL, None), P(ALL)
    placed = (
        (matrix, vector, vector, vector, matrix, vector, matrix, vector)
        + (matrix, vector, matrix, vector, matrix, matrix, matrix, matrix)
    )
    results = (matrix, matrix) + (vector, matrix) * 4 + (vector, matrix, matrix, matrix)
    return jax.shard_map(local, mesh=mesh, in_specs=placed, out_specs=results, check_vma=False)
```

```python
import functools
import math

import jax
import jax.numpy as jnp
from jax import lax
from jax.experimental import pallas as pl
from jax.experimental.pallas import tpu as pltpu
from jax.sharding import PartitionSpec as P

HEADS = 12
KV_HEADS = 2
GROUPS = HEADS // KV_HEADS
HEAD_DIM = 128
KVW = KV_HEADS * HEAD_DIM
INV_ROOT = HEAD_DIM ** (-0.5)
EPSILON = 1e-06
ROPE_BASE = 10000.0
MASKED = -1e30
ALL = ("batch", "ctx")
F32 = jnp.float32
BF16 = jnp.bfloat16
MESH = pl.DeviceIdType.MESH
ANYWHERE = pl.BlockSpec(memory_space=pl.ANY)
IN_VMEM = pl.BlockSpec(memory_space=pltpu.VMEM)
DMA = pltpu.SemaphoreType.DMA


def rope_tables(positions):
    half_dim = HEAD_DIM // 2
    inverse_freq = jnp.exp(
        jnp.arange(half_dim, dtype=F32) * (-2.0 * math.log(ROPE_BASE) / HEAD_DIM)
    )
    angles = positions.astype(F32)[:, None] * inverse_freq[None, :]
    angles = jnp.concatenate([angles, angles], axis=1)
    return (jnp.cos(angles), jnp.sin(angles))


def rotate(values, cosine, sine_table):
    half_dim = values.shape[-1] // 2
    turned = jnp.concatenate([-values[..., half_dim:], values[..., :half_dim]], axis=-1)
    return values * cosine[:, None, :] + turned * sine_table[:, None, :]


def rotate_back(grad_rows, cosine, sine_table):
    half_dim = grad_rows.shape[-1] // 2
    scaled = grad_rows * sine_table[:, None, :]
    turned = jnp.concatenate([scaled[..., half_dim:], -scaled[..., :half_dim]], axis=-1)
    return grad_rows * cosine[:, None, :] + turned


def norm_rows(values, gain_vector):
    factor = lax.rsqrt(jnp.mean(values * values, axis=-1, keepdims=True) + EPSILON)
    return (values * factor * gain_vector, factor)


def norm_back(values, factor, gain_vector, grad_rows):
    scaled = grad_rows * gain_vector
    gain_grad = jnp.sum(grad_rows * values * factor, axis=0)
    value_grad = factor * scaled - values * (factor * factor * factor) * jnp.mean(
        scaled * values, axis=-1, keepdims=True
    )
    return (value_grad, gain_grad)


def dot(lhs, rhs):
    return jnp.dot(lhs, rhs, preferred_element_type=F32)


def contract_rows(lhs, rhs):
    return lax.dot_general(lhs, rhs, (((0,), (0,)), ((), ())), preferred_element_type=F32)


def times_transposed(lhs, rhs):
    return lax.dot_general(lhs, rhs, (((1,), (1,)), ((), ())), preferred_element_type=F32)


def lanes(width):
    return -(-width // 128) * 128


def pack_columns(weight, n_batch, n_ctx):
    rows, width = weight.shape
    piece = width // (n_batch * n_ctx)
    own = n_batch * piece
    packed = weight.reshape(rows, n_batch, n_ctx, piece).transpose(2, 0, 1, 3)
    packed = packed.reshape(n_ctx, rows, own)
    return jnp.pad(packed, ((0, 0), (0, 0), (0, lanes(own) - own)))


def unpack_columns(packed, n_batch, width):
    n_ctx, rows, _ = packed.shape
    piece = width // (n_batch * n_ctx)
    packed = packed[:, :, : n_batch * piece].reshape(n_ctx, rows, n_batch, piece)
    return packed.transpose(1, 2, 0, 3).reshape(rows, width)


def heads_of(rows):
    count = rows.shape[0]
    shaped = rows.reshape(count, KV_HEADS, GROUPS, HEAD_DIM).transpose(1, 2, 0, 3)
    return shaped.reshape(KV_HEADS, GROUPS * count, HEAD_DIM)


def rows_of(heads):
    count = heads.shape[1] // GROUPS
    shaped = heads.reshape(KV_HEADS, GROUPS, count, HEAD_DIM).transpose(2, 0, 1, 3)
    return shaped.reshape(count, HEADS * HEAD_DIM)


def kv_heads_of(rows):
    return rows.reshape(rows.shape[0], KV_HEADS, HEAD_DIM).transpose(1, 0, 2)


def greet(devices):
    barrier = pltpu.get_barrier_semaphore()
    for device in devices:
        pl.semaphore_signal(barrier, inc=1, device_id=device, device_id_type=MESH)
    pl.semaphore_wait(barrier, len(devices))


def remote(source, target, send, receive, device):
    return pltpu.make_async_remote_copy(
        src_ref=source,
        dst_ref=target,
        send_sem=send,
        recv_sem=receive,
        device_id=device,
        device_id_type=MESH,
    )


def gather_kernel(line_len, own, out, own_sem, line_sems, pair_sems):
    b, c = lax.axis_index("batch"), lax.axis_index("ctx")
    line, pair = c // 2, c % 2
    ahead = (b, 2 * lax.rem(line + 1, line_len) + pair)
    behind = (b, 2 * lax.rem(line + line_len - 1, line_len) + pair)
    across = (b, c ^ 1)
    greet((ahead, behind, across))
    keep = pltpu.make_async_copy(own, out.at[c], own_sem)
    keep.start()
    on_line, on_pair = [], []
    for step in range(line_len):
        at = 2 * lax.rem(line - step + line_len, line_len) + pair
        block = own if step == 0 else out.at[at]
        if step > 0:
            on_line[step - 1].wait_recv()
        if step < line_len - 1:
            copy = remote(block, out.at[at], line_sems.at[0, step], line_sems.at[1, step], ahead)
            copy.start()
            on_line.append(copy)
        copy = remote(block, out.at[at], pair_sems.at[0, step], pair_sems.at[1, step], across)
        copy.start()
        on_pair.append(copy)
    for copy in on_pair:
        copy.wait()
    for copy in on_line:
        copy.wait_send()
    keep.wait()


def gather_ctx(block, collective_id, name):
    n_ctx = lax.axis_size("ctx")
    line_len = n_ctx // 2
    return pl.pallas_call(
        functools.partial(gather_kernel, line_len),
        out_shape=jax.ShapeDtypeStruct((n_ctx,) + block.shape, block.dtype),
        in_specs=[ANYWHERE],
        out_specs=ANYWHERE,
        scratch_shapes=[DMA(()), DMA((2, line_len)), DMA((2, line_len))],
        compiler_params=pltpu.CompilerParams(collective_id=collective_id, has_side_effects=True),
        name=name,
    )(block)


def scatter_kernel(
    line_len, parts, out, pair_in, line_in, line_out, pair_sems, line_sems
):
    b, c = lax.axis_index("batch"), lax.axis_index("ctx")
    line, pair = c // 2, c % 2
    ahead = (b, 2 * lax.rem(line + 1, line_len) + pair)
    behind = (b, 2 * lax.rem(line + line_len - 1, line_len) + pair)
    across = (b, c ^ 1)
    greet((ahead, behind, across))
    given, passed = [], []
    for step in range(line_len):
        to = lax.rem(line - 1 - step + line_len, line_len)
        copy = remote(
            parts.at[2 * to + 1 - pair],
            pair_in.at[step],
            pair_sems.at[0, step],
            pair_sems.at[1, step],
            across,
        )
        copy.start()
        given.append(copy)
    for step in range(line_len):
        to = lax.rem(line - 1 - step + line_len, line_len)
        given[step].wait_recv()
        total = parts[2 * to + pair].astype(F32) + pair_in[step].astype(F32)
        if step > 0:
            passed[step - 1].wait_recv()
            total = total + line_in[step - 1].astype(F32)
        if step < line_len - 1:
            line_out[step] = total.astype(line_out.dtype)
            copy = remote(
                line_out.at[step],
                line_in.at[step],
                line_sems.at[0, step],
                line_sems.at[1, step],
                ahead,
            )
            copy.start()
            passed.append(copy)
        else:
            out[...] = total
    for copy in given + passed:
        copy.wait_send()


def scatter_ctx(parts, collective_id, name):
    n_ctx = lax.axis_size("ctx")
    line_len = n_ctx // 2
    block = (parts.shape[0] // n_ctx,) + parts.shape[1:]
    return pl.pallas_call(
        functools.partial(scatter_kernel, line_len),
        out_shape=jax.ShapeDtypeStruct(block, F32),
        in_specs=[IN_VMEM],
        out_specs=IN_VMEM,
        scratch_shapes=[
            pltpu.VMEM((line_len,) + block, parts.dtype),
            pltpu.VMEM((line_len - 1,) + block, parts.dtype),
            pltpu.VMEM((line_len - 1,) + block, parts.dtype),
            DMA((2, line_len)),
            DMA((2, line_len)),
        ],
        compiler_params=pltpu.CompilerParams(
            collective_id=collective_id, has_side_effects=True, vmem_limit_bytes=56 * 2**20
        ),
        name=name,
    )(parts.reshape((n_ctx,) + block))


def spread_kernel(
    line_len, own, columns, out, columns_out, own_sem, line_sems, pair_sems, chip_sems, core_sems,
    column_sems,
):
    b, c = lax.axis_index("batch"), lax.axis_index("ctx")
    n_ctx = 2 * line_len
    line, pair = c // 2, c % 2
    ahead = (b, 2 * lax.rem(line + 1, line_len) + pair)
    across, chip, core = (b, c ^ 1), (b ^ 2, c), (b ^ 1, c)
    others = [(b, lax.rem(c + k, n_ctx)) for k in range(1, n_ctx)]
    greet([chip, core] + others)
    keep = [
        pltpu.make_async_copy(own, out.at[b, c], own_sem.at[0]),
        pltpu.make_async_copy(columns.at[c], columns_out.at[c], own_sem.at[1]),
    ]
    for copy in keep:
        copy.start()

    def place(step, side):
        return 2 * lax.rem(line - step + line_len, line_len) + side

    def hand(block, to_b, to_c, sems, index, device):
        copy = remote(block, out.at[to_b, to_c], sems.at[0, index], sems.at[1, index], device)
        copy.start()
        return copy

    on_line, on_pair, on_chip, on_core, on_columns = [], [], [], [], []
    for step in range(line_len):
        at = place(step, pair)
        block = own if step == 0 else out.at[b, at]
        if step > 0:
            on_line[step - 1].wait_recv()
        if step < line_len - 1:
            on_line.append(hand(block, b, at, line_sems, step, ahead))
        on_pair.append(hand(block, b, at, pair_sems, step, across))
        on_chip.append(hand(block, b, at, chip_sems, step, chip))
        on_core.append(hand(block, b, at, core_sems, step, core))
    for k, device in enumerate(others):
        copy = remote(
            columns.at[device[1]],
            columns_out.at[c],
            column_sems.at[0, k],
            column_sems.at[1, k],
            device,
        )
        copy.start()
        on_columns.append(copy)
    for step in range(line_len):
        at = place(step, 1 - pair)
        on_pair[step].wait_recv()
        on_chip.append(hand(out.at[b, at], b, at, chip_sems, line_len + step, chip))
        on_core.append(hand(out.at[b, at], b, at, core_sems, line_len + step, core))
    for index in range(n_ctx):
        at = place(index % line_len, pair if index < line_len else 1 - pair)
        on_chip[index].wait_recv()
        on_core.append(hand(out.at[b ^ 2, at], b ^ 2, at, core_sems, n_ctx + index, core))
    for copy in on_core + on_columns:
        copy.wait()
    for copy in on_line + on_pair + on_chip:
        copy.wait_send()
    for copy in keep:
        copy.wait()


def spread(own, columns, collective_id, name):
    n_batch, n_ctx = lax.axis_size("batch"), lax.axis_size("ctx")
    line_len = n_ctx // 2
    return pl.pallas_call(
        functools.partial(spread_kernel, line_len),
        out_shape=(
            jax.ShapeDtypeStruct((n_batch, n_ctx) + own.shape, own.dtype),
            jax.ShapeDtypeStruct(columns.shape, columns.dtype),
        ),
        in_specs=[ANYWHERE, ANYWHERE],
        out_specs=(ANYWHERE, ANYWHERE),
        scratch_shapes=[
            DMA((2,)),
            DMA((2, line_len)),
            DMA((2, line_len)),
            DMA((2, n_ctx)),
            DMA((2, 2 * n_ctx)),
            DMA((2, n_ctx)),
        ],
        compiler_params=pltpu.CompilerParams(collective_id=collective_id, has_side_effects=True),
        name=name,
    )(own, columns)


def collect_kernel(
    line_len, grads, columns, out, columns_out, core_in, chip_in, pair_in, line_in, chip_out,
    pair_out, line_out, own_sem, core_sems, chip_sems, pair_sems, line_sems, column_sems,
):
    b, c = lax.axis_index("batch"), lax.axis_index("ctx")
    n_ctx = 2 * line_len
    line, pair = c // 2, c % 2
    ahead = (b, 2 * lax.rem(line + 1, line_len) + pair)
    across, chip, core = (b, c ^ 1), (b ^ 2, c), (b ^ 1, c)
    others = [(b, lax.rem(c + k, n_ctx)) for k in range(1, n_ctx)]
    greet([chip, core] + others)
    keep = pltpu.make_async_copy(columns.at[c], columns_out.at[c], own_sem)
    keep.start()

    def place(index):
        step, side = index // 2, index % 2
        to = lax.rem(line - 1 - step + line_len, line_len)
        return 2 * to + (1 - pair if side == 0 else pair)

    def hand(block, target, sems, index, device):
        copy = remote(block, target.at[index], sems.at[0, index], sems.at[1, index], device)
        copy.start()
        return copy

    on_core, on_chip, on_pair, on_line, on_columns = [], [], [], [], []
    for index in range(n_ctx):
        on_core.append(hand(grads.at[b ^ 3, place(index)], core_in, core_sems, index, core))
    for k, device in enumerate(others):
        copy = remote(
            columns.at[device[1]],
            columns_out.at[c],
            column_sems.at[0, k],
            column_sems.at[1, k],
            device,
        )
        copy.start()
        on_columns.append(copy)
    for index in range(n_ctx):
        on_core.append(hand(grads.at[b ^ 1, place(index)], core_in, core_sems, n_ctx + index, core))
    for index in range(n_ctx):
        on_core[index].wait_recv()
        total = grads[b ^ 2, place(index)].astype(F32) + core_in[index].astype(F32)
        chip_out[index] = total.astype(chip_out.dtype)
        on_chip.append(hand(chip_out.at[index], chip_in, chip_sems, index, chip))

    def mine(index):
        on_core[n_ctx + index].wait_recv()
        on_chip[index].wait_recv()
        return (
            grads[b, place(index)].astype(F32)
            + core_in[n_ctx + index].astype(F32)
            + chip_in[index].astype(F32)
        )

    for step in range(line_len):
        pair_out[step] = mine(2 * step).astype(pair_out.dtype)
        on_pair.append(hand(pair_out.at[step], pair_in, pair_sems, step, across))
        total = mine(2 * step + 1)
        on_pair[step].wait_recv()
        total = total + pair_in[step].astype(F32)
        if step > 0:
            on_line[step - 1].wait_recv()
            total = total + line_in[step - 1].astype(F32)
        if step < line_len - 1:
            line_out[step] = total.astype(line_out.dtype)
            on_line.append(hand(line_out.at[step], line_in, line_sems, step, ahead))
        else:
            out[...] = total
    for copy in on_columns:
        copy.wait()
    for copy in on_core + on_chip + on_pair + on_line:
        copy.wait_send()
    keep.wait()


def collect(grads, columns, collective_id, name):
    n_batch, n_ctx = lax.axis_size("batch"), lax.axis_size("ctx")
    line_len = n_ctx // 2
    block = grads.shape[2:]

    def room(count):
        return pltpu.VMEM((count,) + block, grads.dtype)

    return pl.pallas_call(
        functools.partial(collect_kernel, line_len),
        out_shape=(
            jax.ShapeDtypeStruct(block, F32),
            jax.ShapeDtypeStruct(columns.shape, columns.dtype),
        ),
        in_specs=[IN_VMEM, ANYWHERE],
        out_specs=(IN_VMEM, ANYWHERE),
        scratch_shapes=[
            room(2 * n_ctx),
            room(n_ctx),
            room(line_len),
            room(line_len - 1),
            room(n_ctx),
            room(line_len),
            room(line_len - 1),
            DMA(()),
            DMA((2, 2 * n_ctx)),
            DMA((2, n_ctx)),
            DMA((2, line_len)),
            DMA((2, line_len)),
            DMA((2, n_ctx)),
        ],
        compiler_params=pltpu.CompilerParams(
            collective_id=collective_id, has_side_effects=True, vmem_limit_bytes=60 * 2**20
        ),
        name=name,
    )(grads, columns)


def swap(values, bit):
    size = lax.axis_size("batch")
    return lax.ppermute(values, "batch", [(i, i ^ bit) for i in range(size)])


def by_batch(values, b, n_batch):
    step = values.shape[1] // n_batch
    blocks = [lax.dynamic_slice_in_dim(values, (b ^ k) * step, step, 1) for k in range(n_batch)]
    return jnp.concatenate(blocks, axis=1)


def sum_by_batch(block):
    given = jnp.stack([block(1), block(3)]).astype(BF16)
    taken = swap(given, 1).astype(F32)
    passed = swap((block(2) + taken[1]).astype(BF16), 2)
    return block(0) + taken[0] + passed.astype(F32)


def vector_rows(vectors, rows, pieces):
    laid = [
        jnp.pad(v.reshape(pieces, 1, -1), ((0, 0), (0, 0), (0, 128 - v.shape[0] // pieces)))
        for v in vectors
    ]
    return jnp.pad(jnp.concatenate(laid, axis=1), ((0, 0), (0, rows - len(vectors)), (0, 0)))


def local(
    hidden_in,
    positions,
    doc_ids,
    attn_gain,
    q_weight,
    q_bias,
    k_weight,
    k_bias,
    v_weight,
    v_bias,
    o_weight,
    mlp_gain,
    gate_weight,
    up_weight,
    down_weight,
    out_grad,
):
    n_batch, n_ctx = lax.axis_size("batch"), lax.axis_size("ctx")
    n_all = n_batch * n_ctx
    count, width = hidden_in.shape
    hidden_ff = gate_weight.shape[1]

    b = lax.axis_index("batch")
    w_down = lax.all_gather(down_weight, "batch", axis=0, tiled=True)
    out_grad_all = lax.all_gather(out_grad, "ctx", axis=0, tiled=True)
    rows = q_weight.shape[0]
    small = (attn_gain, mlp_gain, q_bias, k_bias, v_bias)
    places = (positions // 64, positions % 64, doc_ids)
    small = vector_rows(small + tuple(row.astype(BF16) for row in places), rows, 1)[0]
    own = jnp.concatenate([q_weight, k_weight, v_weight, o_weight, small], axis=1)
    packed = jnp.concatenate(
        [pack_columns(gate_weight, n_batch, n_ctx), pack_columns(up_weight, n_batch, n_ctx)], axis=2
    )
    half = packed.shape[2] // 2
    attn_all, packed = spread(own, packed, 1, "spread_weights")
    own_rows = packed.reshape(-1, 2 * half)
    near, far = swap(own_rows, 1), swap(own_rows, 2)
    w_gate_up = jnp.concatenate([own_rows, near, far, swap(far, 1)], axis=0)
    small = attn_all[:, :, :8, own.shape[1] - 128 :].astype(F32)
    gain_one, gain_two, b_query, b_key, b_value = (
        small[:, :, i, : part.shape[0]].reshape(-1)
        for i, part in enumerate((attn_gain, mlp_gain, q_bias, k_bias, v_bias))
    )
    places = lax.dynamic_index_in_dim(small, b, 0, keepdims=False)[:, 5:8, :count]
    key_pos = (places[:, 0] * 64 + places[:, 1]).astype(jnp.int32).reshape(-1)
    key_doc = places[:, 2].astype(jnp.int32).reshape(-1)
    attn_all = attn_all.reshape(width, -1)
    qkv_width = width + 2 * KVW
    w_qkv, w_out = attn_all[:, :qkv_width], attn_all[:, qkv_width : qkv_width + width]
    b_qkv = jnp.concatenate([b_query, b_key, b_value])
    own_ff = w_down.shape[0]
    w_down = jnp.pad(w_down, ((0, half - own_ff), (0, 0)))

    cosine, sine_table = rope_tables(positions)
    hidden_wide = hidden_in.astype(F32)
    normed_wide, factor_one = norm_rows(hidden_wide, gain_one)
    normed_one = normed_wide.astype(BF16)
    lin = dot(normed_one, w_qkv) + b_qkv
    turned = rotate(
        lin[:, : width + KVW].reshape(count, HEADS + KV_HEADS, HEAD_DIM), cosine, sine_table
    ).astype(BF16).reshape(count, width + KVW)
    query_heads = heads_of(turned[:, :width])
    key_value = jnp.concatenate([turned[:, width:], lin[:, width + KVW :].astype(BF16)], axis=1)
    key_value = gather_ctx(key_value, 2, "gather_keys").reshape(-1, 2 * KVW)
    key_heads, value_heads = kv_heads_of(key_value[:, :KVW]), kv_heads_of(key_value[:, KVW:])
    allowed = (key_pos[None, :] <= positions[:, None]) & (key_doc[None, :] == doc_ids[:, None])
    allowed = jnp.tile(allowed, (GROUPS, 1))
    scores = jnp.einsum("jqd,jkd->jqk", query_heads, key_heads, preferred_element_type=F32)
    scores = jnp.where(allowed[None], scores * INV_ROOT, MASKED)
    probs = jax.nn.softmax(scores, axis=-1)
    attn_probs = probs.astype(BF16)
    attn_out = rows_of(
        jnp.einsum("jqk,jkd->jqd", attn_probs, value_heads, preferred_element_type=F32)
    ).astype(BF16)
    residual = hidden_wide + dot(attn_out, w_out)

    normed_mid, factor_two = norm_rows(residual, gain_two)
    normed_two = by_batch(normed_mid.astype(BF16), b, n_batch)
    normed_two = gather_ctx(normed_two, 3, "gather_tokens").reshape(-1, width)
    gate_up = dot(normed_two, w_gate_up)
    gate_lin, up_lin = gate_up[:, :half], gate_up[:, half:]
    sigmoid_gate = jax.nn.sigmoid(gate_lin)
    mixed_rows = (gate_lin * sigmoid_gate * up_lin).astype(BF16)
    d_mixed = times_transposed(out_grad_all, w_down)
    d_gate = d_mixed * up_lin * sigmoid_gate * (1.0 + gate_lin * (1.0 - sigmoid_gate))
    d_up = d_mixed * (gate_lin * sigmoid_gate)
    d_gate_up = jnp.concatenate([d_gate.astype(BF16), d_up.astype(BF16)], axis=1)
    d_normed_two = scatter_ctx(
        times_transposed(d_gate_up, w_gate_up).astype(BF16), 4, "scatter_tokens"
    )
    d_normed_two = by_batch(d_normed_two, b, n_batch)
    ff_out = lax.psum_scatter(
        dot(mixed_rows, w_down).astype(BF16), "ctx", scatter_dimension=0, tiled=True
    )
    hidden_out = (residual + ff_out.astype(F32)).astype(BF16)
    down_grad_all = contract_rows(mixed_rows, out_grad_all)[:own_ff].reshape(n_batch, -1, width)
    down_grad = sum_by_batch(lambda k: lax.dynamic_index_in_dim(down_grad_all, b ^ k, 0, False))
    gate_up_grad_all = contract_rows(normed_two, d_gate_up).reshape(n_batch, -1, 2 * half)
    gate_up_grad = sum_by_batch(lambda k: gate_up_grad_all[k]).astype(BF16)

    d_residual_norm, gain_two_grad = norm_back(residual, factor_two, gain_two, d_normed_two)
    d_residual = out_grad.astype(F32) + d_residual_norm
    d_branch = d_residual.astype(BF16)
    out_proj_grad = contract_rows(attn_out, d_branch)
    grad_heads = heads_of(times_transposed(d_branch, w_out).astype(BF16))
    d_probs = jnp.einsum("jqd,jkd->jqk", grad_heads, value_heads, preferred_element_type=F32)
    row_delta = jnp.sum(probs * d_probs, axis=-1, keepdims=True)
    d_scores = (probs * (d_probs - row_delta)).astype(BF16)
    d_queries = rows_of(
        jnp.einsum("jqk,jkd->jqd", d_scores, key_heads, preferred_element_type=F32) * INV_ROOT
    )
    d_keys = jnp.einsum("jqk,jqd->kjd", d_scores, query_heads, preferred_element_type=F32) * INV_ROOT
    d_values = jnp.einsum("jqk,jqd->kjd", attn_probs, grad_heads, preferred_element_type=F32)
    d_key_value = jnp.concatenate([d_keys.reshape(-1, KVW), d_values.reshape(-1, KVW)], axis=1)
    d_key_value = scatter_ctx(d_key_value.astype(BF16), 5, "scatter_keys")
    d_turned = jnp.concatenate([d_queries, d_key_value[:, :KVW]], axis=1)
    d_turned = rotate_back(
        d_turned.reshape(count, HEADS + KV_HEADS, HEAD_DIM), cosine, sine_table
    ).reshape(count, width + KVW)
    d_lin = jnp.concatenate([d_turned, d_key_value[:, KVW:]], axis=1).astype(BF16)
    qkv_grad = contract_rows(normed_one, d_lin)
    bias_grad = jnp.sum(d_lin.astype(F32), axis=0)
    d_normed_one = times_transposed(d_lin, w_qkv)
    d_hidden_norm, gain_one_grad = norm_back(hidden_wide, factor_one, gain_one, d_normed_one)
    hidden_grad = d_residual + d_hidden_norm

    sums = (
        gain_one_grad,
        gain_two_grad,
        bias_grad[:width],
        bias_grad[width : width + KVW],
        bias_grad[width + KVW :],
    )
    attn_grads = jnp.concatenate(
        [
            qkv_grad.astype(BF16).reshape(n_all, rows, -1),
            out_proj_grad.astype(BF16).reshape(n_all, rows, -1),
            vector_rows(sums, rows, n_all).astype(BF16),
        ],
        axis=2,
    ).reshape(n_batch, n_ctx, rows, -1)
    attn_grads, gate_up_grad = collect(
        attn_grads, gate_up_grad.reshape(n_ctx, rows, -1), 6, "collect_grads"
    )
    gate_up_grad = gate_up_grad.astype(F32)
    gate_grad = unpack_columns(gate_up_grad[:, :, :half], n_batch, hidden_ff)
    up_grad = unpack_columns(gate_up_grad[:, :, half:], n_batch, hidden_ff)
    sums = attn_grads[:8, own.shape[1] - 128 :]
    gain_one_grad, gain_two_grad, query_bias_grad, key_bias_grad, value_bias_grad = (
        sums[i, : part.shape[0]]
        for i, part in enumerate((attn_gain, mlp_gain, q_bias, k_bias, v_bias))
    )
    at_key, at_value, at_out = width, width + KVW, width + 2 * KVW
    return (
        hidden_out,
        hidden_grad,
        gain_one_grad,
        attn_grads[:, :at_key],
        query_bias_grad,
        attn_grads[:, at_key:at_value],
        key_bias_grad,
        attn_grads[:, at_value:at_out],
        value_bias_grad,
        attn_grads[:, at_out : at_out + width],
        gain_two_grad,
        gate_grad,
        up_grad,
        down_grad,
    )


def solution(mesh):
    matrix, vector = P(ALL, None), P(ALL)
    placed = (
        (matrix, vector, vector, vector, matrix, vector, matrix, vector)
        + (matrix, vector, matrix, vector, matrix, matrix, matrix, matrix)
    )
    results = (matrix, matrix) + (vector, matrix) * 4 + (vector, matrix, matrix, matrix)
    return jax.shard_map(local, mesh=mesh, in_specs=placed, out_specs=results, check_vma=False)
```

```python
import functools
import math

import jax
import jax.numpy as jnp
from jax import lax
from jax.experimental import pallas as pl
from jax.experimental.pallas import tpu as pltpu
from jax.sharding import PartitionSpec as P

HEADS = 12
KV_HEADS = 2
GROUPS = HEADS // KV_HEADS
HEAD_DIM = 128
KVW = KV_HEADS * HEAD_DIM
INV_ROOT = HEAD_DIM ** (-0.5)
EPSILON = 1e-06
ROPE_BASE = 10000.0
MASKED = -1e30
ALL = ("batch", "ctx")
F32 = jnp.float32
BF16 = jnp.bfloat16
MESH = pl.DeviceIdType.MESH
ANYWHERE = pl.BlockSpec(memory_space=pl.ANY)
IN_VMEM = pl.BlockSpec(memory_space=pltpu.VMEM)
DMA = pltpu.SemaphoreType.DMA


def rope_tables(positions):
    half_dim = HEAD_DIM // 2
    inverse_freq = jnp.exp(
        jnp.arange(half_dim, dtype=F32) * (-2.0 * math.log(ROPE_BASE) / HEAD_DIM)
    )
    angles = positions.astype(F32)[:, None] * inverse_freq[None, :]
    angles = jnp.concatenate([angles, angles], axis=1)
    return (jnp.cos(angles), jnp.sin(angles))


def dot(lhs, rhs):
    return jnp.dot(lhs, rhs, preferred_element_type=F32)


def contract_rows(lhs, rhs):
    return lax.dot_general(lhs, rhs, (((0,), (0,)), ((), ())), preferred_element_type=F32)


def times_transposed(lhs, rhs):
    return lax.dot_general(lhs, rhs, (((1,), (1,)), ((), ())), preferred_element_type=F32)


def lanes(width):
    return -(-width // 128) * 128


def greet(devices):
    barrier = pltpu.get_barrier_semaphore()
    for device in devices:
        pl.semaphore_signal(barrier, inc=1, device_id=device, device_id_type=MESH)
    pl.semaphore_wait(barrier, len(devices))


def remote(source, target, send, receive, device):
    return pltpu.make_async_remote_copy(
        src_ref=source,
        dst_ref=target,
        send_sem=send,
        recv_sem=receive,
        device_id=device,
        device_id_type=MESH,
    )


def lasting(microseconds):
    return pl.CostEstimate(flops=0, bytes_accessed=int(3.3e6 * microseconds), transcendentals=0)


def gather_kernel(line_len, own, out, own_sem, line_sems, pair_sems):
    b, c = lax.axis_index("batch"), lax.axis_index("ctx")
    line, pair = c // 2, c % 2
    ahead = (b, 2 * lax.rem(line + 1, line_len) + pair)
    behind = (b, 2 * lax.rem(line + line_len - 1, line_len) + pair)
    across = (b, c ^ 1)
    greet((ahead, behind, across))
    keep = pltpu.make_async_copy(own, out.at[c], own_sem)
    keep.start()
    on_line, on_pair = [], []
    for step in range(line_len):
        at = 2 * lax.rem(line - step + line_len, line_len) + pair
        block = own if step == 0 else out.at[at]
        if step > 0:
            on_line[step - 1].wait_recv()
        if step < line_len - 1:
            copy = remote(block, out.at[at], line_sems.at[0, step], line_sems.at[1, step], ahead)
            copy.start()
            on_line.append(copy)
        copy = remote(block, out.at[at], pair_sems.at[0, step], pair_sems.at[1, step], across)
        copy.start()
        on_pair.append(copy)
    for copy in on_pair:
        copy.wait()
    for copy in on_line:
        copy.wait_send()
    keep.wait()


def gather_ctx(block, collective_id, name):
    n_ctx = lax.axis_size("ctx")
    line_len = n_ctx // 2
    return pl.pallas_call(
        functools.partial(gather_kernel, line_len),
        out_shape=jax.ShapeDtypeStruct((n_ctx,) + block.shape, block.dtype),
        in_specs=[ANYWHERE],
        out_specs=ANYWHERE,
        scratch_shapes=[DMA(()), DMA((2, line_len)), DMA((2, line_len))],
        compiler_params=pltpu.CompilerParams(collective_id=collective_id, has_side_effects=True),
        cost_estimate=lasting(20),
        name=name,
    )(block)


def scatter_kernel(line_len, many, *refs):
    parts, outs = refs[:many], refs[many : 2 * many]
    pair_in, line_in, line_out = (refs[(2 + i) * many : (3 + i) * many] for i in range(3))
    pair_sems, line_sems = refs[5 * many :]
    b, c = lax.axis_index("batch"), lax.axis_index("ctx")
    line, pair = c // 2, c % 2
    ahead = (b, 2 * lax.rem(line + 1, line_len) + pair)
    behind = (b, 2 * lax.rem(line + line_len - 1, line_len) + pair)
    across = (b, c ^ 1)
    greet((ahead, behind, across))

    def to(step):
        return 2 * lax.rem(line - 1 - step + line_len, line_len)

    sent, given = [], []
    for i in range(many):
        for step in range(line_len):
            copy = remote(
                parts[i].at[to(step) + 1 - pair],
                pair_in[i].at[step],
                pair_sems.at[0, i, step],
                pair_sems.at[1, i, step],
                across,
            )
            copy.start()
            given.append(copy)
    for i in range(many):
        for step in range(line_len):
            given[i * line_len + step].wait_recv()
            total = parts[i][to(step) + pair].astype(F32) + pair_in[i][step].astype(F32)
            if step > 0:
                passed.wait_recv()
                total = total + line_in[i][step - 1].astype(F32)
            if step < line_len - 1:
                line_out[i][step] = total.astype(BF16)
                passed = remote(
                    line_out[i].at[step],
                    line_in[i].at[step],
                    line_sems.at[0, i, step],
                    line_sems.at[1, i, step],
                    ahead,
                )
                passed.start()
                sent.append(passed)
            else:
                outs[i][...] = total
    for copy in given + sent:
        copy.wait_send()


def scatter_ctx(parts, collective_id, name):
    n_ctx = lax.axis_size("ctx")
    line_len, many = n_ctx // 2, len(parts)
    blocks = [(part.shape[0] // n_ctx,) + part.shape[1:] for part in parts]

    def room(size):
        return [pltpu.VMEM((size,) + block, BF16) for block in blocks]

    return pl.pallas_call(
        functools.partial(scatter_kernel, line_len, many),
        out_shape=[jax.ShapeDtypeStruct(block, F32) for block in blocks],
        in_specs=[IN_VMEM] * many,
        out_specs=[IN_VMEM] * many,
        scratch_shapes=[
            *room(line_len),
            *room(line_len - 1),
            *room(line_len - 1),
            DMA((2, many, line_len)),
            DMA((2, many, line_len)),
        ],
        compiler_params=pltpu.CompilerParams(
            collective_id=collective_id, has_side_effects=True, vmem_limit_bytes=60 * 2**20
        ),
        cost_estimate=lasting(40),
        name=name,
    )(*[part.reshape((n_ctx,) + block) for part, block in zip(parts, blocks)])


def spread_kernel(
    line_len, q_weight, k_weight, v_weight, o_weight, small, gate, up, out, columns_out, own,
    columns, own_sem, line_sems, pair_sems, chip_sems, core_sems, column_sems,
):
    b, c = lax.axis_index("batch"), lax.axis_index("ctx")
    n_ctx = 2 * line_len
    line, pair = c // 2, c % 2
    ahead = (b, 2 * lax.rem(line + 1, line_len) + pair)
    across, chip, core = (b, c ^ 1), (b ^ 2, c), (b ^ 1, c)
    others = [(b, lax.rem(c + k, n_ctx)) for k in range(1, n_ctx)]
    at = 0
    for part in (q_weight, k_weight, v_weight, o_weight, small):
        own[:, at : at + part.shape[1]] = part[...]
        at += part.shape[1]
    greet([chip, core] + others)
    keep = [pltpu.make_async_copy(own, out.at[b, c], own_sem.at[0])]
    keep[0].start()

    def pack():
        n_batch, half = out.shape[0], columns.shape[2] // 2
        piece = gate.shape[1] // (n_batch * n_ctx)
        for first, weight in ((0, gate), (half, up)):
            if n_batch * piece < half:
                columns[:, :, first + half - 128 : first + half] = jnp.zeros(
                    (n_ctx, columns.shape[1], 128), BF16
                )
            for k in range(n_batch):
                for i in range(n_ctx):
                    to = (k * n_ctx + i) * piece
                    at = first + k * piece
                    columns[i, :, at : at + piece] = weight[:, to : to + piece]
        keep.append(pltpu.make_async_copy(columns.at[c], columns_out.at[c], own_sem.at[1]))
        keep[1].start()

    def place(step, side):
        return 2 * lax.rem(line - step + line_len, line_len) + side

    def hand(block, to_b, to_c, sems, index, device):
        copy = remote(block, out.at[to_b, to_c], sems.at[0, index], sems.at[1, index], device)
        copy.start()
        return copy

    on_line, on_pair, on_chip, on_core, on_columns = [], [], [], [], []
    for step in range(line_len):
        at = place(step, pair)
        block = own if step == 0 else out.at[b, at]
        if step > 0:
            on_line[step - 1].wait_recv()
        if step < line_len - 1:
            on_line.append(hand(block, b, at, line_sems, step, ahead))
        on_pair.append(hand(block, b, at, pair_sems, step, across))
        on_chip.append(hand(block, b, at, chip_sems, step, chip))
        on_core.append(hand(block, b, at, core_sems, step, core))
        if step == 0:
            pack()
    for k, device in enumerate(others):
        copy = remote(
            columns.at[device[1]],
            columns_out.at[c],
            column_sems.at[0, k],
            column_sems.at[1, k],
            device,
        )
        copy.start()
        on_columns.append(copy)
    for step in range(line_len):
        at = place(step, 1 - pair)
        on_pair[step].wait_recv()
        on_chip.append(hand(out.at[b, at], b, at, chip_sems, line_len + step, chip))
        on_core.append(hand(out.at[b, at], b, at, core_sems, line_len + step, core))
    for index in range(n_ctx):
        at = place(index % line_len, pair if index < line_len else 1 - pair)
        on_chip[index].wait_recv()
        on_core.append(hand(out.at[b ^ 2, at], b ^ 2, at, core_sems, n_ctx + index, core))
    for copy in on_core + on_columns:
        copy.wait()
    for copy in on_line + on_pair + on_chip:
        copy.wait_send()
    for copy in keep:
        copy.wait()


def spread(matrices, gate, up, collective_id, name):
    n_batch, n_ctx = lax.axis_size("batch"), lax.axis_size("ctx")
    line_len = n_ctx // 2
    rows = gate.shape[0]
    own = (rows, sum(matrix.shape[1] for matrix in matrices))
    columns = (n_ctx, rows, 2 * lanes(gate.shape[1] // n_ctx))
    return pl.pallas_call(
        functools.partial(spread_kernel, line_len),
        out_shape=(
            jax.ShapeDtypeStruct((n_batch, n_ctx) + own, BF16),
            jax.ShapeDtypeStruct(columns, BF16),
        ),
        in_specs=[IN_VMEM] * 7,
        out_specs=(ANYWHERE, ANYWHERE),
        scratch_shapes=[
            pltpu.VMEM(own, BF16),
            pltpu.VMEM(columns, BF16),
            DMA((2,)),
            DMA((2, line_len)),
            DMA((2, line_len)),
            DMA((2, n_ctx)),
            DMA((2, 2 * n_ctx)),
            DMA((2, n_ctx)),
        ],
        compiler_params=pltpu.CompilerParams(
            collective_id=collective_id, has_side_effects=True, vmem_limit_bytes=40 * 2**20
        ),
        cost_estimate=lasting(75),
        name=name,
    )(*matrices, gate, up)


def collect_kernel(line_len, *refs):
    grads, (sums_in, columns) = refs[:2], refs[2:4]
    outs, (sums_out, columns_out) = refs[4:6], refs[6:8]
    core_in, chip_in, pair_in, line_in, chip_out, pair_out, line_out = [
        refs[8 + 2 * i : 10 + 2 * i] for i in range(7)
    ]
    sums_got, sums_mine, own_sem = refs[22:25]
    core_sems, chip_sems, pair_sems, line_sems, column_sems, sums_sems = refs[25:]
    b, c = lax.axis_index("batch"), lax.axis_index("ctx")
    n_ctx = 2 * line_len
    line, pair = c // 2, c % 2
    ahead = (b, 2 * lax.rem(line + 1, line_len) + pair)
    across, chip, core = (b, c ^ 1), (b ^ 2, c), (b ^ 1, c)
    others = [(b, lax.rem(c + k, n_ctx)) for k in range(1, n_ctx)]
    on_same_line = others[1::2]
    greet([chip, core] + others)
    keep = pltpu.make_async_copy(columns.at[c], columns_out.at[c], own_sem)
    keep.start()

    def place(index):
        step, side = index // 2, index % 2
        to = lax.rem(line - 1 - step + line_len, line_len)
        return 2 * to + (1 - pair if side == 0 else pair)

    waits = []

    def send(block, target, sems, index, device):
        copy = remote(block, target, sems.at[0, index], sems.at[1, index], device)
        copy.start()
        waits.append(copy)
        return copy

    def start_sums(index, device):
        copy = remote(
            sums_mine, sums_got.at[index], sums_sems.at[0, index], sums_sems.at[1, index], device
        )
        copy.start()
        return copy

    def add_sums(index, copy):
        copy.wait()
        sums_mine[...] += sums_got[index]

    sums_mine[...] = sums_in[...]
    by_core = start_sums(0, core)
    to_core = [[], []]
    for index in range(2 * n_ctx):
        row = b ^ 3 if index < n_ctx else b ^ 1
        for i in range(2):
            to_core[i].append(
                send(
                    grads[i].at[row, place(index % n_ctx)],
                    core_in[i].at[index],
                    core_sems.at[i],
                    index,
                    core,
                )
            )
    add_sums(0, by_core)
    by_chip = start_sums(1, chip)
    on_columns = []
    for k, device in enumerate(others):
        copy = remote(
            columns.at[device[1]],
            columns_out.at[c],
            column_sems.at[0, k],
            column_sems.at[1, k],
            device,
        )
        copy.start()
        on_columns.append(copy)
    to_chip = [[], []]
    for index in range(n_ctx):
        for i in range(2):
            to_core[i][index].wait_recv()
            total = grads[i][b ^ 2, place(index)].astype(F32) + core_in[i][index].astype(F32)
            chip_out[i][index] = total.astype(BF16)
            to_chip[i].append(
                send(chip_out[i].at[index], chip_in[i].at[index], chip_sems.at[i], index, chip)
            )
    add_sums(1, by_chip)
    by_pair = start_sums(2, across)

    def mine(i, index):
        to_core[i][n_ctx + index].wait_recv()
        to_chip[i][index].wait_recv()
        return (
            grads[i][b, place(index)].astype(F32)
            + core_in[i][n_ctx + index].astype(F32)
            + chip_in[i][index].astype(F32)
        )

    to_pair, to_line = [[], []], [[], []]
    for step in range(line_len):
        for i in range(2):
            pair_out[i][step] = mine(i, 2 * step).astype(BF16)
            to_pair[i].append(
                send(pair_out[i].at[step], pair_in[i].at[step], pair_sems.at[i], step, across)
            )
        if step == 0:
            add_sums(2, by_pair)
            own_sums = [
                send(sums_mine, sums_got.at[3 + k], sums_sems, 3 + k, device)
                for k, device in enumerate(on_same_line)
            ]
        for i in range(2):
            total = mine(i, 2 * step + 1)
            to_pair[i][step].wait_recv()
            total = total + pair_in[i][step].astype(F32)
            if step > 0:
                to_line[i][step - 1].wait_recv()
                total = total + line_in[i][step - 1].astype(F32)
            if step < line_len - 1:
                line_out[i][step] = total.astype(BF16)
                to_line[i].append(
                    send(line_out[i].at[step], line_in[i].at[step], line_sems.at[i], step, ahead)
                )
            else:
                outs[i][...] = total
    total = sums_mine[...]
    for k, copy in enumerate(own_sums):
        copy.wait_recv()
        total = total + sums_got[3 + k]
    sums_out[...] = total
    for copy in on_columns:
        copy.wait()
    for copy in waits:
        copy.wait_send()
    keep.wait()


def collect(grads, sums, columns, collective_id, name):
    n_batch, n_ctx = lax.axis_size("batch"), lax.axis_size("ctx")
    line_len = n_ctx // 2
    blocks = [grad.shape[2:] for grad in grads]

    def room(size):
        return [pltpu.VMEM((size,) + block, BF16) for block in blocks]

    return pl.pallas_call(
        functools.partial(collect_kernel, line_len),
        out_shape=(
            *[jax.ShapeDtypeStruct(block, F32) for block in blocks],
            jax.ShapeDtypeStruct(sums.shape, F32),
            jax.ShapeDtypeStruct(columns.shape, BF16),
        ),
        in_specs=[IN_VMEM] * 3 + [ANYWHERE],
        out_specs=(IN_VMEM,) * 3 + (ANYWHERE,),
        scratch_shapes=[
            *room(2 * n_ctx),
            *room(n_ctx),
            *room(line_len),
            *room(line_len - 1),
            *room(n_ctx),
            *room(line_len),
            *room(line_len - 1),
            pltpu.VMEM((2 + line_len,) + sums.shape, F32),
            pltpu.VMEM(sums.shape, F32),
            DMA(()),
            DMA((2, 2, 2 * n_ctx)),
            DMA((2, 2, n_ctx)),
            DMA((2, 2, line_len)),
            DMA((2, 2, line_len)),
            DMA((2, n_ctx)),
            DMA((2, 2 + line_len)),
        ],
        compiler_params=pltpu.CompilerParams(
            collective_id=collective_id, has_side_effects=True, vmem_limit_bytes=60 * 2**20
        ),
        cost_estimate=lasting(70),
        name=name,
    )(*grads, sums, columns)


def row_scale(values):
    return lax.rsqrt(jnp.mean(values * values, axis=-1, keepdims=True) + EPSILON)


def turn_head(values, cosine, signed_sine, back=False):
    turned = pltpu.roll(values, HEAD_DIM // 2, 1) * signed_sine
    return values * cosine - turned if back else values * cosine + turned


def whole(*shape):
    return pl.BlockSpec(shape, lambda j: (0,) * len(shape))


def project_kernel(hidden, gain, weight, bias, cosine, signed_sine, normed, query, key_value, kept):
    j = pl.program_id(0)

    @pl.when(j == 0)
    def _():
        values = hidden[...].astype(F32)
        kept[...] = (values * row_scale(values) * gain[...]).astype(BF16)
        normed[...] = kept[...]

    lin = dot(kept[...], weight[...]) + bias[...]
    tables = cosine[...], signed_sine[...]
    heads = [lin[:, i * HEAD_DIM : (i + 1) * HEAD_DIM] for i in range(4)]

    @pl.when(j < 3)
    def _():
        for i in range(4):
            turned = turn_head(heads[i], *tables)
            query[:, i * HEAD_DIM : (i + 1) * HEAD_DIM] = turned.astype(BF16)

    @pl.when(j == 3)
    def _():
        for i in range(4):
            value = turn_head(heads[i], *tables) if i < KV_HEADS else heads[i]
            key_value[:, i * HEAD_DIM : (i + 1) * HEAD_DIM] = value.astype(BF16)


def project(hidden, gain, weights, bias, tables):
    count, width = hidden.shape
    wide = 2 * KVW
    table = whole(count, HEAD_DIM)
    return pl.pallas_call(
        project_kernel,
        grid=(4,),
        out_shape=(
            jax.ShapeDtypeStruct((count, width), BF16),
            jax.ShapeDtypeStruct((count, width), BF16),
            jax.ShapeDtypeStruct((count, wide), BF16),
        ),
        in_specs=[
            whole(count, width),
            whole(1, width),
            pl.BlockSpec((width, wide), lambda j: (0, j)),
            pl.BlockSpec((1, wide), lambda j: (0, j)),
            table,
            table,
        ],
        out_specs=(
            whole(count, width),
            pl.BlockSpec((count, wide), lambda j: (0, jnp.minimum(j, 2))),
            whole(count, wide),
        ),
        scratch_shapes=[pltpu.VMEM((count, width), BF16)],
        compiler_params=pltpu.CompilerParams(vmem_limit_bytes=40 * 2**20),
        cost_estimate=lasting(4),
        name="project",
    )(hidden, gain, weights, bias, *tables)


def mark_allowed(key_pos, key_doc, own_pos, own_doc, allowed):
    count = own_pos.shape[1]
    pos_column, doc_column = key_pos[...].T, key_doc[...].T
    for i in range(key_pos.shape[0]):
        seen = (pos_column[:, i : i + 1] <= own_pos[...]) & (doc_column[:, i : i + 1] == own_doc[...])
        allowed[i * count : (i + 1) * count] = jnp.where(seen, 1.0, 0.0)


def stack_heads(block, group):
    return jnp.concatenate(
        [block[:, i * HEAD_DIM : (i + 1) * HEAD_DIM] for i in range(group)], axis=0
    )


def lay_heads(stacked, group):
    count = stacked.shape[0] // group
    return jnp.concatenate([stacked[i * count : (i + 1) * count] for i in range(group)], axis=1)


def probabilities(keys, queries, allowed, group):
    scores = times_transposed(keys, queries) * INV_ROOT
    seen = jnp.concatenate([allowed[...]] * group, axis=1) > 0.0
    scores = jnp.where(seen, scores, MASKED)
    raised = jnp.exp(scores - jnp.max(scores, axis=0, keepdims=True))
    return raised * (1.0 / jnp.sum(raised, axis=0, keepdims=True))


def attend_kernel(
    group, last, query, keys, values, out_0, out_1, out_2, key_pos, key_doc, own_pos, own_doc,
    hidden, gain, attn_out, residual, normed, total, allowed,
):
    j = pl.program_id(0)

    @pl.when(j == 0)
    def _():
        total[...] = hidden[...].astype(F32)
        mark_allowed(key_pos, key_doc, own_pos, own_doc, allowed)

    probs = probabilities(keys[...], stack_heads(query[...], group), allowed, group)
    result = contract_rows(values[...], probs.astype(BF16)).T
    block = lay_heads(result, group).astype(BF16)
    attn_out[...] = block
    for t, weight in enumerate((out_0, out_1, out_2)):
        total[:, t * 512 : (t + 1) * 512] += dot(block, weight[...])

    @pl.when(j == last)
    def _():
        values = total[...]
        residual[...] = values
        normed[...] = (values * row_scale(values) * gain[...]).astype(BF16)


def head_specs(count, width, keys, group, weights_at):
    rows = group * HEAD_DIM
    per_key = GROUPS // group
    query = pl.BlockSpec((count, rows), lambda j: (0, j))
    heads = [
        pl.BlockSpec((keys, HEAD_DIM), lambda j, i=i: (0, KV_HEADS * i + j // per_key))
        for i in range(2)
    ]
    out = [
        pl.BlockSpec((rows, 512), lambda j, t=t: (j, weights_at // 512 + t))
        for t in range(width // 512)
    ]
    places = [whole(keys // count, count)] * 2 + [whole(1, count)] * 2
    return query, heads, out, places


def attend(query, key_value, weights, places, hidden, gain):
    count, width = hidden.shape
    keys = key_value.shape[0]
    group = 3 if keys <= 1024 else 1
    steps = HEADS // group
    query_spec, head_spec, out_spec, place_spec = head_specs(
        count, width, keys, group, width + 2 * KVW
    )
    return pl.pallas_call(
        functools.partial(attend_kernel, group, steps - 1),
        grid=(steps,),
        out_shape=(
            jax.ShapeDtypeStruct((count, width), BF16),
            jax.ShapeDtypeStruct((count, width), F32),
            jax.ShapeDtypeStruct((count, width), BF16),
        ),
        in_specs=[query_spec, *head_spec, *out_spec, *place_spec]
        + [whole(count, width), whole(1, width)],
        out_specs=(query_spec, whole(count, width), whole(count, width)),
        scratch_shapes=[pltpu.VMEM((count, width), F32), pltpu.VMEM((keys, count), F32)],
        compiler_params=pltpu.CompilerParams(vmem_limit_bytes=56 * 2**20),
        cost_estimate=lasting(10),
        name="attend",
    )(query, key_value, key_value, *[weights] * 3, *places, hidden, gain)


def attend_back_kernel(
    group, per_key, query, keys, values, out_0, out_1, out_2, key_pos, key_doc, own_pos, own_doc,
    attn_out, residual, gain, out_grad, d_normed, cosine, signed_sine, d_query, d_key_value,
    o_grad, d_residual, gain_grad, branch, allowed, key_sum, value_sum,
):
    j = pl.program_id(0)

    @pl.when(j == 0)
    def _():
        rows, grads = residual[...], d_normed[...]
        factor = row_scale(rows)
        scaled = grads * gain[...]
        gain_grad[...] = jnp.sum(grads * rows * factor, axis=0, keepdims=True)
        total = out_grad[...].astype(F32) + (
            factor * scaled
            - rows * (factor * factor * factor) * jnp.mean(scaled * rows, axis=-1, keepdims=True)
        )
        d_residual[...] = total
        branch[...] = total.astype(BF16)
        mark_allowed(key_pos, key_doc, own_pos, own_doc, allowed)

    @pl.when(lax.rem(j, per_key) == 0)
    def _():
        key_sum[...] = jnp.zeros_like(key_sum)
        value_sum[...] = jnp.zeros_like(value_sum)

    o_grad[...] = contract_rows(attn_out[...], branch[...]).astype(BF16)
    d_attn = sum(
        times_transposed(branch[:, t * 512 : (t + 1) * 512], weight[...])
        for t, weight in enumerate((out_0, out_1, out_2))
    ).astype(BF16)
    grads = stack_heads(d_attn, group)
    queries = stack_heads(query[...], group)
    probs = probabilities(keys[...], queries, allowed, group)
    d_probs = times_transposed(values[...], grads)
    delta = jnp.sum(probs * d_probs, axis=0, keepdims=True)
    d_scores = (probs * (d_probs - delta)).astype(BF16)
    key_sum[...] += dot(d_scores, queries)
    value_sum[...] += dot(probs.astype(BF16), grads)
    result = contract_rows(keys[...], d_scores).T * INV_ROOT
    count = result.shape[0] // group
    for i in range(group):
        head = turn_head(
            result[i * count : (i + 1) * count], cosine[...], signed_sine[...], back=True
        )
        d_query[:, i * HEAD_DIM : (i + 1) * HEAD_DIM] = head.astype(BF16)

    @pl.when(lax.rem(j, per_key) == per_key - 1)
    def _():
        at = pl.multiple_of(j // per_key * HEAD_DIM, HEAD_DIM)
        d_key_value[:, pl.ds(at, HEAD_DIM)] = (key_sum[...] * INV_ROOT).astype(BF16)
        d_key_value[:, pl.ds(KVW + at, HEAD_DIM)] = value_sum[...].astype(BF16)


def attend_back(query, key_value, weights, places, attn_out, residual, gain, out_grad, d_normed, tables):
    count, width = query.shape
    keys = key_value.shape[0]
    group = 3 if keys <= 1024 else 1
    steps = HEADS // group
    query_spec, head_spec, out_spec, place_spec = head_specs(
        count, width, keys, group, width + 2 * KVW
    )
    rows, table = whole(count, width), whole(count, HEAD_DIM)
    return pl.pallas_call(
        functools.partial(attend_back_kernel, group, GROUPS // group),
        grid=(steps,),
        out_shape=(
            jax.ShapeDtypeStruct((count, width), BF16),
            jax.ShapeDtypeStruct((keys, 2 * KVW), BF16),
            jax.ShapeDtypeStruct((width, width), BF16),
            jax.ShapeDtypeStruct((count, width), F32),
            jax.ShapeDtypeStruct((1, width), F32),
        ),
        in_specs=[query_spec, *head_spec, *out_spec, *place_spec, query_spec]
        + [rows, whole(1, width), rows, rows, table, table],
        out_specs=(
            query_spec,
            whole(keys, 2 * KVW),
            pl.BlockSpec((group * HEAD_DIM, width), lambda j: (j, 0)),
            rows,
            whole(1, width),
        ),
        scratch_shapes=[
            pltpu.VMEM((count, width), BF16),
            pltpu.VMEM((keys, count), F32),
            pltpu.VMEM((keys, HEAD_DIM), F32),
            pltpu.VMEM((keys, HEAD_DIM), F32),
        ],
        compiler_params=pltpu.CompilerParams(vmem_limit_bytes=60 * 2**20),
        cost_estimate=lasting(17),
        name="attend_back",
    )(
        query, key_value, key_value, *[weights] * 3, *places, attn_out, residual, gain, out_grad,
        d_normed, *tables,
    )


def project_back_kernel(
    d_query, d_key_value, weight, normed, hidden, gain, d_residual, gain_two_grad, cosine,
    signed_sine, grad, hidden_grad, sums, flipped, total, biases,
):
    j = pl.program_id(0)
    wide = weight.shape[1]

    @pl.when(j == 0)
    def _():
        flipped[...] = normed[...].astype(F32).T.astype(BF16)
        total[...] = jnp.zeros_like(total)
        sums[...] = jnp.zeros_like(sums)

    def add(d_lin):
        grad[...] = dot(flipped[...], d_lin).astype(BF16)
        total[...] += times_transposed(d_lin, weight[...])
        return jnp.sum(d_lin.astype(F32), axis=0, keepdims=True)

    for i in range(3):

        @pl.when(j == i)
        def _():
            sums[1:2, i * wide : (i + 1) * wide] = add(d_query[...])

    @pl.when(j == 3)
    def _():
        heads = [
            turn_head(
                d_key_value[:, i * HEAD_DIM : (i + 1) * HEAD_DIM],
                cosine[...],
                signed_sine[...],
                back=True,
            )
            for i in range(KV_HEADS)
        ]
        d_lin = jnp.concatenate(heads + [d_key_value[:, KVW:]], axis=1).astype(BF16)
        sums[2:3, :wide] = add(d_lin)
        rows, grads = hidden[...].astype(F32), total[...]
        factor = row_scale(rows)
        scaled = grads * gain[...]
        sums[0:1] = jnp.sum(grads * rows * factor, axis=0, keepdims=True)
        sums[3:4] = gain_two_grad[...]
        hidden_grad[...] = d_residual[...] + (
            factor * scaled
            - rows * (factor * factor * factor) * jnp.mean(scaled * rows, axis=-1, keepdims=True)
        )


def project_back(d_query, d_key_value, weights, normed, hidden, gain, d_residual, gain_two_grad, tables):
    count, width = hidden.shape
    wide = 2 * KVW
    rows, table = whole(count, width), whole(count, HEAD_DIM)
    return pl.pallas_call(
        project_back_kernel,
        grid=(4,),
        out_shape=(
            jax.ShapeDtypeStruct((width, width + wide), BF16),
            jax.ShapeDtypeStruct((count, width), F32),
            jax.ShapeDtypeStruct((8, width), F32),
        ),
        in_specs=[
            pl.BlockSpec((count, wide), lambda j: (0, jnp.minimum(j, 2))),
            whole(count, wide),
            pl.BlockSpec((width, wide), lambda j: (0, j)),
            rows,
            rows,
            whole(1, width),
            rows,
            whole(1, width),
            table,
            table,
        ],
        out_specs=(
            pl.BlockSpec((width, wide), lambda j: (0, j)),
            rows,
            whole(8, width),
        ),
        scratch_shapes=[
            pltpu.VMEM((width, count), BF16),
            pltpu.VMEM((count, width), F32),
            pltpu.VMEM((8, wide), F32),
        ],
        compiler_params=pltpu.CompilerParams(vmem_limit_bytes=48 * 2**20),
        cost_estimate=lasting(9),
        name="project_back",
    )(
        d_query, d_key_value, weights, normed, hidden, gain, d_residual, gain_two_grad, *tables
    )


def unpack_kernel(n_batch, piece, packed, gate, up):
    n_ctx, _, both = packed.shape
    for out, first in ((gate, 0), (up, both // 2)):
        for k in range(n_batch):
            for i in range(n_ctx):
                at = first + k * piece
                to = (k * n_ctx + i) * piece
                out[:, to : to + piece] = packed[i, :, at : at + piece].astype(F32)


def unpack(packed, n_batch, width):
    n_ctx, rows, _ = packed.shape
    out = jax.ShapeDtypeStruct((rows, width), F32)
    return pl.pallas_call(
        functools.partial(unpack_kernel, n_batch, width // (n_batch * n_ctx)),
        out_shape=(out, out),
        in_specs=[IN_VMEM],
        out_specs=(IN_VMEM, IN_VMEM),
        compiler_params=pltpu.CompilerParams(vmem_limit_bytes=40 * 2**20),
        cost_estimate=lasting(3),
        name="unpack",
    )(packed)


def mlp_kernel(
    line_len, tile, own_rows, *refs
):
    n_batch, n_ctx = 4, 2 * line_len
    weights, (down, grads_in) = refs[:n_batch], refs[n_batch : n_batch + 2]
    total_out, ff_out, down_out = refs[n_batch + 2 : n_batch + 5]
    grad_outs = refs[n_batch + 5 : 2 * n_batch + 5]
    (
        tokens, gate_up, down_in, grads, mixed, d_gate_up, parts, pair_in, line_in, line_out,
        ff_part, gate_up_grad, down_grad, own, load_sems, store_sems, line_sems, pair_sems,
        back_pair, back_line,
    ) = refs[2 * n_batch + 5 :]
    b, c = lax.axis_index("batch"), lax.axis_index("ctx")
    line, pair = c // 2, c % 2
    ahead = (b, 2 * lax.rem(line + 1, line_len) + pair)
    behind = (b, 2 * lax.rem(line + line_len - 1, line_len) + pair)
    across = (b, c ^ 1)
    count, width = own.shape
    half = gate_up.shape[1] // 2
    own_ff = down.shape[0]
    depth = width // n_batch
    for k in range(n_batch):
        source = pl.ds(pl.multiple_of((b ^ k) * depth, 128), depth)
        own[:, k * depth : (k + 1) * depth] = own_rows[:, source]
    greet((ahead, behind, across))

    def at(step):
        return 2 * lax.rem(line - step + line_len, line_len)

    on_line, on_pair, on_back, on_passed = [], [], [], []

    def forward(step):
        block = own if step == 0 else tokens.at[at(step) + pair]
        target = tokens.at[at(step) + pair]
        if step > 0:
            on_line[step - 1].wait_recv()
        if step < line_len - 1:
            copy = remote(block, target, line_sems.at[0, step], line_sems.at[1, step], ahead)
            copy.start()
            on_line.append(copy)
        copy = remote(block, target, pair_sems.at[0, step], pair_sems.at[1, step], across)
        copy.start()
        on_pair.append(copy)

    forward(0)
    loads = [pltpu.make_async_copy(own, tokens.at[c], load_sems.at[0])]
    for k, weight in enumerate(weights):
        loads.append(
            pltpu.make_async_copy(
                weight, gate_up.at[pl.ds(k * depth, depth)], load_sems.at[1 + k]
            )
        )
    loads.append(
        pltpu.make_async_copy(down, down_in.at[pl.ds(0, own_ff)], load_sems.at[1 + n_batch])
    )
    loads.append(pltpu.make_async_copy(grads_in, grads, load_sems.at[2 + n_batch]))
    for copy in loads:
        copy.start()
    if own_ff < half:
        down_in[own_ff:half] = jnp.zeros((half - own_ff, width), BF16)
    for copy in loads:
        copy.wait()

    def chunk(step):
        first = pl.multiple_of(at(step) * count, 2 * count)
        rows = pl.ds(first, 2 * count)
        block = tokens[pl.ds(at(step), 2)].reshape(2 * count, width)
        grad_block = grads[pl.ds(at(step), 2)].reshape(2 * count, width)

        def columns(index, _):
            low = pl.multiple_of(index * tile, 128)
            high = pl.multiple_of(half + index * tile, 128)
            gate_lin = dot(block, gate_up[:, pl.ds(low, tile)])
            up_lin = dot(block, gate_up[:, pl.ds(high, tile)])
            d_mixed = times_transposed(grad_block, down_in[pl.ds(low, tile)])
            sigmoid = 1.0 / (1.0 + jnp.exp(-gate_lin))
            silu = gate_lin * sigmoid
            mixed[rows, pl.ds(low, tile)] = (silu * up_lin).astype(BF16)
            d_gate = d_mixed * up_lin * sigmoid * (1.0 + gate_lin * (1.0 - sigmoid))
            d_gate_up[rows, pl.ds(low, tile)] = d_gate.astype(BF16)
            d_gate_up[rows, pl.ds(high, tile)] = (d_mixed * silu).astype(BF16)
            return 0

        lax.fori_loop(0, half // tile, columns, 0)

        def features(index, _):
            low = pl.multiple_of(index * depth, 128)
            back = times_transposed(d_gate_up[rows], gate_up[pl.ds(low, depth)])
            parts[pl.ds(at(step), 2), :, pl.ds(low, depth)] = back.astype(BF16).reshape(
                2, count, depth
            )
            return 0

        lax.fori_loop(0, n_batch, features, 0)

    def give(step):
        index = (step + line_len - 1) % line_len
        copy = remote(
            parts.at[at(step) + 1 - pair],
            pair_in.at[index],
            back_pair.at[0, index],
            back_pair.at[1, index],
            across,
        )
        copy.start()
        on_back.append(copy)

    for step in range(line_len):
        if step + 1 < line_len:
            forward(step + 1)
        on_pair[step].wait_recv()
        chunk(step)
        if step > 0:
            give(step)
    give(0)

    def passing(index):
        on_back[index].wait_recv()
        total = parts[at(index + 1) + pair].astype(F32) + pair_in[index].astype(F32)
        if index > 0:
            on_passed[index - 1].wait_recv()
            total = total + line_in[index - 1].astype(F32)
        if index < line_len - 1:
            line_out[index] = total.astype(BF16)
            copy = remote(
                line_out.at[index],
                line_in.at[index],
                back_line.at[0, index],
                back_line.at[1, index],
                ahead,
            )
            copy.start()
            on_passed.append(copy)
        else:
            for k in range(n_batch):
                target = pl.ds(pl.multiple_of((b ^ k) * depth, 128), depth)
                total_out[:, target] = total[:, k * depth : (k + 1) * depth]

    stores = []

    def store(source, target):
        copy = pltpu.make_async_copy(source, target, store_sems.at[len(stores)])
        copy.start()
        stores.append(copy)

    def weight_grad(k):
        block = tokens[:, :, k * depth : (k + 1) * depth].reshape(n_ctx * count, depth)

        def columns(index, _):
            low = pl.multiple_of(index * tile, 128)
            grad = contract_rows(block, d_gate_up[:, pl.ds(low, tile)])
            gate_up_grad[k, :, pl.ds(low, tile)] = grad.astype(BF16)
            return 0

        lax.fori_loop(0, 2 * half // tile, columns, 0)
        store(gate_up_grad.at[k], grad_outs[k])

    def down_grads():
        def columns(index, _):
            low = pl.multiple_of(index * tile, 128)
            grad = contract_rows(
                mixed[:, pl.ds(low, tile)], grads[...].reshape(n_ctx * count, width)
            )
            down_grad[pl.ds(low, tile)] = grad.astype(BF16)
            return 0

        lax.fori_loop(0, half // tile, columns, 0)
        store(down_grad.at[pl.ds(0, own_ff)], down_out)

    def ff_parts():
        def rows(index, _):
            low = pl.multiple_of(index * 2 * count, 2 * count)
            out = dot(mixed[pl.ds(low, 2 * count)], down_in[...])
            ff_part[pl.ds(low, 2 * count)] = out.astype(BF16)
            return 0

        lax.fori_loop(0, line_len, rows, 0)
        store(ff_part, ff_out)

    work = [
        lambda: (weight_grad(1), weight_grad(3)),
        lambda: (weight_grad(2), weight_grad(0)),
        down_grads,
        ff_parts,
    ]
    for index in range(max(line_len, len(work))):
        if index < len(work):
            work[index]()
        if index < line_len:
            passing(index)
    for copy in on_line + on_pair + on_back + on_passed:
        copy.wait_send()
    for copy in stores:
        copy.wait()


def mlp_scratch(n_ctx, n_batch, count, width, half):
    line_len = n_ctx // 2

    def room(*shape):
        return pltpu.VMEM(shape, BF16)

    return [
        room(n_ctx, count, width),
        room(width, 2 * half),
        room(half, width),
        room(n_ctx, count, width),
        room(n_ctx * count, half),
        room(n_ctx * count, 2 * half),
        room(n_ctx, count, width),
        room(line_len, count, width),
        room(line_len - 1, count, width),
        room(line_len - 1, count, width),
        room(n_ctx * count, width),
        room(n_batch, width // n_batch, 2 * half),
        room(half, width),
        room(count, width),
    ]


def mlp(own, weights, down, grads, collective_id, name):
    n_batch, n_ctx = lax.axis_size("batch"), lax.axis_size("ctx")
    line_len = n_ctx // 2
    count, width = own.shape
    half = weights[0].shape[1] // 2
    depth = width // n_batch
    tile = 384 if half % 384 == 0 else 128
    return pl.pallas_call(
        functools.partial(mlp_kernel, line_len, tile),
        out_shape=(
            jax.ShapeDtypeStruct((count, width), F32),
            jax.ShapeDtypeStruct((n_ctx * count, width), BF16),
            jax.ShapeDtypeStruct(down.shape, BF16),
            *[jax.ShapeDtypeStruct((depth, 2 * half), BF16)] * n_batch,
        ),
        in_specs=[IN_VMEM] + [ANYWHERE] * (n_batch + 2),
        out_specs=(IN_VMEM,) + (ANYWHERE,) * (n_batch + 2),
        scratch_shapes=mlp_scratch(n_ctx, n_batch, count, width, half)
        + [
            DMA((3 + n_batch,)),
            DMA((2 + n_batch,)),
            DMA((2, line_len)),
            DMA((2, line_len)),
            DMA((2, line_len)),
            DMA((2, line_len)),
        ],
        compiler_params=pltpu.CompilerParams(
            collective_id=collective_id, has_side_effects=True, vmem_limit_bytes=60 * 2**20
        ),
        cost_estimate=lasting(90),
        name=name,
    )(own, *weights, down, grads.reshape(n_ctx, count, width))


def swap(values, bit):
    size = lax.axis_size("batch")
    return lax.ppermute(values, "batch", [(i, i ^ bit) for i in range(size)])


def by_batch(values, b, n_batch):
    step = values.shape[1] // n_batch
    blocks = [lax.dynamic_slice_in_dim(values, (b ^ k) * step, step, 1) for k in range(n_batch)]
    return jnp.concatenate(blocks, axis=1)


def half_sum(terms):
    passed = swap((terms[2].astype(F32) + swap(terms[3], 1).astype(F32)).astype(BF16), 2)
    return terms[0], swap(terms[1], 1), passed


def mlp_room(n_ctx, n_batch, count, width, half):
    return sum(math.prod(room.shape) for room in mlp_scratch(n_ctx, n_batch, count, width, half))


def mlp_in_steps(normed_two, w_gate_up, w_down, out_grad_all):
    n_ctx = lax.axis_size("ctx")
    w_gate_up = jnp.concatenate(w_gate_up, axis=0)
    half, width = w_gate_up.shape[1] // 2, normed_two.shape[1]
    own_ff = w_down.shape[0]
    w_down = jnp.pad(w_down, ((0, half - own_ff), (0, 0)))
    normed_two = gather_ctx(normed_two, 3, "gather_tokens").reshape(-1, width)
    gate_up = dot(normed_two, w_gate_up)
    gate_lin, up_lin = gate_up[:, :half], gate_up[:, half:]
    sigmoid_gate = jax.nn.sigmoid(gate_lin)
    mixed_rows = (gate_lin * sigmoid_gate * up_lin).astype(BF16)
    d_mixed = times_transposed(out_grad_all, w_down)
    d_gate = d_mixed * up_lin * sigmoid_gate * (1.0 + gate_lin * (1.0 - sigmoid_gate))
    d_up = d_mixed * (gate_lin * sigmoid_gate)
    d_gate_up = jnp.concatenate([d_gate.astype(BF16), d_up.astype(BF16)], axis=1)
    (d_normed_two,) = scatter_ctx(
        [times_transposed(d_gate_up, w_gate_up).astype(BF16)], 4, "scatter_tokens"
    )
    grads = contract_rows(normed_two, d_gate_up).astype(BF16).reshape(4, -1, 2 * half)
    return (
        d_normed_two,
        dot(mixed_rows, w_down).astype(BF16),
        contract_rows(mixed_rows, out_grad_all).astype(BF16)[:own_ff],
        *grads,
    )


def vector_rows(vectors, rows, pieces):
    laid = [
        jnp.pad(v.reshape(pieces, 1, -1), ((0, 0), (0, 0), (0, 128 - v.shape[0] // pieces)))
        for v in vectors
    ]
    return jnp.pad(jnp.concatenate(laid, axis=1), ((0, 0), (0, rows - len(vectors)), (0, 0)))


def local(
    hidden_in,
    positions,
    doc_ids,
    attn_gain,
    q_weight,
    q_bias,
    k_weight,
    k_bias,
    v_weight,
    v_bias,
    o_weight,
    mlp_gain,
    gate_weight,
    up_weight,
    down_weight,
    out_grad,
):
    n_batch, n_ctx = lax.axis_size("batch"), lax.axis_size("ctx")
    n_all = n_batch * n_ctx
    count, width = hidden_in.shape
    hidden_ff = gate_weight.shape[1]

    b = lax.axis_index("batch")
    w_down = lax.all_gather(down_weight, "batch", axis=0, tiled=True)
    out_grad_all = lax.all_gather(out_grad, "ctx", axis=0, tiled=True)
    rows = q_weight.shape[0]
    small = (attn_gain, mlp_gain, q_bias, k_bias, v_bias)
    places = (positions // 64, positions % 64, doc_ids)
    small = vector_rows(small + tuple(row.astype(BF16) for row in places), rows, 1)[0]
    matrices = (q_weight, k_weight, v_weight, o_weight, small)
    attn_all, packed = spread(matrices, gate_weight, up_weight, 1, "spread_weights")
    half = packed.shape[2] // 2
    own_rows = packed.reshape(-1, 2 * half)
    near, far = swap(own_rows, 1), swap(own_rows, 2)
    small = attn_all[:, :, :8, attn_all.shape[3] - 128 :].astype(F32)
    gain_one, gain_two, b_query, b_key, b_value = (
        small[:, :, i, : part.shape[0]].reshape(-1)
        for i, part in enumerate((attn_gain, mlp_gain, q_bias, k_bias, v_bias))
    )
    places = lax.dynamic_index_in_dim(small, b, 0, keepdims=False)[:, 5:8, :count]
    key_pos, key_doc = places[:, 0] * 64 + places[:, 1], places[:, 2]
    attn_all = attn_all.reshape(width, -1)
    b_qkv = jnp.concatenate([b_query, b_key, b_value])

    cosine, sine_table = rope_tables(positions)
    half_lane = jnp.arange(HEAD_DIM) < HEAD_DIM // 2
    tables = cosine, jnp.where(half_lane[None], -sine_table, sine_table)
    normed_one, query, key_value = project(hidden_in, gain_one[None], attn_all, b_qkv[None], tables)
    key_value = gather_ctx(key_value, 2, "gather_keys").reshape(-1, 2 * KVW)
    far, key_value = lax.optimization_barrier((far, key_value))
    w_gate_up = (own_rows, near, far, swap(far, 1))
    places = (
        key_pos, key_doc, positions.astype(F32)[None], doc_ids.astype(F32)[None]
    )
    attn_out, residual, normed_two = attend(
        query, key_value, attn_all, places, hidden_in, gain_two[None]
    )

    fused = 2 * mlp_room(n_ctx, n_batch, count, width, half) < 52 * 2**20
    d_normed_two, ff_out, down_terms, *gate_up_terms = (
        mlp(normed_two, w_gate_up, w_down, out_grad_all, 3, "mlp")
        if fused
        else mlp_in_steps(by_batch(normed_two, b, n_batch), w_gate_up, w_down, out_grad_all)
    )
    if not fused:
        d_normed_two = by_batch(d_normed_two, b, n_batch)
    gate_up_sum = half_sum(gate_up_terms)
    down_terms = down_terms.reshape(n_batch, -1, width)
    down_sum = half_sum(
        [lax.dynamic_index_in_dim(down_terms, b ^ k, 0, False) for k in range(n_batch)]
    )

    d_query, d_key_value, o_grad, d_residual, gain_two_grad = attend_back(
        query, key_value, attn_all, places, attn_out, residual, gain_two[None], out_grad,
        d_normed_two, tables,
    )
    d_key_value, ff_out = scatter_ctx([d_key_value, ff_out], 5, "scatter_rows")
    hidden_out = (residual + ff_out).astype(BF16)
    d_key_value, down_sum, gate_up_sum = lax.optimization_barrier(
        (d_key_value, down_sum, gate_up_sum)
    )
    down_grad = sum(term.astype(F32) for term in down_sum)
    gate_up_grad = sum(term.astype(F32) for term in gate_up_sum).astype(BF16)
    qkv_grad, hidden_grad, sums = project_back(
        d_query, d_key_value, attn_all, normed_one, hidden_in, gain_one[None], d_residual,
        gain_two_grad, tables,
    )
    grads = [grad.reshape(n_batch, n_ctx, rows, -1) for grad in (qkv_grad, o_grad)]
    attn_grads, o_grad, sums, gate_up_grad = collect(
        grads, sums, gate_up_grad.reshape(n_ctx, rows, 2 * half), 6, "collect"
    )
    gate_grad, up_grad = unpack(gate_up_grad, n_batch, hidden_ff)

    def own_part(row, first, total):
        size = total // n_all
        at = first + (b * n_ctx + lax.axis_index("ctx")) * size
        return lax.dynamic_slice(sums, (row, at), (1, size))[0]

    at_key, at_value, at_out = width, width + KVW, width + 2 * KVW
    return (
        hidden_out,
        hidden_grad,
        own_part(0, 0, width),
        attn_grads[:, :at_key],
        own_part(1, 0, width),
        attn_grads[:, at_key:at_value],
        own_part(2, 0, KVW),
        attn_grads[:, at_value:at_out],
        own_part(2, KVW, KVW),
        o_grad,
        own_part(3, 0, width),
        gate_grad,
        up_grad,
        down_grad,
    )


def solution(mesh):
    matrix, vector = P(ALL, None), P(ALL)
    placed = (
        (matrix, vector, vector, vector, matrix, vector, matrix, vector)
        + (matrix, vector, matrix, vector, matrix, matrix, matrix, matrix)
    )
    results = (matrix, matrix) + (vector, matrix) * 4 + (vector, matrix, matrix, matrix)
    return jax.shard_map(local, mesh=mesh, in_specs=placed, out_specs=results, check_vma=False)
```

```python
import functools
import math

import jax
import jax.numpy as jnp
from jax import lax
from jax.experimental import pallas as pl
from jax.experimental.pallas import tpu as pltpu
from jax.sharding import PartitionSpec as P

HEADS = 12
KV_HEADS = 2
GROUPS = HEADS // KV_HEADS
HEAD_DIM = 128
KVW = KV_HEADS * HEAD_DIM
INV_ROOT = HEAD_DIM ** (-0.5)
EPSILON = 1e-06
ROPE_BASE = 10000.0
MASKED = -1e30
ALL = ("batch", "ctx")
F32 = jnp.float32
BF16 = jnp.bfloat16
MESH = pl.DeviceIdType.MESH
ANYWHERE = pl.BlockSpec(memory_space=pl.ANY)
IN_VMEM = pl.BlockSpec(memory_space=pltpu.VMEM)
DMA = pltpu.SemaphoreType.DMA


def rope_tables(positions):
    half_dim = HEAD_DIM // 2
    inverse_freq = jnp.exp(
        jnp.arange(half_dim, dtype=F32) * (-2.0 * math.log(ROPE_BASE) / HEAD_DIM)
    )
    angles = positions.astype(F32)[:, None] * inverse_freq[None, :]
    angles = jnp.concatenate([angles, angles], axis=1)
    return (jnp.cos(angles), jnp.sin(angles))


def dot(lhs, rhs):
    return jnp.dot(lhs, rhs, preferred_element_type=F32)


def contract_rows(lhs, rhs):
    return lax.dot_general(lhs, rhs, (((0,), (0,)), ((), ())), preferred_element_type=F32)


def times_transposed(lhs, rhs):
    return lax.dot_general(lhs, rhs, (((1,), (1,)), ((), ())), preferred_element_type=F32)


def lanes(width):
    return -(-width // 128) * 128


def greet(devices):
    barrier = pltpu.get_barrier_semaphore()
    for device in devices:
        pl.semaphore_signal(barrier, inc=1, device_id=device, device_id_type=MESH)
    pl.semaphore_wait(barrier, len(devices))


def remote(source, target, send, receive, device):
    return pltpu.make_async_remote_copy(
        src_ref=source,
        dst_ref=target,
        send_sem=send,
        recv_sem=receive,
        device_id=device,
        device_id_type=MESH,
    )


def lasting(microseconds):
    return pl.CostEstimate(flops=0, bytes_accessed=int(3.3e6 * microseconds), transcendentals=0)


def gather_kernel(line_len, own, out, own_sem, line_sems, pair_sems):
    b, c = lax.axis_index("batch"), lax.axis_index("ctx")
    line, pair = c // 2, c % 2
    ahead = (b, 2 * lax.rem(line + 1, line_len) + pair)
    behind = (b, 2 * lax.rem(line + line_len - 1, line_len) + pair)
    across = (b, c ^ 1)
    greet((ahead, behind, across))
    keep = pltpu.make_async_copy(own, out.at[c], own_sem)
    keep.start()
    on_line, on_pair = [], []
    for step in range(line_len):
        at = 2 * lax.rem(line - step + line_len, line_len) + pair
        block = own if step == 0 else out.at[at]
        if step > 0:
            on_line[step - 1].wait_recv()
        if step < line_len - 1:
            copy = remote(block, out.at[at], line_sems.at[0, step], line_sems.at[1, step], ahead)
            copy.start()
            on_line.append(copy)
        copy = remote(block, out.at[at], pair_sems.at[0, step], pair_sems.at[1, step], across)
        copy.start()
        on_pair.append(copy)
    for copy in on_pair:
        copy.wait()
    for copy in on_line:
        copy.wait_send()
    keep.wait()


def gather_ctx(block, collective_id, name):
    n_ctx = lax.axis_size("ctx")
    line_len = n_ctx // 2
    return pl.pallas_call(
        functools.partial(gather_kernel, line_len),
        out_shape=jax.ShapeDtypeStruct((n_ctx,) + block.shape, block.dtype),
        in_specs=[ANYWHERE],
        out_specs=ANYWHERE,
        scratch_shapes=[DMA(()), DMA((2, line_len)), DMA((2, line_len))],
        compiler_params=pltpu.CompilerParams(collective_id=collective_id, has_side_effects=True),
        cost_estimate=lasting(20),
        name=name,
    )(block)


def scatter_kernel(line_len, many, *refs):
    parts, outs = refs[:many], refs[many : 2 * many]
    pair_in, line_in, line_out = (refs[(2 + i) * many : (3 + i) * many] for i in range(3))
    pair_sems, line_sems = refs[5 * many :]
    b, c = lax.axis_index("batch"), lax.axis_index("ctx")
    line, pair = c // 2, c % 2
    ahead = (b, 2 * lax.rem(line + 1, line_len) + pair)
    behind = (b, 2 * lax.rem(line + line_len - 1, line_len) + pair)
    across = (b, c ^ 1)
    greet((ahead, behind, across))

    def to(step):
        return 2 * lax.rem(line - 1 - step + line_len, line_len)

    sent, given = [], []
    for i in range(many):
        for step in range(line_len):
            copy = remote(
                parts[i].at[to(step) + 1 - pair],
                pair_in[i].at[step],
                pair_sems.at[0, i, step],
                pair_sems.at[1, i, step],
                across,
            )
            copy.start()
            given.append(copy)
    for i in range(many):
        for step in range(line_len):
            given[i * line_len + step].wait_recv()
            total = parts[i][to(step) + pair].astype(F32) + pair_in[i][step].astype(F32)
            if step > 0:
                passed.wait_recv()
                total = total + line_in[i][step - 1].astype(F32)
            if step < line_len - 1:
                line_out[i][step] = total.astype(BF16)
                passed = remote(
                    line_out[i].at[step],
                    line_in[i].at[step],
                    line_sems.at[0, i, step],
                    line_sems.at[1, i, step],
                    ahead,
                )
                passed.start()
                sent.append(passed)
            else:
                outs[i][...] = total
    for copy in given + sent:
        copy.wait_send()


def scatter_ctx(parts, collective_id, name):
    n_ctx = lax.axis_size("ctx")
    line_len, many = n_ctx // 2, len(parts)
    blocks = [(part.shape[0] // n_ctx,) + part.shape[1:] for part in parts]

    def room(size):
        return [pltpu.VMEM((size,) + block, BF16) for block in blocks]

    return pl.pallas_call(
        functools.partial(scatter_kernel, line_len, many),
        out_shape=[jax.ShapeDtypeStruct(block, F32) for block in blocks],
        in_specs=[IN_VMEM] * many,
        out_specs=[IN_VMEM] * many,
        scratch_shapes=[
            *room(line_len),
            *room(line_len - 1),
            *room(line_len - 1),
            DMA((2, many, line_len)),
            DMA((2, many, line_len)),
        ],
        compiler_params=pltpu.CompilerParams(
            collective_id=collective_id, has_side_effects=True, vmem_limit_bytes=60 * 2**20
        ),
        cost_estimate=lasting(40),
        name=name,
    )(*[part.reshape((n_ctx,) + block) for part, block in zip(parts, blocks)])


def spread_kernel(
    line_len, q_weight, k_weight, v_weight, o_weight, small, gate, up, out, columns_out, own,
    columns, own_sem, line_sems, pair_sems, chip_sems, core_sems, column_sems,
):
    b, c = lax.axis_index("batch"), lax.axis_index("ctx")
    n_ctx = 2 * line_len
    line, pair = c // 2, c % 2
    ahead = (b, 2 * lax.rem(line + 1, line_len) + pair)
    across, chip, core = (b, c ^ 1), (b ^ 2, c), (b ^ 1, c)
    others = [(b, lax.rem(c + k, n_ctx)) for k in range(1, n_ctx)]
    at = 0
    for part in (q_weight, k_weight, v_weight, o_weight, small):
        own[:, at : at + part.shape[1]] = part[...]
        at += part.shape[1]
    greet([chip, core] + others)
    keep = [pltpu.make_async_copy(own, out.at[b, c], own_sem.at[0])]
    keep[0].start()

    def pack():
        n_batch, half = out.shape[0], columns.shape[2] // 2
        piece = gate.shape[1] // (n_batch * n_ctx)
        for first, weight in ((0, gate), (half, up)):
            if n_batch * piece < half:
                columns[:, :, first + half - 128 : first + half] = jnp.zeros(
                    (n_ctx, columns.shape[1], 128), BF16
                )
            for k in range(n_batch):
                for i in range(n_ctx):
                    to = (k * n_ctx + i) * piece
                    at = first + k * piece
                    columns[i, :, at : at + piece] = weight[:, to : to + piece]
        keep.append(pltpu.make_async_copy(columns.at[c], columns_out.at[c], own_sem.at[1]))
        keep[1].start()

    def place(step, side):
        return 2 * lax.rem(line - step + line_len, line_len) + side

    def hand(block, to_b, to_c, sems, index, device):
        copy = remote(block, out.at[to_b, to_c], sems.at[0, index], sems.at[1, index], device)
        copy.start()
        return copy

    on_line, on_pair, on_chip, on_core, on_columns = [], [], [], [], []
    for step in range(line_len):
        at = place(step, pair)
        block = own if step == 0 else out.at[b, at]
        if step > 0:
            on_line[step - 1].wait_recv()
        if step < line_len - 1:
            on_line.append(hand(block, b, at, line_sems, step, ahead))
        on_pair.append(hand(block, b, at, pair_sems, step, across))
        on_chip.append(hand(block, b, at, chip_sems, step, chip))
        on_core.append(hand(block, b, at, core_sems, step, core))
        if step == 0:
            pack()
    for k, device in enumerate(others):
        copy = remote(
            columns.at[device[1]],
            columns_out.at[c],
            column_sems.at[0, k],
            column_sems.at[1, k],
            device,
        )
        copy.start()
        on_columns.append(copy)
    for step in range(line_len):
        at = place(step, 1 - pair)
        on_pair[step].wait_recv()
        on_chip.append(hand(out.at[b, at], b, at, chip_sems, line_len + step, chip))
        on_core.append(hand(out.at[b, at], b, at, core_sems, line_len + step, core))
    for index in range(n_ctx):
        at = place(index % line_len, pair if index < line_len else 1 - pair)
        on_chip[index].wait_recv()
        on_core.append(hand(out.at[b ^ 2, at], b ^ 2, at, core_sems, n_ctx + index, core))
    for copy in on_core + on_columns:
        copy.wait()
    for copy in on_line + on_pair + on_chip:
        copy.wait_send()
    for copy in keep:
        copy.wait()


def spread(matrices, gate, up, collective_id, name):
    n_batch, n_ctx = lax.axis_size("batch"), lax.axis_size("ctx")
    line_len = n_ctx // 2
    rows = gate.shape[0]
    own = (rows, sum(matrix.shape[1] for matrix in matrices))
    columns = (n_ctx, rows, 2 * lanes(gate.shape[1] // n_ctx))
    return pl.pallas_call(
        functools.partial(spread_kernel, line_len),
        out_shape=(
            jax.ShapeDtypeStruct((n_batch, n_ctx) + own, BF16),
            jax.ShapeDtypeStruct(columns, BF16),
        ),
        in_specs=[IN_VMEM] * 7,
        out_specs=(ANYWHERE, ANYWHERE),
        scratch_shapes=[
            pltpu.VMEM(own, BF16),
            pltpu.VMEM(columns, BF16),
            DMA((2,)),
            DMA((2, line_len)),
            DMA((2, line_len)),
            DMA((2, n_ctx)),
            DMA((2, 2 * n_ctx)),
            DMA((2, n_ctx)),
        ],
        compiler_params=pltpu.CompilerParams(
            collective_id=collective_id, has_side_effects=True, vmem_limit_bytes=40 * 2**20
        ),
        cost_estimate=lasting(75),
        name=name,
    )(*matrices, gate, up)


def collect_kernel(line_len, *refs):
    grads, (sums_in, columns) = refs[:2], refs[2:4]
    outs, (sums_out, columns_out) = refs[4:6], refs[6:8]
    core_in, chip_in, pair_in, line_in, chip_out, pair_out, line_out = [
        refs[8 + 2 * i : 10 + 2 * i] for i in range(7)
    ]
    sums_got, sums_mine, own_sem = refs[22:25]
    core_sems, chip_sems, pair_sems, line_sems, column_sems, sums_sems = refs[25:]
    b, c = lax.axis_index("batch"), lax.axis_index("ctx")
    n_ctx = 2 * line_len
    line, pair = c // 2, c % 2
    ahead = (b, 2 * lax.rem(line + 1, line_len) + pair)
    across, chip, core = (b, c ^ 1), (b ^ 2, c), (b ^ 1, c)
    others = [(b, lax.rem(c + k, n_ctx)) for k in range(1, n_ctx)]
    on_same_line = others[1::2]
    greet([chip, core] + others)
    keep = pltpu.make_async_copy(columns.at[c], columns_out.at[c], own_sem)
    keep.start()

    def place(index):
        step, side = index // 2, index % 2
        to = lax.rem(line - 1 - step + line_len, line_len)
        return 2 * to + (1 - pair if side == 0 else pair)

    waits = []

    def send(block, target, sems, index, device):
        copy = remote(block, target, sems.at[0, index], sems.at[1, index], device)
        copy.start()
        waits.append(copy)
        return copy

    def start_sums(index, device):
        copy = remote(
            sums_mine, sums_got.at[index], sums_sems.at[0, index], sums_sems.at[1, index], device
        )
        copy.start()
        return copy

    def add_sums(index, copy):
        copy.wait()
        sums_mine[...] += sums_got[index]

    sums_mine[...] = sums_in[...]
    by_core = start_sums(0, core)
    to_core = [[], []]
    for index in range(2 * n_ctx):
        row = b ^ 3 if index < n_ctx else b ^ 1
        for i in range(2):
            to_core[i].append(
                send(
                    grads[i].at[row, place(index % n_ctx)],
                    core_in[i].at[index],
                    core_sems.at[i],
                    index,
                    core,
                )
            )
    add_sums(0, by_core)
    by_chip = start_sums(1, chip)
    on_columns = []
    for k, device in enumerate(others):
        copy = remote(
            columns.at[device[1]],
            columns_out.at[c],
            column_sems.at[0, k],
            column_sems.at[1, k],
            device,
        )
        copy.start()
        on_columns.append(copy)
    to_chip = [[], []]
    for index in range(n_ctx):
        for i in range(2):
            to_core[i][index].wait_recv()
            total = grads[i][b ^ 2, place(index)].astype(F32) + core_in[i][index].astype(F32)
            chip_out[i][index] = total.astype(BF16)
            to_chip[i].append(
                send(chip_out[i].at[index], chip_in[i].at[index], chip_sems.at[i], index, chip)
            )
    add_sums(1, by_chip)
    by_pair = start_sums(2, across)

    def mine(i, index):
        to_core[i][n_ctx + index].wait_recv()
        to_chip[i][index].wait_recv()
        return (
            grads[i][b, place(index)].astype(F32)
            + core_in[i][n_ctx + index].astype(F32)
            + chip_in[i][index].astype(F32)
        )

    to_pair, to_line = [[], []], [[], []]
    for step in range(line_len):
        for i in range(2):
            pair_out[i][step] = mine(i, 2 * step).astype(BF16)
            to_pair[i].append(
                send(pair_out[i].at[step], pair_in[i].at[step], pair_sems.at[i], step, across)
            )
        if step == 0:
            add_sums(2, by_pair)
            own_sums = [
                send(sums_mine, sums_got.at[3 + k], sums_sems, 3 + k, device)
                for k, device in enumerate(on_same_line)
            ]
        for i in range(2):
            total = mine(i, 2 * step + 1)
            to_pair[i][step].wait_recv()
            total = total + pair_in[i][step].astype(F32)
            if step > 0:
                to_line[i][step - 1].wait_recv()
                total = total + line_in[i][step - 1].astype(F32)
            if step < line_len - 1:
                line_out[i][step] = total.astype(BF16)
                to_line[i].append(
                    send(line_out[i].at[step], line_in[i].at[step], line_sems.at[i], step, ahead)
                )
            else:
                outs[i][...] = total
    total = sums_mine[...]
    for k, copy in enumerate(own_sums):
        copy.wait_recv()
        total = total + sums_got[3 + k]
    sums_out[...] = total
    for copy in on_columns:
        copy.wait()
    for copy in waits:
        copy.wait_send()
    keep.wait()


def collect(grads, sums, columns, collective_id, name):
    n_batch, n_ctx = lax.axis_size("batch"), lax.axis_size("ctx")
    line_len = n_ctx // 2
    blocks = [grad.shape[2:] for grad in grads]

    def room(size):
        return [pltpu.VMEM((size,) + block, BF16) for block in blocks]

    return pl.pallas_call(
        functools.partial(collect_kernel, line_len),
        out_shape=(
            *[jax.ShapeDtypeStruct(block, F32) for block in blocks],
            jax.ShapeDtypeStruct(sums.shape, F32),
            jax.ShapeDtypeStruct(columns.shape, BF16),
        ),
        in_specs=[IN_VMEM] * 3 + [ANYWHERE],
        out_specs=(IN_VMEM,) * 3 + (ANYWHERE,),
        scratch_shapes=[
            *room(2 * n_ctx),
            *room(n_ctx),
            *room(line_len),
            *room(line_len - 1),
            *room(n_ctx),
            *room(line_len),
            *room(line_len - 1),
            pltpu.VMEM((2 + line_len,) + sums.shape, F32),
            pltpu.VMEM(sums.shape, F32),
            DMA(()),
            DMA((2, 2, 2 * n_ctx)),
            DMA((2, 2, n_ctx)),
            DMA((2, 2, line_len)),
            DMA((2, 2, line_len)),
            DMA((2, n_ctx)),
            DMA((2, 2 + line_len)),
        ],
        compiler_params=pltpu.CompilerParams(
            collective_id=collective_id, has_side_effects=True, vmem_limit_bytes=60 * 2**20
        ),
        cost_estimate=lasting(70),
        name=name,
    )(*grads, sums, columns)


def row_scale(values):
    return lax.rsqrt(jnp.mean(values * values, axis=-1, keepdims=True) + EPSILON)


def turn_head(values, cosine, signed_sine, back=False):
    turned = pltpu.roll(values, HEAD_DIM // 2, 1) * signed_sine
    return values * cosine - turned if back else values * cosine + turned


def whole(*shape):
    return pl.BlockSpec(shape, lambda j: (0,) * len(shape))


def project_kernel(hidden, gain, weight, bias, cosine, signed_sine, normed, query, key_value, kept):
    j = pl.program_id(0)

    @pl.when(j == 0)
    def _():
        values = hidden[...].astype(F32)
        kept[...] = (values * row_scale(values) * gain[...]).astype(BF16)
        normed[...] = kept[...]

    lin = dot(kept[...], weight[...]) + bias[...]
    tables = cosine[...], signed_sine[...]
    heads = [lin[:, i * HEAD_DIM : (i + 1) * HEAD_DIM] for i in range(4)]

    @pl.when(j < 3)
    def _():
        for i in range(4):
            turned = turn_head(heads[i], *tables)
            query[:, i * HEAD_DIM : (i + 1) * HEAD_DIM] = turned.astype(BF16)

    @pl.when(j == 3)
    def _():
        for i in range(4):
            value = turn_head(heads[i], *tables) if i < KV_HEADS else heads[i]
            key_value[:, i * HEAD_DIM : (i + 1) * HEAD_DIM] = value.astype(BF16)


def project(hidden, gain, weights, bias, tables):
    count, width = hidden.shape
    wide = 2 * KVW
    table = whole(count, HEAD_DIM)
    return pl.pallas_call(
        project_kernel,
        grid=(4,),
        out_shape=(
            jax.ShapeDtypeStruct((count, width), BF16),
            jax.ShapeDtypeStruct((count, width), BF16),
            jax.ShapeDtypeStruct((count, wide), BF16),
        ),
        in_specs=[
            whole(count, width),
            whole(1, width),
            pl.BlockSpec((width, wide), lambda j: (0, j)),
            pl.BlockSpec((1, wide), lambda j: (0, j)),
            table,
            table,
        ],
        out_specs=(
            whole(count, width),
            pl.BlockSpec((count, wide), lambda j: (0, jnp.minimum(j, 2))),
            whole(count, wide),
        ),
        scratch_shapes=[pltpu.VMEM((count, width), BF16)],
        compiler_params=pltpu.CompilerParams(vmem_limit_bytes=40 * 2**20),
        cost_estimate=lasting(4),
        name="project",
    )(hidden, gain, weights, bias, *tables)


def mark_allowed(key_pos, key_doc, own_pos, own_doc, allowed):
    count = own_pos.shape[1]
    pos_column, doc_column = key_pos[...].T, key_doc[...].T
    for i in range(key_pos.shape[0]):
        seen = (pos_column[:, i : i + 1] <= own_pos[...]) & (doc_column[:, i : i + 1] == own_doc[...])
        allowed[i * count : (i + 1) * count] = jnp.where(seen, 1.0, 0.0)


def stack_heads(block, group):
    return jnp.concatenate(
        [block[:, i * HEAD_DIM : (i + 1) * HEAD_DIM] for i in range(group)], axis=0
    )


def lay_heads(stacked, group):
    count = stacked.shape[0] // group
    return jnp.concatenate([stacked[i * count : (i + 1) * count] for i in range(group)], axis=1)


def probabilities(keys, queries, allowed, group):
    scores = times_transposed(keys, queries) * INV_ROOT
    seen = jnp.concatenate([allowed[...]] * group, axis=1) > 0.0
    scores = jnp.where(seen, scores, MASKED)
    raised = jnp.exp(scores - jnp.max(scores, axis=0, keepdims=True))
    return raised * (1.0 / jnp.sum(raised, axis=0, keepdims=True))


def attend_kernel(
    group, last, query, keys, values, out_0, out_1, out_2, key_pos, key_doc, own_pos, own_doc,
    hidden, gain, attn_out, residual, normed, total, allowed,
):
    j = pl.program_id(0)

    @pl.when(j == 0)
    def _():
        total[...] = hidden[...].astype(F32)
        mark_allowed(key_pos, key_doc, own_pos, own_doc, allowed)

    probs = probabilities(keys[...], stack_heads(query[...], group), allowed, group)
    result = contract_rows(values[...], probs.astype(BF16)).T
    block = lay_heads(result, group).astype(BF16)
    attn_out[...] = block
    for t, weight in enumerate((out_0, out_1, out_2)):
        total[:, t * 512 : (t + 1) * 512] += dot(block, weight[...])

    @pl.when(j == last)
    def _():
        values = total[...]
        residual[...] = values
        normed[...] = (values * row_scale(values) * gain[...]).astype(BF16)


def head_specs(count, width, keys, group, weights_at):
    rows = group * HEAD_DIM
    per_key = GROUPS // group
    query = pl.BlockSpec((count, rows), lambda j: (0, j))
    heads = [
        pl.BlockSpec((keys, HEAD_DIM), lambda j, i=i: (0, KV_HEADS * i + j // per_key))
        for i in range(2)
    ]
    out = [
        pl.BlockSpec((rows, 512), lambda j, t=t: (j, weights_at // 512 + t))
        for t in range(width // 512)
    ]
    places = [whole(keys // count, count)] * 2 + [whole(1, count)] * 2
    return query, heads, out, places


def attend(query, key_value, weights, places, hidden, gain):
    count, width = hidden.shape
    keys = key_value.shape[0]
    group = 3 if keys <= 1024 else 1
    steps = HEADS // group
    query_spec, head_spec, out_spec, place_spec = head_specs(
        count, width, keys, group, width + 2 * KVW
    )
    return pl.pallas_call(
        functools.partial(attend_kernel, group, steps - 1),
        grid=(steps,),
        out_shape=(
            jax.ShapeDtypeStruct((count, width), BF16),
            jax.ShapeDtypeStruct((count, width), F32),
            jax.ShapeDtypeStruct((count, width), BF16),
        ),
        in_specs=[query_spec, *head_spec, *out_spec, *place_spec]
        + [whole(count, width), whole(1, width)],
        out_specs=(query_spec, whole(count, width), whole(count, width)),
        scratch_shapes=[pltpu.VMEM((count, width), F32), pltpu.VMEM((keys, count), F32)],
        compiler_params=pltpu.CompilerParams(vmem_limit_bytes=56 * 2**20),
        cost_estimate=lasting(10),
        name="attend",
    )(query, key_value, key_value, *[weights] * 3, *places, hidden, gain)


def attend_back_kernel(
    group, per_key, query, keys, values, out_0, out_1, out_2, key_pos, key_doc, own_pos, own_doc,
    attn_out, residual, gain, out_grad, d_normed, cosine, signed_sine, d_query, d_key_value,
    o_grad, d_residual, gain_grad, branch, allowed, key_sum, value_sum,
):
    j = pl.program_id(0)

    @pl.when(j == 0)
    def _():
        rows, grads = residual[...], d_normed[...]
        factor = row_scale(rows)
        scaled = grads * gain[...]
        gain_grad[...] = jnp.sum(grads * rows * factor, axis=0, keepdims=True)
        total = out_grad[...].astype(F32) + (
            factor * scaled
            - rows * (factor * factor * factor) * jnp.mean(scaled * rows, axis=-1, keepdims=True)
        )
        d_residual[...] = total
        branch[...] = total.astype(BF16)
        mark_allowed(key_pos, key_doc, own_pos, own_doc, allowed)

    @pl.when(lax.rem(j, per_key) == 0)
    def _():
        key_sum[...] = jnp.zeros_like(key_sum)
        value_sum[...] = jnp.zeros_like(value_sum)

    o_grad[...] = contract_rows(attn_out[...], branch[...]).astype(BF16)
    d_attn = sum(
        times_transposed(branch[:, t * 512 : (t + 1) * 512], weight[...])
        for t, weight in enumerate((out_0, out_1, out_2))
    ).astype(BF16)
    grads = stack_heads(d_attn, group)
    queries = stack_heads(query[...], group)
    probs = probabilities(keys[...], queries, allowed, group)
    d_probs = times_transposed(values[...], grads)
    delta = jnp.sum(probs * d_probs, axis=0, keepdims=True)
    d_scores = (probs * (d_probs - delta)).astype(BF16)
    key_sum[...] += dot(d_scores, queries)
    value_sum[...] += dot(probs.astype(BF16), grads)
    result = contract_rows(keys[...], d_scores).T * INV_ROOT
    count = result.shape[0] // group
    for i in range(group):
        head = turn_head(
            result[i * count : (i + 1) * count], cosine[...], signed_sine[...], back=True
        )
        d_query[:, i * HEAD_DIM : (i + 1) * HEAD_DIM] = head.astype(BF16)

    @pl.when(lax.rem(j, per_key) == per_key - 1)
    def _():
        at = pl.multiple_of(j // per_key * HEAD_DIM, HEAD_DIM)
        d_key_value[:, pl.ds(at, HEAD_DIM)] = (key_sum[...] * INV_ROOT).astype(BF16)
        d_key_value[:, pl.ds(KVW + at, HEAD_DIM)] = value_sum[...].astype(BF16)


def attend_back(query, key_value, weights, places, attn_out, residual, gain, out_grad, d_normed, tables):
    count, width = query.shape
    keys = key_value.shape[0]
    group = 3 if keys <= 1024 else 1
    steps = HEADS // group
    query_spec, head_spec, out_spec, place_spec = head_specs(
        count, width, keys, group, width + 2 * KVW
    )
    rows, table = whole(count, width), whole(count, HEAD_DIM)
    return pl.pallas_call(
        functools.partial(attend_back_kernel, group, GROUPS // group),
        grid=(steps,),
        out_shape=(
            jax.ShapeDtypeStruct((count, width), BF16),
            jax.ShapeDtypeStruct((keys, 2 * KVW), BF16),
            jax.ShapeDtypeStruct((width, width), BF16),
            jax.ShapeDtypeStruct((count, width), F32),
            jax.ShapeDtypeStruct((1, width), F32),
        ),
        in_specs=[query_spec, *head_spec, *out_spec, *place_spec, query_spec]
        + [rows, whole(1, width), rows, rows, table, table],
        out_specs=(
            query_spec,
            whole(keys, 2 * KVW),
            pl.BlockSpec((group * HEAD_DIM, width), lambda j: (j, 0)),
            rows,
            whole(1, width),
        ),
        scratch_shapes=[
            pltpu.VMEM((count, width), BF16),
            pltpu.VMEM((keys, count), F32),
            pltpu.VMEM((keys, HEAD_DIM), F32),
            pltpu.VMEM((keys, HEAD_DIM), F32),
        ],
        compiler_params=pltpu.CompilerParams(vmem_limit_bytes=60 * 2**20),
        cost_estimate=lasting(17),
        name="attend_back",
    )(
        query, key_value, key_value, *[weights] * 3, *places, attn_out, residual, gain, out_grad,
        d_normed, *tables,
    )


def project_back_kernel(
    d_query, d_key_value, weight, normed, hidden, gain, d_residual, gain_two_grad, cosine,
    signed_sine, grad, hidden_grad, sums, flipped, total, biases,
):
    j = pl.program_id(0)
    wide = weight.shape[1]

    @pl.when(j == 0)
    def _():
        flipped[...] = normed[...].astype(F32).T.astype(BF16)
        total[...] = jnp.zeros_like(total)
        sums[...] = jnp.zeros_like(sums)

    def add(d_lin):
        grad[...] = dot(flipped[...], d_lin).astype(BF16)
        total[...] += times_transposed(d_lin, weight[...])
        return jnp.sum(d_lin.astype(F32), axis=0, keepdims=True)

    for i in range(3):

        @pl.when(j == i)
        def _():
            sums[1:2, i * wide : (i + 1) * wide] = add(d_query[...])

    @pl.when(j == 3)
    def _():
        heads = [
            turn_head(
                d_key_value[:, i * HEAD_DIM : (i + 1) * HEAD_DIM],
                cosine[...],
                signed_sine[...],
                back=True,
            )
            for i in range(KV_HEADS)
        ]
        d_lin = jnp.concatenate(heads + [d_key_value[:, KVW:]], axis=1).astype(BF16)
        sums[2:3, :wide] = add(d_lin)
        rows, grads = hidden[...].astype(F32), total[...]
        factor = row_scale(rows)
        scaled = grads * gain[...]
        sums[0:1] = jnp.sum(grads * rows * factor, axis=0, keepdims=True)
        sums[3:4] = gain_two_grad[...]
        hidden_grad[...] = d_residual[...] + (
            factor * scaled
            - rows * (factor * factor * factor) * jnp.mean(scaled * rows, axis=-1, keepdims=True)
        )


def project_back(d_query, d_key_value, weights, normed, hidden, gain, d_residual, gain_two_grad, tables):
    count, width = hidden.shape
    wide = 2 * KVW
    rows, table = whole(count, width), whole(count, HEAD_DIM)
    return pl.pallas_call(
        project_back_kernel,
        grid=(4,),
        out_shape=(
            jax.ShapeDtypeStruct((width, width + wide), BF16),
            jax.ShapeDtypeStruct((count, width), F32),
            jax.ShapeDtypeStruct((8, width), F32),
        ),
        in_specs=[
            pl.BlockSpec((count, wide), lambda j: (0, jnp.minimum(j, 2))),
            whole(count, wide),
            pl.BlockSpec((width, wide), lambda j: (0, j)),
            rows,
            rows,
            whole(1, width),
            rows,
            whole(1, width),
            table,
            table,
        ],
        out_specs=(
            pl.BlockSpec((width, wide), lambda j: (0, j)),
            rows,
            whole(8, width),
        ),
        scratch_shapes=[
            pltpu.VMEM((width, count), BF16),
            pltpu.VMEM((count, width), F32),
            pltpu.VMEM((8, wide), F32),
        ],
        compiler_params=pltpu.CompilerParams(vmem_limit_bytes=48 * 2**20),
        cost_estimate=lasting(9),
        name="project_back",
    )(
        d_query, d_key_value, weights, normed, hidden, gain, d_residual, gain_two_grad, *tables
    )


def unpack_kernel(n_batch, piece, packed, gate, up):
    n_ctx, _, both = packed.shape
    for out, first in ((gate, 0), (up, both // 2)):
        for k in range(n_batch):
            for i in range(n_ctx):
                at = first + k * piece
                to = (k * n_ctx + i) * piece
                out[:, to : to + piece] = packed[i, :, at : at + piece].astype(F32)


def unpack(packed, n_batch, width):
    n_ctx, rows, _ = packed.shape
    out = jax.ShapeDtypeStruct((rows, width), F32)
    return pl.pallas_call(
        functools.partial(unpack_kernel, n_batch, width // (n_batch * n_ctx)),
        out_shape=(out, out),
        in_specs=[IN_VMEM],
        out_specs=(IN_VMEM, IN_VMEM),
        compiler_params=pltpu.CompilerParams(vmem_limit_bytes=40 * 2**20),
        cost_estimate=lasting(3),
        name="unpack",
    )(packed)


def mlp_kernel(line_len, tile, own_rows, *refs):
    n_batch, n_ctx = 4, 2 * line_len
    weights, (down, grads_in) = refs[:n_batch], refs[n_batch : n_batch + 2]
    d_rows_out, ff_out, down_out, gate_up_out = refs[n_batch + 2 : n_batch + 6]
    (
        tokens, flipped, gate_up, down_in, grads, mixed, mixed_flipped, d_gate_up, d_parts, ff_parts,
        d_pair, d_line, d_pass, ff_pair, ff_line, ff_pass, core_wide, chip_wide, down_terms,
        core_down, chip_down, own, load_sems, store_sems,
        line_sems, pair_sems, back_pair, back_line, batch_sems,
    ) = refs[n_batch + 6 :]
    b, c = lax.axis_index("batch"), lax.axis_index("ctx")
    line, pair = c // 2, c % 2
    ahead = (b, 2 * lax.rem(line + 1, line_len) + pair)
    behind = (b, 2 * lax.rem(line + line_len - 1, line_len) + pair)
    across, chip, core = (b, c ^ 1), (b ^ 2, c), (b ^ 1, c)
    count, width = own.shape
    half = gate_up.shape[1] // 2
    own_ff = down.shape[0]
    piece = own_ff // n_batch
    depth = width // n_batch
    for k in range(n_batch):
        source = pl.ds(pl.multiple_of((b ^ k) * depth, 128), depth)
        own[:, k * depth : (k + 1) * depth] = own_rows[:, source]
    greet((ahead, behind, across, chip, core))

    def at(step):
        return 2 * lax.rem(line - step + line_len, line_len)

    sent = []

    def send(source, target, sems, device):
        copy = remote(source, target, sems[0], sems[1], device)
        copy.start()
        sent.append(copy)
        return copy

    on_line, on_pair = [], []

    def forward(step):
        block = own if step == 0 else tokens.at[at(step) + pair]
        target = tokens.at[at(step) + pair]
        if step > 0:
            on_line[step - 1].wait_recv()
        if step < line_len - 1:
            sems = line_sems.at[0, step], line_sems.at[1, step]
            on_line.append(send(block, target, sems, ahead))
        sems = pair_sems.at[0, step], pair_sems.at[1, step]
        on_pair.append(send(block, target, sems, across))

    forward(0)
    loads = [pltpu.make_async_copy(own, tokens.at[c], load_sems.at[0])]
    for k, weight in enumerate(weights):
        loads.append(
            pltpu.make_async_copy(
                weight, gate_up.at[pl.ds(k * depth, depth)], load_sems.at[1 + k]
            )
        )
    loads.append(
        pltpu.make_async_copy(down, down_in.at[pl.ds(0, own_ff)], load_sems.at[1 + n_batch])
    )
    loads.append(pltpu.make_async_copy(grads_in, grads, load_sems.at[2 + n_batch]))
    for copy in loads:
        copy.start()
    if own_ff < half:
        down_in[own_ff:half] = jnp.zeros((half - own_ff, width), BF16)
    for copy in loads:
        copy.wait()

    def chunk(step):
        first = pl.multiple_of(at(step) * count, 2 * count)
        rows, pair_rows = pl.ds(first, 2 * count), pl.ds(at(step), 2)
        block = tokens[pair_rows].reshape(2 * count, width)
        grad_block = grads[pair_rows].reshape(2 * count, width)

        def columns(index, _):
            low = pl.multiple_of(index * tile, 128)
            high = pl.multiple_of(half + index * tile, 128)
            gate_lin = dot(block, gate_up[:, pl.ds(low, tile)])
            up_lin = dot(block, gate_up[:, pl.ds(high, tile)])
            d_mixed = times_transposed(grad_block, down_in[pl.ds(low, tile)])
            sigmoid = 1.0 / (1.0 + jnp.exp(-gate_lin))
            silu = gate_lin * sigmoid
            product = silu * up_lin
            mixed[:, pl.ds(low, tile)] = product.astype(BF16)
            mixed_flipped[pl.ds(low, tile), rows] = product.T.astype(BF16)
            d_gate = d_mixed * up_lin * sigmoid * (1.0 + gate_lin * (1.0 - sigmoid))
            d_gate_up[rows, pl.ds(low, tile)] = d_gate.astype(BF16)
            d_gate_up[rows, pl.ds(high, tile)] = (d_mixed * silu).astype(BF16)
            return 0

        lax.fori_loop(0, half // tile, columns, 0)

        def features(index, _):
            low = pl.multiple_of(index * depth, 128)
            at_low = pl.ds(low, depth)
            back = times_transposed(d_gate_up[rows], gate_up[at_low])
            d_parts[pair_rows, :, at_low] = back.astype(BF16).reshape(2, count, depth)
            return 0

        lax.fori_loop(0, n_batch, features, 0)

        def outputs(index, _):
            low = pl.multiple_of(index * depth, 128)
            at_low = pl.ds(low, depth)
            out = dot(mixed[...], down_in[:, at_low])
            ff_parts[pair_rows, :, at_low] = out.astype(BF16).reshape(2, count, depth)
            flipped[at_low, rows] = (
                tokens[pair_rows, :, at_low].reshape(2 * count, depth).astype(F32).T.astype(BF16)
            )
            return 0

        lax.fori_loop(0, n_batch, outputs, 0)

    moves = (
        (d_parts, d_pair, d_line, d_pass, d_rows_out),
        (ff_parts, ff_pair, ff_line, ff_pass, ff_out),
    )
    given = {}

    def give(index, which=0):
        parts, pairs = moves[which][:2]
        sems = back_pair.at[0, which, index], back_pair.at[1, which, index]
        source = parts.at[at(index + 1) + 1 - pair]
        given[index, which] = send(source, pairs.at[index], sems, across)

    for step in range(line_len):
        if step + 1 < line_len:
            forward(step + 1)
        on_pair[step].wait_recv()
        chunk(step)
        if step == line_len - 2:
            for index in range(line_len - 2):
                give(index)
    give(line_len - 2)
    give(line_len - 1)
    stores = []

    def store(source, target):
        copy = pltpu.make_async_copy(source, target, store_sems.at[len(stores)])
        copy.start()
        stores.append(copy)

    passed = {}

    def passing(index, which=0):
        parts, pairs, lines, passes, out = moves[which]
        given[index, which].wait_recv()
        total = parts[at(index + 1) + pair].astype(F32) + pairs[index].astype(F32)
        if index > 0:
            passed[index - 1, which].wait_recv()
            total = total + lines[index - 1].astype(F32)
        if index < line_len - 1:
            passes[index] = total.astype(BF16)
            sems = back_line.at[0, which, index], back_line.at[1, which, index]
            passed[index, which] = send(passes.at[index], lines.at[index], sems, ahead)
        elif which:
            out[...] = total
        else:
            for k in range(n_batch):
                target = pl.ds(pl.multiple_of((b ^ k) * depth, 128), depth)
                out[:, target] = total[:, k * depth : (k + 1) * depth]

    def batch_send(source, target, index, device):
        sems = batch_sems.at[0, index], batch_sems.at[1, index]
        return send(source, target, sems, device)

    def wide(k, side):
        return gate_up.at[pl.ds(k * depth, depth), pl.ds(side * half, half)]

    def weight_grad(k, side):
        def columns(index, _):
            at_low = pl.ds(pl.multiple_of(side * half + index * tile, 128), tile)
            grad = dot(flipped[k * depth : (k + 1) * depth], d_gate_up[:, at_low])
            gate_up[k * depth : (k + 1) * depth, at_low] = grad.astype(BF16)
            return 0

        lax.fori_loop(0, half // tile, columns, 0)

    def down_grads():
        for k in range(n_batch):
            grad = dot(
                mixed_flipped[k * piece : (k + 1) * piece],
                grads[...].reshape(n_ctx * count, width),
            )
            down_terms[k] = grad.astype(BF16)
        for slot, row in ((1, b ^ 3), (0, b ^ 1)):
            to_core["down", slot] = batch_send(
                down_terms.at[row], core_down.at[slot], 6 + slot, core
            )

    def pass_down():
        to_core["down", 1].wait_recv()
        total = down_terms[b ^ 2].astype(F32) + core_down[1].astype(F32)
        down_terms[b ^ 2] = total.astype(BF16)
        to_chip.append(batch_send(down_terms.at[b ^ 2], chip_down, 8, chip))

    def add_wide(k, side, terms):
        def columns(index, _):
            low = pl.multiple_of(index * tile, 128)
            at_low = pl.ds(pl.multiple_of(side * half + low, 128), tile)
            rows = slice(k * depth, (k + 1) * depth)
            total = gate_up[rows, at_low].astype(F32)
            for term in terms:
                total = total + term[:, pl.ds(low, tile)].astype(F32)
            gate_up[rows, at_low] = total.astype(BF16)
            return 0

        lax.fori_loop(0, half // tile, columns, 0)

    to_core, to_chip = {}, []

    def compute_and_send(k, side):
        weight_grad(k, side)
        slot = k // 2
        target = core_wide.at[slot, side]
        to_core[k, side] = batch_send(wide(k, side), target, 2 * slot + side, core)

    def compute_and_pass(side):
        weight_grad(2, side)
        to_core[3, side].wait_recv()
        add_wide(2, side, [core_wide.at[1, side]])
        to_chip.append(batch_send(wide(2, side), chip_wide.at[side], 4 + side, chip))

    compute_and_send(3, 0)
    compute_and_pass(0)
    compute_and_send(3, 1)
    compute_and_pass(1)
    work = [
        down_grads,
        lambda: (pass_down(), compute_and_send(1, 0)),
        lambda: compute_and_send(1, 1),
        lambda: (weight_grad(0, 0), weight_grad(0, 1)),
    ]
    for index in range(max(line_len, len(work))):
        if index < line_len:
            passing(index)
            give(index, 1)
        if index < len(work):
            work[index]()
    for index in range(line_len - 1):
        passing(index, 1)
    for side in range(2):
        to_core[1, side].wait_recv()
        to_chip[side].wait_recv()
        add_wide(0, side, [core_wide.at[0, side], chip_wide.at[side]])
        store(wide(0, side), gate_up_out.at[:, pl.ds(side * half, half)])
    to_core["down", 0].wait_recv()
    to_chip[2].wait_recv()
    down_out[...] = (
        down_terms[b].astype(F32) + core_down[0].astype(F32) + chip_down[...].astype(F32)
    )
    passing(line_len - 1, 1)
    for copy in sent:
        copy.wait_send()
    for copy in stores:
        copy.wait()


def mlp_scratch(n_ctx, n_batch, count, width, hidden_own):
    line_len, half = n_ctx // 2, lanes(hidden_own)
    tokens, piece = n_ctx * count, hidden_own // n_batch

    def room(*shape):
        return pltpu.VMEM(shape, BF16)

    return [
        room(n_ctx, count, width),
        room(width, tokens),
        room(width, 2 * half),
        room(half, width),
        room(n_ctx, count, width),
        room(2 * count, half),
        room(half, tokens),
        room(tokens, 2 * half),
        room(n_ctx, count, width),
        room(n_ctx, count, width),
        *[room(line_len, count, width), *[room(line_len - 1, count, width)] * 2] * 2,
        room(2, 2, width // n_batch, half),
        room(2, width // n_batch, half),
        room(n_batch, piece, width),
        room(2, piece, width),
        room(piece, width),
        room(count, width),
    ]


def mlp(own, weights, down, grads, collective_id, name):
    n_batch, n_ctx = lax.axis_size("batch"), lax.axis_size("ctx")
    line_len = n_ctx // 2
    count, width = own.shape
    half = weights[0].shape[1] // 2
    tile = 384 if half % 384 == 0 else 128
    return pl.pallas_call(
        functools.partial(mlp_kernel, line_len, tile),
        out_shape=(
            jax.ShapeDtypeStruct((count, width), F32),
            jax.ShapeDtypeStruct((count, width), F32),
            jax.ShapeDtypeStruct((down.shape[0] // n_batch, width), F32),
            jax.ShapeDtypeStruct(weights[0].shape, BF16),
        ),
        in_specs=[IN_VMEM] + [ANYWHERE] * (n_batch + 2),
        out_specs=(IN_VMEM, IN_VMEM, IN_VMEM, ANYWHERE),
        scratch_shapes=mlp_scratch(n_ctx, n_batch, count, width, down.shape[0])
        + [
            DMA((3 + n_batch,)),
            DMA((2,)),
            DMA((2, line_len)),
            DMA((2, line_len)),
            DMA((2, 2, line_len)),
            DMA((2, 2, line_len)),
            DMA((2, 9)),
        ],
        compiler_params=pltpu.CompilerParams(
            collective_id=collective_id, has_side_effects=True, vmem_limit_bytes=60 * 2**20
        ),
        cost_estimate=lasting(100),
        name=name,
    )(own, *weights, down, grads.reshape(n_ctx, count, width))


def back_kernel(line_len, group, *refs):
    (
        query, key_value, key_pos, key_doc, own_pos, own_doc, attn_out, residual, gain_two, out_grad,
        d_normed, cosine, signed_sine, normed, hidden, gain_one, weights, columns,
    ) = refs[:18]
    hidden_grad, o_out, q_out, kv_out, sums_out, columns_out = refs[18:24]
    w_out, w_in, branch, allowed, key_sum, value_sum, d_query, flipped, d_residual = refs[24:33]
    d_key_value, keys_pair, keys_line, keys_pass, sums_got, sums_mine = refs[33:39]
    grads = refs[39:42]
    core_in, chip_in, pair_in, line_in, chip_out, pair_out, line_out = [
        refs[42 + 3 * i : 45 + 3 * i] for i in range(7)
    ]
    (
        load_sems, column_sems, keys_pair_sems, keys_line_sems, sums_sems, core_sems, chip_sems,
        pair_sems, line_sems,
    ) = refs[63:]
    outs = o_out, q_out, kv_out
    b, c = lax.axis_index("batch"), lax.axis_index("ctx")
    n_ctx = 2 * line_len
    line, pair = c // 2, c % 2
    ahead = (b, 2 * lax.rem(line + 1, line_len) + pair)
    across, chip, core = (b, c ^ 1), (b ^ 2, c), (b ^ 1, c)
    others = [(b, lax.rem(c + k, n_ctx)) for k in range(1, n_ctx)]
    on_same_line = others[1::2]
    count, width = query.shape
    wide = group * HEAD_DIM
    rows = q_out.shape[0]
    greet([chip, core] + others)
    sent = []

    def send(source, target, sems, index, device):
        copy = remote(source, target, sems.at[(0, *index)], sems.at[(1, *index)], device)
        copy.start()
        sent.append(copy)
        return copy

    loads = [
        pltpu.make_async_copy(
            weights.at[:, pl.ds(width + 2 * KVW, width)], w_out, load_sems.at[0]
        ),
        pltpu.make_async_copy(weights.at[:, pl.ds(0, width + 2 * KVW)], w_in, load_sems.at[1]),
        pltpu.make_async_copy(columns.at[c], columns_out.at[c], load_sems.at[2]),
    ]
    for copy in loads:
        copy.start()
    on_columns = []

    def exchange_columns(first, last):
        for k in range(first, last):
            source = columns.at[others[k][1]]
            on_columns.append(send(source, columns_out.at[c], column_sems, (k,), others[k]))

    exchange_columns(0, n_ctx - 1)

    def to(step):
        return 2 * lax.rem(line - 1 - step + line_len, line_len)

    def place(index):
        return to(index // 2) + (1 - pair if index % 2 == 0 else pair)

    def block(row, index):
        at = (row * n_ctx + place(index)) * rows
        return pl.ds(pl.multiple_of(at, rows), rows)

    to_core, to_chip, to_pair, to_line = {}, {}, {}, {}

    def core_stage(p):
        for index in range(2 * n_ctx):
            row = b ^ 3 if index < n_ctx else b ^ 1
            source = grads[p].at[block(row, index % n_ctx)]
            to_core[p, index] = send(source, core_in[p].at[index], core_sems, (p, index), core)

    def chip_stage(p):
        for index in range(n_ctx):
            to_core[p, index].wait_recv()
            total = grads[p][block(b ^ 2, index)].astype(F32) + core_in[p][index].astype(F32)
            chip_out[p][index] = total.astype(BF16)
            to_chip[p, index] = send(
                chip_out[p].at[index], chip_in[p].at[index], chip_sems, (p, index), chip
            )

    def mine(p, index):
        to_core[p, n_ctx + index].wait_recv()
        to_chip[p, index].wait_recv()
        return (
            grads[p][block(b, index)].astype(F32)
            + core_in[p][n_ctx + index].astype(F32)
            + chip_in[p][index].astype(F32)
        )

    def pair_stage(p, step):
        pair_out[p][step] = mine(p, 2 * step).astype(BF16)
        to_pair[p, step] = send(
            pair_out[p].at[step], pair_in[p].at[step], pair_sems, (p, step), across
        )

    def line_stage(p, step):
        total = mine(p, 2 * step + 1)
        to_pair[p, step].wait_recv()
        total = total + pair_in[p][step].astype(F32)
        if step > 0:
            to_line[p, step - 1].wait_recv()
            total = total + line_in[p][step - 1].astype(F32)
        if step < line_len - 1:
            line_out[p][step] = total.astype(BF16)
            to_line[p, step] = send(
                line_out[p].at[step], line_in[p].at[step], line_sems, (p, step), ahead
            )
        else:
            outs[p][...] = total

    values, gradient = residual[...], d_normed[...]
    factor = row_scale(values)
    scaled = gradient * gain_two[...]
    sums_mine[...] = jnp.zeros_like(sums_mine)
    sums_mine[3:4] = jnp.sum(gradient * values * factor, axis=0, keepdims=True)
    total = out_grad[...].astype(F32) + (
        factor * scaled
        - values * (factor * factor * factor) * jnp.mean(scaled * values, axis=-1, keepdims=True)
    )
    d_residual[...] = total
    branch[...] = total.astype(BF16)
    for i in range(HEADS // group):
        part = slice(i * wide, (i + 1) * wide)
        grads[0][part] = contract_rows(attn_out[:, part], branch[...]).astype(BF16)
    core_stage(0)
    mark_allowed(key_pos, key_doc, own_pos, own_doc, allowed)
    flipped[...] = normed[...].astype(F32).T.astype(BF16)
    tables = cosine[...], signed_sine[...]

    def attention(i):
        part = slice(i * wide, (i + 1) * wide)
        head = i * group // GROUPS
        key_part = slice(head * HEAD_DIM, (head + 1) * HEAD_DIM)
        value_part = slice(KVW + head * HEAD_DIM, KVW + (head + 1) * HEAD_DIM)
        keys, values = key_value[:, key_part], key_value[:, value_part]
        d_attn = times_transposed(branch[...], w_out[part]).astype(BF16)
        head_grads, queries = stack_heads(d_attn, group), stack_heads(query[:, part], group)
        probs = probabilities(keys, queries, allowed, group)
        d_probs = times_transposed(values, head_grads)
        delta = jnp.sum(probs * d_probs, axis=0, keepdims=True)
        d_scores = (probs * (d_probs - delta)).astype(BF16)
        key_term = dot(d_scores, queries)
        value_term = dot(probs.astype(BF16), head_grads)
        first = i * group % GROUPS == 0
        key_sum[...] = key_term if first else key_sum[...] + key_term
        value_sum[...] = value_term if first else value_sum[...] + value_term
        result = contract_rows(keys, d_scores).T * INV_ROOT
        for k in range(group):
            turned = turn_head(result[k * count : (k + 1) * count], *tables, back=True)
            at = (i * group + k) * HEAD_DIM
            d_query[:, at : at + HEAD_DIM] = turned.astype(BF16)
        if (i + 1) * group % GROUPS == 0:
            shape = d_key_value.shape[:2] + (HEAD_DIM,)
            d_key_value[:, :, key_part] = (key_sum[...] * INV_ROOT).astype(BF16).reshape(shape)
            d_key_value[:, :, value_part] = value_sum[...].astype(BF16).reshape(shape)

    loads[0].wait()
    attention(0)
    chip_stage(0)
    for i in range(1, HEADS // group):
        attention(i)

    given, passed = [], []
    for step in range(line_len):
        source = d_key_value.at[to(step) + 1 - pair]
        given.append(send(source, keys_pair.at[step], keys_pair_sems, (step,), across))
    key_total = None

    def keys_stage(step):
        given[step].wait_recv()
        total = d_key_value[to(step) + pair].astype(F32) + keys_pair[step].astype(F32)
        if step > 0:
            passed[step - 1].wait_recv()
            total = total + keys_line[step - 1].astype(F32)
        if step < line_len - 1:
            keys_pass[step] = total.astype(BF16)
            passed.append(
                send(keys_pass.at[step], keys_line.at[step], keys_line_sems, (step,), ahead)
            )
        return total

    last = line_len - 1
    for step in range(line_len // 2):
        pair_stage(0, step)
    half = width // 2
    for i in range(2):
        part = slice(i * half, (i + 1) * half)
        grads[1][:, part] = dot(flipped[...], d_query[:, part]).astype(BF16)
        if i == 0:
            keys_stage(0)
    core_stage(1)
    loads[1].wait()
    d_one = times_transposed(d_query[...], w_in[:, :width])
    for step in range(1, line_len):
        key_total = keys_stage(step)
        if step == 1:
            chip_stage(1)
        if line_len // 2 + step - 1 < line_len:
            pair_stage(0, line_len // 2 + step - 1)
        if step < last:
            line_stage(0, step - 1)
    heads = [
        turn_head(key_total[:, i * HEAD_DIM : (i + 1) * HEAD_DIM], *tables, back=True)
        for i in range(KV_HEADS)
    ]
    d_lin = jnp.concatenate(heads + [key_total[:, KVW:]], axis=1).astype(BF16)
    grads[2][...] = dot(flipped[...], d_lin).astype(BF16)
    core_stage(2)
    line_stage(0, last - 1)
    d_one = d_one + times_transposed(d_lin, w_in[:, width:])
    sums_mine[1:2] = jnp.sum(d_query[...].astype(F32), axis=0, keepdims=True)
    sums_mine[2:3, : 2 * KVW] = jnp.sum(d_lin.astype(F32), axis=0, keepdims=True)
    values = hidden[...].astype(F32)
    factor = row_scale(values)
    scaled = d_one * gain_one[...]
    sums_mine[0:1] = jnp.sum(d_one * values * factor, axis=0, keepdims=True)

    def start_sums(index, device):
        copy = remote(
            sums_mine, sums_got.at[index], sums_sems.at[0, index], sums_sems.at[1, index], device
        )
        copy.start()
        return copy

    def add_sums(index, copy):
        copy.wait()
        sums_mine[...] += sums_got[index]

    by_core = start_sums(0, core)
    pair_stage(1, 0)
    line_stage(0, last)
    add_sums(0, by_core)
    by_chip = start_sums(1, chip)
    chip_stage(2)
    hidden_grad[...] = d_residual[...] + (
        factor * scaled
        - values * (factor * factor * factor) * jnp.mean(scaled * values, axis=-1, keepdims=True)
    )
    for step in range(1, line_len):
        pair_stage(1, step)
        line_stage(1, step - 1)
    add_sums(1, by_chip)
    by_pair = start_sums(2, across)
    pair_stage(2, 0)
    line_stage(1, last)
    for step in range(1, line_len):
        pair_stage(2, step)
        line_stage(2, step - 1)
        if step == 1:
            add_sums(2, by_pair)
            by_line = [start_sums(3 + k, device) for k, device in enumerate(on_same_line)]
    line_stage(2, last)
    total = sums_mine[...]
    for k, copy in enumerate(by_line):
        copy.wait()
        total = total + sums_got[3 + k]
    sums_out[...] = total
    for copy in on_columns:
        copy.wait_recv()
    for copy in sent:
        copy.wait_send()
    loads[2].wait()


def back(query, key_value, weights, places, attn_out, residual, gain_two, out_grad, d_normed, tables, normed, hidden, gain_one, columns, collective_id, name):
    n_ctx = columns.shape[0]
    line_len, rows = n_ctx // 2, columns.shape[1]
    count, width = query.shape
    keys = key_value.shape[0]
    widths = width, width, 2 * KVW

    def room(*shape, dtype=BF16):
        return pltpu.VMEM(shape, dtype)

    def rooms(size):
        return [room(size, rows, part) for part in widths]

    outs = [(count, width)] + [(rows, part) for part in widths] + [(8, width)]
    return pl.pallas_call(
        functools.partial(back_kernel, line_len, 3),
        out_shape=(
            *[jax.ShapeDtypeStruct(shape, F32) for shape in outs],
            jax.ShapeDtypeStruct(columns.shape, BF16),
        ),
        in_specs=[IN_VMEM] * 16 + [ANYWHERE] * 2,
        out_specs=(IN_VMEM,) * 5 + (ANYWHERE,),
        scratch_shapes=[
            room(width, width),
            room(width, width + 2 * KVW),
            room(count, width),
            room(keys, count, dtype=F32),
            room(keys, HEAD_DIM, dtype=F32),
            room(keys, HEAD_DIM, dtype=F32),
            room(count, width),
            room(width, count),
            room(count, width, dtype=F32),
            room(n_ctx, count, 2 * KVW),
            room(line_len, count, 2 * KVW),
            room(line_len - 1, count, 2 * KVW),
            room(line_len - 1, count, 2 * KVW),
            room(2 + line_len, 8, width, dtype=F32),
            room(8, width, dtype=F32),
            *[room(width, part) for part in widths],
            *rooms(2 * n_ctx),
            *rooms(n_ctx),
            *rooms(line_len),
            *rooms(line_len - 1),
            *rooms(n_ctx),
            *rooms(line_len),
            *rooms(line_len - 1),
            DMA((3,)),
            DMA((2, n_ctx)),
            DMA((2, line_len)),
            DMA((2, line_len)),
            DMA((2, 2 + line_len)),
            DMA((2, 3, 2 * n_ctx)),
            DMA((2, 3, n_ctx)),
            DMA((2, 3, line_len)),
            DMA((2, 3, line_len)),
        ],
        compiler_params=pltpu.CompilerParams(
            collective_id=collective_id, has_side_effects=True, vmem_limit_bytes=60 * 2**20
        ),
        cost_estimate=lasting(90),
        name=name,
    )(
        query, key_value, *places, attn_out, residual, gain_two, out_grad, d_normed, *tables, normed,
        hidden, gain_one, weights, columns,
    )


def swap(values, bit):
    size = lax.axis_size("batch")
    return lax.ppermute(values, "batch", [(i, i ^ bit) for i in range(size)])


def by_batch(values, b, n_batch):
    step = values.shape[1] // n_batch
    blocks = [lax.dynamic_slice_in_dim(values, (b ^ k) * step, step, 1) for k in range(n_batch)]
    return jnp.concatenate(blocks, axis=1)


def batch_terms(terms):
    passed = swap((terms[2].astype(F32) + swap(terms[3], 1).astype(F32)).astype(BF16), 2)
    return [term.astype(F32) for term in (terms[0], swap(terms[1], 1), passed)]


def mlp_room(*sizes):
    return 2 * sum(math.prod(room.shape) for room in mlp_scratch(*sizes))


def mlp_in_steps(normed_two, w_gate_up, w_down, out_grad_all):
    n_batch, b = lax.axis_size("batch"), lax.axis_index("batch")
    normed_two = by_batch(normed_two, b, n_batch)
    w_gate_up = jnp.concatenate(w_gate_up, axis=0)
    half, width = w_gate_up.shape[1] // 2, normed_two.shape[1]
    own_ff = w_down.shape[0]
    w_down = jnp.pad(w_down, ((0, half - own_ff), (0, 0)))
    normed_two = gather_ctx(normed_two, 3, "gather_tokens").reshape(-1, width)
    gate_up = dot(normed_two, w_gate_up)
    gate_lin, up_lin = gate_up[:, :half], gate_up[:, half:]
    sigmoid_gate = jax.nn.sigmoid(gate_lin)
    mixed_rows = (gate_lin * sigmoid_gate * up_lin).astype(BF16)
    d_mixed = times_transposed(out_grad_all, w_down)
    d_gate = d_mixed * up_lin * sigmoid_gate * (1.0 + gate_lin * (1.0 - sigmoid_gate))
    d_up = d_mixed * (gate_lin * sigmoid_gate)
    d_gate_up = jnp.concatenate([d_gate.astype(BF16), d_up.astype(BF16)], axis=1)
    (d_normed_two,) = scatter_ctx(
        [times_transposed(d_gate_up, w_gate_up).astype(BF16)], 4, "scatter_tokens"
    )
    (ff_out,) = scatter_ctx([dot(mixed_rows, w_down).astype(BF16)], 8, "scatter_outputs")
    gate_up_grad = contract_rows(normed_two, d_gate_up).astype(BF16).reshape(n_batch, -1, 2 * half)
    down_grad = contract_rows(mixed_rows, out_grad_all).astype(BF16)[:own_ff]
    return (
        by_batch(d_normed_two, b, n_batch),
        ff_out,
        sum(
            batch_terms(
                [
                    lax.dynamic_index_in_dim(
                        down_grad.reshape(n_batch, -1, width), b ^ k, 0, keepdims=False
                    )
                    for k in range(n_batch)
                ]
            )
        ),
        sum(batch_terms(gate_up_grad)).astype(BF16),
    )


def vector_rows(vectors, rows, pieces):
    laid = [
        jnp.pad(v.reshape(pieces, 1, -1), ((0, 0), (0, 0), (0, 128 - v.shape[0] // pieces)))
        for v in vectors
    ]
    return jnp.pad(jnp.concatenate(laid, axis=1), ((0, 0), (0, rows - len(vectors)), (0, 0)))


def local(
    hidden_in,
    positions,
    doc_ids,
    attn_gain,
    q_weight,
    q_bias,
    k_weight,
    k_bias,
    v_weight,
    v_bias,
    o_weight,
    mlp_gain,
    gate_weight,
    up_weight,
    down_weight,
    out_grad,
):
    n_batch, n_ctx = lax.axis_size("batch"), lax.axis_size("ctx")
    n_all = n_batch * n_ctx
    count, width = hidden_in.shape
    hidden_ff = gate_weight.shape[1]

    b = lax.axis_index("batch")
    w_down = lax.all_gather(down_weight, "batch", axis=0, tiled=True)
    out_grad_all = lax.all_gather(out_grad, "ctx", axis=0, tiled=True)
    rows = q_weight.shape[0]
    small = (attn_gain, mlp_gain, q_bias, k_bias, v_bias)
    places = (positions // 64, positions % 64, doc_ids)
    small = vector_rows(small + tuple(row.astype(BF16) for row in places), rows, 1)[0]
    matrices = (q_weight, k_weight, v_weight, o_weight, small)
    attn_all, packed = spread(matrices, gate_weight, up_weight, 1, "spread_weights")
    half = packed.shape[2] // 2
    own_rows = packed.reshape(-1, 2 * half)
    near, far = swap(own_rows, 1), swap(own_rows, 2)
    small = attn_all[:, :, :8, attn_all.shape[3] - 128 :].astype(F32)
    gain_one, gain_two, b_query, b_key, b_value = (
        small[:, :, i, : part.shape[0]].reshape(-1)
        for i, part in enumerate((attn_gain, mlp_gain, q_bias, k_bias, v_bias))
    )
    places = lax.dynamic_index_in_dim(small, b, 0, keepdims=False)[:, 5:8, :count]
    key_pos, key_doc = places[:, 0] * 64 + places[:, 1], places[:, 2]
    attn_all = attn_all.reshape(width, -1)
    b_qkv = jnp.concatenate([b_query, b_key, b_value])

    cosine, sine_table = rope_tables(positions)
    half_lane = jnp.arange(HEAD_DIM) < HEAD_DIM // 2
    tables = cosine, jnp.where(half_lane[None], -sine_table, sine_table)
    normed_one, query, key_value = project(hidden_in, gain_one[None], attn_all, b_qkv[None], tables)
    key_value = gather_ctx(key_value, 2, "gather_keys").reshape(-1, 2 * KVW)
    far, key_value = lax.optimization_barrier((far, key_value))
    w_gate_up = (own_rows, near, far, swap(far, 1))
    places = (
        key_pos, key_doc, positions.astype(F32)[None], doc_ids.astype(F32)[None]
    )
    attn_out, residual, normed_two = attend(
        query, key_value, attn_all, places, hidden_in, gain_two[None]
    )

    fits = mlp_room(n_ctx, n_batch, count, width, w_down.shape[0]) < 56 * 2**20
    feed_forward = functools.partial(mlp, collective_id=3, name="mlp") if fits else mlp_in_steps
    d_normed_two, ff_out, down_grad, gate_up_grad = feed_forward(
        normed_two, w_gate_up, w_down, out_grad_all
    )
    hidden_out = (residual + ff_out).astype(BF16)

    columns = gate_up_grad.reshape(n_ctx, rows, 2 * half)
    if rows % 16 == 0:
        hidden_grad, o_grad, q_grad, kv_grad, sums, gate_up_grad = back(
            query, key_value, attn_all, places, attn_out, residual, gain_two[None], out_grad,
            d_normed_two, tables, normed_one, hidden_in, gain_one[None], columns, 7, "back"
        )
        k_grad, v_grad = kv_grad[:, :KVW], kv_grad[:, KVW:]
    else:
        d_query, d_key_value, o_grad, d_residual, gain_two_grad = attend_back(
            query, key_value, attn_all, places, attn_out, residual, gain_two[None], out_grad,
            d_normed_two, tables,
        )
        (d_key_value,) = scatter_ctx([d_key_value], 5, "scatter_keys")
        qkv_grad, hidden_grad, sums = project_back(
            d_query, d_key_value, attn_all, normed_one, hidden_in, gain_one[None], d_residual,
            gain_two_grad, tables,
        )
        grads = [grad.reshape(n_batch, n_ctx, rows, -1) for grad in (qkv_grad, o_grad)]
        qkv_grad, o_grad, sums, gate_up_grad = collect(grads, sums, columns, 6, "collect")
        q_grad, k_grad = qkv_grad[:, :width], qkv_grad[:, width : width + KVW]
        v_grad = qkv_grad[:, width + KVW :]
    gate_grad, up_grad = unpack(gate_up_grad, n_batch, hidden_ff)

    def own_part(row, first, total):
        size = total // n_all
        at = first + (b * n_ctx + lax.axis_index("ctx")) * size
        return lax.dynamic_slice(sums, (row, at), (1, size))[0]

    return (
        hidden_out,
        hidden_grad,
        own_part(0, 0, width),
        q_grad,
        own_part(1, 0, width),
        k_grad,
        own_part(2, 0, KVW),
        v_grad,
        own_part(2, KVW, KVW),
        o_grad,
        own_part(3, 0, width),
        gate_grad,
        up_grad,
        down_grad,
    )


def solution(mesh):
    matrix, vector = P(ALL, None), P(ALL)
    placed = (
        (matrix, vector, vector, vector, matrix, vector, matrix, vector)
        + (matrix, vector, matrix, vector, matrix, matrix, matrix, matrix)
    )
    results = (matrix, matrix) + (vector, matrix) * 4 + (vector, matrix, matrix, matrix)
    return jax.shard_map(local, mesh=mesh, in_specs=placed, out_specs=results, check_vma=False)
```

```python
import functools
import math

import jax
import jax.numpy as jnp
from jax import lax
from jax.experimental import pallas as pl
from jax.experimental.pallas import tpu as pltpu
from jax.sharding import PartitionSpec as P

HEADS = 12
KV_HEADS = 2
GROUPS = HEADS // KV_HEADS
HEAD_DIM = 128
KVW = KV_HEADS * HEAD_DIM
INV_ROOT = HEAD_DIM ** (-0.5)
EPSILON = 1e-06
ROPE_BASE = 10000.0
MASKED = -1e30
ALL = ("batch", "ctx")
F32 = jnp.float32
BF16 = jnp.bfloat16
MESH = pl.DeviceIdType.MESH
ANYWHERE = pl.BlockSpec(memory_space=pl.ANY)
IN_VMEM = pl.BlockSpec(memory_space=pltpu.VMEM)
DMA = pltpu.SemaphoreType.DMA


def rope_tables(positions):
    half_dim = HEAD_DIM // 2
    inverse_freq = jnp.exp(
        jnp.arange(half_dim, dtype=F32) * (-2.0 * math.log(ROPE_BASE) / HEAD_DIM)
    )
    angles = positions.astype(F32)[:, None] * inverse_freq[None, :]
    angles = jnp.concatenate([angles, angles], axis=1)
    return (jnp.cos(angles), jnp.sin(angles))


def dot(lhs, rhs):
    return jnp.dot(lhs, rhs, preferred_element_type=F32)


def contract_rows(lhs, rhs):
    return lax.dot_general(lhs, rhs, (((0,), (0,)), ((), ())), preferred_element_type=F32)


def times_transposed(lhs, rhs):
    return lax.dot_general(lhs, rhs, (((1,), (1,)), ((), ())), preferred_element_type=F32)


def lanes(width):
    return -(-width // 128) * 128


def greet(devices):
    barrier = pltpu.get_barrier_semaphore()
    for device in devices:
        pl.semaphore_signal(barrier, inc=1, device_id=device, device_id_type=MESH)
    pl.semaphore_wait(barrier, len(devices))


def remote(source, target, send, receive, device):
    return pltpu.make_async_remote_copy(
        src_ref=source,
        dst_ref=target,
        send_sem=send,
        recv_sem=receive,
        device_id=device,
        device_id_type=MESH,
    )


def lasting(microseconds):
    return pl.CostEstimate(flops=0, bytes_accessed=int(3.3e6 * microseconds), transcendentals=0)


def gather_kernel(line_len, own, out, own_sem, line_sems, pair_sems):
    b, c = lax.axis_index("batch"), lax.axis_index("ctx")
    line, pair = c // 2, c % 2
    ahead = (b, 2 * lax.rem(line + 1, line_len) + pair)
    behind = (b, 2 * lax.rem(line + line_len - 1, line_len) + pair)
    across = (b, c ^ 1)
    greet((ahead, behind, across))
    keep = pltpu.make_async_copy(own, out.at[c], own_sem)
    keep.start()
    on_line, on_pair = [], []
    for step in range(line_len):
        at = 2 * lax.rem(line - step + line_len, line_len) + pair
        block = own if step == 0 else out.at[at]
        if step > 0:
            on_line[step - 1].wait_recv()
        if step < line_len - 1:
            copy = remote(block, out.at[at], line_sems.at[0, step], line_sems.at[1, step], ahead)
            copy.start()
            on_line.append(copy)
        copy = remote(block, out.at[at], pair_sems.at[0, step], pair_sems.at[1, step], across)
        copy.start()
        on_pair.append(copy)
    for copy in on_pair:
        copy.wait()
    for copy in on_line:
        copy.wait_send()
    keep.wait()


def gather_ctx(block, collective_id, name):
    n_ctx = lax.axis_size("ctx")
    line_len = n_ctx // 2
    return pl.pallas_call(
        functools.partial(gather_kernel, line_len),
        out_shape=jax.ShapeDtypeStruct((n_ctx,) + block.shape, block.dtype),
        in_specs=[ANYWHERE],
        out_specs=ANYWHERE,
        scratch_shapes=[DMA(()), DMA((2, line_len)), DMA((2, line_len))],
        compiler_params=pltpu.CompilerParams(collective_id=collective_id, has_side_effects=True),
        cost_estimate=lasting(20),
        name=name,
    )(block)


def scatter_kernel(line_len, many, *refs):
    parts, outs = refs[:many], refs[many : 2 * many]
    pair_in, line_in, line_out = (refs[(2 + i) * many : (3 + i) * many] for i in range(3))
    pair_sems, line_sems = refs[5 * many :]
    b, c = lax.axis_index("batch"), lax.axis_index("ctx")
    line, pair = c // 2, c % 2
    ahead = (b, 2 * lax.rem(line + 1, line_len) + pair)
    behind = (b, 2 * lax.rem(line + line_len - 1, line_len) + pair)
    across = (b, c ^ 1)
    greet((ahead, behind, across))

    def to(step):
        return 2 * lax.rem(line - 1 - step + line_len, line_len)

    sent, given = [], []
    for i in range(many):
        for step in range(line_len):
            copy = remote(
                parts[i].at[to(step) + 1 - pair],
                pair_in[i].at[step],
                pair_sems.at[0, i, step],
                pair_sems.at[1, i, step],
                across,
            )
            copy.start()
            given.append(copy)
    for i in range(many):
        for step in range(line_len):
            given[i * line_len + step].wait_recv()
            total = parts[i][to(step) + pair].astype(F32) + pair_in[i][step].astype(F32)
            if step > 0:
                passed.wait_recv()
                total = total + line_in[i][step - 1].astype(F32)
            if step < line_len - 1:
                line_out[i][step] = total.astype(BF16)
                passed = remote(
                    line_out[i].at[step],
                    line_in[i].at[step],
                    line_sems.at[0, i, step],
                    line_sems.at[1, i, step],
                    ahead,
                )
                passed.start()
                sent.append(passed)
            else:
                outs[i][...] = total
    for copy in given + sent:
        copy.wait_send()


def scatter_ctx(parts, collective_id, name):
    n_ctx = lax.axis_size("ctx")
    line_len, many = n_ctx // 2, len(parts)
    blocks = [(part.shape[0] // n_ctx,) + part.shape[1:] for part in parts]

    def room(size):
        return [pltpu.VMEM((size,) + block, BF16) for block in blocks]

    return pl.pallas_call(
        functools.partial(scatter_kernel, line_len, many),
        out_shape=[jax.ShapeDtypeStruct(block, F32) for block in blocks],
        in_specs=[IN_VMEM] * many,
        out_specs=[IN_VMEM] * many,
        scratch_shapes=[
            *room(line_len),
            *room(line_len - 1),
            *room(line_len - 1),
            DMA((2, many, line_len)),
            DMA((2, many, line_len)),
        ],
        compiler_params=pltpu.CompilerParams(
            collective_id=collective_id, has_side_effects=True, vmem_limit_bytes=60 * 2**20
        ),
        cost_estimate=lasting(40),
        name=name,
    )(*[part.reshape((n_ctx,) + block) for part, block in zip(parts, blocks)])


def spread_kernel(
    line_len, q_weight, k_weight, v_weight, o_weight, small, gate, up, out, columns_out, own,
    columns, own_sem, line_sems, pair_sems, chip_sems, core_sems, column_sems,
):
    b, c = lax.axis_index("batch"), lax.axis_index("ctx")
    n_ctx = 2 * line_len
    line, pair = c // 2, c % 2
    ahead = (b, 2 * lax.rem(line + 1, line_len) + pair)
    across, chip, core = (b, c ^ 1), (b ^ 2, c), (b ^ 1, c)
    others = [(b, lax.rem(c + k, n_ctx)) for k in range(1, n_ctx)]
    at = 0
    for part in (q_weight, k_weight, v_weight, o_weight, small):
        own[:, at : at + part.shape[1]] = part[...]
        at += part.shape[1]
    greet([chip, core] + others)
    keep = [pltpu.make_async_copy(own, out.at[b, c], own_sem.at[0])]
    keep[0].start()

    def pack():
        n_batch, half = out.shape[0], columns.shape[2] // 2
        piece = gate.shape[1] // (n_batch * n_ctx)
        for first, weight in ((0, gate), (half, up)):
            if n_batch * piece < half:
                columns[:, :, first + half - 128 : first + half] = jnp.zeros(
                    (n_ctx, columns.shape[1], 128), BF16
                )
            for k in range(n_batch):
                for i in range(n_ctx):
                    to = (k * n_ctx + i) * piece
                    at = first + k * piece
                    columns[i, :, at : at + piece] = weight[:, to : to + piece]
        keep.append(pltpu.make_async_copy(columns.at[c], columns_out.at[c], own_sem.at[1]))
        keep[1].start()

    def place(step, side):
        return 2 * lax.rem(line - step + line_len, line_len) + side

    def hand(block, to_b, to_c, sems, index, device):
        copy = remote(block, out.at[to_b, to_c], sems.at[0, index], sems.at[1, index], device)
        copy.start()
        return copy

    on_line, on_pair, on_chip, on_core, on_columns = [], [], [], [], []
    for step in range(line_len):
        at = place(step, pair)
        block = own if step == 0 else out.at[b, at]
        if step > 0:
            on_line[step - 1].wait_recv()
        if step < line_len - 1:
            on_line.append(hand(block, b, at, line_sems, step, ahead))
        on_pair.append(hand(block, b, at, pair_sems, step, across))
        on_chip.append(hand(block, b, at, chip_sems, step, chip))
        on_core.append(hand(block, b, at, core_sems, step, core))
        if step == 0:
            pack()
    for k, device in enumerate(others):
        copy = remote(
            columns.at[device[1]],
            columns_out.at[c],
            column_sems.at[0, k],
            column_sems.at[1, k],
            device,
        )
        copy.start()
        on_columns.append(copy)
    for step in range(line_len):
        at = place(step, 1 - pair)
        on_pair[step].wait_recv()
        on_chip.append(hand(out.at[b, at], b, at, chip_sems, line_len + step, chip))
        on_core.append(hand(out.at[b, at], b, at, core_sems, line_len + step, core))
    for index in range(n_ctx):
        at = place(index % line_len, pair if index < line_len else 1 - pair)
        on_chip[index].wait_recv()
        on_core.append(hand(out.at[b ^ 2, at], b ^ 2, at, core_sems, n_ctx + index, core))
    for copy in on_core + on_columns:
        copy.wait()
    for copy in on_line + on_pair + on_chip:
        copy.wait_send()
    for copy in keep:
        copy.wait()


def spread(matrices, gate, up, collective_id, name):
    n_batch, n_ctx = lax.axis_size("batch"), lax.axis_size("ctx")
    line_len = n_ctx // 2
    rows = gate.shape[0]
    own = (rows, sum(matrix.shape[1] for matrix in matrices))
    columns = (n_ctx, rows, 2 * lanes(gate.shape[1] // n_ctx))
    return pl.pallas_call(
        functools.partial(spread_kernel, line_len),
        out_shape=(
            jax.ShapeDtypeStruct((n_batch, n_ctx) + own, BF16),
            jax.ShapeDtypeStruct(columns, BF16),
        ),
        in_specs=[IN_VMEM] * 7,
        out_specs=(ANYWHERE, ANYWHERE),
        scratch_shapes=[
            pltpu.VMEM(own, BF16),
            pltpu.VMEM(columns, BF16),
            DMA((2,)),
            DMA((2, line_len)),
            DMA((2, line_len)),
            DMA((2, n_ctx)),
            DMA((2, 2 * n_ctx)),
            DMA((2, n_ctx)),
        ],
        compiler_params=pltpu.CompilerParams(
            collective_id=collective_id, has_side_effects=True, vmem_limit_bytes=40 * 2**20
        ),
        cost_estimate=lasting(75),
        name=name,
    )(*matrices, gate, up)


def collect_kernel(line_len, *refs):
    grads, (sums_in, columns) = refs[:2], refs[2:4]
    outs, (sums_out, columns_out) = refs[4:6], refs[6:8]
    core_in, chip_in, pair_in, line_in, chip_out, pair_out, line_out = [
        refs[8 + 2 * i : 10 + 2 * i] for i in range(7)
    ]
    sums_got, sums_mine, own_sem = refs[22:25]
    core_sems, chip_sems, pair_sems, line_sems, column_sems, sums_sems = refs[25:]
    b, c = lax.axis_index("batch"), lax.axis_index("ctx")
    n_ctx = 2 * line_len
    line, pair = c // 2, c % 2
    ahead = (b, 2 * lax.rem(line + 1, line_len) + pair)
    across, chip, core = (b, c ^ 1), (b ^ 2, c), (b ^ 1, c)
    others = [(b, lax.rem(c + k, n_ctx)) for k in range(1, n_ctx)]
    on_same_line = others[1::2]
    greet([chip, core] + others)
    keep = pltpu.make_async_copy(columns.at[c], columns_out.at[c], own_sem)
    keep.start()

    def place(index):
        step, side = index // 2, index % 2
        to = lax.rem(line - 1 - step + line_len, line_len)
        return 2 * to + (1 - pair if side == 0 else pair)

    waits = []

    def send(block, target, sems, index, device):
        copy = remote(block, target, sems.at[0, index], sems.at[1, index], device)
        copy.start()
        waits.append(copy)
        return copy

    def start_sums(index, device):
        copy = remote(
            sums_mine, sums_got.at[index], sums_sems.at[0, index], sums_sems.at[1, index], device
        )
        copy.start()
        return copy

    def add_sums(index, copy):
        copy.wait()
        sums_mine[...] += sums_got[index]

    sums_mine[...] = sums_in[...]
    by_core = start_sums(0, core)
    to_core = [[], []]
    for index in range(2 * n_ctx):
        row = b ^ 3 if index < n_ctx else b ^ 1
        for i in range(2):
            to_core[i].append(
                send(
                    grads[i].at[row, place(index % n_ctx)],
                    core_in[i].at[index],
                    core_sems.at[i],
                    index,
                    core,
                )
            )
    add_sums(0, by_core)
    by_chip = start_sums(1, chip)
    on_columns = []
    for k, device in enumerate(others):
        copy = remote(
            columns.at[device[1]],
            columns_out.at[c],
            column_sems.at[0, k],
            column_sems.at[1, k],
            device,
        )
        copy.start()
        on_columns.append(copy)
    to_chip = [[], []]
    for index in range(n_ctx):
        for i in range(2):
            to_core[i][index].wait_recv()
            total = grads[i][b ^ 2, place(index)].astype(F32) + core_in[i][index].astype(F32)
            chip_out[i][index] = total.astype(BF16)
            to_chip[i].append(
                send(chip_out[i].at[index], chip_in[i].at[index], chip_sems.at[i], index, chip)
            )
    add_sums(1, by_chip)
    by_pair = start_sums(2, across)

    def mine(i, index):
        to_core[i][n_ctx + index].wait_recv()
        to_chip[i][index].wait_recv()
        return (
            grads[i][b, place(index)].astype(F32)
            + core_in[i][n_ctx + index].astype(F32)
            + chip_in[i][index].astype(F32)
        )

    to_pair, to_line = [[], []], [[], []]
    for step in range(line_len):
        for i in range(2):
            pair_out[i][step] = mine(i, 2 * step).astype(BF16)
            to_pair[i].append(
                send(pair_out[i].at[step], pair_in[i].at[step], pair_sems.at[i], step, across)
            )
        if step == 0:
            add_sums(2, by_pair)
            own_sums = [
                send(sums_mine, sums_got.at[3 + k], sums_sems, 3 + k, device)
                for k, device in enumerate(on_same_line)
            ]
        for i in range(2):
            total = mine(i, 2 * step + 1)
            to_pair[i][step].wait_recv()
            total = total + pair_in[i][step].astype(F32)
            if step > 0:
                to_line[i][step - 1].wait_recv()
                total = total + line_in[i][step - 1].astype(F32)
            if step < line_len - 1:
                line_out[i][step] = total.astype(BF16)
                to_line[i].append(
                    send(line_out[i].at[step], line_in[i].at[step], line_sems.at[i], step, ahead)
                )
            else:
                outs[i][...] = total
    total = sums_mine[...]
    for k, copy in enumerate(own_sums):
        copy.wait_recv()
        total = total + sums_got[3 + k]
    sums_out[...] = total
    for copy in on_columns:
        copy.wait()
    for copy in waits:
        copy.wait_send()
    keep.wait()


def collect(grads, sums, columns, collective_id, name):
    n_batch, n_ctx = lax.axis_size("batch"), lax.axis_size("ctx")
    line_len = n_ctx // 2
    blocks = [grad.shape[2:] for grad in grads]

    def room(size):
        return [pltpu.VMEM((size,) + block, BF16) for block in blocks]

    return pl.pallas_call(
        functools.partial(collect_kernel, line_len),
        out_shape=(
            *[jax.ShapeDtypeStruct(block, F32) for block in blocks],
            jax.ShapeDtypeStruct(sums.shape, F32),
            jax.ShapeDtypeStruct(columns.shape, BF16),
        ),
        in_specs=[IN_VMEM] * 3 + [ANYWHERE],
        out_specs=(IN_VMEM,) * 3 + (ANYWHERE,),
        scratch_shapes=[
            *room(2 * n_ctx),
            *room(n_ctx),
            *room(line_len),
            *room(line_len - 1),
            *room(n_ctx),
            *room(line_len),
            *room(line_len - 1),
            pltpu.VMEM((2 + line_len,) + sums.shape, F32),
            pltpu.VMEM(sums.shape, F32),
            DMA(()),
            DMA((2, 2, 2 * n_ctx)),
            DMA((2, 2, n_ctx)),
            DMA((2, 2, line_len)),
            DMA((2, 2, line_len)),
            DMA((2, n_ctx)),
            DMA((2, 2 + line_len)),
        ],
        compiler_params=pltpu.CompilerParams(
            collective_id=collective_id, has_side_effects=True, vmem_limit_bytes=60 * 2**20
        ),
        cost_estimate=lasting(70),
        name=name,
    )(*grads, sums, columns)


def row_scale(values):
    return lax.rsqrt(jnp.mean(values * values, axis=-1, keepdims=True) + EPSILON)


def turn_head(values, cosine, signed_sine, back=False):
    turned = pltpu.roll(values, HEAD_DIM // 2, 1) * signed_sine
    return values * cosine - turned if back else values * cosine + turned


def whole(*shape):
    return pl.BlockSpec(shape, lambda j: (0,) * len(shape))


def project_kernel(hidden, gain, weight, bias, cosine, signed_sine, normed, query, key_value, kept):
    j = pl.program_id(0)

    @pl.when(j == 0)
    def _():
        values = hidden[...].astype(F32)
        kept[...] = (values * row_scale(values) * gain[...]).astype(BF16)
        normed[...] = kept[...]

    lin = dot(kept[...], weight[...]) + bias[...]
    tables = cosine[...], signed_sine[...]
    heads = [lin[:, i * HEAD_DIM : (i + 1) * HEAD_DIM] for i in range(4)]

    @pl.when(j < 3)
    def _():
        for i in range(4):
            turned = turn_head(heads[i], *tables)
            query[:, i * HEAD_DIM : (i + 1) * HEAD_DIM] = turned.astype(BF16)

    @pl.when(j == 3)
    def _():
        for i in range(4):
            value = turn_head(heads[i], *tables) if i < KV_HEADS else heads[i]
            key_value[:, i * HEAD_DIM : (i + 1) * HEAD_DIM] = value.astype(BF16)


def project(hidden, gain, weights, bias, tables):
    count, width = hidden.shape
    wide = 2 * KVW
    table = whole(count, HEAD_DIM)
    return pl.pallas_call(
        project_kernel,
        grid=(4,),
        out_shape=(
            jax.ShapeDtypeStruct((count, width), BF16),
            jax.ShapeDtypeStruct((count, width), BF16),
            jax.ShapeDtypeStruct((count, wide), BF16),
        ),
        in_specs=[
            whole(count, width),
            whole(1, width),
            pl.BlockSpec((width, wide), lambda j: (0, j)),
            pl.BlockSpec((1, wide), lambda j: (0, j)),
            table,
            table,
        ],
        out_specs=(
            whole(count, width),
            pl.BlockSpec((count, wide), lambda j: (0, jnp.minimum(j, 2))),
            whole(count, wide),
        ),
        scratch_shapes=[pltpu.VMEM((count, width), BF16)],
        compiler_params=pltpu.CompilerParams(vmem_limit_bytes=40 * 2**20),
        cost_estimate=lasting(4),
        name="project",
    )(hidden, gain, weights, bias, *tables)


def mark_allowed(key_pos, key_doc, own_pos, own_doc, allowed):
    count = own_pos.shape[1]
    pos_column, doc_column = key_pos[...].T, key_doc[...].T
    for i in range(key_pos.shape[0]):
        seen = (pos_column[:, i : i + 1] <= own_pos[...]) & (doc_column[:, i : i + 1] == own_doc[...])
        allowed[i * count : (i + 1) * count] = jnp.where(seen, 1.0, 0.0)


def stack_heads(block, group):
    return jnp.concatenate(
        [block[:, i * HEAD_DIM : (i + 1) * HEAD_DIM] for i in range(group)], axis=0
    )


def lay_heads(stacked, group):
    count = stacked.shape[0] // group
    return jnp.concatenate([stacked[i * count : (i + 1) * count] for i in range(group)], axis=1)


def probabilities(keys, queries, allowed, group):
    scores = times_transposed(keys, queries) * INV_ROOT
    seen = jnp.concatenate([allowed[...]] * group, axis=1) > 0.0
    scores = jnp.where(seen, scores, MASKED)
    raised = jnp.exp(scores - jnp.max(scores, axis=0, keepdims=True))
    return raised * (1.0 / jnp.sum(raised, axis=0, keepdims=True))


def attend_kernel(
    group, last, query, keys, values, out_0, out_1, out_2, key_pos, key_doc, own_pos, own_doc,
    hidden, gain, attn_out, residual, normed, total, allowed,
):
    j = pl.program_id(0)

    @pl.when(j == 0)
    def _():
        total[...] = hidden[...].astype(F32)
        mark_allowed(key_pos, key_doc, own_pos, own_doc, allowed)

    probs = probabilities(keys[...], stack_heads(query[...], group), allowed, group)
    result = contract_rows(values[...], probs.astype(BF16)).T
    block = lay_heads(result, group).astype(BF16)
    attn_out[...] = block
    for t, weight in enumerate((out_0, out_1, out_2)):
        total[:, t * 512 : (t + 1) * 512] += dot(block, weight[...])

    @pl.when(j == last)
    def _():
        values = total[...]
        residual[...] = values
        normed[...] = (values * row_scale(values) * gain[...]).astype(BF16)


def head_specs(count, width, keys, group, weights_at):
    rows = group * HEAD_DIM
    per_key = GROUPS // group
    query = pl.BlockSpec((count, rows), lambda j: (0, j))
    heads = [
        pl.BlockSpec((keys, HEAD_DIM), lambda j, i=i: (0, KV_HEADS * i + j // per_key))
        for i in range(2)
    ]
    out = [
        pl.BlockSpec((rows, 512), lambda j, t=t: (j, weights_at // 512 + t))
        for t in range(width // 512)
    ]
    places = [whole(keys // count, count)] * 2 + [whole(1, count)] * 2
    return query, heads, out, places


def attend(query, key_value, weights, places, hidden, gain):
    count, width = hidden.shape
    keys = key_value.shape[0]
    group = 3 if keys <= 1024 else 1
    steps = HEADS // group
    query_spec, head_spec, out_spec, place_spec = head_specs(
        count, width, keys, group, width + 2 * KVW
    )
    return pl.pallas_call(
        functools.partial(attend_kernel, group, steps - 1),
        grid=(steps,),
        out_shape=(
            jax.ShapeDtypeStruct((count, width), BF16),
            jax.ShapeDtypeStruct((count, width), F32),
            jax.ShapeDtypeStruct((count, width), BF16),
        ),
        in_specs=[query_spec, *head_spec, *out_spec, *place_spec]
        + [whole(count, width), whole(1, width)],
        out_specs=(query_spec, whole(count, width), whole(count, width)),
        scratch_shapes=[pltpu.VMEM((count, width), F32), pltpu.VMEM((keys, count), F32)],
        compiler_params=pltpu.CompilerParams(vmem_limit_bytes=56 * 2**20),
        cost_estimate=lasting(10),
        name="attend",
    )(query, key_value, key_value, *[weights] * 3, *places, hidden, gain)


def attend_back_kernel(
    group, per_key, query, keys, values, out_0, out_1, out_2, key_pos, key_doc, own_pos, own_doc,
    attn_out, residual, gain, out_grad, d_normed, cosine, signed_sine, d_query, d_key_value,
    o_grad, d_residual, gain_grad, branch, allowed, key_sum, value_sum,
):
    j = pl.program_id(0)

    @pl.when(j == 0)
    def _():
        rows, grads = residual[...], d_normed[...]
        factor = row_scale(rows)
        scaled = grads * gain[...]
        gain_grad[...] = jnp.sum(grads * rows * factor, axis=0, keepdims=True)
        total = out_grad[...].astype(F32) + (
            factor * scaled
            - rows * (factor * factor * factor) * jnp.mean(scaled * rows, axis=-1, keepdims=True)
        )
        d_residual[...] = total
        branch[...] = total.astype(BF16)
        mark_allowed(key_pos, key_doc, own_pos, own_doc, allowed)

    @pl.when(lax.rem(j, per_key) == 0)
    def _():
        key_sum[...] = jnp.zeros_like(key_sum)
        value_sum[...] = jnp.zeros_like(value_sum)

    o_grad[...] = contract_rows(attn_out[...], branch[...]).astype(BF16)
    d_attn = sum(
        times_transposed(branch[:, t * 512 : (t + 1) * 512], weight[...])
        for t, weight in enumerate((out_0, out_1, out_2))
    ).astype(BF16)
    grads = stack_heads(d_attn, group)
    queries = stack_heads(query[...], group)
    probs = probabilities(keys[...], queries, allowed, group)
    d_probs = times_transposed(values[...], grads)
    delta = jnp.sum(probs * d_probs, axis=0, keepdims=True)
    d_scores = (probs * (d_probs - delta)).astype(BF16)
    key_sum[...] += dot(d_scores, queries)
    value_sum[...] += dot(probs.astype(BF16), grads)
    result = contract_rows(keys[...], d_scores).T * INV_ROOT
    count = result.shape[0] // group
    for i in range(group):
        head = turn_head(
            result[i * count : (i + 1) * count], cosine[...], signed_sine[...], back=True
        )
        d_query[:, i * HEAD_DIM : (i + 1) * HEAD_DIM] = head.astype(BF16)

    @pl.when(lax.rem(j, per_key) == per_key - 1)
    def _():
        at = pl.multiple_of(j // per_key * HEAD_DIM, HEAD_DIM)
        d_key_value[:, pl.ds(at, HEAD_DIM)] = (key_sum[...] * INV_ROOT).astype(BF16)
        d_key_value[:, pl.ds(KVW + at, HEAD_DIM)] = value_sum[...].astype(BF16)


def attend_back(query, key_value, weights, places, attn_out, residual, gain, out_grad, d_normed, tables):
    count, width = query.shape
    keys = key_value.shape[0]
    group = 3 if keys <= 1024 else 1
    steps = HEADS // group
    query_spec, head_spec, out_spec, place_spec = head_specs(
        count, width, keys, group, width + 2 * KVW
    )
    rows, table = whole(count, width), whole(count, HEAD_DIM)
    return pl.pallas_call(
        functools.partial(attend_back_kernel, group, GROUPS // group),
        grid=(steps,),
        out_shape=(
            jax.ShapeDtypeStruct((count, width), BF16),
            jax.ShapeDtypeStruct((keys, 2 * KVW), BF16),
            jax.ShapeDtypeStruct((width, width), BF16),
            jax.ShapeDtypeStruct((count, width), F32),
            jax.ShapeDtypeStruct((1, width), F32),
        ),
        in_specs=[query_spec, *head_spec, *out_spec, *place_spec, query_spec]
        + [rows, whole(1, width), rows, rows, table, table],
        out_specs=(
            query_spec,
            whole(keys, 2 * KVW),
            pl.BlockSpec((group * HEAD_DIM, width), lambda j: (j, 0)),
            rows,
            whole(1, width),
        ),
        scratch_shapes=[
            pltpu.VMEM((count, width), BF16),
            pltpu.VMEM((keys, count), F32),
            pltpu.VMEM((keys, HEAD_DIM), F32),
            pltpu.VMEM((keys, HEAD_DIM), F32),
        ],
        compiler_params=pltpu.CompilerParams(vmem_limit_bytes=60 * 2**20),
        cost_estimate=lasting(17),
        name="attend_back",
    )(
        query, key_value, key_value, *[weights] * 3, *places, attn_out, residual, gain, out_grad,
        d_normed, *tables,
    )


def project_back_kernel(
    d_query, d_key_value, weight, normed, hidden, gain, d_residual, gain_two_grad, cosine,
    signed_sine, grad, hidden_grad, sums, flipped, total, biases,
):
    j = pl.program_id(0)
    wide = weight.shape[1]

    @pl.when(j == 0)
    def _():
        flipped[...] = normed[...].astype(F32).T.astype(BF16)
        total[...] = jnp.zeros_like(total)
        sums[...] = jnp.zeros_like(sums)

    def add(d_lin):
        grad[...] = dot(flipped[...], d_lin).astype(BF16)
        total[...] += times_transposed(d_lin, weight[...])
        return jnp.sum(d_lin.astype(F32), axis=0, keepdims=True)

    for i in range(3):

        @pl.when(j == i)
        def _():
            sums[1:2, i * wide : (i + 1) * wide] = add(d_query[...])

    @pl.when(j == 3)
    def _():
        heads = [
            turn_head(
                d_key_value[:, i * HEAD_DIM : (i + 1) * HEAD_DIM],
                cosine[...],
                signed_sine[...],
                back=True,
            )
            for i in range(KV_HEADS)
        ]
        d_lin = jnp.concatenate(heads + [d_key_value[:, KVW:]], axis=1).astype(BF16)
        sums[2:3, :wide] = add(d_lin)
        rows, grads = hidden[...].astype(F32), total[...]
        factor = row_scale(rows)
        scaled = grads * gain[...]
        sums[0:1] = jnp.sum(grads * rows * factor, axis=0, keepdims=True)
        sums[3:4] = gain_two_grad[...]
        hidden_grad[...] = d_residual[...] + (
            factor * scaled
            - rows * (factor * factor * factor) * jnp.mean(scaled * rows, axis=-1, keepdims=True)
        )


def project_back(d_query, d_key_value, weights, normed, hidden, gain, d_residual, gain_two_grad, tables):
    count, width = hidden.shape
    wide = 2 * KVW
    rows, table = whole(count, width), whole(count, HEAD_DIM)
    return pl.pallas_call(
        project_back_kernel,
        grid=(4,),
        out_shape=(
            jax.ShapeDtypeStruct((width, width + wide), BF16),
            jax.ShapeDtypeStruct((count, width), F32),
            jax.ShapeDtypeStruct((8, width), F32),
        ),
        in_specs=[
            pl.BlockSpec((count, wide), lambda j: (0, jnp.minimum(j, 2))),
            whole(count, wide),
            pl.BlockSpec((width, wide), lambda j: (0, j)),
            rows,
            rows,
            whole(1, width),
            rows,
            whole(1, width),
            table,
            table,
        ],
        out_specs=(
            pl.BlockSpec((width, wide), lambda j: (0, j)),
            rows,
            whole(8, width),
        ),
        scratch_shapes=[
            pltpu.VMEM((width, count), BF16),
            pltpu.VMEM((count, width), F32),
            pltpu.VMEM((8, wide), F32),
        ],
        compiler_params=pltpu.CompilerParams(vmem_limit_bytes=48 * 2**20),
        cost_estimate=lasting(9),
        name="project_back",
    )(
        d_query, d_key_value, weights, normed, hidden, gain, d_residual, gain_two_grad, *tables
    )


def unpack_kernel(n_batch, piece, packed, gate, up):
    n_ctx, _, both = packed.shape
    for out, first in ((gate, 0), (up, both // 2)):
        for k in range(n_batch):
            for i in range(n_ctx):
                at = first + k * piece
                to = (k * n_ctx + i) * piece
                out[:, to : to + piece] = packed[i, :, at : at + piece].astype(F32)


def unpack(packed, n_batch, width):
    n_ctx, rows, _ = packed.shape
    out = jax.ShapeDtypeStruct((rows, width), F32)
    return pl.pallas_call(
        functools.partial(unpack_kernel, n_batch, width // (n_batch * n_ctx)),
        out_shape=(out, out),
        in_specs=[IN_VMEM],
        out_specs=(IN_VMEM, IN_VMEM),
        compiler_params=pltpu.CompilerParams(vmem_limit_bytes=40 * 2**20),
        cost_estimate=lasting(3),
        name="unpack",
    )(packed)


def mlp_kernel(line_len, tile, own_rows, *refs):
    n_batch, n_ctx = 4, 2 * line_len
    weights, (down, grads_in) = refs[:n_batch], refs[n_batch : n_batch + 2]
    d_rows_out, ff_out, down_out, gate_up_out = refs[n_batch + 2 : n_batch + 6]
    (
        tokens, flipped, gate_up, down_in, grads, mixed, mixed_flipped, d_gate_up, d_parts, ff_parts,
        d_pair, d_line, d_pass, ff_pair, ff_line, ff_pass, core_wide, chip_wide, down_terms,
        core_down, chip_down, own, load_sems, store_sems,
        line_sems, pair_sems, back_pair, back_line, batch_sems,
    ) = refs[n_batch + 6 :]
    b, c = lax.axis_index("batch"), lax.axis_index("ctx")
    line, pair = c // 2, c % 2
    ahead = (b, 2 * lax.rem(line + 1, line_len) + pair)
    behind = (b, 2 * lax.rem(line + line_len - 1, line_len) + pair)
    across, chip, core = (b, c ^ 1), (b ^ 2, c), (b ^ 1, c)
    count, width = own.shape
    half = gate_up.shape[1] // 2
    own_ff = down.shape[0]
    piece = own_ff // n_batch
    depth = width // n_batch
    for k in range(n_batch):
        source = pl.ds(pl.multiple_of((b ^ k) * depth, 128), depth)
        own[:, k * depth : (k + 1) * depth] = own_rows[:, source]
    greet((ahead, behind, across, chip, core))

    def at(step):
        return 2 * lax.rem(line - step + line_len, line_len)

    sent = []

    def send(source, target, sems, device):
        copy = remote(source, target, sems[0], sems[1], device)
        copy.start()
        sent.append(copy)
        return copy

    on_line, on_pair = [], []

    def forward(step):
        block = own if step == 0 else tokens.at[at(step) + pair]
        target = tokens.at[at(step) + pair]
        if step > 0:
            on_line[step - 1].wait_recv()
        if step < line_len - 1:
            sems = line_sems.at[0, step], line_sems.at[1, step]
            on_line.append(send(block, target, sems, ahead))
        sems = pair_sems.at[0, step], pair_sems.at[1, step]
        on_pair.append(send(block, target, sems, across))

    forward(0)
    loads = [pltpu.make_async_copy(own, tokens.at[c], load_sems.at[0])]
    for k, weight in enumerate(weights):
        loads.append(
            pltpu.make_async_copy(
                weight, gate_up.at[pl.ds(k * depth, depth)], load_sems.at[1 + k]
            )
        )
    loads.append(
        pltpu.make_async_copy(down, down_in.at[pl.ds(0, own_ff)], load_sems.at[1 + n_batch])
    )
    loads.append(pltpu.make_async_copy(grads_in, grads, load_sems.at[2 + n_batch]))
    for copy in loads:
        copy.start()
    if own_ff < half:
        down_in[own_ff:half] = jnp.zeros((half - own_ff, width), BF16)
    for copy in loads:
        copy.wait()

    def chunk(step):
        first = pl.multiple_of(at(step) * count, 2 * count)
        rows, pair_rows = pl.ds(first, 2 * count), pl.ds(at(step), 2)
        block = tokens[pair_rows].reshape(2 * count, width)
        grad_block = grads[pair_rows].reshape(2 * count, width)

        def columns(index, _):
            low = pl.multiple_of(index * tile, 128)
            high = pl.multiple_of(half + index * tile, 128)
            gate_lin = dot(block, gate_up[:, pl.ds(low, tile)])
            up_lin = dot(block, gate_up[:, pl.ds(high, tile)])
            d_mixed = times_transposed(grad_block, down_in[pl.ds(low, tile)])
            sigmoid = 1.0 / (1.0 + jnp.exp(-gate_lin))
            silu = gate_lin * sigmoid
            product = silu * up_lin
            mixed[:, pl.ds(low, tile)] = product.astype(BF16)
            mixed_flipped[pl.ds(low, tile), rows] = product.T.astype(BF16)
            d_gate = d_mixed * up_lin * sigmoid * (1.0 + gate_lin * (1.0 - sigmoid))
            d_gate_up[rows, pl.ds(low, tile)] = d_gate.astype(BF16)
            d_gate_up[rows, pl.ds(high, tile)] = (d_mixed * silu).astype(BF16)
            return 0

        lax.fori_loop(0, half // tile, columns, 0)

        def features(index, _):
            low = pl.multiple_of(index * depth, 128)
            at_low = pl.ds(low, depth)
            back = times_transposed(d_gate_up[rows], gate_up[at_low])
            d_parts[pair_rows, :, at_low] = back.astype(BF16).reshape(2, count, depth)
            return 0

        lax.fori_loop(0, n_batch, features, 0)

        def outputs(index, _):
            low = pl.multiple_of(index * depth, 128)
            at_low = pl.ds(low, depth)
            out = dot(mixed[...], down_in[:, at_low])
            ff_parts[pair_rows, :, at_low] = out.astype(BF16).reshape(2, count, depth)
            flipped[at_low, rows] = (
                tokens[pair_rows, :, at_low].reshape(2 * count, depth).astype(F32).T.astype(BF16)
            )
            return 0

        lax.fori_loop(0, n_batch, outputs, 0)

    moves = (
        (d_parts, d_pair, d_line, d_pass, d_rows_out),
        (ff_parts, ff_pair, ff_line, ff_pass, ff_out),
    )
    given = {}

    def give(index, which=0):
        parts, pairs = moves[which][:2]
        sems = back_pair.at[0, which, index], back_pair.at[1, which, index]
        source = parts.at[at(index + 1) + 1 - pair]
        given[index, which] = send(source, pairs.at[index], sems, across)

    for step in range(line_len):
        if step + 1 < line_len:
            forward(step + 1)
        on_pair[step].wait_recv()
        chunk(step)
        if step == line_len - 2:
            for index in range(line_len - 2):
                give(index)
    give(line_len - 2)
    give(line_len - 1)
    stores = []

    def store(source, target):
        copy = pltpu.make_async_copy(source, target, store_sems.at[len(stores)])
        copy.start()
        stores.append(copy)

    passed = {}

    def passing(index, which=0):
        parts, pairs, lines, passes, out = moves[which]
        given[index, which].wait_recv()
        total = parts[at(index + 1) + pair].astype(F32) + pairs[index].astype(F32)
        if index > 0:
            passed[index - 1, which].wait_recv()
            total = total + lines[index - 1].astype(F32)
        if index < line_len - 1:
            passes[index] = total.astype(BF16)
            sems = back_line.at[0, which, index], back_line.at[1, which, index]
            passed[index, which] = send(passes.at[index], lines.at[index], sems, ahead)
        elif which:
            out[...] = total
        else:
            for k in range(n_batch):
                target = pl.ds(pl.multiple_of((b ^ k) * depth, 128), depth)
                out[:, target] = total[:, k * depth : (k + 1) * depth]

    def batch_send(source, target, index, device):
        sems = batch_sems.at[0, index], batch_sems.at[1, index]
        return send(source, target, sems, device)

    def wide(k, side):
        return gate_up.at[pl.ds(k * depth, depth), pl.ds(side * half, half)]

    def weight_grad(k, side):
        def columns(index, _):
            at_low = pl.ds(pl.multiple_of(side * half + index * tile, 128), tile)
            grad = dot(flipped[k * depth : (k + 1) * depth], d_gate_up[:, at_low])
            gate_up[k * depth : (k + 1) * depth, at_low] = grad.astype(BF16)
            return 0

        lax.fori_loop(0, half // tile, columns, 0)

    def down_grads():
        for k in range(n_batch):
            grad = dot(
                mixed_flipped[k * piece : (k + 1) * piece],
                grads[...].reshape(n_ctx * count, width),
            )
            down_terms[k] = grad.astype(BF16)
        for slot, row in ((1, b ^ 3), (0, b ^ 1)):
            to_core["down", slot] = batch_send(
                down_terms.at[row], core_down.at[slot], 6 + slot, core
            )

    def pass_down():
        to_core["down", 1].wait_recv()
        total = down_terms[b ^ 2].astype(F32) + core_down[1].astype(F32)
        down_terms[b ^ 2] = total.astype(BF16)
        to_chip.append(batch_send(down_terms.at[b ^ 2], chip_down, 8, chip))

    def add_wide(k, side, terms):
        def columns(index, _):
            low = pl.multiple_of(index * tile, 128)
            at_low = pl.ds(pl.multiple_of(side * half + low, 128), tile)
            rows = slice(k * depth, (k + 1) * depth)
            total = gate_up[rows, at_low].astype(F32)
            for term in terms:
                total = total + term[:, pl.ds(low, tile)].astype(F32)
            gate_up[rows, at_low] = total.astype(BF16)
            return 0

        lax.fori_loop(0, half // tile, columns, 0)

    to_core, to_chip = {}, []

    def compute_and_send(k, side):
        weight_grad(k, side)
        slot = k // 2
        target = core_wide.at[slot, side]
        to_core[k, side] = batch_send(wide(k, side), target, 2 * slot + side, core)

    def compute_and_pass(side):
        weight_grad(2, side)
        to_core[3, side].wait_recv()
        add_wide(2, side, [core_wide.at[1, side]])
        to_chip.append(batch_send(wide(2, side), chip_wide.at[side], 4 + side, chip))

    compute_and_send(3, 0)
    compute_and_pass(0)
    compute_and_send(3, 1)
    compute_and_pass(1)
    work = [
        down_grads,
        lambda: (pass_down(), compute_and_send(1, 0)),
        lambda: compute_and_send(1, 1),
        lambda: (weight_grad(0, 0), weight_grad(0, 1)),
    ]
    for index in range(max(line_len, len(work))):
        if index < line_len:
            passing(index)
            give(index, 1)
        if index < len(work):
            work[index]()
    for index in range(line_len - 1):
        passing(index, 1)
    for side in range(2):
        to_core[1, side].wait_recv()
        to_chip[side].wait_recv()
        add_wide(0, side, [core_wide.at[0, side], chip_wide.at[side]])
        store(wide(0, side), gate_up_out.at[:, pl.ds(side * half, half)])
    to_core["down", 0].wait_recv()
    to_chip[2].wait_recv()
    down_out[...] = (
        down_terms[b].astype(F32) + core_down[0].astype(F32) + chip_down[...].astype(F32)
    )
    passing(line_len - 1, 1)
    for copy in sent:
        copy.wait_send()
    for copy in stores:
        copy.wait()


def mlp_scratch(n_ctx, n_batch, count, width, hidden_own):
    line_len, half = n_ctx // 2, lanes(hidden_own)
    tokens, piece = n_ctx * count, hidden_own // n_batch

    def room(*shape):
        return pltpu.VMEM(shape, BF16)

    return [
        room(n_ctx, count, width),
        room(width, tokens),
        room(width, 2 * half),
        room(half, width),
        room(n_ctx, count, width),
        room(2 * count, half),
        room(half, tokens),
        room(tokens, 2 * half),
        room(n_ctx, count, width),
        room(n_ctx, count, width),
        *[room(line_len, count, width), *[room(line_len - 1, count, width)] * 2] * 2,
        room(2, 2, width // n_batch, half),
        room(2, width // n_batch, half),
        room(n_batch, piece, width),
        room(2, piece, width),
        room(piece, width),
        room(count, width),
    ]


def mlp(own, weights, down, grads, collective_id, name):
    n_batch, n_ctx = lax.axis_size("batch"), lax.axis_size("ctx")
    line_len = n_ctx // 2
    count, width = own.shape
    half = weights[0].shape[1] // 2
    tile = 384 if half % 384 == 0 else 128
    return pl.pallas_call(
        functools.partial(mlp_kernel, line_len, tile),
        out_shape=(
            jax.ShapeDtypeStruct((count, width), F32),
            jax.ShapeDtypeStruct((count, width), F32),
            jax.ShapeDtypeStruct((down.shape[0] // n_batch, width), F32),
            jax.ShapeDtypeStruct(weights[0].shape, BF16),
        ),
        in_specs=[IN_VMEM] + [ANYWHERE] * (n_batch + 2),
        out_specs=(IN_VMEM, IN_VMEM, IN_VMEM, ANYWHERE),
        scratch_shapes=mlp_scratch(n_ctx, n_batch, count, width, down.shape[0])
        + [
            DMA((3 + n_batch,)),
            DMA((2,)),
            DMA((2, line_len)),
            DMA((2, line_len)),
            DMA((2, 2, line_len)),
            DMA((2, 2, line_len)),
            DMA((2, 9)),
        ],
        compiler_params=pltpu.CompilerParams(
            collective_id=collective_id, has_side_effects=True, vmem_limit_bytes=60 * 2**20
        ),
        cost_estimate=lasting(100),
        name=name,
    )(own, *weights, down, grads.reshape(n_ctx, count, width))


def front_kernel(line_len, group, *refs):
    (
        q_weight, k_weight, v_weight, o_weight, small, gate, up, hidden, cosine, signed_sine,
        own_pos, own_doc, down, out_grad,
    ) = refs[:14]
    (
        normed_out, query, attn_out, residual, normed_two, gain_one, gain_two, key_pos, key_doc,
        key_value_out, w_in_out, w_out_out, columns_out, near, far, farther, down_out, grads_out,
    ) = refs[14:32]
    own_in, w_in, w_out, columns, key_own, key_value, allowed, vectors, bias = refs[32:41]
    (
        load_sems, line_sems, first_sems, second_sems, core_sems, column_sems, near_sems, far_sems,
        farther_sems, keys_line_sems, keys_pair_sems, grads_line_sems, grads_pair_sems, down_sems,
    ) = refs[41:]
    b, c = lax.axis_index("batch"), lax.axis_index("ctx")
    n_batch, n_ctx = 4, 2 * line_len
    line, pair = c // 2, c % 2
    ahead = (b, 2 * lax.rem(line + 1, line_len) + pair)
    across, chip, core = (b, c ^ 1), (b ^ 2, c), (b ^ 1, c)
    others = [(b, lax.rem(c + k, n_ctx)) for k in range(1, n_ctx)]
    count, width = hidden.shape
    rows = q_weight.shape[0]
    wide = width + 2 * KVW
    at = 0
    for part in (q_weight, k_weight, v_weight):
        own_in[:, at : at + part.shape[1]] = part[...]
        at += part.shape[1]
    own_in[:, at:] = small[...]
    greet([chip, core] + others)
    sent, local = [], []

    def send(source, target, sems, index, device):
        copy = remote(source, target, sems.at[(0, *index)], sems.at[(1, *index)], device)
        copy.start()
        sent.append(copy)
        return copy

    def store(source, target):
        copy = pltpu.make_async_copy(source, target, load_sems.at[len(local)])
        copy.start()
        local.append(copy)

    owns, wholes = (own_in, o_weight), (w_in, w_out)
    first_to, second_to = (across, chip), (chip, across)
    on_line, on_first, on_second, on_core = {}, {}, {}, {}

    def place(step, side):
        return 2 * lax.rem(line - step + line_len, line_len) + side

    def block(p, row, column):
        first = pl.multiple_of((row * n_ctx + column) * rows, rows)
        return wholes[p].at[pl.ds(first, rows)]

    def line_step(p, step):
        target = block(p, b, place(step, pair))
        source = owns[p] if step == 0 else target
        if step > 0:
            on_line[p, step - 1].wait_recv()
        if step < line_len - 1:
            on_line[p, step] = send(source, target, line_sems, (p, step), ahead)
        on_first[p, step] = send(source, target, first_sems, (p, step), first_to[p])
        on_second[p, step] = send(source, target, second_sems, (p, step), second_to[p])
        on_core[p, step] = send(source, target, core_sems, (p, step), core)

    def first_step(p, step):
        on_first[p, step].wait_recv()
        row, side = ((b, 1 - pair), (b ^ 2, pair))[p]
        landed = block(p, row, place(step, side))
        index = line_len + step
        on_second[p, index] = send(landed, landed, second_sems, (p, index), second_to[p])
        on_core[p, index] = send(landed, landed, core_sems, (p, index), core)

    def second_step(p, index):
        on_second[p, index].wait_recv()
        late = index >= line_len
        row = b ^ 2 if p == 0 or late else b
        side = 1 - pair if p == 1 or late else pair
        landed = block(p, row, place(index % line_len, side))
        on_core[p, n_ctx + index] = send(landed, landed, core_sems, (p, n_ctx + index), core)

    def complete(p):
        for index in range(2 * n_ctx):
            on_core[p, index].wait_recv()

    on_down = []

    def down_step(step):
        if step == 0:
            store(down, down_out.at[b])
            on_down.append(send(down, down_out.at[b], down_sems, (0,), chip))
            on_down.append(send(down, down_out.at[b], down_sems, (1,), core))
        else:
            on_down[0].wait_recv()
            landed = down_out.at[b ^ 2]
            on_down.append(send(landed, landed, down_sems, (2,), core))

    def pack():
        half = columns.shape[2] // 2
        piece = gate.shape[1] // (n_batch * n_ctx)
        for first, weight in ((0, gate), (half, up)):
            if n_batch * piece < half:
                columns[:, :, first + half - 128 : first + half] = jnp.zeros(
                    (n_ctx, columns.shape[1], 128), BF16
                )
            for k in range(n_batch):
                for i in range(n_ctx):
                    to = (k * n_ctx + i) * piece
                    low = first + k * piece
                    columns[i, :, low : low + piece] = weight[:, to : to + piece]
        store(columns.at[c], columns_out.at[c])

    on_columns, on_near, on_far, on_farther = [], [], [], []

    def exchange_columns(first, last):
        for k in range(first, last):
            source = columns.at[others[k][1]]
            on_columns.append(send(source, columns_out.at[c], column_sems, (k,), others[k]))

    def spread_columns(k):
        slot = lax.rem(c - k + n_ctx, n_ctx)
        if k > 0:
            on_columns[k - 1].wait_recv()
        source = columns_out.at[slot] if k > 0 else columns.at[c]
        on_far.append(send(source, far.at[slot], far_sems, (k,), chip))
        on_near.append(send(source, near.at[slot], near_sems, (k,), core))

    def spread_farther(k):
        slot = lax.rem(c - k + n_ctx, n_ctx)
        on_far[k].wait_recv()
        on_farther.append(send(far.at[slot], farther.at[slot], farther_sems, (k,), core))

    keys_line, keys_pair = [], []

    def keys_step(step):
        column = place(step, pair)
        source = key_own if step == 0 else key_value.at[column]
        if step > 0:
            keys_line[step - 1].wait_recv()
        if step < line_len - 1:
            keys_line.append(send(source, key_value.at[column], keys_line_sems, (step,), ahead))
        keys_pair.append(send(source, key_value.at[column], keys_pair_sems, (step,), across))

    grads_line, grads_pair = [], []

    def grads_step(step):
        target = grads_out.at[place(step, pair)]
        source = out_grad if step == 0 else target
        if step > 0:
            grads_line[step - 1].wait_recv()
        if step < line_len - 1:
            grads_line.append(send(source, target, grads_line_sems, (step,), ahead))
        grads_pair.append(send(source, target, grads_pair_sems, (step,), across))

    line_step(0, 0)
    mine = pl.ds(pl.multiple_of((b * n_ctx + c) * rows, rows), rows)
    w_in[mine] = own_in[...]
    w_out[mine] = o_weight[...]
    pack()
    for step in range(1, line_len):
        line_step(0, step)
    exchange_columns(0, 2)
    line_step(1, 0)
    for step in range(line_len):
        first_step(0, step)
    between = [functools.partial(line_step, 1, step) for step in range(1, line_len)]
    between += [functools.partial(first_step, 1, step) for step in range(line_len)]
    between += [functools.partial(down_step, 0)]
    for index in range(n_ctx):
        second_step(0, index)
        between[index]()
        if index in (1, 3, 4, 5, 6):
            exchange_columns(len(on_columns), len(on_columns) + 1)
    store(out_grad, grads_out.at[c])
    complete(0)

    values = hidden[...].astype(F32)
    for d in range(n_batch * n_ctx):
        piece = w_in[d * rows : d * rows + 16, wide:].astype(F32)
        vectors[0:3, d * rows : (d + 1) * rows] = piece[0:3, :rows]
        part = KVW // (n_batch * n_ctx)
        for i in range(2):
            bias[0:1, i * KVW + d * part : i * KVW + (d + 1) * part] = piece[3 + i : 4 + i, :part]
    for k in range(n_ctx):
        first = pl.multiple_of((b * n_ctx + k) * rows, rows)
        piece = w_in[pl.ds(first, 16), wide:].astype(F32)
        key_pos[k : k + 1] = piece[5:6] * 64.0 + piece[6:7]
        key_doc[k : k + 1] = piece[7:8]
    gain_one[...] = vectors[0:1]
    gain_two[...] = vectors[1:2]
    normed_out[...] = (values * row_scale(values) * vectors[0:1]).astype(BF16)
    tables = cosine[...], signed_sine[...]
    lin = dot(normed_out[...], w_in[:, width:wide]) + bias[...]
    for i in range(2 * KV_HEADS):
        head = lin[:, i * HEAD_DIM : (i + 1) * HEAD_DIM]
        head = turn_head(head, *tables) if i < KV_HEADS else head
        key_own[:, i * HEAD_DIM : (i + 1) * HEAD_DIM] = head.astype(BF16)
    keys_step(0)
    key_value[c] = key_own[...]
    for k in range(3):
        step = width // 3
        part = slice(k * step, (k + 1) * step)
        lin = dot(normed_out[...], w_in[:, part]) + vectors[2:3, part]
        for i in range(step // HEAD_DIM):
            head = turn_head(lin[:, i * HEAD_DIM : (i + 1) * HEAD_DIM], *tables)
            low = k * step + i * HEAD_DIM
            query[:, low : low + HEAD_DIM] = head.astype(BF16)
    store(w_in, w_in_out)
    mark_allowed(key_pos, key_doc, own_pos, own_doc, allowed)
    spread_columns(0)
    for step in range(1, line_len):
        second_step(1, step - 1)
        keys_step(step)
    for step in range(line_len):
        keys_pair[step].wait_recv()
    store(key_value, key_value_out)
    grads_step(0)

    def attention(i):
        wide_part = group * HEAD_DIM
        part = slice(i * wide_part, (i + 1) * wide_part)
        head = i * group // GROUPS * HEAD_DIM
        keys = key_value[:, :, head : head + HEAD_DIM].reshape(n_ctx * count, HEAD_DIM)
        low = KVW + head
        values = key_value[:, :, low : low + HEAD_DIM].reshape(n_ctx * count, HEAD_DIM)
        probs = probabilities(keys, stack_heads(query[:, part], group), allowed, group)
        result = contract_rows(values, probs.astype(BF16)).T
        attn_out[:, part] = lay_heads(result, group).astype(BF16)

    steps = HEADS // group
    for i in range(steps):
        attention(i)
        for index in range(line_len - 1 + i, n_ctx, steps):
            second_step(1, index)
        for k in range(1 + 2 * i, min(3 + 2 * i, n_ctx)):
            spread_columns(k)
        if i == steps // 2:
            grads_step(1)
    down_step(1)
    complete(1)
    store(w_out, w_out_out)
    total = hidden[...].astype(F32) + dot(attn_out[...], w_out[...])
    residual[...] = total
    normed_two[...] = (total * row_scale(total) * vectors[1:2]).astype(BF16)
    grads_step(2)
    for k in range(n_ctx // 2):
        spread_farther(k)
    for step in range(3, line_len):
        grads_step(step)
    for k in range(n_ctx // 2, n_ctx):
        spread_farther(k)
    for copy in on_near + on_farther + grads_pair + on_down[1:]:
        copy.wait_recv()
    for copy in sent:
        copy.wait_send()
    for copy in local:
        copy.wait()


def front(matrices, gate, up, hidden, tables, own_places, down, out_grad, collective_id, name):
    n_batch, n_ctx = lax.axis_size("batch"), lax.axis_size("ctx")
    line_len = n_ctx // 2
    rows = gate.shape[0]
    count, width = hidden.shape
    wide = width + 2 * KVW
    columns = (n_ctx, rows, 2 * lanes(gate.shape[1] // n_ctx))

    def shaped(dtype, *shape):
        return jax.ShapeDtypeStruct(shape, dtype)

    def room(*shape, dtype=BF16):
        return pltpu.VMEM(shape, dtype)

    return pl.pallas_call(
        functools.partial(front_kernel, line_len, 3),
        out_shape=(
            shaped(BF16, count, width),
            shaped(BF16, count, width),
            shaped(BF16, count, width),
            shaped(F32, count, width),
            shaped(BF16, count, width),
            shaped(F32, 1, width),
            shaped(F32, 1, width),
            shaped(F32, n_ctx, count),
            shaped(F32, n_ctx, count),
            shaped(BF16, n_ctx, count, 2 * KVW),
            shaped(BF16, width, wide + 128),
            shaped(BF16, width, width),
            *[shaped(BF16, *columns)] * 4,
            shaped(BF16, n_batch, *down.shape),
            shaped(BF16, n_ctx, count, width),
        ),
        in_specs=[IN_VMEM] * 14,
        out_specs=(IN_VMEM,) * 9 + (ANYWHERE,) * 9,
        scratch_shapes=[
            room(rows, wide + 128),
            room(width, wide + 128),
            room(width, width),
            room(*columns),
            room(count, 2 * KVW),
            room(n_ctx, count, 2 * KVW),
            room(n_ctx * count, count, dtype=F32),
            room(8, width, dtype=F32),
            room(1, 2 * KVW, dtype=F32),
            DMA((6,)),
            DMA((2, 2, line_len)),
            DMA((2, 2, line_len)),
            DMA((2, 2, n_ctx)),
            DMA((2, 2, 2 * n_ctx)),
            DMA((2, n_ctx)),
            DMA((2, n_ctx)),
            DMA((2, n_ctx)),
            DMA((2, n_ctx)),
            DMA((2, line_len)),
            DMA((2, line_len)),
            DMA((2, line_len)),
            DMA((2, line_len)),
            DMA((2, 3)),
        ],
        compiler_params=pltpu.CompilerParams(
            collective_id=collective_id, has_side_effects=True, vmem_limit_bytes=58 * 2**20
        ),
        cost_estimate=lasting(100),
        name=name,
    )(*matrices, gate, up, hidden, *tables, *own_places, down, out_grad)


def back_kernel(line_len, group, *refs):
    (
        query, key_value, key_pos, key_doc, own_pos, own_doc, attn_out, residual, gain_two, out_grad,
        d_normed, cosine, signed_sine, normed, hidden, gain_one, in_weights, out_weights, columns,
    ) = refs[:19]
    hidden_grad, o_out, q_out, kv_out, sums_out, columns_out = refs[19:25]
    w_out, w_in, branch, allowed, key_sum, value_sum, d_query, flipped, d_residual = refs[25:34]
    d_key_value, keys_pair, keys_line, keys_pass, sums_got, sums_mine = refs[34:40]
    grads = refs[40:43]
    core_in, chip_in, pair_in, line_in, chip_out, pair_out, line_out = [
        refs[43 + 3 * i : 46 + 3 * i] for i in range(7)
    ]
    (
        load_sems, column_sems, keys_pair_sems, keys_line_sems, sums_sems, core_sems, chip_sems,
        pair_sems, line_sems,
    ) = refs[64:]
    outs = o_out, q_out, kv_out
    b, c = lax.axis_index("batch"), lax.axis_index("ctx")
    n_ctx = 2 * line_len
    line, pair = c // 2, c % 2
    ahead = (b, 2 * lax.rem(line + 1, line_len) + pair)
    across, chip, core = (b, c ^ 1), (b ^ 2, c), (b ^ 1, c)
    others = [(b, lax.rem(c + k, n_ctx)) for k in range(1, n_ctx)]
    on_same_line = others[1::2]
    count, width = query.shape
    wide = group * HEAD_DIM
    rows = q_out.shape[0]
    greet([chip, core] + others)
    sent = []

    def send(source, target, sems, index, device):
        copy = remote(source, target, sems.at[(0, *index)], sems.at[(1, *index)], device)
        copy.start()
        sent.append(copy)
        return copy

    loads = [
        pltpu.make_async_copy(out_weights, w_out, load_sems.at[0]),
        pltpu.make_async_copy(in_weights.at[:, pl.ds(0, width + 2 * KVW)], w_in, load_sems.at[1]),
        pltpu.make_async_copy(columns.at[c], columns_out.at[c], load_sems.at[2]),
    ]
    for copy in loads:
        copy.start()
    on_columns = []

    def exchange_columns(first, last):
        for k in range(first, last):
            source = columns.at[others[k][1]]
            on_columns.append(send(source, columns_out.at[c], column_sems, (k,), others[k]))

    exchange_columns(0, n_ctx - 1)

    def to(step):
        return 2 * lax.rem(line - 1 - step + line_len, line_len)

    def place(index):
        return to(index // 2) + (1 - pair if index % 2 == 0 else pair)

    def block(row, index):
        at = (row * n_ctx + place(index)) * rows
        return pl.ds(pl.multiple_of(at, rows), rows)

    to_core, to_chip, to_pair, to_line = {}, {}, {}, {}

    def core_stage(p):
        for index in range(2 * n_ctx):
            row = b ^ 3 if index < n_ctx else b ^ 1
            source = grads[p].at[block(row, index % n_ctx)]
            to_core[p, index] = send(source, core_in[p].at[index], core_sems, (p, index), core)

    def chip_stage(p):
        for index in range(n_ctx):
            to_core[p, index].wait_recv()
            total = grads[p][block(b ^ 2, index)].astype(F32) + core_in[p][index].astype(F32)
            chip_out[p][index] = total.astype(BF16)
            to_chip[p, index] = send(
                chip_out[p].at[index], chip_in[p].at[index], chip_sems, (p, index), chip
            )

    def mine(p, index):
        to_core[p, n_ctx + index].wait_recv()
        to_chip[p, index].wait_recv()
        return (
            grads[p][block(b, index)].astype(F32)
            + core_in[p][n_ctx + index].astype(F32)
            + chip_in[p][index].astype(F32)
        )

    def pair_stage(p, step):
        pair_out[p][step] = mine(p, 2 * step).astype(BF16)
        to_pair[p, step] = send(
            pair_out[p].at[step], pair_in[p].at[step], pair_sems, (p, step), across
        )

    def line_stage(p, step):
        total = mine(p, 2 * step + 1)
        to_pair[p, step].wait_recv()
        total = total + pair_in[p][step].astype(F32)
        if step > 0:
            to_line[p, step - 1].wait_recv()
            total = total + line_in[p][step - 1].astype(F32)
        if step < line_len - 1:
            line_out[p][step] = total.astype(BF16)
            to_line[p, step] = send(
                line_out[p].at[step], line_in[p].at[step], line_sems, (p, step), ahead
            )
        else:
            outs[p][...] = total

    values, gradient = residual[...], d_normed[...]
    factor = row_scale(values)
    scaled = gradient * gain_two[...]
    sums_mine[...] = jnp.zeros_like(sums_mine)
    sums_mine[3:4] = jnp.sum(gradient * values * factor, axis=0, keepdims=True)
    total = out_grad[...].astype(F32) + (
        factor * scaled
        - values * (factor * factor * factor) * jnp.mean(scaled * values, axis=-1, keepdims=True)
    )
    d_residual[...] = total
    branch[...] = total.astype(BF16)
    for i in range(HEADS // group):
        part = slice(i * wide, (i + 1) * wide)
        grads[0][part] = contract_rows(attn_out[:, part], branch[...]).astype(BF16)
    core_stage(0)
    mark_allowed(key_pos, key_doc, own_pos, own_doc, allowed)
    flipped[...] = normed[...].astype(F32).T.astype(BF16)
    tables = cosine[...], signed_sine[...]

    def attention(i):
        part = slice(i * wide, (i + 1) * wide)
        head = i * group // GROUPS
        key_part = slice(head * HEAD_DIM, (head + 1) * HEAD_DIM)
        value_part = slice(KVW + head * HEAD_DIM, KVW + (head + 1) * HEAD_DIM)
        keys, values = key_value[:, key_part], key_value[:, value_part]
        d_attn = times_transposed(branch[...], w_out[part]).astype(BF16)
        head_grads, queries = stack_heads(d_attn, group), stack_heads(query[:, part], group)
        probs = probabilities(keys, queries, allowed, group)
        d_probs = times_transposed(values, head_grads)
        delta = jnp.sum(probs * d_probs, axis=0, keepdims=True)
        d_scores = (probs * (d_probs - delta)).astype(BF16)
        key_term = dot(d_scores, queries)
        value_term = dot(probs.astype(BF16), head_grads)
        first = i * group % GROUPS == 0
        key_sum[...] = key_term if first else key_sum[...] + key_term
        value_sum[...] = value_term if first else value_sum[...] + value_term
        result = contract_rows(keys, d_scores).T * INV_ROOT
        for k in range(group):
            turned = turn_head(result[k * count : (k + 1) * count], *tables, back=True)
            at = (i * group + k) * HEAD_DIM
            d_query[:, at : at + HEAD_DIM] = turned.astype(BF16)
        if (i + 1) * group % GROUPS == 0:
            shape = d_key_value.shape[:2] + (HEAD_DIM,)
            d_key_value[:, :, key_part] = (key_sum[...] * INV_ROOT).astype(BF16).reshape(shape)
            d_key_value[:, :, value_part] = value_sum[...].astype(BF16).reshape(shape)

    loads[0].wait()
    attention(0)
    chip_stage(0)
    for i in range(1, HEADS // group):
        attention(i)

    given, passed = [], []
    for step in range(line_len):
        source = d_key_value.at[to(step) + 1 - pair]
        given.append(send(source, keys_pair.at[step], keys_pair_sems, (step,), across))
    key_total = None

    def keys_stage(step):
        given[step].wait_recv()
        total = d_key_value[to(step) + pair].astype(F32) + keys_pair[step].astype(F32)
        if step > 0:
            passed[step - 1].wait_recv()
            total = total + keys_line[step - 1].astype(F32)
        if step < line_len - 1:
            keys_pass[step] = total.astype(BF16)
            passed.append(
                send(keys_pass.at[step], keys_line.at[step], keys_line_sems, (step,), ahead)
            )
        return total

    last = line_len - 1
    for step in range(line_len // 2):
        pair_stage(0, step)
    half = width // 2
    for i in range(2):
        part = slice(i * half, (i + 1) * half)
        grads[1][:, part] = dot(flipped[...], d_query[:, part]).astype(BF16)
        if i == 0:
            keys_stage(0)
    core_stage(1)
    loads[1].wait()
    d_one = times_transposed(d_query[...], w_in[:, :width])
    for step in range(1, line_len):
        key_total = keys_stage(step)
        if step == 1:
            chip_stage(1)
        if line_len // 2 + step - 1 < line_len:
            pair_stage(0, line_len // 2 + step - 1)
        if step < last:
            line_stage(0, step - 1)
    heads = [
        turn_head(key_total[:, i * HEAD_DIM : (i + 1) * HEAD_DIM], *tables, back=True)
        for i in range(KV_HEADS)
    ]
    d_lin = jnp.concatenate(heads + [key_total[:, KVW:]], axis=1).astype(BF16)
    grads[2][...] = dot(flipped[...], d_lin).astype(BF16)
    core_stage(2)
    line_stage(0, last - 1)
    d_one = d_one + times_transposed(d_lin, w_in[:, width:])
    sums_mine[1:2] = jnp.sum(d_query[...].astype(F32), axis=0, keepdims=True)
    sums_mine[2:3, : 2 * KVW] = jnp.sum(d_lin.astype(F32), axis=0, keepdims=True)
    values = hidden[...].astype(F32)
    factor = row_scale(values)
    scaled = d_one * gain_one[...]
    sums_mine[0:1] = jnp.sum(d_one * values * factor, axis=0, keepdims=True)

    def start_sums(index, device):
        copy = remote(
            sums_mine, sums_got.at[index], sums_sems.at[0, index], sums_sems.at[1, index], device
        )
        copy.start()
        return copy

    def add_sums(index, copy):
        copy.wait()
        sums_mine[...] += sums_got[index]

    by_core = start_sums(0, core)
    pair_stage(1, 0)
    line_stage(0, last)
    add_sums(0, by_core)
    by_chip = start_sums(1, chip)
    chip_stage(2)
    hidden_grad[...] = d_residual[...] + (
        factor * scaled
        - values * (factor * factor * factor) * jnp.mean(scaled * values, axis=-1, keepdims=True)
    )
    for step in range(1, line_len):
        pair_stage(1, step)
        line_stage(1, step - 1)
    add_sums(1, by_chip)
    by_pair = start_sums(2, across)
    pair_stage(2, 0)
    line_stage(1, last)
    for step in range(1, line_len):
        pair_stage(2, step)
        line_stage(2, step - 1)
        if step == 1:
            add_sums(2, by_pair)
            by_line = [start_sums(3 + k, device) for k, device in enumerate(on_same_line)]
    line_stage(2, last)
    total = sums_mine[...]
    for k, copy in enumerate(by_line):
        copy.wait()
        total = total + sums_got[3 + k]
    sums_out[...] = total
    for copy in on_columns:
        copy.wait_recv()
    for copy in sent:
        copy.wait_send()
    loads[2].wait()


def back(query, key_value, weights, places, attn_out, residual, gain_two, out_grad, d_normed, tables, normed, hidden, gain_one, columns, collective_id, name):
    n_ctx = columns.shape[0]
    line_len, rows = n_ctx // 2, columns.shape[1]
    count, width = query.shape
    keys = key_value.shape[0]
    widths = width, width, 2 * KVW

    def room(*shape, dtype=BF16):
        return pltpu.VMEM(shape, dtype)

    def rooms(size):
        return [room(size, rows, part) for part in widths]

    outs = [(count, width)] + [(rows, part) for part in widths] + [(8, width)]
    return pl.pallas_call(
        functools.partial(back_kernel, line_len, 3),
        out_shape=(
            *[jax.ShapeDtypeStruct(shape, F32) for shape in outs],
            jax.ShapeDtypeStruct(columns.shape, BF16),
        ),
        in_specs=[IN_VMEM] * 16 + [ANYWHERE] * 3,
        out_specs=(IN_VMEM,) * 5 + (ANYWHERE,),
        scratch_shapes=[
            room(width, width),
            room(width, width + 2 * KVW),
            room(count, width),
            room(keys, count, dtype=F32),
            room(keys, HEAD_DIM, dtype=F32),
            room(keys, HEAD_DIM, dtype=F32),
            room(count, width),
            room(width, count),
            room(count, width, dtype=F32),
            room(n_ctx, count, 2 * KVW),
            room(line_len, count, 2 * KVW),
            room(line_len - 1, count, 2 * KVW),
            room(line_len - 1, count, 2 * KVW),
            room(2 + line_len, 8, width, dtype=F32),
            room(8, width, dtype=F32),
            *[room(width, part) for part in widths],
            *rooms(2 * n_ctx),
            *rooms(n_ctx),
            *rooms(line_len),
            *rooms(line_len - 1),
            *rooms(n_ctx),
            *rooms(line_len),
            *rooms(line_len - 1),
            DMA((3,)),
            DMA((2, n_ctx)),
            DMA((2, line_len)),
            DMA((2, line_len)),
            DMA((2, 2 + line_len)),
            DMA((2, 3, 2 * n_ctx)),
            DMA((2, 3, n_ctx)),
            DMA((2, 3, line_len)),
            DMA((2, 3, line_len)),
        ],
        compiler_params=pltpu.CompilerParams(
            collective_id=collective_id, has_side_effects=True, vmem_limit_bytes=60 * 2**20
        ),
        cost_estimate=lasting(90),
        name=name,
    )(
        query, key_value, *places, attn_out, residual, gain_two, out_grad, d_normed, *tables, normed,
        hidden, gain_one, *weights, columns,
    )


def swap(values, bit):
    size = lax.axis_size("batch")
    return lax.ppermute(values, "batch", [(i, i ^ bit) for i in range(size)])


def by_batch(values, b, n_batch):
    step = values.shape[1] // n_batch
    blocks = [lax.dynamic_slice_in_dim(values, (b ^ k) * step, step, 1) for k in range(n_batch)]
    return jnp.concatenate(blocks, axis=1)


def batch_terms(terms):
    passed = swap((terms[2].astype(F32) + swap(terms[3], 1).astype(F32)).astype(BF16), 2)
    return [term.astype(F32) for term in (terms[0], swap(terms[1], 1), passed)]


def mlp_room(*sizes):
    return 2 * sum(math.prod(room.shape) for room in mlp_scratch(*sizes))


def mlp_in_steps(normed_two, w_gate_up, w_down, out_grad_all):
    n_batch, b = lax.axis_size("batch"), lax.axis_index("batch")
    normed_two = by_batch(normed_two, b, n_batch)
    w_gate_up = jnp.concatenate(w_gate_up, axis=0)
    half, width = w_gate_up.shape[1] // 2, normed_two.shape[1]
    own_ff = w_down.shape[0]
    w_down = jnp.pad(w_down, ((0, half - own_ff), (0, 0)))
    normed_two = gather_ctx(normed_two, 3, "gather_tokens").reshape(-1, width)
    gate_up = dot(normed_two, w_gate_up)
    gate_lin, up_lin = gate_up[:, :half], gate_up[:, half:]
    sigmoid_gate = jax.nn.sigmoid(gate_lin)
    mixed_rows = (gate_lin * sigmoid_gate * up_lin).astype(BF16)
    d_mixed = times_transposed(out_grad_all, w_down)
    d_gate = d_mixed * up_lin * sigmoid_gate * (1.0 + gate_lin * (1.0 - sigmoid_gate))
    d_up = d_mixed * (gate_lin * sigmoid_gate)
    d_gate_up = jnp.concatenate([d_gate.astype(BF16), d_up.astype(BF16)], axis=1)
    (d_normed_two,) = scatter_ctx(
        [times_transposed(d_gate_up, w_gate_up).astype(BF16)], 4, "scatter_tokens"
    )
    (ff_out,) = scatter_ctx([dot(mixed_rows, w_down).astype(BF16)], 8, "scatter_outputs")
    gate_up_grad = contract_rows(normed_two, d_gate_up).astype(BF16).reshape(n_batch, -1, 2 * half)
    down_grad = contract_rows(mixed_rows, out_grad_all).astype(BF16)[:own_ff]
    return (
        by_batch(d_normed_two, b, n_batch),
        ff_out,
        sum(
            batch_terms(
                [
                    lax.dynamic_index_in_dim(
                        down_grad.reshape(n_batch, -1, width), b ^ k, 0, keepdims=False
                    )
                    for k in range(n_batch)
                ]
            )
        ),
        sum(batch_terms(gate_up_grad)).astype(BF16),
    )


def vector_rows(vectors, rows, pieces):
    laid = [
        jnp.pad(v.reshape(pieces, 1, -1), ((0, 0), (0, 0), (0, 128 - v.shape[0] // pieces)))
        for v in vectors
    ]
    return jnp.pad(jnp.concatenate(laid, axis=1), ((0, 0), (0, rows - len(vectors)), (0, 0)))


def local(
    hidden_in,
    positions,
    doc_ids,
    attn_gain,
    q_weight,
    q_bias,
    k_weight,
    k_bias,
    v_weight,
    v_bias,
    o_weight,
    mlp_gain,
    gate_weight,
    up_weight,
    down_weight,
    out_grad,
):
    n_batch, n_ctx = lax.axis_size("batch"), lax.axis_size("ctx")
    n_all = n_batch * n_ctx
    count, width = hidden_in.shape
    hidden_ff = gate_weight.shape[1]

    b = lax.axis_index("batch")
    rows = q_weight.shape[0]
    small = (attn_gain, mlp_gain, q_bias, k_bias, v_bias)
    places = (positions // 64, positions % 64, doc_ids)
    small = vector_rows(small + tuple(row.astype(BF16) for row in places), rows, 1)[0]
    matrices = (q_weight, k_weight, v_weight, o_weight, small)
    cosine, sine_table = rope_tables(positions)
    half_lane = jnp.arange(HEAD_DIM) < HEAD_DIM // 2
    tables = cosine, jnp.where(half_lane[None], -sine_table, sine_table)
    own_places = positions.astype(F32)[None], doc_ids.astype(F32)[None]
    together = rows % 16 == 0
    if together:
        (
            normed_one, query, attn_out, residual, normed_two, gain_one, gain_two, key_pos, key_doc,
            key_value, *weights, packed, near, far, farther, w_down, out_grad_all,
        ) = front(
            matrices, gate_weight, up_weight, hidden_in, tables, own_places, down_weight, out_grad, 1,
            "front",
        )
        w_down = w_down.reshape(-1, width)
        half = packed.shape[2] // 2
        key_value = key_value.reshape(-1, 2 * KVW)
        w_gate_up = [columns.reshape(-1, 2 * half) for columns in (packed, near, far, farther)]
        places = (key_pos, key_doc, *own_places)
    else:
        w_down = lax.all_gather(down_weight, "batch", axis=0, tiled=True)
        out_grad_all = lax.all_gather(out_grad, "ctx", axis=0, tiled=True)
        attn_all, packed = spread(matrices, gate_weight, up_weight, 1, "spread_weights")
        half = packed.shape[2] // 2
        own_rows = packed.reshape(-1, 2 * half)
        near, far = swap(own_rows, 1), swap(own_rows, 2)
        small = attn_all[:, :, :8, attn_all.shape[3] - 128 :].astype(F32)
        gain_one, gain_two, b_query, b_key, b_value = (
            small[:, :, i, : part.shape[0]].reshape(-1)
            for i, part in enumerate((attn_gain, mlp_gain, q_bias, k_bias, v_bias))
        )
        places = lax.dynamic_index_in_dim(small, b, 0, keepdims=False)[:, 5:8, :count]
        key_pos, key_doc = places[:, 0] * 64 + places[:, 1], places[:, 2]
        attn_all = attn_all.reshape(width, -1)
        b_qkv = jnp.concatenate([b_query, b_key, b_value])
        gain_one, gain_two = gain_one[None], gain_two[None]

        normed_one, query, key_value = project(hidden_in, gain_one, attn_all, b_qkv[None], tables)
        key_value = gather_ctx(key_value, 2, "gather_keys").reshape(-1, 2 * KVW)
        far, key_value = lax.optimization_barrier((far, key_value))
        w_gate_up = (own_rows, near, far, swap(far, 1))
        places = (key_pos, key_doc, *own_places)
        attn_out, residual, normed_two = attend(
            query, key_value, attn_all, places, hidden_in, gain_two
        )

    fits = mlp_room(n_ctx, n_batch, count, width, w_down.shape[0]) < 56 * 2**20
    feed_forward = functools.partial(mlp, collective_id=3, name="mlp") if fits else mlp_in_steps
    d_normed_two, ff_out, down_grad, gate_up_grad = feed_forward(
        normed_two, w_gate_up, w_down, out_grad_all.reshape(-1, width)
    )
    hidden_out = (residual + ff_out).astype(BF16)

    columns = gate_up_grad.reshape(n_ctx, rows, 2 * half)
    if together:
        hidden_grad, o_grad, q_grad, kv_grad, sums, gate_up_grad = back(
            query, key_value, weights, places, attn_out, residual, gain_two, out_grad,
            d_normed_two, tables, normed_one, hidden_in, gain_one, columns, 7, "back"
        )
        k_grad, v_grad = kv_grad[:, :KVW], kv_grad[:, KVW:]
    else:
        d_query, d_key_value, o_grad, d_residual, gain_two_grad = attend_back(
            query, key_value, attn_all, places, attn_out, residual, gain_two, out_grad,
            d_normed_two, tables,
        )
        (d_key_value,) = scatter_ctx([d_key_value], 5, "scatter_keys")
        qkv_grad, hidden_grad, sums = project_back(
            d_query, d_key_value, attn_all, normed_one, hidden_in, gain_one, d_residual,
            gain_two_grad, tables,
        )
        grads = [grad.reshape(n_batch, n_ctx, rows, -1) for grad in (qkv_grad, o_grad)]
        qkv_grad, o_grad, sums, gate_up_grad = collect(grads, sums, columns, 6, "collect")
        q_grad, k_grad = qkv_grad[:, :width], qkv_grad[:, width : width + KVW]
        v_grad = qkv_grad[:, width + KVW :]
    gate_grad, up_grad = unpack(gate_up_grad, n_batch, hidden_ff)

    def own_part(row, first, total):
        size = total // n_all
        at = first + (b * n_ctx + lax.axis_index("ctx")) * size
        return lax.dynamic_slice(sums, (row, at), (1, size))[0]

    return (
        hidden_out,
        hidden_grad,
        own_part(0, 0, width),
        q_grad,
        own_part(1, 0, width),
        k_grad,
        own_part(2, 0, KVW),
        v_grad,
        own_part(2, KVW, KVW),
        o_grad,
        own_part(3, 0, width),
        gate_grad,
        up_grad,
        down_grad,
    )


def solution(mesh):
    matrix, vector = P(ALL, None), P(ALL)
    placed = (
        (matrix, vector, vector, vector, matrix, vector, matrix, vector)
        + (matrix, vector, matrix, vector, matrix, matrix, matrix, matrix)
    )
    results = (matrix, matrix) + (vector, matrix) * 4 + (vector, matrix, matrix, matrix)
    return jax.shard_map(local, mesh=mesh, in_specs=placed, out_specs=results, check_vma=False)
```

```python
import functools
import math

import jax
import jax.numpy as jnp
from jax import lax
from jax.experimental import pallas as pl
from jax.experimental.pallas import tpu as pltpu
from jax.sharding import PartitionSpec as P

HEADS = 12
KV_HEADS = 2
GROUPS = HEADS // KV_HEADS
HEAD_DIM = 128
KVW = KV_HEADS * HEAD_DIM
INV_ROOT = HEAD_DIM ** (-0.5)
EPSILON = 1e-06
ROPE_BASE = 10000.0
MASKED = -1e30
ALL = ("batch", "ctx")
F32 = jnp.float32
BF16 = jnp.bfloat16
MESH = pl.DeviceIdType.MESH
ANYWHERE = pl.BlockSpec(memory_space=pl.ANY)
IN_VMEM = pl.BlockSpec(memory_space=pltpu.VMEM)
DMA = pltpu.SemaphoreType.DMA


def rope_tables(positions):
    half_dim = HEAD_DIM // 2
    inverse_freq = jnp.exp(
        jnp.arange(half_dim, dtype=F32) * (-2.0 * math.log(ROPE_BASE) / HEAD_DIM)
    )
    angles = positions.astype(F32)[:, None] * inverse_freq[None, :]
    angles = jnp.concatenate([angles, angles], axis=1)
    return (jnp.cos(angles), jnp.sin(angles))


def dot(lhs, rhs):
    return jnp.dot(lhs, rhs, preferred_element_type=F32)


def contract_rows(lhs, rhs):
    return lax.dot_general(lhs, rhs, (((0,), (0,)), ((), ())), preferred_element_type=F32)


def times_transposed(lhs, rhs):
    return lax.dot_general(lhs, rhs, (((1,), (1,)), ((), ())), preferred_element_type=F32)


def lanes(width):
    return -(-width // 128) * 128


def greet(devices):
    barrier = pltpu.get_barrier_semaphore()
    for device in devices:
        pl.semaphore_signal(barrier, inc=1, device_id=device, device_id_type=MESH)
    pl.semaphore_wait(barrier, len(devices))


def remote(source, target, send, receive, device):
    return pltpu.make_async_remote_copy(
        src_ref=source,
        dst_ref=target,
        send_sem=send,
        recv_sem=receive,
        device_id=device,
        device_id_type=MESH,
    )


def lasting(microseconds):
    return pl.CostEstimate(flops=0, bytes_accessed=int(3.3e6 * microseconds), transcendentals=0)


def gather_kernel(line_len, own, out, own_sem, line_sems, pair_sems):
    b, c = lax.axis_index("batch"), lax.axis_index("ctx")
    line, pair = c // 2, c % 2
    ahead = (b, 2 * lax.rem(line + 1, line_len) + pair)
    behind = (b, 2 * lax.rem(line + line_len - 1, line_len) + pair)
    across = (b, c ^ 1)
    greet((ahead, behind, across))
    keep = pltpu.make_async_copy(own, out.at[c], own_sem)
    keep.start()
    on_line, on_pair = [], []
    for step in range(line_len):
        at = 2 * lax.rem(line - step + line_len, line_len) + pair
        block = own if step == 0 else out.at[at]
        if step > 0:
            on_line[step - 1].wait_recv()
        if step < line_len - 1:
            copy = remote(block, out.at[at], line_sems.at[0, step], line_sems.at[1, step], ahead)
            copy.start()
            on_line.append(copy)
        copy = remote(block, out.at[at], pair_sems.at[0, step], pair_sems.at[1, step], across)
        copy.start()
        on_pair.append(copy)
    for copy in on_pair:
        copy.wait()
    for copy in on_line:
        copy.wait_send()
    keep.wait()


def gather_ctx(block, collective_id, name):
    n_ctx = lax.axis_size("ctx")
    line_len = n_ctx // 2
    return pl.pallas_call(
        functools.partial(gather_kernel, line_len),
        out_shape=jax.ShapeDtypeStruct((n_ctx,) + block.shape, block.dtype),
        in_specs=[ANYWHERE],
        out_specs=ANYWHERE,
        scratch_shapes=[DMA(()), DMA((2, line_len)), DMA((2, line_len))],
        compiler_params=pltpu.CompilerParams(collective_id=collective_id, has_side_effects=True),
        cost_estimate=lasting(20),
        name=name,
    )(block)


def scatter_kernel(line_len, many, *refs):
    parts, outs = refs[:many], refs[many : 2 * many]
    pair_in, line_in, line_out = (refs[(2 + i) * many : (3 + i) * many] for i in range(3))
    pair_sems, line_sems = refs[5 * many :]
    b, c = lax.axis_index("batch"), lax.axis_index("ctx")
    line, pair = c // 2, c % 2
    ahead = (b, 2 * lax.rem(line + 1, line_len) + pair)
    behind = (b, 2 * lax.rem(line + line_len - 1, line_len) + pair)
    across = (b, c ^ 1)
    greet((ahead, behind, across))

    def to(step):
        return 2 * lax.rem(line - 1 - step + line_len, line_len)

    sent, given = [], []
    for i in range(many):
        for step in range(line_len):
            copy = remote(
                parts[i].at[to(step) + 1 - pair],
                pair_in[i].at[step],
                pair_sems.at[0, i, step],
                pair_sems.at[1, i, step],
                across,
            )
            copy.start()
            given.append(copy)
    for i in range(many):
        for step in range(line_len):
            given[i * line_len + step].wait_recv()
            total = parts[i][to(step) + pair].astype(F32) + pair_in[i][step].astype(F32)
            if step > 0:
                passed.wait_recv()
                total = total + line_in[i][step - 1].astype(F32)
            if step < line_len - 1:
                line_out[i][step] = total.astype(BF16)
                passed = remote(
                    line_out[i].at[step],
                    line_in[i].at[step],
                    line_sems.at[0, i, step],
                    line_sems.at[1, i, step],
                    ahead,
                )
                passed.start()
                sent.append(passed)
            else:
                outs[i][...] = total
    for copy in given + sent:
        copy.wait_send()


def scatter_ctx(parts, collective_id, name):
    n_ctx = lax.axis_size("ctx")
    line_len, many = n_ctx // 2, len(parts)
    blocks = [(part.shape[0] // n_ctx,) + part.shape[1:] for part in parts]

    def room(size):
        return [pltpu.VMEM((size,) + block, BF16) for block in blocks]

    return pl.pallas_call(
        functools.partial(scatter_kernel, line_len, many),
        out_shape=[jax.ShapeDtypeStruct(block, F32) for block in blocks],
        in_specs=[IN_VMEM] * many,
        out_specs=[IN_VMEM] * many,
        scratch_shapes=[
            *room(line_len),
            *room(line_len - 1),
            *room(line_len - 1),
            DMA((2, many, line_len)),
            DMA((2, many, line_len)),
        ],
        compiler_params=pltpu.CompilerParams(
            collective_id=collective_id, has_side_effects=True, vmem_limit_bytes=60 * 2**20
        ),
        cost_estimate=lasting(40),
        name=name,
    )(*[part.reshape((n_ctx,) + block) for part, block in zip(parts, blocks)])


def spread_kernel(
    line_len, q_weight, k_weight, v_weight, o_weight, small, gate, up, out, columns_out, own,
    columns, own_sem, line_sems, pair_sems, chip_sems, core_sems, column_sems,
):
    b, c = lax.axis_index("batch"), lax.axis_index("ctx")
    n_ctx = 2 * line_len
    line, pair = c // 2, c % 2
    ahead = (b, 2 * lax.rem(line + 1, line_len) + pair)
    across, chip, core = (b, c ^ 1), (b ^ 2, c), (b ^ 1, c)
    others = [(b, lax.rem(c + k, n_ctx)) for k in range(1, n_ctx)]
    at = 0
    for part in (q_weight, k_weight, v_weight, o_weight, small):
        own[:, at : at + part.shape[1]] = part[...]
        at += part.shape[1]
    greet([chip, core] + others)
    keep = [pltpu.make_async_copy(own, out.at[b, c], own_sem.at[0])]
    keep[0].start()

    def pack():
        n_batch, half = out.shape[0], columns.shape[2] // 2
        piece = gate.shape[1] // (n_batch * n_ctx)
        for first, weight in ((0, gate), (half, up)):
            if n_batch * piece < half:
                columns[:, :, first + half - 128 : first + half] = jnp.zeros(
                    (n_ctx, columns.shape[1], 128), BF16
                )
            for k in range(n_batch):
                for i in range(n_ctx):
                    to = (k * n_ctx + i) * piece
                    at = first + k * piece
                    columns[i, :, at : at + piece] = weight[:, to : to + piece]
        keep.append(pltpu.make_async_copy(columns.at[c], columns_out.at[c], own_sem.at[1]))
        keep[1].start()

    def place(step, side):
        return 2 * lax.rem(line - step + line_len, line_len) + side

    def hand(block, to_b, to_c, sems, index, device):
        copy = remote(block, out.at[to_b, to_c], sems.at[0, index], sems.at[1, index], device)
        copy.start()
        return copy

    on_line, on_pair, on_chip, on_core, on_columns = [], [], [], [], []
    for step in range(line_len):
        at = place(step, pair)
        block = own if step == 0 else out.at[b, at]
        if step > 0:
            on_line[step - 1].wait_recv()
        if step < line_len - 1:
            on_line.append(hand(block, b, at, line_sems, step, ahead))
        on_pair.append(hand(block, b, at, pair_sems, step, across))
        on_chip.append(hand(block, b, at, chip_sems, step, chip))
        on_core.append(hand(block, b, at, core_sems, step, core))
        if step == 0:
            pack()
    for k, device in enumerate(others):
        copy = remote(
            columns.at[device[1]],
            columns_out.at[c],
            column_sems.at[0, k],
            column_sems.at[1, k],
            device,
        )
        copy.start()
        on_columns.append(copy)
    for step in range(line_len):
        at = place(step, 1 - pair)
        on_pair[step].wait_recv()
        on_chip.append(hand(out.at[b, at], b, at, chip_sems, line_len + step, chip))
        on_core.append(hand(out.at[b, at], b, at, core_sems, line_len + step, core))
    for index in range(n_ctx):
        at = place(index % line_len, pair if index < line_len else 1 - pair)
        on_chip[index].wait_recv()
        on_core.append(hand(out.at[b ^ 2, at], b ^ 2, at, core_sems, n_ctx + index, core))
    for copy in on_core + on_columns:
        copy.wait()
    for copy in on_line + on_pair + on_chip:
        copy.wait_send()
    for copy in keep:
        copy.wait()


def spread(matrices, gate, up, collective_id, name):
    n_batch, n_ctx = lax.axis_size("batch"), lax.axis_size("ctx")
    line_len = n_ctx // 2
    rows = gate.shape[0]
    own = (rows, sum(matrix.shape[1] for matrix in matrices))
    columns = (n_ctx, rows, 2 * lanes(gate.shape[1] // n_ctx))
    return pl.pallas_call(
        functools.partial(spread_kernel, line_len),
        out_shape=(
            jax.ShapeDtypeStruct((n_batch, n_ctx) + own, BF16),
            jax.ShapeDtypeStruct(columns, BF16),
        ),
        in_specs=[IN_VMEM] * 7,
        out_specs=(ANYWHERE, ANYWHERE),
        scratch_shapes=[
            pltpu.VMEM(own, BF16),
            pltpu.VMEM(columns, BF16),
            DMA((2,)),
            DMA((2, line_len)),
            DMA((2, line_len)),
            DMA((2, n_ctx)),
            DMA((2, 2 * n_ctx)),
            DMA((2, n_ctx)),
        ],
        compiler_params=pltpu.CompilerParams(
            collective_id=collective_id, has_side_effects=True, vmem_limit_bytes=40 * 2**20
        ),
        cost_estimate=lasting(75),
        name=name,
    )(*matrices, gate, up)


def collect_kernel(line_len, *refs):
    grads, (sums_in, columns) = refs[:2], refs[2:4]
    outs, (sums_out, columns_out) = refs[4:6], refs[6:8]
    core_in, chip_in, pair_in, line_in, chip_out, pair_out, line_out = [
        refs[8 + 2 * i : 10 + 2 * i] for i in range(7)
    ]
    sums_got, sums_mine, own_sem = refs[22:25]
    core_sems, chip_sems, pair_sems, line_sems, column_sems, sums_sems = refs[25:]
    b, c = lax.axis_index("batch"), lax.axis_index("ctx")
    n_ctx = 2 * line_len
    line, pair = c // 2, c % 2
    ahead = (b, 2 * lax.rem(line + 1, line_len) + pair)
    across, chip, core = (b, c ^ 1), (b ^ 2, c), (b ^ 1, c)
    others = [(b, lax.rem(c + k, n_ctx)) for k in range(1, n_ctx)]
    on_same_line = others[1::2]
    greet([chip, core] + others)
    keep = pltpu.make_async_copy(columns.at[c], columns_out.at[c], own_sem)
    keep.start()

    def place(index):
        step, side = index // 2, index % 2
        to = lax.rem(line - 1 - step + line_len, line_len)
        return 2 * to + (1 - pair if side == 0 else pair)

    waits = []

    def send(block, target, sems, index, device):
        copy = remote(block, target, sems.at[0, index], sems.at[1, index], device)
        copy.start()
        waits.append(copy)
        return copy

    def start_sums(index, device):
        copy = remote(
            sums_mine, sums_got.at[index], sums_sems.at[0, index], sums_sems.at[1, index], device
        )
        copy.start()
        return copy

    def add_sums(index, copy):
        copy.wait()
        sums_mine[...] += sums_got[index]

    sums_mine[...] = sums_in[...]
    by_core = start_sums(0, core)
    to_core = [[], []]
    for index in range(2 * n_ctx):
        row = b ^ 3 if index < n_ctx else b ^ 1
        for i in range(2):
            to_core[i].append(
                send(
                    grads[i].at[row, place(index % n_ctx)],
                    core_in[i].at[index],
                    core_sems.at[i],
                    index,
                    core,
                )
            )
    add_sums(0, by_core)
    by_chip = start_sums(1, chip)
    on_columns = []
    for k, device in enumerate(others):
        copy = remote(
            columns.at[device[1]],
            columns_out.at[c],
            column_sems.at[0, k],
            column_sems.at[1, k],
            device,
        )
        copy.start()
        on_columns.append(copy)
    to_chip = [[], []]
    for index in range(n_ctx):
        for i in range(2):
            to_core[i][index].wait_recv()
            total = grads[i][b ^ 2, place(index)].astype(F32) + core_in[i][index].astype(F32)
            chip_out[i][index] = total.astype(BF16)
            to_chip[i].append(
                send(chip_out[i].at[index], chip_in[i].at[index], chip_sems.at[i], index, chip)
            )
    add_sums(1, by_chip)
    by_pair = start_sums(2, across)

    def mine(i, index):
        to_core[i][n_ctx + index].wait_recv()
        to_chip[i][index].wait_recv()
        return (
            grads[i][b, place(index)].astype(F32)
            + core_in[i][n_ctx + index].astype(F32)
            + chip_in[i][index].astype(F32)
        )

    to_pair, to_line = [[], []], [[], []]
    for step in range(line_len):
        for i in range(2):
            pair_out[i][step] = mine(i, 2 * step).astype(BF16)
            to_pair[i].append(
                send(pair_out[i].at[step], pair_in[i].at[step], pair_sems.at[i], step, across)
            )
        if step == 0:
            add_sums(2, by_pair)
            own_sums = [
                send(sums_mine, sums_got.at[3 + k], sums_sems, 3 + k, device)
                for k, device in enumerate(on_same_line)
            ]
        for i in range(2):
            total = mine(i, 2 * step + 1)
            to_pair[i][step].wait_recv()
            total = total + pair_in[i][step].astype(F32)
            if step > 0:
                to_line[i][step - 1].wait_recv()
                total = total + line_in[i][step - 1].astype(F32)
            if step < line_len - 1:
                line_out[i][step] = total.astype(BF16)
                to_line[i].append(
                    send(line_out[i].at[step], line_in[i].at[step], line_sems.at[i], step, ahead)
                )
            else:
                outs[i][...] = total
    total = sums_mine[...]
    for k, copy in enumerate(own_sums):
        copy.wait_recv()
        total = total + sums_got[3 + k]
    sums_out[...] = total
    for copy in on_columns:
        copy.wait()
    for copy in waits:
        copy.wait_send()
    keep.wait()


def collect(grads, sums, columns, collective_id, name):
    n_batch, n_ctx = lax.axis_size("batch"), lax.axis_size("ctx")
    line_len = n_ctx // 2
    blocks = [grad.shape[2:] for grad in grads]

    def room(size):
        return [pltpu.VMEM((size,) + block, BF16) for block in blocks]

    return pl.pallas_call(
        functools.partial(collect_kernel, line_len),
        out_shape=(
            *[jax.ShapeDtypeStruct(block, F32) for block in blocks],
            jax.ShapeDtypeStruct(sums.shape, F32),
            jax.ShapeDtypeStruct(columns.shape, BF16),
        ),
        in_specs=[IN_VMEM] * 3 + [ANYWHERE],
        out_specs=(IN_VMEM,) * 3 + (ANYWHERE,),
        scratch_shapes=[
            *room(2 * n_ctx),
            *room(n_ctx),
            *room(line_len),
            *room(line_len - 1),
            *room(n_ctx),
            *room(line_len),
            *room(line_len - 1),
            pltpu.VMEM((2 + line_len,) + sums.shape, F32),
            pltpu.VMEM(sums.shape, F32),
            DMA(()),
            DMA((2, 2, 2 * n_ctx)),
            DMA((2, 2, n_ctx)),
            DMA((2, 2, line_len)),
            DMA((2, 2, line_len)),
            DMA((2, n_ctx)),
            DMA((2, 2 + line_len)),
        ],
        compiler_params=pltpu.CompilerParams(
            collective_id=collective_id, has_side_effects=True, vmem_limit_bytes=60 * 2**20
        ),
        cost_estimate=lasting(70),
        name=name,
    )(*grads, sums, columns)


def row_scale(values):
    return lax.rsqrt(jnp.mean(values * values, axis=-1, keepdims=True) + EPSILON)


def turn_head(values, cosine, signed_sine, back=False):
    turned = pltpu.roll(values, HEAD_DIM // 2, 1) * signed_sine
    return values * cosine - turned if back else values * cosine + turned


def whole(*shape):
    return pl.BlockSpec(shape, lambda j: (0,) * len(shape))


def project_kernel(hidden, gain, weight, bias, cosine, signed_sine, normed, query, key_value, kept):
    j = pl.program_id(0)

    @pl.when(j == 0)
    def _():
        values = hidden[...].astype(F32)
        kept[...] = (values * row_scale(values) * gain[...]).astype(BF16)
        normed[...] = kept[...]

    lin = dot(kept[...], weight[...]) + bias[...]
    tables = cosine[...], signed_sine[...]
    heads = [lin[:, i * HEAD_DIM : (i + 1) * HEAD_DIM] for i in range(4)]

    @pl.when(j < 3)
    def _():
        for i in range(4):
            turned = turn_head(heads[i], *tables)
            query[:, i * HEAD_DIM : (i + 1) * HEAD_DIM] = turned.astype(BF16)

    @pl.when(j == 3)
    def _():
        for i in range(4):
            value = turn_head(heads[i], *tables) if i < KV_HEADS else heads[i]
            key_value[:, i * HEAD_DIM : (i + 1) * HEAD_DIM] = value.astype(BF16)


def project(hidden, gain, weights, bias, tables):
    count, width = hidden.shape
    wide = 2 * KVW
    table = whole(count, HEAD_DIM)
    return pl.pallas_call(
        project_kernel,
        grid=(4,),
        out_shape=(
            jax.ShapeDtypeStruct((count, width), BF16),
            jax.ShapeDtypeStruct((count, width), BF16),
            jax.ShapeDtypeStruct((count, wide), BF16),
        ),
        in_specs=[
            whole(count, width),
            whole(1, width),
            pl.BlockSpec((width, wide), lambda j: (0, j)),
            pl.BlockSpec((1, wide), lambda j: (0, j)),
            table,
            table,
        ],
        out_specs=(
            whole(count, width),
            pl.BlockSpec((count, wide), lambda j: (0, jnp.minimum(j, 2))),
            whole(count, wide),
        ),
        scratch_shapes=[pltpu.VMEM((count, width), BF16)],
        compiler_params=pltpu.CompilerParams(vmem_limit_bytes=40 * 2**20),
        cost_estimate=lasting(4),
        name="project",
    )(hidden, gain, weights, bias, *tables)


def mark_allowed(key_pos, key_doc, own_pos, own_doc, allowed):
    count = own_pos.shape[1]
    pos_column, doc_column = key_pos[...].T, key_doc[...].T
    for i in range(key_pos.shape[0]):
        seen = (pos_column[:, i : i + 1] <= own_pos[...]) & (doc_column[:, i : i + 1] == own_doc[...])
        allowed[i * count : (i + 1) * count] = jnp.where(seen, 1.0, 0.0)


def stack_heads(block, group):
    return jnp.concatenate(
        [block[:, i * HEAD_DIM : (i + 1) * HEAD_DIM] for i in range(group)], axis=0
    )


def lay_heads(stacked, group):
    count = stacked.shape[0] // group
    return jnp.concatenate([stacked[i * count : (i + 1) * count] for i in range(group)], axis=1)


def probabilities(keys, queries, allowed, group):
    scores = times_transposed(keys, queries) * INV_ROOT
    seen = jnp.concatenate([allowed[...]] * group, axis=1) > 0.0
    scores = jnp.where(seen, scores, MASKED)
    raised = jnp.exp(scores - jnp.max(scores, axis=0, keepdims=True))
    return raised * (1.0 / jnp.sum(raised, axis=0, keepdims=True))


def attend_kernel(
    group, last, query, keys, values, out_0, out_1, out_2, key_pos, key_doc, own_pos, own_doc,
    hidden, gain, attn_out, residual, normed, total, allowed,
):
    j = pl.program_id(0)

    @pl.when(j == 0)
    def _():
        total[...] = hidden[...].astype(F32)
        mark_allowed(key_pos, key_doc, own_pos, own_doc, allowed)

    probs = probabilities(keys[...], stack_heads(query[...], group), allowed, group)
    result = contract_rows(values[...], probs.astype(BF16)).T
    block = lay_heads(result, group).astype(BF16)
    attn_out[...] = block
    for t, weight in enumerate((out_0, out_1, out_2)):
        total[:, t * 512 : (t + 1) * 512] += dot(block, weight[...])

    @pl.when(j == last)
    def _():
        values = total[...]
        residual[...] = values
        normed[...] = (values * row_scale(values) * gain[...]).astype(BF16)


def head_specs(count, width, keys, group, weights_at):
    rows = group * HEAD_DIM
    per_key = GROUPS // group
    query = pl.BlockSpec((count, rows), lambda j: (0, j))
    heads = [
        pl.BlockSpec((keys, HEAD_DIM), lambda j, i=i: (0, KV_HEADS * i + j // per_key))
        for i in range(2)
    ]
    out = [
        pl.BlockSpec((rows, 512), lambda j, t=t: (j, weights_at // 512 + t))
        for t in range(width // 512)
    ]
    places = [whole(keys // count, count)] * 2 + [whole(1, count)] * 2
    return query, heads, out, places


def attend(query, key_value, weights, places, hidden, gain):
    count, width = hidden.shape
    keys = key_value.shape[0]
    group = 3 if keys <= 1024 else 1
    steps = HEADS // group
    query_spec, head_spec, out_spec, place_spec = head_specs(
        count, width, keys, group, width + 2 * KVW
    )
    return pl.pallas_call(
        functools.partial(attend_kernel, group, steps - 1),
        grid=(steps,),
        out_shape=(
            jax.ShapeDtypeStruct((count, width), BF16),
            jax.ShapeDtypeStruct((count, width), F32),
            jax.ShapeDtypeStruct((count, width), BF16),
        ),
        in_specs=[query_spec, *head_spec, *out_spec, *place_spec]
        + [whole(count, width), whole(1, width)],
        out_specs=(query_spec, whole(count, width), whole(count, width)),
        scratch_shapes=[pltpu.VMEM((count, width), F32), pltpu.VMEM((keys, count), F32)],
        compiler_params=pltpu.CompilerParams(vmem_limit_bytes=56 * 2**20),
        cost_estimate=lasting(10),
        name="attend",
    )(query, key_value, key_value, *[weights] * 3, *places, hidden, gain)


def attend_back_kernel(
    group, per_key, query, keys, values, out_0, out_1, out_2, key_pos, key_doc, own_pos, own_doc,
    attn_out, residual, gain, out_grad, d_normed, cosine, signed_sine, d_query, d_key_value,
    o_grad, d_residual, gain_grad, branch, allowed, key_sum, value_sum,
):
    j = pl.program_id(0)

    @pl.when(j == 0)
    def _():
        rows, grads = residual[...], d_normed[...]
        factor = row_scale(rows)
        scaled = grads * gain[...]
        gain_grad[...] = jnp.sum(grads * rows * factor, axis=0, keepdims=True)
        total = out_grad[...].astype(F32) + (
            factor * scaled
            - rows * (factor * factor * factor) * jnp.mean(scaled * rows, axis=-1, keepdims=True)
        )
        d_residual[...] = total
        branch[...] = total.astype(BF16)
        mark_allowed(key_pos, key_doc, own_pos, own_doc, allowed)

    @pl.when(lax.rem(j, per_key) == 0)
    def _():
        key_sum[...] = jnp.zeros_like(key_sum)
        value_sum[...] = jnp.zeros_like(value_sum)

    o_grad[...] = contract_rows(attn_out[...], branch[...]).astype(BF16)
    d_attn = sum(
        times_transposed(branch[:, t * 512 : (t + 1) * 512], weight[...])
        for t, weight in enumerate((out_0, out_1, out_2))
    ).astype(BF16)
    grads = stack_heads(d_attn, group)
    queries = stack_heads(query[...], group)
    probs = probabilities(keys[...], queries, allowed, group)
    d_probs = times_transposed(values[...], grads)
    delta = jnp.sum(probs * d_probs, axis=0, keepdims=True)
    d_scores = (probs * (d_probs - delta)).astype(BF16)
    key_sum[...] += dot(d_scores, queries)
    value_sum[...] += dot(probs.astype(BF16), grads)
    result = contract_rows(keys[...], d_scores).T * INV_ROOT
    count = result.shape[0] // group
    for i in range(group):
        head = turn_head(
            result[i * count : (i + 1) * count], cosine[...], signed_sine[...], back=True
        )
        d_query[:, i * HEAD_DIM : (i + 1) * HEAD_DIM] = head.astype(BF16)

    @pl.when(lax.rem(j, per_key) == per_key - 1)
    def _():
        at = pl.multiple_of(j // per_key * HEAD_DIM, HEAD_DIM)
        d_key_value[:, pl.ds(at, HEAD_DIM)] = (key_sum[...] * INV_ROOT).astype(BF16)
        d_key_value[:, pl.ds(KVW + at, HEAD_DIM)] = value_sum[...].astype(BF16)


def attend_back(query, key_value, weights, places, attn_out, residual, gain, out_grad, d_normed, tables):
    count, width = query.shape
    keys = key_value.shape[0]
    group = 3 if keys <= 1024 else 1
    steps = HEADS // group
    query_spec, head_spec, out_spec, place_spec = head_specs(
        count, width, keys, group, width + 2 * KVW
    )
    rows, table = whole(count, width), whole(count, HEAD_DIM)
    return pl.pallas_call(
        functools.partial(attend_back_kernel, group, GROUPS // group),
        grid=(steps,),
        out_shape=(
            jax.ShapeDtypeStruct((count, width), BF16),
            jax.ShapeDtypeStruct((keys, 2 * KVW), BF16),
            jax.ShapeDtypeStruct((width, width), BF16),
            jax.ShapeDtypeStruct((count, width), F32),
            jax.ShapeDtypeStruct((1, width), F32),
        ),
        in_specs=[query_spec, *head_spec, *out_spec, *place_spec, query_spec]
        + [rows, whole(1, width), rows, rows, table, table],
        out_specs=(
            query_spec,
            whole(keys, 2 * KVW),
            pl.BlockSpec((group * HEAD_DIM, width), lambda j: (j, 0)),
            rows,
            whole(1, width),
        ),
        scratch_shapes=[
            pltpu.VMEM((count, width), BF16),
            pltpu.VMEM((keys, count), F32),
            pltpu.VMEM((keys, HEAD_DIM), F32),
            pltpu.VMEM((keys, HEAD_DIM), F32),
        ],
        compiler_params=pltpu.CompilerParams(vmem_limit_bytes=60 * 2**20),
        cost_estimate=lasting(17),
        name="attend_back",
    )(
        query, key_value, key_value, *[weights] * 3, *places, attn_out, residual, gain, out_grad,
        d_normed, *tables,
    )


def project_back_kernel(
    d_query, d_key_value, weight, normed, hidden, gain, d_residual, gain_two_grad, cosine,
    signed_sine, grad, hidden_grad, sums, flipped, total, biases,
):
    j = pl.program_id(0)
    wide = weight.shape[1]

    @pl.when(j == 0)
    def _():
        flipped[...] = normed[...].astype(F32).T.astype(BF16)
        total[...] = jnp.zeros_like(total)
        sums[...] = jnp.zeros_like(sums)

    def add(d_lin):
        grad[...] = dot(flipped[...], d_lin).astype(BF16)
        total[...] += times_transposed(d_lin, weight[...])
        return jnp.sum(d_lin.astype(F32), axis=0, keepdims=True)

    for i in range(3):

        @pl.when(j == i)
        def _():
            sums[1:2, i * wide : (i + 1) * wide] = add(d_query[...])

    @pl.when(j == 3)
    def _():
        heads = [
            turn_head(
                d_key_value[:, i * HEAD_DIM : (i + 1) * HEAD_DIM],
                cosine[...],
                signed_sine[...],
                back=True,
            )
            for i in range(KV_HEADS)
        ]
        d_lin = jnp.concatenate(heads + [d_key_value[:, KVW:]], axis=1).astype(BF16)
        sums[2:3, :wide] = add(d_lin)
        rows, grads = hidden[...].astype(F32), total[...]
        factor = row_scale(rows)
        scaled = grads * gain[...]
        sums[0:1] = jnp.sum(grads * rows * factor, axis=0, keepdims=True)
        sums[3:4] = gain_two_grad[...]
        hidden_grad[...] = d_residual[...] + (
            factor * scaled
            - rows * (factor * factor * factor) * jnp.mean(scaled * rows, axis=-1, keepdims=True)
        )


def project_back(d_query, d_key_value, weights, normed, hidden, gain, d_residual, gain_two_grad, tables):
    count, width = hidden.shape
    wide = 2 * KVW
    rows, table = whole(count, width), whole(count, HEAD_DIM)
    return pl.pallas_call(
        project_back_kernel,
        grid=(4,),
        out_shape=(
            jax.ShapeDtypeStruct((width, width + wide), BF16),
            jax.ShapeDtypeStruct((count, width), F32),
            jax.ShapeDtypeStruct((8, width), F32),
        ),
        in_specs=[
            pl.BlockSpec((count, wide), lambda j: (0, jnp.minimum(j, 2))),
            whole(count, wide),
            pl.BlockSpec((width, wide), lambda j: (0, j)),
            rows,
            rows,
            whole(1, width),
            rows,
            whole(1, width),
            table,
            table,
        ],
        out_specs=(
            pl.BlockSpec((width, wide), lambda j: (0, j)),
            rows,
            whole(8, width),
        ),
        scratch_shapes=[
            pltpu.VMEM((width, count), BF16),
            pltpu.VMEM((count, width), F32),
            pltpu.VMEM((8, wide), F32),
        ],
        compiler_params=pltpu.CompilerParams(vmem_limit_bytes=48 * 2**20),
        cost_estimate=lasting(9),
        name="project_back",
    )(
        d_query, d_key_value, weights, normed, hidden, gain, d_residual, gain_two_grad, *tables
    )


def unpack_kernel(n_batch, piece, packed, gate, up):
    n_ctx, _, both = packed.shape
    for out, first in ((gate, 0), (up, both // 2)):
        for k in range(n_batch):
            for i in range(n_ctx):
                at = first + k * piece
                to = (k * n_ctx + i) * piece
                out[:, to : to + piece] = packed[i, :, at : at + piece].astype(F32)


def finish_kernel(
    n_batch, piece, packed, hidden_grad, o_grad, q_grad, kv_grad, residual, ff_rows, down_grad, sums,
    gate, up, hidden_grad_out, o_out, q_out, k_out, v_out, hidden_out, down_out, own_sums,
):
    unpack_kernel(n_batch, piece, packed, gate, up)
    hidden_grad_out[...] = hidden_grad[...]
    o_out[...] = o_grad[...]
    q_out[...] = q_grad[...]
    k_out[...] = kv_grad[:, :KVW]
    v_out[...] = kv_grad[:, KVW:]
    hidden_out[...] = (residual[...] + ff_rows[...]).astype(BF16)
    down_out[...] = down_grad[...]
    n_ctx, rows, _ = packed.shape
    width = sums.shape[1]
    own = lax.axis_index("batch") * n_ctx + lax.axis_index("ctx")
    small = KVW // (n_batch * n_ctx)
    for row, first in ((0, own * rows), (1, own * small), (2, KVW + own * small)):
        rolled = pltpu.roll(sums[...], lax.rem(width - first, width), 1)
        own_sums[8 * row : 8 * row + 8] = rolled[:, :128]


def finish(packed, hidden_grad, o_grad, q_grad, kv_grad, residual, ff_rows, down_grad, sums, n_batch, width):
    n_ctx, rows, _ = packed.shape
    wide = jax.ShapeDtypeStruct((rows, width), F32)
    half = jax.ShapeDtypeStruct((rows, KVW), F32)

    def like(array, dtype=F32):
        return jax.ShapeDtypeStruct(array.shape, dtype)

    return pl.pallas_call(
        functools.partial(finish_kernel, n_batch, width // (n_batch * n_ctx)),
        out_shape=(
            wide, wide, like(hidden_grad), like(o_grad), like(q_grad), half, half,
            like(residual, BF16), like(down_grad), jax.ShapeDtypeStruct((24, 128), F32),
        ),
        in_specs=[IN_VMEM] * 9,
        out_specs=(IN_VMEM,) * 10,
        compiler_params=pltpu.CompilerParams(vmem_limit_bytes=56 * 2**20),
        cost_estimate=lasting(5),
        name="finish",
    )(packed, hidden_grad, o_grad, q_grad, kv_grad, residual, ff_rows, down_grad, sums)


def unpack(packed, n_batch, width):
    n_ctx, rows, _ = packed.shape
    out = jax.ShapeDtypeStruct((rows, width), F32)
    return pl.pallas_call(
        functools.partial(unpack_kernel, n_batch, width // (n_batch * n_ctx)),
        out_shape=(out, out),
        in_specs=[IN_VMEM],
        out_specs=(IN_VMEM, IN_VMEM),
        compiler_params=pltpu.CompilerParams(vmem_limit_bytes=40 * 2**20),
        cost_estimate=lasting(3),
        name="unpack",
    )(packed)


def mlp_kernel(line_len, tile, span, own_rows, *refs):
    n_batch, n_ctx = 4, 2 * line_len
    weights, (down, grads_in) = refs[:n_batch], refs[n_batch : n_batch + 2]
    d_rows_out, ff_out, down_out, gate_up_out = refs[n_batch + 2 : n_batch + 6]
    (
        tokens, flipped, gate_up, down_in, grads, mixed, mixed_flipped, d_gate_up, d_parts, ff_parts,
        d_pair, d_line, ff_pair, ff_line, core_wide, chip_wide, down_terms,
        core_down, chip_down, own, lin, d_mixed_rows, load_sems, store_sems,
        line_sems, pair_sems, back_pair, back_line, batch_sems,
    ) = refs[n_batch + 6 :]
    b, c = lax.axis_index("batch"), lax.axis_index("ctx")
    line, pair = c // 2, c % 2
    ahead = (b, 2 * lax.rem(line + 1, line_len) + pair)
    behind = (b, 2 * lax.rem(line + line_len - 1, line_len) + pair)
    across, chip, core = (b, c ^ 1), (b ^ 2, c), (b ^ 1, c)
    count, width = own.shape
    half = gate_up.shape[1] // 2
    own_ff = down.shape[0]
    piece = own_ff // n_batch
    depth = width // n_batch
    for k in range(n_batch):
        source = pl.ds(pl.multiple_of((b ^ k) * depth, 128), depth)
        own[:, k * depth : (k + 1) * depth] = own_rows[:, source]
    greet((ahead, behind, across, chip, core))

    def at(step):
        return 2 * lax.rem(line - step + line_len, line_len)

    sent = []

    def send(source, target, sems, device):
        copy = remote(source, target, sems[0], sems[1], device)
        copy.start()
        sent.append(copy)
        return copy

    on_line, on_pair = [], []

    def forward(step):
        block = own if step == 0 else tokens.at[at(step) + pair]
        target = tokens.at[at(step) + pair]
        if step > 0:
            on_line[step - 1].wait_recv()
        if step < line_len - 1:
            sems = line_sems.at[0, step], line_sems.at[1, step]
            on_line.append(send(block, target, sems, ahead))
        sems = pair_sems.at[0, step], pair_sems.at[1, step]
        on_pair.append(send(block, target, sems, across))

    forward(0)
    loads = [pltpu.make_async_copy(own, tokens.at[c], load_sems.at[0])]
    for k, weight in enumerate(weights):
        loads.append(
            pltpu.make_async_copy(
                weight, gate_up.at[pl.ds(k * depth, depth)], load_sems.at[1 + k]
            )
        )
    loads.append(
        pltpu.make_async_copy(down, down_in.at[pl.ds(0, own_ff)], load_sems.at[1 + n_batch])
    )
    loads.append(pltpu.make_async_copy(grads_in, grads, load_sems.at[2 + n_batch]))
    for copy in loads:
        copy.start()
    if own_ff < half:
        down_in[own_ff:half] = jnp.zeros((half - own_ff, width), BF16)
    for copy in loads:
        copy.wait()

    def chunk(step):
        first = pl.multiple_of(at(step) * count, 2 * count)
        rows, pair_rows = pl.ds(first, 2 * count), pl.ds(at(step), 2)
        block = tokens[pair_rows].reshape(2 * count, width)
        grad_block = grads[pair_rows].reshape(2 * count, width)

        for low in range(0, 2 * half, span):
            lin[:, low : low + span] = dot(block, gate_up[:, low : low + span])
        d_mixed_rows[...] = times_transposed(grad_block, down_in[...])

        def columns(index, _):
            low = pl.multiple_of(index * tile, 128)
            high = pl.multiple_of(half + index * tile, 128)
            gate_lin, up_lin = lin[:, pl.ds(low, tile)], lin[:, pl.ds(high, tile)]
            d_mixed = d_mixed_rows[:, pl.ds(low, tile)]
            sigmoid = 1.0 / (1.0 + jnp.exp(-gate_lin))
            silu = gate_lin * sigmoid
            product = silu * up_lin
            mixed[:, pl.ds(low, tile)] = product.astype(BF16)
            mixed_flipped[pl.ds(low, tile), rows] = product.T.astype(BF16)
            d_gate = d_mixed * up_lin * sigmoid * (1.0 + gate_lin * (1.0 - sigmoid))
            d_gate_up[rows, pl.ds(low, tile)] = d_gate.astype(BF16)
            d_gate_up[rows, pl.ds(high, tile)] = (d_mixed * silu).astype(BF16)
            return 0

        lax.fori_loop(0, half // tile, columns, 0)
        for low in range(0, width, width // 2):
            part = slice(low, low + width // 2)
            back = times_transposed(d_gate_up[rows], gate_up[part])
            d_parts[pair_rows, :, part] = back.astype(BF16).reshape(2, count, width // 2)
        for low in range(0, width, width // 2):
            part = slice(low, low + width // 2)
            out = dot(mixed[...], down_in[:, part])
            ff_parts[pair_rows, :, part] = out.astype(BF16).reshape(2, count, width // 2)
            flipped[part, rows] = (
                tokens[pair_rows, :, part].reshape(2 * count, width // 2).astype(F32).T.astype(BF16)
            )

    moves = (
        (d_parts, d_pair, d_line, d_rows_out),
        (ff_parts, ff_pair, ff_line, ff_out),
    )
    given = {}

    def give(index, which=0):
        parts, pairs = moves[which][:2]
        sems = back_pair.at[0, which, index], back_pair.at[1, which, index]
        source = parts.at[at(index + 1) + 1 - pair]
        given[index, which] = send(source, pairs.at[index], sems, across)

    for step in range(line_len):
        if step + 1 < line_len:
            forward(step + 1)
        on_pair[step].wait_recv()
        chunk(step)
        if step == line_len - 2:
            for index in range(line_len - 2):
                give(index)
    give(line_len - 2)
    give(line_len - 1)
    stores = []

    def store(source, target):
        copy = pltpu.make_async_copy(source, target, store_sems.at[len(stores)])
        copy.start()
        stores.append(copy)

    passed = {}

    def passing(index, which=0):
        parts, pairs, lines, out = moves[which]
        place = at(index + 1) + pair
        given[index, which].wait_recv()
        total = parts[place].astype(F32) + pairs[index].astype(F32)
        if index > 0:
            passed[index - 1, which].wait_recv()
            total = total + lines[index - 1].astype(F32)
        if index < line_len - 1:
            parts[place] = total.astype(BF16)
            sems = back_line.at[0, which, index], back_line.at[1, which, index]
            passed[index, which] = send(parts.at[place], lines.at[index], sems, ahead)
        elif which:
            out[...] = total
        else:
            for k in range(n_batch):
                target = pl.ds(pl.multiple_of((b ^ k) * depth, 128), depth)
                out[:, target] = total[:, k * depth : (k + 1) * depth]

    def batch_send(source, target, index, device):
        sems = batch_sems.at[0, index], batch_sems.at[1, index]
        return send(source, target, sems, device)

    def wide(k, side):
        return gate_up.at[pl.ds(k * depth, depth), pl.ds(side * half, half)]

    def weight_grad(k, side):
        part = slice(k * depth, (k + 1) * depth), slice(side * half, (side + 1) * half)
        gate_up[part] = dot(flipped[part[0]], d_gate_up[:, part[1]]).astype(BF16)

    def down_grads():
        for k in range(n_batch):
            grad = dot(
                mixed_flipped[k * piece : (k + 1) * piece],
                grads[...].reshape(n_ctx * count, width),
            )
            down_terms[k] = grad.astype(BF16)
        for slot, row in ((1, b ^ 3), (0, b ^ 1)):
            to_core["down", slot] = batch_send(
                down_terms.at[row], core_down.at[slot], 6 + slot, core
            )

    def pass_down():
        to_core["down", 1].wait_recv()
        total = down_terms[b ^ 2].astype(F32) + core_down[1].astype(F32)
        down_terms[b ^ 2] = total.astype(BF16)
        to_chip.append(batch_send(down_terms.at[b ^ 2], chip_down, 8, chip))

    def add_wide(k, side, terms):
        def columns(index, _):
            low = pl.multiple_of(index * tile, 128)
            at_low = pl.ds(pl.multiple_of(side * half + low, 128), tile)
            rows = slice(k * depth, (k + 1) * depth)
            total = gate_up[rows, at_low].astype(F32)
            for term in terms:
                total = total + term[:, pl.ds(low, tile)].astype(F32)
            gate_up[rows, at_low] = total.astype(BF16)
            return 0

        lax.fori_loop(0, half // tile, columns, 0)

    to_core, to_chip = {}, []

    def compute_and_send(k, side):
        weight_grad(k, side)
        slot = k // 2
        target = core_wide.at[slot, side]
        to_core[k, side] = batch_send(wide(k, side), target, 2 * slot + side, core)

    def compute_and_pass(side):
        weight_grad(2, side)
        to_core[3, side].wait_recv()
        add_wide(2, side, [core_wide.at[1, side]])
        to_chip.append(batch_send(wide(2, side), chip_wide.at[side], 4 + side, chip))

    compute_and_send(3, 0)
    compute_and_pass(0)
    compute_and_send(3, 1)
    compute_and_pass(1)
    work = [
        down_grads,
        lambda: (pass_down(), compute_and_send(1, 0)),
        lambda: compute_and_send(1, 1),
        lambda: (weight_grad(0, 0), weight_grad(0, 1)),
    ]
    for index in range(max(line_len, len(work))):
        if index < line_len:
            passing(index)
            give(index, 1)
        if index < len(work):
            work[index]()
    for index in range(line_len - 1):
        passing(index, 1)
    for side in range(2):
        to_core[1, side].wait_recv()
        to_chip[side].wait_recv()
        add_wide(0, side, [core_wide.at[0, side], chip_wide.at[side]])
        store(wide(0, side), gate_up_out.at[:, pl.ds(side * half, half)])
    to_core["down", 0].wait_recv()
    to_chip[2].wait_recv()
    down_out[...] = (
        down_terms[b].astype(F32) + core_down[0].astype(F32) + chip_down[...].astype(F32)
    )
    passing(line_len - 1, 1)
    for copy in sent:
        copy.wait_send()
    for copy in stores:
        copy.wait()


def mlp_scratch(n_ctx, n_batch, count, width, hidden_own):
    line_len, half = n_ctx // 2, lanes(hidden_own)
    tokens, piece = n_ctx * count, hidden_own // n_batch

    def room(*shape):
        return pltpu.VMEM(shape, BF16)

    return [
        room(n_ctx, count, width),
        room(width, tokens),
        room(width, 2 * half),
        room(half, width),
        room(n_ctx, count, width),
        room(2 * count, half),
        room(half, tokens),
        room(tokens, 2 * half),
        room(n_ctx, count, width),
        room(n_ctx, count, width),
        *[room(line_len, count, width), room(line_len - 1, count, width)] * 2,
        room(2, 2, width // n_batch, half),
        room(2, width // n_batch, half),
        room(n_batch, piece, width),
        room(2, piece, width),
        room(piece, width),
        room(count, width),
        pltpu.VMEM((2 * count, 2 * half), F32),
        pltpu.VMEM((2 * count, half), F32),
    ]


def mlp(own, weights, down, grads, collective_id, name):
    n_batch, n_ctx = lax.axis_size("batch"), lax.axis_size("ctx")
    line_len = n_ctx // 2
    count, width = own.shape
    half = weights[0].shape[1] // 2
    tile = 384 if half % 384 == 0 else 128
    span = 768 if 2 * half % 768 == 0 else tile
    return pl.pallas_call(
        functools.partial(mlp_kernel, line_len, tile, span),
        out_shape=(
            jax.ShapeDtypeStruct((count, width), F32),
            jax.ShapeDtypeStruct((count, width), F32),
            jax.ShapeDtypeStruct((down.shape[0] // n_batch, width), F32),
            jax.ShapeDtypeStruct(weights[0].shape, BF16),
        ),
        in_specs=[IN_VMEM] + [ANYWHERE] * (n_batch + 2),
        out_specs=(IN_VMEM, IN_VMEM, IN_VMEM, ANYWHERE),
        scratch_shapes=mlp_scratch(n_ctx, n_batch, count, width, down.shape[0])
        + [
            DMA((3 + n_batch,)),
            DMA((2,)),
            DMA((2, line_len)),
            DMA((2, line_len)),
            DMA((2, 2, line_len)),
            DMA((2, 2, line_len)),
            DMA((2, 9)),
        ],
        compiler_params=pltpu.CompilerParams(
            collective_id=collective_id, has_side_effects=True, vmem_limit_bytes=62 * 2**20
        ),
        cost_estimate=lasting(100),
        name=name,
    )(own, *weights, down, grads.reshape(n_ctx, count, width))


def front_kernel(line_len, group, *refs):
    (
        q_weight, k_weight, v_weight, o_weight, gate, up, hidden, cosine, signed_sine, own_pos,
        own_doc, down, out_grad,
    ) = refs[:13]
    own_vectors = refs[13:18]
    (
        normed_out, query, attn_out, residual, normed_two, gain_one, gain_two, key_pos, key_doc,
        key_value_out, w_in_out, w_out_out, columns_out, near, far, farther, down_out, grads_out,
    ) = refs[18:36]
    own_in, w_in, w_out, columns, key_own, key_value, allowed, vectors, bias, small = refs[36:46]
    (
        load_sems, line_sems, first_sems, second_sems, core_sems, column_sems, near_sems, far_sems,
        farther_sems, keys_line_sems, keys_pair_sems, grads_line_sems, grads_pair_sems, down_sems,
    ) = refs[46:]
    b, c = lax.axis_index("batch"), lax.axis_index("ctx")
    n_batch, n_ctx = 4, 2 * line_len
    line, pair = c // 2, c % 2
    ahead = (b, 2 * lax.rem(line + 1, line_len) + pair)
    across, chip, core = (b, c ^ 1), (b ^ 2, c), (b ^ 1, c)
    others = [(b, lax.rem(c + k, n_ctx)) for k in range(1, n_ctx)]
    count, width = hidden.shape
    rows = q_weight.shape[0]
    wide = width + 2 * KVW
    at = 0
    for part in (q_weight, k_weight, v_weight):
        own_in[:, at : at + part.shape[1]] = part[...]
        at += part.shape[1]
    small[...] = jnp.zeros_like(small)
    for row, vector in enumerate(own_vectors):
        small[row : row + 1, : vector.shape[1]] = vector[...].astype(F32)
    small[5:6] = jnp.right_shift(own_pos[...], 6).astype(F32)
    small[6:7] = jnp.bitwise_and(own_pos[...], 63).astype(F32)
    small[7:8] = own_doc[...].astype(F32)
    own_in[:, at:] = jnp.zeros((rows, 128), BF16)
    own_in[:8, at:] = small[...].astype(BF16)
    greet([chip, core] + others)
    sent, local = [], []

    def send(source, target, sems, index, device):
        copy = remote(source, target, sems.at[(0, *index)], sems.at[(1, *index)], device)
        copy.start()
        sent.append(copy)
        return copy

    def store(source, target):
        copy = pltpu.make_async_copy(source, target, load_sems.at[len(local)])
        copy.start()
        local.append(copy)

    owns, wholes = (own_in, o_weight), (w_in, w_out)
    first_to, second_to = (across, chip), (chip, across)
    on_line, on_first, on_second, on_core = {}, {}, {}, {}

    def place(step, side):
        return 2 * lax.rem(line - step + line_len, line_len) + side

    def block(p, row, column):
        first = pl.multiple_of((row * n_ctx + column) * rows, rows)
        return wholes[p].at[pl.ds(first, rows)]

    def line_step(p, step):
        target = block(p, b, place(step, pair))
        source = owns[p] if step == 0 else target
        if step > 0:
            on_line[p, step - 1].wait_recv()
        if step < line_len - 1:
            on_line[p, step] = send(source, target, line_sems, (p, step), ahead)
        on_first[p, step] = send(source, target, first_sems, (p, step), first_to[p])
        on_second[p, step] = send(source, target, second_sems, (p, step), second_to[p])
        on_core[p, step] = send(source, target, core_sems, (p, step), core)

    def first_step(p, step):
        on_first[p, step].wait_recv()
        row, side = ((b, 1 - pair), (b ^ 2, pair))[p]
        landed = block(p, row, place(step, side))
        index = line_len + step
        on_second[p, index] = send(landed, landed, second_sems, (p, index), second_to[p])
        on_core[p, index] = send(landed, landed, core_sems, (p, index), core)

    def second_step(p, index):
        on_second[p, index].wait_recv()
        late = index >= line_len
        row = b ^ 2 if p == 0 or late else b
        side = 1 - pair if p == 1 or late else pair
        landed = block(p, row, place(index % line_len, side))
        on_core[p, n_ctx + index] = send(landed, landed, core_sems, (p, n_ctx + index), core)

    def complete(p):
        for index in range(2 * n_ctx):
            on_core[p, index].wait_recv()

    on_down = []

    def down_step(step):
        if step == 0:
            store(down, down_out.at[b])
            on_down.append(send(down, down_out.at[b], down_sems, (0,), chip))
            on_down.append(send(down, down_out.at[b], down_sems, (1,), core))
        else:
            on_down[0].wait_recv()
            landed = down_out.at[b ^ 2]
            on_down.append(send(landed, landed, down_sems, (2,), core))

    def pack():
        half = columns.shape[2] // 2
        piece = gate.shape[1] // (n_batch * n_ctx)
        for first, weight in ((0, gate), (half, up)):
            if n_batch * piece < half:
                columns[:, :, first + half - 128 : first + half] = jnp.zeros(
                    (n_ctx, columns.shape[1], 128), BF16
                )
            for k in range(n_batch):
                for i in range(n_ctx):
                    to = (k * n_ctx + i) * piece
                    low = first + k * piece
                    columns[i, :, low : low + piece] = weight[:, to : to + piece]
        store(columns.at[c], columns_out.at[c])

    on_columns, on_near, on_far, on_farther = [], [], [], []

    def exchange_columns(first, last):
        for k in range(first, last):
            source = columns.at[others[k][1]]
            on_columns.append(send(source, columns_out.at[c], column_sems, (k,), others[k]))

    def spread_columns(k):
        slot = lax.rem(c - k + n_ctx, n_ctx)
        if k > 0:
            on_columns[k - 1].wait_recv()
        source = columns_out.at[slot] if k > 0 else columns.at[c]
        on_far.append(send(source, far.at[slot], far_sems, (k,), chip))
        on_near.append(send(source, near.at[slot], near_sems, (k,), core))

    def spread_farther(k):
        slot = lax.rem(c - k + n_ctx, n_ctx)
        on_far[k].wait_recv()
        on_farther.append(send(far.at[slot], farther.at[slot], farther_sems, (k,), core))

    keys_line, keys_pair = [], []

    def keys_step(step):
        column = place(step, pair)
        source = key_own if step == 0 else key_value.at[column]
        if step > 0:
            keys_line[step - 1].wait_recv()
        if step < line_len - 1:
            keys_line.append(send(source, key_value.at[column], keys_line_sems, (step,), ahead))
        keys_pair.append(send(source, key_value.at[column], keys_pair_sems, (step,), across))

    grads_line, grads_pair = [], []

    def grads_step(step):
        target = grads_out.at[place(step, pair)]
        source = out_grad if step == 0 else target
        if step > 0:
            grads_line[step - 1].wait_recv()
        if step < line_len - 1:
            grads_line.append(send(source, target, grads_line_sems, (step,), ahead))
        grads_pair.append(send(source, target, grads_pair_sems, (step,), across))

    line_step(0, 0)
    mine = pl.ds(pl.multiple_of((b * n_ctx + c) * rows, rows), rows)
    w_in[mine] = own_in[...]
    w_out[mine] = o_weight[...]
    pack()
    for step in range(1, line_len):
        line_step(0, step)
    exchange_columns(0, 2)
    line_step(1, 0)
    for step in range(line_len):
        first_step(0, step)
    between = [functools.partial(line_step, 1, step) for step in range(1, line_len)]
    between += [functools.partial(first_step, 1, step) for step in range(line_len)]
    between += [functools.partial(down_step, 0)]
    for index in range(n_ctx):
        second_step(0, index)
        between[index]()
        if index in (1, 3, 4, 5, 6):
            exchange_columns(len(on_columns), len(on_columns) + 1)
    store(out_grad, grads_out.at[c])
    complete(0)
    for k in range(3):
        spread_columns(k)

    values = hidden[...].astype(F32)
    for d in range(n_batch * n_ctx):
        piece = w_in[d * rows : d * rows + 16, wide:].astype(F32)
        vectors[0:3, d * rows : (d + 1) * rows] = piece[0:3, :rows]
        part = KVW // (n_batch * n_ctx)
        for i in range(2):
            bias[0:1, i * KVW + d * part : i * KVW + (d + 1) * part] = piece[3 + i : 4 + i, :part]
    for k in range(n_ctx):
        first = pl.multiple_of((b * n_ctx + k) * rows, rows)
        piece = w_in[pl.ds(first, 16), wide:].astype(F32)
        key_pos[k : k + 1] = piece[5:6] * 64.0 + piece[6:7]
        key_doc[k : k + 1] = piece[7:8]
    gain_one[...] = vectors[0:1]
    gain_two[...] = vectors[1:2]
    normed_out[...] = (values * row_scale(values) * vectors[0:1]).astype(BF16)
    tables = cosine[...], signed_sine[...]
    lin = dot(normed_out[...], w_in[:, width:wide]) + bias[...]
    for i in range(2 * KV_HEADS):
        head = lin[:, i * HEAD_DIM : (i + 1) * HEAD_DIM]
        head = turn_head(head, *tables) if i < KV_HEADS else head
        key_own[:, i * HEAD_DIM : (i + 1) * HEAD_DIM] = head.astype(BF16)
    keys_step(0)
    key_value[c] = key_own[...]
    for k in range(3):
        step = width // 3
        part = slice(k * step, (k + 1) * step)
        lin = dot(normed_out[...], w_in[:, part]) + vectors[2:3, part]
        for i in range(step // HEAD_DIM):
            head = turn_head(lin[:, i * HEAD_DIM : (i + 1) * HEAD_DIM], *tables)
            low = k * step + i * HEAD_DIM
            query[:, low : low + HEAD_DIM] = head.astype(BF16)
    store(w_in, w_in_out)
    mark_allowed(key_pos, key_doc, own_pos, own_doc, allowed)
    for step in range(1, line_len):
        second_step(1, step - 1)
        keys_step(step)
        spread_columns(len(on_near))
    grads_step(0)
    for step in range(line_len):
        keys_pair[step].wait_recv()
    store(key_value, key_value_out)

    def attention(i):
        wide_part = group * HEAD_DIM
        part = slice(i * wide_part, (i + 1) * wide_part)
        head = i * group // GROUPS * HEAD_DIM
        keys = key_value[:, :, head : head + HEAD_DIM].reshape(n_ctx * count, HEAD_DIM)
        low = KVW + head
        values = key_value[:, :, low : low + HEAD_DIM].reshape(n_ctx * count, HEAD_DIM)
        probs = probabilities(keys, stack_heads(query[:, part], group), allowed, group)
        result = contract_rows(values, probs.astype(BF16)).T
        attn_out[:, part] = lay_heads(result, group).astype(BF16)

    steps = HEADS // group
    for i in range(steps):
        attention(i)
        if i + 1 < line_len:
            grads_step(i + 1)
        for index in range(line_len - 1 + i, n_ctx, steps):
            second_step(1, index)
        if len(on_near) < n_ctx:
            spread_columns(len(on_near))
    down_step(1)
    complete(1)
    store(w_out, w_out_out)
    total = hidden[...].astype(F32) + dot(attn_out[...], w_out[...])
    residual[...] = total
    normed_two[...] = (total * row_scale(total) * vectors[1:2]).astype(BF16)
    for k in range(n_ctx // 2):
        spread_farther(k)
    for k in range(n_ctx // 2, n_ctx):
        spread_farther(k)
    for copy in on_near + on_farther + grads_pair + on_down[1:]:
        copy.wait_recv()
    for copy in sent:
        copy.wait_send()
    for copy in local:
        copy.wait()


def front(matrices, gate, up, hidden, tables, own_places, down, out_grad, vectors, collective_id, name):
    n_batch, n_ctx = lax.axis_size("batch"), lax.axis_size("ctx")
    line_len = n_ctx // 2
    rows = gate.shape[0]
    count, width = hidden.shape
    wide = width + 2 * KVW
    columns = (n_ctx, rows, 2 * lanes(gate.shape[1] // n_ctx))

    def shaped(dtype, *shape):
        return jax.ShapeDtypeStruct(shape, dtype)

    def room(*shape, dtype=BF16):
        return pltpu.VMEM(shape, dtype)

    return pl.pallas_call(
        functools.partial(front_kernel, line_len, 3),
        out_shape=(
            shaped(BF16, count, width),
            shaped(BF16, count, width),
            shaped(BF16, count, width),
            shaped(F32, count, width),
            shaped(BF16, count, width),
            shaped(F32, 1, width),
            shaped(F32, 1, width),
            shaped(F32, n_ctx, count),
            shaped(F32, n_ctx, count),
            shaped(BF16, n_ctx, count, 2 * KVW),
            shaped(BF16, width, wide + 128),
            shaped(BF16, width, width),
            *[shaped(BF16, *columns)] * 4,
            shaped(BF16, n_batch, *down.shape),
            shaped(BF16, n_ctx, count, width),
        ),
        in_specs=[IN_VMEM] * 11 + [ANYWHERE] * 2 + [IN_VMEM] * 5,
        out_specs=(IN_VMEM,) * 9 + (ANYWHERE,) * 9,
        scratch_shapes=[
            room(rows, wide + 128),
            room(width, wide + 128),
            room(width, width),
            room(*columns),
            room(count, 2 * KVW),
            room(n_ctx, count, 2 * KVW),
            room(n_ctx * count, count, dtype=F32),
            room(8, width, dtype=F32),
            room(1, 2 * KVW, dtype=F32),
            room(8, 128, dtype=F32),
            DMA((6,)),
            DMA((2, 2, line_len)),
            DMA((2, 2, line_len)),
            DMA((2, 2, n_ctx)),
            DMA((2, 2, 2 * n_ctx)),
            DMA((2, n_ctx)),
            DMA((2, n_ctx)),
            DMA((2, n_ctx)),
            DMA((2, n_ctx)),
            DMA((2, line_len)),
            DMA((2, line_len)),
            DMA((2, line_len)),
            DMA((2, line_len)),
            DMA((2, 3)),
        ],
        compiler_params=pltpu.CompilerParams(
            collective_id=collective_id, has_side_effects=True, vmem_limit_bytes=58 * 2**20
        ),
        cost_estimate=lasting(100),
        name=name,
    )(*matrices, gate, up, hidden, *tables, *own_places, down, out_grad, *vectors)


def back_kernel(line_len, group, *refs):
    (
        query, key_value, key_pos, key_doc, own_pos, own_doc, attn_out, residual, gain_two, out_grad,
        d_normed, cosine, signed_sine, normed, hidden, gain_one, in_weights, out_weights, columns,
    ) = refs[:19]
    hidden_grad, o_out, q_out, kv_out, sums_out, columns_out = refs[19:25]
    w_out, w_in, branch, allowed, key_sum, value_sum, d_query, flipped, d_residual = refs[25:34]
    d_key_value, keys_pair, keys_line, keys_pass, sums_got, sums_mine = refs[34:40]
    grads = refs[40:43]
    core_in, chip_in, pair_in, line_in, chip_out, pair_out, line_out = [
        refs[43 + 3 * i : 46 + 3 * i] for i in range(7)
    ]
    (
        load_sems, column_sems, keys_pair_sems, keys_line_sems, sums_sems, core_sems, chip_sems,
        pair_sems, line_sems,
    ) = refs[64:]
    outs = o_out, q_out, kv_out
    b, c = lax.axis_index("batch"), lax.axis_index("ctx")
    n_ctx = 2 * line_len
    line, pair = c // 2, c % 2
    ahead = (b, 2 * lax.rem(line + 1, line_len) + pair)
    across, chip, core = (b, c ^ 1), (b ^ 2, c), (b ^ 1, c)
    others = [(b, lax.rem(c + k, n_ctx)) for k in range(1, n_ctx)]
    on_same_line = others[1::2]
    count, width = query.shape
    wide = group * HEAD_DIM
    rows = q_out.shape[0]
    greet([chip, core] + others)
    sent = []

    def send(source, target, sems, index, device):
        copy = remote(source, target, sems.at[(0, *index)], sems.at[(1, *index)], device)
        copy.start()
        sent.append(copy)
        return copy

    loads = [
        pltpu.make_async_copy(out_weights, w_out, load_sems.at[0]),
        pltpu.make_async_copy(in_weights.at[:, pl.ds(0, width + 2 * KVW)], w_in, load_sems.at[1]),
        pltpu.make_async_copy(columns.at[c], columns_out.at[c], load_sems.at[2]),
    ]
    for copy in loads:
        copy.start()
    on_columns = []

    def exchange_columns(first, last):
        for k in range(first, last):
            source = columns.at[others[k][1]]
            on_columns.append(send(source, columns_out.at[c], column_sems, (k,), others[k]))

    exchange_columns(0, n_ctx - 1)

    def to(step):
        return 2 * lax.rem(line - 1 - step + line_len, line_len)

    def place(index):
        return to(index // 2) + (1 - pair if index % 2 == 0 else pair)

    def block(row, index):
        at = (row * n_ctx + place(index)) * rows
        return pl.ds(pl.multiple_of(at, rows), rows)

    to_core, to_chip, to_pair, to_line = {}, {}, {}, {}

    def core_stage(p):
        for index in range(2 * n_ctx):
            row = b ^ 3 if index < n_ctx else b ^ 1
            source = grads[p].at[block(row, index % n_ctx)]
            to_core[p, index] = send(source, core_in[p].at[index], core_sems, (p, index), core)

    def chip_stage(p):
        for index in range(n_ctx):
            to_core[p, index].wait_recv()
            total = grads[p][block(b ^ 2, index)].astype(F32) + core_in[p][index].astype(F32)
            chip_out[p][index] = total.astype(BF16)
            to_chip[p, index] = send(
                chip_out[p].at[index], chip_in[p].at[index], chip_sems, (p, index), chip
            )

    def mine(p, index):
        to_core[p, n_ctx + index].wait_recv()
        to_chip[p, index].wait_recv()
        return (
            grads[p][block(b, index)].astype(F32)
            + core_in[p][n_ctx + index].astype(F32)
            + chip_in[p][index].astype(F32)
        )

    def pair_stage(p, step):
        pair_out[p][step] = mine(p, 2 * step).astype(BF16)
        to_pair[p, step] = send(
            pair_out[p].at[step], pair_in[p].at[step], pair_sems, (p, step), across
        )

    def line_stage(p, step):
        total = mine(p, 2 * step + 1)
        to_pair[p, step].wait_recv()
        total = total + pair_in[p][step].astype(F32)
        if step > 0:
            to_line[p, step - 1].wait_recv()
            total = total + line_in[p][step - 1].astype(F32)
        if step < line_len - 1:
            line_out[p][step] = total.astype(BF16)
            to_line[p, step] = send(
                line_out[p].at[step], line_in[p].at[step], line_sems, (p, step), ahead
            )
        else:
            outs[p][...] = total

    values, gradient = residual[...], d_normed[...]
    factor = row_scale(values)
    scaled = gradient * gain_two[...]
    sums_mine[...] = jnp.zeros_like(sums_mine)
    sums_mine[3:4] = jnp.sum(gradient * values * factor, axis=0, keepdims=True)
    total = out_grad[...].astype(F32) + (
        factor * scaled
        - values * (factor * factor * factor) * jnp.mean(scaled * values, axis=-1, keepdims=True)
    )
    d_residual[...] = total
    branch[...] = total.astype(BF16)
    for i in range(HEADS // group):
        part = slice(i * wide, (i + 1) * wide)
        grads[0][part] = contract_rows(attn_out[:, part], branch[...]).astype(BF16)
    core_stage(0)
    mark_allowed(key_pos, key_doc, own_pos, own_doc, allowed)
    flipped[...] = normed[...].astype(F32).T.astype(BF16)
    tables = cosine[...], signed_sine[...]

    def attention(i):
        part = slice(i * wide, (i + 1) * wide)
        head = i * group // GROUPS
        key_part = slice(head * HEAD_DIM, (head + 1) * HEAD_DIM)
        value_part = slice(KVW + head * HEAD_DIM, KVW + (head + 1) * HEAD_DIM)
        keys, values = key_value[:, key_part], key_value[:, value_part]
        d_attn = times_transposed(branch[...], w_out[part]).astype(BF16)
        head_grads, queries = stack_heads(d_attn, group), stack_heads(query[:, part], group)
        probs = probabilities(keys, queries, allowed, group)
        d_probs = times_transposed(values, head_grads)
        delta = jnp.sum(probs * d_probs, axis=0, keepdims=True)
        d_scores = (probs * (d_probs - delta)).astype(BF16)
        key_term = dot(d_scores, queries)
        value_term = dot(probs.astype(BF16), head_grads)
        first = i * group % GROUPS == 0
        key_sum[...] = key_term if first else key_sum[...] + key_term
        value_sum[...] = value_term if first else value_sum[...] + value_term
        result = contract_rows(keys, d_scores).T * INV_ROOT
        for k in range(group):
            turned = turn_head(result[k * count : (k + 1) * count], *tables, back=True)
            at = (i * group + k) * HEAD_DIM
            d_query[:, at : at + HEAD_DIM] = turned.astype(BF16)
        if (i + 1) * group % GROUPS == 0:
            shape = d_key_value.shape[:2] + (HEAD_DIM,)
            d_key_value[:, :, key_part] = (key_sum[...] * INV_ROOT).astype(BF16).reshape(shape)
            d_key_value[:, :, value_part] = value_sum[...].astype(BF16).reshape(shape)

    loads[0].wait()
    attention(0)
    chip_stage(0)
    for i in range(1, HEADS // group):
        attention(i)

    given, passed = [], []
    for step in range(line_len):
        source = d_key_value.at[to(step) + 1 - pair]
        given.append(send(source, keys_pair.at[step], keys_pair_sems, (step,), across))
    key_total = None

    def keys_stage(step):
        given[step].wait_recv()
        total = d_key_value[to(step) + pair].astype(F32) + keys_pair[step].astype(F32)
        if step > 0:
            passed[step - 1].wait_recv()
            total = total + keys_line[step - 1].astype(F32)
        if step < line_len - 1:
            keys_pass[step] = total.astype(BF16)
            passed.append(
                send(keys_pass.at[step], keys_line.at[step], keys_line_sems, (step,), ahead)
            )
        return total

    last = line_len - 1
    for step in range(line_len // 2):
        pair_stage(0, step)
    half = width // 2
    for i in range(2):
        part = slice(i * half, (i + 1) * half)
        grads[1][:, part] = dot(flipped[...], d_query[:, part]).astype(BF16)
        if i == 0:
            keys_stage(0)
    core_stage(1)
    loads[1].wait()
    d_one = times_transposed(d_query[...], w_in[:, :width])
    for step in range(1, line_len):
        key_total = keys_stage(step)
        if step == 1:
            chip_stage(1)
        if line_len // 2 + step - 1 < line_len:
            pair_stage(0, line_len // 2 + step - 1)
        if step < last:
            line_stage(0, step - 1)
    heads = [
        turn_head(key_total[:, i * HEAD_DIM : (i + 1) * HEAD_DIM], *tables, back=True)
        for i in range(KV_HEADS)
    ]
    d_lin = jnp.concatenate(heads + [key_total[:, KVW:]], axis=1).astype(BF16)
    grads[2][...] = dot(flipped[...], d_lin).astype(BF16)
    core_stage(2)
    line_stage(0, last - 1)
    d_one = d_one + times_transposed(d_lin, w_in[:, width:])
    sums_mine[1:2] = jnp.sum(d_query[...].astype(F32), axis=0, keepdims=True)
    sums_mine[2:3, : 2 * KVW] = jnp.sum(d_lin.astype(F32), axis=0, keepdims=True)
    values = hidden[...].astype(F32)
    factor = row_scale(values)
    scaled = d_one * gain_one[...]
    sums_mine[0:1] = jnp.sum(d_one * values * factor, axis=0, keepdims=True)

    def start_sums(index, device):
        copy = remote(
            sums_mine, sums_got.at[index], sums_sems.at[0, index], sums_sems.at[1, index], device
        )
        copy.start()
        return copy

    def add_sums(index, copy):
        copy.wait()
        sums_mine[...] += sums_got[index]

    by_core = start_sums(0, core)
    pair_stage(1, 0)
    line_stage(0, last)
    add_sums(0, by_core)
    by_chip = start_sums(1, chip)
    chip_stage(2)
    hidden_grad[...] = d_residual[...] + (
        factor * scaled
        - values * (factor * factor * factor) * jnp.mean(scaled * values, axis=-1, keepdims=True)
    )
    for step in range(1, line_len):
        pair_stage(1, step)
        line_stage(1, step - 1)
    add_sums(1, by_chip)
    by_pair = start_sums(2, across)
    pair_stage(2, 0)
    line_stage(1, last)
    for step in range(1, line_len):
        pair_stage(2, step)
        line_stage(2, step - 1)
        if step == 1:
            add_sums(2, by_pair)
            by_line = [start_sums(3 + k, device) for k, device in enumerate(on_same_line)]
    line_stage(2, last)
    total = sums_mine[...]
    for k, copy in enumerate(by_line):
        copy.wait()
        total = total + sums_got[3 + k]
    sums_out[...] = total
    for copy in on_columns:
        copy.wait_recv()
    for copy in sent:
        copy.wait_send()
    loads[2].wait()


def back(query, key_value, weights, places, attn_out, residual, gain_two, out_grad, d_normed, tables, normed, hidden, gain_one, columns, collective_id, name):
    n_ctx = columns.shape[0]
    line_len, rows = n_ctx // 2, columns.shape[1]
    count, width = query.shape
    keys = key_value.shape[0]
    widths = width, width, 2 * KVW

    def room(*shape, dtype=BF16):
        return pltpu.VMEM(shape, dtype)

    def rooms(size):
        return [room(size, rows, part) for part in widths]

    outs = [(count, width)] + [(rows, part) for part in widths] + [(8, width)]
    return pl.pallas_call(
        functools.partial(back_kernel, line_len, 3),
        out_shape=(
            *[jax.ShapeDtypeStruct(shape, F32) for shape in outs],
            jax.ShapeDtypeStruct(columns.shape, BF16),
        ),
        in_specs=[IN_VMEM] * 16 + [ANYWHERE] * 3,
        out_specs=(IN_VMEM,) * 5 + (ANYWHERE,),
        scratch_shapes=[
            room(width, width),
            room(width, width + 2 * KVW),
            room(count, width),
            room(keys, count, dtype=F32),
            room(keys, HEAD_DIM, dtype=F32),
            room(keys, HEAD_DIM, dtype=F32),
            room(count, width),
            room(width, count),
            room(count, width, dtype=F32),
            room(n_ctx, count, 2 * KVW),
            room(line_len, count, 2 * KVW),
            room(line_len - 1, count, 2 * KVW),
            room(line_len - 1, count, 2 * KVW),
            room(2 + line_len, 8, width, dtype=F32),
            room(8, width, dtype=F32),
            *[room(width, part) for part in widths],
            *rooms(2 * n_ctx),
            *rooms(n_ctx),
            *rooms(line_len),
            *rooms(line_len - 1),
            *rooms(n_ctx),
            *rooms(line_len),
            *rooms(line_len - 1),
            DMA((3,)),
            DMA((2, n_ctx)),
            DMA((2, line_len)),
            DMA((2, line_len)),
            DMA((2, 2 + line_len)),
            DMA((2, 3, 2 * n_ctx)),
            DMA((2, 3, n_ctx)),
            DMA((2, 3, line_len)),
            DMA((2, 3, line_len)),
        ],
        compiler_params=pltpu.CompilerParams(
            collective_id=collective_id, has_side_effects=True, vmem_limit_bytes=60 * 2**20
        ),
        cost_estimate=lasting(90),
        name=name,
    )(
        query, key_value, *places, attn_out, residual, gain_two, out_grad, d_normed, *tables, normed,
        hidden, gain_one, *weights, columns,
    )


def swap(values, bit):
    size = lax.axis_size("batch")
    return lax.ppermute(values, "batch", [(i, i ^ bit) for i in range(size)])


def by_batch(values, b, n_batch):
    step = values.shape[1] // n_batch
    blocks = [lax.dynamic_slice_in_dim(values, (b ^ k) * step, step, 1) for k in range(n_batch)]
    return jnp.concatenate(blocks, axis=1)


def batch_terms(terms):
    passed = swap((terms[2].astype(F32) + swap(terms[3], 1).astype(F32)).astype(BF16), 2)
    return [term.astype(F32) for term in (terms[0], swap(terms[1], 1), passed)]


def mlp_room(*sizes):
    rooms = mlp_scratch(*sizes)
    return sum(math.prod(room.shape) * jnp.dtype(room.dtype).itemsize for room in rooms)


def mlp_in_steps(normed_two, w_gate_up, w_down, out_grad_all):
    n_batch, b = lax.axis_size("batch"), lax.axis_index("batch")
    normed_two = by_batch(normed_two, b, n_batch)
    w_gate_up = jnp.concatenate(w_gate_up, axis=0)
    half, width = w_gate_up.shape[1] // 2, normed_two.shape[1]
    own_ff = w_down.shape[0]
    w_down = jnp.pad(w_down, ((0, half - own_ff), (0, 0)))
    normed_two = gather_ctx(normed_two, 3, "gather_tokens").reshape(-1, width)
    gate_up = dot(normed_two, w_gate_up)
    gate_lin, up_lin = gate_up[:, :half], gate_up[:, half:]
    sigmoid_gate = jax.nn.sigmoid(gate_lin)
    mixed_rows = (gate_lin * sigmoid_gate * up_lin).astype(BF16)
    d_mixed = times_transposed(out_grad_all, w_down)
    d_gate = d_mixed * up_lin * sigmoid_gate * (1.0 + gate_lin * (1.0 - sigmoid_gate))
    d_up = d_mixed * (gate_lin * sigmoid_gate)
    d_gate_up = jnp.concatenate([d_gate.astype(BF16), d_up.astype(BF16)], axis=1)
    (d_normed_two,) = scatter_ctx(
        [times_transposed(d_gate_up, w_gate_up).astype(BF16)], 4, "scatter_tokens"
    )
    (ff_out,) = scatter_ctx([dot(mixed_rows, w_down).astype(BF16)], 8, "scatter_outputs")
    gate_up_grad = contract_rows(normed_two, d_gate_up).astype(BF16).reshape(n_batch, -1, 2 * half)
    down_grad = contract_rows(mixed_rows, out_grad_all).astype(BF16)[:own_ff]
    return (
        by_batch(d_normed_two, b, n_batch),
        ff_out,
        sum(
            batch_terms(
                [
                    lax.dynamic_index_in_dim(
                        down_grad.reshape(n_batch, -1, width), b ^ k, 0, keepdims=False
                    )
                    for k in range(n_batch)
                ]
            )
        ),
        sum(batch_terms(gate_up_grad)).astype(BF16),
    )


def vector_rows(vectors):
    pieces = []
    for vector in vectors:
        pieces += [vector, jnp.zeros((128 - vector.shape[0],), vector.dtype)]
    pieces.append(jnp.zeros((128 * (8 - len(vectors)),), vectors[0].dtype))
    return jnp.concatenate(pieces).reshape(8, 128)


def local(
    hidden_in,
    positions,
    doc_ids,
    attn_gain,
    q_weight,
    q_bias,
    k_weight,
    k_bias,
    v_weight,
    v_bias,
    o_weight,
    mlp_gain,
    gate_weight,
    up_weight,
    down_weight,
    out_grad,
):
    n_batch, n_ctx = lax.axis_size("batch"), lax.axis_size("ctx")
    n_all = n_batch * n_ctx
    count, width = hidden_in.shape
    hidden_ff = gate_weight.shape[1]

    b = lax.axis_index("batch")
    rows = q_weight.shape[0]
    vectors = (attn_gain, mlp_gain, q_bias, k_bias, v_bias)
    weights = (q_weight, k_weight, v_weight, o_weight)
    cosine, sine_table = rope_tables(positions)
    half_lane = jnp.arange(HEAD_DIM) < HEAD_DIM // 2
    tables = cosine, jnp.where(half_lane[None], -sine_table, sine_table)
    own_places = positions[None], doc_ids[None]
    together = rows % 16 == 0
    if together:
        (
            normed_one, query, attn_out, residual, normed_two, gain_one, gain_two, key_pos, key_doc,
            key_value, *weights, packed, near, far, farther, w_down, out_grad_all,
        ) = front(
            weights, gate_weight, up_weight, hidden_in, tables, own_places, down_weight, out_grad,
            [vector[None] for vector in vectors], 1, "front",
        )
        w_down = w_down.reshape(-1, width)
        half = packed.shape[2] // 2
        key_value = key_value.reshape(-1, 2 * KVW)
        w_gate_up = [columns.reshape(-1, 2 * half) for columns in (packed, near, far, farther)]
        places = (key_pos, key_doc, *own_places)
    else:
        w_down = lax.all_gather(down_weight, "batch", axis=0, tiled=True)
        out_grad_all = lax.all_gather(out_grad, "ctx", axis=0, tiled=True)
        marks = (positions // 64, positions % 64, doc_ids)
        small = vector_rows(vectors + tuple(mark.astype(BF16) for mark in marks))
        small = jnp.pad(small, ((0, rows - 8), (0, 0)))
        attn_all, packed = spread(
            (*weights, small), gate_weight, up_weight, 1, "spread_weights"
        )
        half = packed.shape[2] // 2
        own_rows = packed.reshape(-1, 2 * half)
        near, far = swap(own_rows, 1), swap(own_rows, 2)
        small = attn_all[:, :, :8, attn_all.shape[3] - 128 :].astype(F32)
        gain_one, gain_two, b_query, b_key, b_value = (
            small[:, :, i, : part.shape[0]].reshape(-1)
            for i, part in enumerate((attn_gain, mlp_gain, q_bias, k_bias, v_bias))
        )
        places = lax.dynamic_index_in_dim(small, b, 0, keepdims=False)[:, 5:8, :count]
        key_pos, key_doc = places[:, 0] * 64 + places[:, 1], places[:, 2]
        attn_all = attn_all.reshape(width, -1)
        b_qkv = jnp.concatenate([b_query, b_key, b_value])
        gain_one, gain_two = gain_one[None], gain_two[None]

        normed_one, query, key_value = project(hidden_in, gain_one, attn_all, b_qkv[None], tables)
        key_value = gather_ctx(key_value, 2, "gather_keys").reshape(-1, 2 * KVW)
        far, key_value = lax.optimization_barrier((far, key_value))
        w_gate_up = (own_rows, near, far, swap(far, 1))
        places = (key_pos, key_doc, *own_places)
        attn_out, residual, normed_two = attend(
            query, key_value, attn_all, places, hidden_in, gain_two
        )

    fits = mlp_room(n_ctx, n_batch, count, width, w_down.shape[0]) < 60 * 2**20
    feed_forward = functools.partial(mlp, collective_id=3, name="mlp") if fits else mlp_in_steps
    d_normed_two, ff_out, down_grad, gate_up_grad = feed_forward(
        normed_two, w_gate_up, w_down, out_grad_all.reshape(-1, width)
    )

    columns = gate_up_grad.reshape(n_ctx, rows, 2 * half)
    if together:
        hidden_grad, o_grad, q_grad, kv_grad, sums, gate_up_grad = back(
            query, key_value, weights, places, attn_out, residual, gain_two, out_grad,
            d_normed_two, tables, normed_one, hidden_in, gain_one, columns, 7, "back"
        )
        (
            gate_grad, up_grad, hidden_grad, o_grad, q_grad, k_grad, v_grad, hidden_out, down_grad, sums,
        ) = finish(
            gate_up_grad, hidden_grad, o_grad, q_grad, kv_grad, residual, ff_out, down_grad, sums,
            n_batch, hidden_ff,
        )
        gain_one_grad, q_bias_grad, gain_two_grad = (sums[i, :rows] for i in (0, 1, 3))
        k_bias_grad, v_bias_grad = (sums[i, : KVW // n_all] for i in (10, 18))
    else:
        d_query, d_key_value, o_grad, d_residual, gain_two_grad = attend_back(
            query, key_value, attn_all, places, attn_out, residual, gain_two, out_grad,
            d_normed_two, tables,
        )
        (d_key_value,) = scatter_ctx([d_key_value], 5, "scatter_keys")
        qkv_grad, hidden_grad, sums = project_back(
            d_query, d_key_value, attn_all, normed_one, hidden_in, gain_one, d_residual,
            gain_two_grad, tables,
        )
        grads = [grad.reshape(n_batch, n_ctx, rows, -1) for grad in (qkv_grad, o_grad)]
        qkv_grad, o_grad, sums, gate_up_grad = collect(grads, sums, columns, 6, "collect")
        q_grad, k_grad = qkv_grad[:, :width], qkv_grad[:, width : width + KVW]
        v_grad = qkv_grad[:, width + KVW :]
        gate_grad, up_grad = unpack(gate_up_grad, n_batch, hidden_ff)
        hidden_out = (residual + ff_out).astype(BF16)

        def own_part(row, first, total):
            size = total // n_all
            at = first + (b * n_ctx + lax.axis_index("ctx")) * size
            return lax.dynamic_slice(sums, (row, at), (1, size))[0]

        gain_one_grad, q_bias_grad = own_part(0, 0, width), own_part(1, 0, width)
        k_bias_grad, v_bias_grad = own_part(2, 0, KVW), own_part(2, KVW, KVW)
        gain_two_grad = own_part(3, 0, width)
    return (
        hidden_out,
        hidden_grad,
        gain_one_grad,
        q_grad,
        q_bias_grad,
        k_grad,
        k_bias_grad,
        v_grad,
        v_bias_grad,
        o_grad,
        gain_two_grad,
        gate_grad,
        up_grad,
        down_grad,
    )


def solution(mesh):
    matrix, vector = P(ALL, None), P(ALL)
    placed = (
        (matrix, vector, vector, vector, matrix, vector, matrix, vector)
        + (matrix, vector, matrix, vector, matrix, matrix, matrix, matrix)
    )
    results = (matrix, matrix) + (vector, matrix) * 4 + (vector, matrix, matrix, matrix)
    return jax.shard_map(local, mesh=mesh, in_specs=placed, out_specs=results, check_vma=False)
```

```python
import functools
import math

import jax
import jax.numpy as jnp
from jax import lax
from jax.experimental import pallas as pl
from jax.experimental.pallas import tpu as pltpu
from jax.sharding import PartitionSpec as P

HEADS = 12
KV_HEADS = 2
GROUPS = HEADS // KV_HEADS
HEAD_DIM = 128
KVW = KV_HEADS * HEAD_DIM
INV_ROOT = HEAD_DIM ** (-0.5)
EPSILON = 1e-06
ROPE_BASE = 10000.0
MASKED = -1e30
ALL = ("batch", "ctx")
F32 = jnp.float32
BF16 = jnp.bfloat16
MESH = pl.DeviceIdType.MESH
ANYWHERE = pl.BlockSpec(memory_space=pl.ANY)
IN_VMEM = pl.BlockSpec(memory_space=pltpu.VMEM)
DMA = pltpu.SemaphoreType.DMA


def rope_tables(positions):
    half_dim = HEAD_DIM // 2
    inverse_freq = jnp.exp(
        jnp.arange(half_dim, dtype=F32) * (-2.0 * math.log(ROPE_BASE) / HEAD_DIM)
    )
    angles = positions.astype(F32)[:, None] * inverse_freq[None, :]
    angles = jnp.concatenate([angles, angles], axis=1)
    return (jnp.cos(angles), jnp.sin(angles))


def dot(lhs, rhs):
    return jnp.dot(lhs, rhs, preferred_element_type=F32)


def contract_rows(lhs, rhs):
    return lax.dot_general(lhs, rhs, (((0,), (0,)), ((), ())), preferred_element_type=F32)


def times_transposed(lhs, rhs):
    return lax.dot_general(lhs, rhs, (((1,), (1,)), ((), ())), preferred_element_type=F32)


def lanes(width):
    return -(-width // 128) * 128


def greet(devices):
    barrier = pltpu.get_barrier_semaphore()
    for device in devices:
        pl.semaphore_signal(barrier, inc=1, device_id=device, device_id_type=MESH)
    pl.semaphore_wait(barrier, len(devices))


def remote(source, target, send, receive, device):
    return pltpu.make_async_remote_copy(
        src_ref=source,
        dst_ref=target,
        send_sem=send,
        recv_sem=receive,
        device_id=device,
        device_id_type=MESH,
    )


def lasting(microseconds):
    return pl.CostEstimate(flops=0, bytes_accessed=int(3.3e6 * microseconds), transcendentals=0)


def gather_kernel(line_len, own, out, own_sem, line_sems, pair_sems):
    b, c = lax.axis_index("batch"), lax.axis_index("ctx")
    line, pair = c // 2, c % 2
    ahead = (b, 2 * lax.rem(line + 1, line_len) + pair)
    behind = (b, 2 * lax.rem(line + line_len - 1, line_len) + pair)
    across = (b, c ^ 1)
    greet((ahead, behind, across))
    keep = pltpu.make_async_copy(own, out.at[c], own_sem)
    keep.start()
    on_line, on_pair = [], []
    for step in range(line_len):
        at = 2 * lax.rem(line - step + line_len, line_len) + pair
        block = own if step == 0 else out.at[at]
        if step > 0:
            on_line[step - 1].wait_recv()
        if step < line_len - 1:
            copy = remote(block, out.at[at], line_sems.at[0, step], line_sems.at[1, step], ahead)
            copy.start()
            on_line.append(copy)
        copy = remote(block, out.at[at], pair_sems.at[0, step], pair_sems.at[1, step], across)
        copy.start()
        on_pair.append(copy)
    for copy in on_pair:
        copy.wait()
    for copy in on_line:
        copy.wait_send()
    keep.wait()


def gather_ctx(block, collective_id, name):
    n_ctx = lax.axis_size("ctx")
    line_len = n_ctx // 2
    return pl.pallas_call(
        functools.partial(gather_kernel, line_len),
        out_shape=jax.ShapeDtypeStruct((n_ctx,) + block.shape, block.dtype),
        in_specs=[ANYWHERE],
        out_specs=ANYWHERE,
        scratch_shapes=[DMA(()), DMA((2, line_len)), DMA((2, line_len))],
        compiler_params=pltpu.CompilerParams(collective_id=collective_id, has_side_effects=True),
        cost_estimate=lasting(20),
        name=name,
    )(block)


def scatter_kernel(line_len, many, *refs):
    parts, outs = refs[:many], refs[many : 2 * many]
    pair_in, line_in, line_out = (refs[(2 + i) * many : (3 + i) * many] for i in range(3))
    pair_sems, line_sems = refs[5 * many :]
    b, c = lax.axis_index("batch"), lax.axis_index("ctx")
    line, pair = c // 2, c % 2
    ahead = (b, 2 * lax.rem(line + 1, line_len) + pair)
    behind = (b, 2 * lax.rem(line + line_len - 1, line_len) + pair)
    across = (b, c ^ 1)
    greet((ahead, behind, across))

    def to(step):
        return 2 * lax.rem(line - 1 - step + line_len, line_len)

    sent, given = [], []
    for i in range(many):
        for step in range(line_len):
            copy = remote(
                parts[i].at[to(step) + 1 - pair],
                pair_in[i].at[step],
                pair_sems.at[0, i, step],
                pair_sems.at[1, i, step],
                across,
            )
            copy.start()
            given.append(copy)
    for i in range(many):
        for step in range(line_len):
            given[i * line_len + step].wait_recv()
            total = parts[i][to(step) + pair].astype(F32) + pair_in[i][step].astype(F32)
            if step > 0:
                passed.wait_recv()
                total = total + line_in[i][step - 1].astype(F32)
            if step < line_len - 1:
                line_out[i][step] = total.astype(BF16)
                passed = remote(
                    line_out[i].at[step],
                    line_in[i].at[step],
                    line_sems.at[0, i, step],
                    line_sems.at[1, i, step],
                    ahead,
                )
                passed.start()
                sent.append(passed)
            else:
                outs[i][...] = total
    for copy in given + sent:
        copy.wait_send()


def scatter_ctx(parts, collective_id, name):
    n_ctx = lax.axis_size("ctx")
    line_len, many = n_ctx // 2, len(parts)
    blocks = [(part.shape[0] // n_ctx,) + part.shape[1:] for part in parts]

    def room(size):
        return [pltpu.VMEM((size,) + block, BF16) for block in blocks]

    return pl.pallas_call(
        functools.partial(scatter_kernel, line_len, many),
        out_shape=[jax.ShapeDtypeStruct(block, F32) for block in blocks],
        in_specs=[IN_VMEM] * many,
        out_specs=[IN_VMEM] * many,
        scratch_shapes=[
            *room(line_len),
            *room(line_len - 1),
            *room(line_len - 1),
            DMA((2, many, line_len)),
            DMA((2, many, line_len)),
        ],
        compiler_params=pltpu.CompilerParams(
            collective_id=collective_id, has_side_effects=True, vmem_limit_bytes=60 * 2**20
        ),
        cost_estimate=lasting(40),
        name=name,
    )(*[part.reshape((n_ctx,) + block) for part, block in zip(parts, blocks)])


def spread_kernel(
    line_len, q_weight, k_weight, v_weight, o_weight, small, gate, up, out, columns_out, own,
    columns, own_sem, line_sems, pair_sems, chip_sems, core_sems, column_sems,
):
    b, c = lax.axis_index("batch"), lax.axis_index("ctx")
    n_ctx = 2 * line_len
    line, pair = c // 2, c % 2
    ahead = (b, 2 * lax.rem(line + 1, line_len) + pair)
    across, chip, core = (b, c ^ 1), (b ^ 2, c), (b ^ 1, c)
    others = [(b, lax.rem(c + k, n_ctx)) for k in range(1, n_ctx)]
    at = 0
    for part in (q_weight, k_weight, v_weight, o_weight, small):
        own[:, at : at + part.shape[1]] = part[...]
        at += part.shape[1]
    greet([chip, core] + others)
    keep = [pltpu.make_async_copy(own, out.at[b, c], own_sem.at[0])]
    keep[0].start()

    def pack():
        n_batch, half = out.shape[0], columns.shape[2] // 2
        piece = gate.shape[1] // (n_batch * n_ctx)
        for first, weight in ((0, gate), (half, up)):
            if n_batch * piece < half:
                columns[:, :, first + half - 128 : first + half] = jnp.zeros(
                    (n_ctx, columns.shape[1], 128), BF16
                )
            for k in range(n_batch):
                for i in range(n_ctx):
                    to = (k * n_ctx + i) * piece
                    at = first + k * piece
                    columns[i, :, at : at + piece] = weight[:, to : to + piece]
        keep.append(pltpu.make_async_copy(columns.at[c], columns_out.at[c], own_sem.at[1]))
        keep[1].start()

    def place(step, side):
        return 2 * lax.rem(line - step + line_len, line_len) + side

    def hand(block, to_b, to_c, sems, index, device):
        copy = remote(block, out.at[to_b, to_c], sems.at[0, index], sems.at[1, index], device)
        copy.start()
        return copy

    on_line, on_pair, on_chip, on_core, on_columns = [], [], [], [], []
    for step in range(line_len):
        at = place(step, pair)
        block = own if step == 0 else out.at[b, at]
        if step > 0:
            on_line[step - 1].wait_recv()
        if step < line_len - 1:
            on_line.append(hand(block, b, at, line_sems, step, ahead))
        on_pair.append(hand(block, b, at, pair_sems, step, across))
        on_chip.append(hand(block, b, at, chip_sems, step, chip))
        on_core.append(hand(block, b, at, core_sems, step, core))
        if step == 0:
            pack()
    for k, device in enumerate(others):
        copy = remote(
            columns.at[device[1]],
            columns_out.at[c],
            column_sems.at[0, k],
            column_sems.at[1, k],
            device,
        )
        copy.start()
        on_columns.append(copy)
    for step in range(line_len):
        at = place(step, 1 - pair)
        on_pair[step].wait_recv()
        on_chip.append(hand(out.at[b, at], b, at, chip_sems, line_len + step, chip))
        on_core.append(hand(out.at[b, at], b, at, core_sems, line_len + step, core))
    for index in range(n_ctx):
        at = place(index % line_len, pair if index < line_len else 1 - pair)
        on_chip[index].wait_recv()
        on_core.append(hand(out.at[b ^ 2, at], b ^ 2, at, core_sems, n_ctx + index, core))
    for copy in on_core + on_columns:
        copy.wait()
    for copy in on_line + on_pair + on_chip:
        copy.wait_send()
    for copy in keep:
        copy.wait()


def spread(matrices, gate, up, collective_id, name):
    n_batch, n_ctx = lax.axis_size("batch"), lax.axis_size("ctx")
    line_len = n_ctx // 2
    rows = gate.shape[0]
    own = (rows, sum(matrix.shape[1] for matrix in matrices))
    columns = (n_ctx, rows, 2 * lanes(gate.shape[1] // n_ctx))
    return pl.pallas_call(
        functools.partial(spread_kernel, line_len),
        out_shape=(
            jax.ShapeDtypeStruct((n_batch, n_ctx) + own, BF16),
            jax.ShapeDtypeStruct(columns, BF16),
        ),
        in_specs=[IN_VMEM] * 7,
        out_specs=(ANYWHERE, ANYWHERE),
        scratch_shapes=[
            pltpu.VMEM(own, BF16),
            pltpu.VMEM(columns, BF16),
            DMA((2,)),
            DMA((2, line_len)),
            DMA((2, line_len)),
            DMA((2, n_ctx)),
            DMA((2, 2 * n_ctx)),
            DMA((2, n_ctx)),
        ],
        compiler_params=pltpu.CompilerParams(
            collective_id=collective_id, has_side_effects=True, vmem_limit_bytes=40 * 2**20
        ),
        cost_estimate=lasting(75),
        name=name,
    )(*matrices, gate, up)


def collect_kernel(line_len, *refs):
    grads, (sums_in, columns) = refs[:2], refs[2:4]
    outs, (sums_out, columns_out) = refs[4:6], refs[6:8]
    core_in, chip_in, pair_in, line_in, chip_out, pair_out, line_out = [
        refs[8 + 2 * i : 10 + 2 * i] for i in range(7)
    ]
    sums_got, sums_mine, own_sem = refs[22:25]
    core_sems, chip_sems, pair_sems, line_sems, column_sems, sums_sems = refs[25:]
    b, c = lax.axis_index("batch"), lax.axis_index("ctx")
    n_ctx = 2 * line_len
    line, pair = c // 2, c % 2
    ahead = (b, 2 * lax.rem(line + 1, line_len) + pair)
    across, chip, core = (b, c ^ 1), (b ^ 2, c), (b ^ 1, c)
    others = [(b, lax.rem(c + k, n_ctx)) for k in range(1, n_ctx)]
    on_same_line = others[1::2]
    greet([chip, core] + others)
    keep = pltpu.make_async_copy(columns.at[c], columns_out.at[c], own_sem)
    keep.start()

    def place(index):
        step, side = index // 2, index % 2
        to = lax.rem(line - 1 - step + line_len, line_len)
        return 2 * to + (1 - pair if side == 0 else pair)

    waits = []

    def send(block, target, sems, index, device):
        copy = remote(block, target, sems.at[0, index], sems.at[1, index], device)
        copy.start()
        waits.append(copy)
        return copy

    def start_sums(index, device):
        copy = remote(
            sums_mine, sums_got.at[index], sums_sems.at[0, index], sums_sems.at[1, index], device
        )
        copy.start()
        return copy

    def add_sums(index, copy):
        copy.wait()
        sums_mine[...] += sums_got[index]

    sums_mine[...] = sums_in[...]
    by_core = start_sums(0, core)
    to_core = [[], []]
    for index in range(2 * n_ctx):
        row = b ^ 3 if index < n_ctx else b ^ 1
        for i in range(2):
            to_core[i].append(
                send(
                    grads[i].at[row, place(index % n_ctx)],
                    core_in[i].at[index],
                    core_sems.at[i],
                    index,
                    core,
                )
            )
    add_sums(0, by_core)
    by_chip = start_sums(1, chip)
    on_columns = []
    for k, device in enumerate(others):
        copy = remote(
            columns.at[device[1]],
            columns_out.at[c],
            column_sems.at[0, k],
            column_sems.at[1, k],
            device,
        )
        copy.start()
        on_columns.append(copy)
    to_chip = [[], []]
    for index in range(n_ctx):
        for i in range(2):
            to_core[i][index].wait_recv()
            total = grads[i][b ^ 2, place(index)].astype(F32) + core_in[i][index].astype(F32)
            chip_out[i][index] = total.astype(BF16)
            to_chip[i].append(
                send(chip_out[i].at[index], chip_in[i].at[index], chip_sems.at[i], index, chip)
            )
    add_sums(1, by_chip)
    by_pair = start_sums(2, across)

    def mine(i, index):
        to_core[i][n_ctx + index].wait_recv()
        to_chip[i][index].wait_recv()
        return (
            grads[i][b, place(index)].astype(F32)
            + core_in[i][n_ctx + index].astype(F32)
            + chip_in[i][index].astype(F32)
        )

    to_pair, to_line = [[], []], [[], []]
    for step in range(line_len):
        for i in range(2):
            pair_out[i][step] = mine(i, 2 * step).astype(BF16)
            to_pair[i].append(
                send(pair_out[i].at[step], pair_in[i].at[step], pair_sems.at[i], step, across)
            )
        if step == 0:
            add_sums(2, by_pair)
            own_sums = [
                send(sums_mine, sums_got.at[3 + k], sums_sems, 3 + k, device)
                for k, device in enumerate(on_same_line)
            ]
        for i in range(2):
            total = mine(i, 2 * step + 1)
            to_pair[i][step].wait_recv()
            total = total + pair_in[i][step].astype(F32)
            if step > 0:
                to_line[i][step - 1].wait_recv()
                total = total + line_in[i][step - 1].astype(F32)
            if step < line_len - 1:
                line_out[i][step] = total.astype(BF16)
                to_line[i].append(
                    send(line_out[i].at[step], line_in[i].at[step], line_sems.at[i], step, ahead)
                )
            else:
                outs[i][...] = total
    total = sums_mine[...]
    for k, copy in enumerate(own_sums):
        copy.wait_recv()
        total = total + sums_got[3 + k]
    sums_out[...] = total
    for copy in on_columns:
        copy.wait()
    for copy in waits:
        copy.wait_send()
    keep.wait()


def collect(grads, sums, columns, collective_id, name):
    n_batch, n_ctx = lax.axis_size("batch"), lax.axis_size("ctx")
    line_len = n_ctx // 2
    blocks = [grad.shape[2:] for grad in grads]

    def room(size):
        return [pltpu.VMEM((size,) + block, BF16) for block in blocks]

    return pl.pallas_call(
        functools.partial(collect_kernel, line_len),
        out_shape=(
            *[jax.ShapeDtypeStruct(block, F32) for block in blocks],
            jax.ShapeDtypeStruct(sums.shape, F32),
            jax.ShapeDtypeStruct(columns.shape, BF16),
        ),
        in_specs=[IN_VMEM] * 3 + [ANYWHERE],
        out_specs=(IN_VMEM,) * 3 + (ANYWHERE,),
        scratch_shapes=[
            *room(2 * n_ctx),
            *room(n_ctx),
            *room(line_len),
            *room(line_len - 1),
            *room(n_ctx),
            *room(line_len),
            *room(line_len - 1),
            pltpu.VMEM((2 + line_len,) + sums.shape, F32),
            pltpu.VMEM(sums.shape, F32),
            DMA(()),
            DMA((2, 2, 2 * n_ctx)),
            DMA((2, 2, n_ctx)),
            DMA((2, 2, line_len)),
            DMA((2, 2, line_len)),
            DMA((2, n_ctx)),
            DMA((2, 2 + line_len)),
        ],
        compiler_params=pltpu.CompilerParams(
            collective_id=collective_id, has_side_effects=True, vmem_limit_bytes=60 * 2**20
        ),
        cost_estimate=lasting(70),
        name=name,
    )(*grads, sums, columns)


def row_scale(values):
    return lax.rsqrt(jnp.mean(values * values, axis=-1, keepdims=True) + EPSILON)


def turn_head(values, cosine, signed_sine, back=False):
    turned = pltpu.roll(values, HEAD_DIM // 2, 1) * signed_sine
    return values * cosine - turned if back else values * cosine + turned


def whole(*shape):
    return pl.BlockSpec(shape, lambda j: (0,) * len(shape))


def project_kernel(hidden, gain, weight, bias, cosine, signed_sine, normed, query, key_value, kept):
    j = pl.program_id(0)

    @pl.when(j == 0)
    def _():
        values = hidden[...].astype(F32)
        kept[...] = (values * row_scale(values) * gain[...]).astype(BF16)
        normed[...] = kept[...]

    lin = dot(kept[...], weight[...]) + bias[...]
    tables = cosine[...], signed_sine[...]
    heads = [lin[:, i * HEAD_DIM : (i + 1) * HEAD_DIM] for i in range(4)]

    @pl.when(j < 3)
    def _():
        for i in range(4):
            turned = turn_head(heads[i], *tables)
            query[:, i * HEAD_DIM : (i + 1) * HEAD_DIM] = turned.astype(BF16)

    @pl.when(j == 3)
    def _():
        for i in range(4):
            value = turn_head(heads[i], *tables) if i < KV_HEADS else heads[i]
            key_value[:, i * HEAD_DIM : (i + 1) * HEAD_DIM] = value.astype(BF16)


def project(hidden, gain, weights, bias, tables):
    count, width = hidden.shape
    wide = 2 * KVW
    table = whole(count, HEAD_DIM)
    return pl.pallas_call(
        project_kernel,
        grid=(4,),
        out_shape=(
            jax.ShapeDtypeStruct((count, width), BF16),
            jax.ShapeDtypeStruct((count, width), BF16),
            jax.ShapeDtypeStruct((count, wide), BF16),
        ),
        in_specs=[
            whole(count, width),
            whole(1, width),
            pl.BlockSpec((width, wide), lambda j: (0, j)),
            pl.BlockSpec((1, wide), lambda j: (0, j)),
            table,
            table,
        ],
        out_specs=(
            whole(count, width),
            pl.BlockSpec((count, wide), lambda j: (0, jnp.minimum(j, 2))),
            whole(count, wide),
        ),
        scratch_shapes=[pltpu.VMEM((count, width), BF16)],
        compiler_params=pltpu.CompilerParams(vmem_limit_bytes=40 * 2**20),
        cost_estimate=lasting(4),
        name="project",
    )(hidden, gain, weights, bias, *tables)


def mark_allowed(key_pos, key_doc, own_pos, own_doc, allowed):
    count = own_pos.shape[1]
    pos_column, doc_column = key_pos[...].T, key_doc[...].T
    for i in range(key_pos.shape[0]):
        seen = (pos_column[:, i : i + 1] <= own_pos[...]) & (doc_column[:, i : i + 1] == own_doc[...])
        allowed[i * count : (i + 1) * count] = jnp.where(seen, 1.0, 0.0)


def stack_heads(block, group):
    return jnp.concatenate(
        [block[:, i * HEAD_DIM : (i + 1) * HEAD_DIM] for i in range(group)], axis=0
    )


def lay_heads(stacked, group):
    count = stacked.shape[0] // group
    return jnp.concatenate([stacked[i * count : (i + 1) * count] for i in range(group)], axis=1)


def probabilities(keys, queries, allowed, group):
    scores = times_transposed(keys, queries) * INV_ROOT
    seen = jnp.concatenate([allowed[...]] * group, axis=1) > 0.0
    scores = jnp.where(seen, scores, MASKED)
    raised = jnp.exp(scores - jnp.max(scores, axis=0, keepdims=True))
    return raised * (1.0 / jnp.sum(raised, axis=0, keepdims=True))


def attend_kernel(
    group, last, query, keys, values, out_0, out_1, out_2, key_pos, key_doc, own_pos, own_doc,
    hidden, gain, attn_out, residual, normed, total, allowed,
):
    j = pl.program_id(0)

    @pl.when(j == 0)
    def _():
        total[...] = hidden[...].astype(F32)
        mark_allowed(key_pos, key_doc, own_pos, own_doc, allowed)

    probs = probabilities(keys[...], stack_heads(query[...], group), allowed, group)
    result = contract_rows(values[...], probs.astype(BF16)).T
    block = lay_heads(result, group).astype(BF16)
    attn_out[...] = block
    for t, weight in enumerate((out_0, out_1, out_2)):
        total[:, t * 512 : (t + 1) * 512] += dot(block, weight[...])

    @pl.when(j == last)
    def _():
        values = total[...]
        residual[...] = values
        normed[...] = (values * row_scale(values) * gain[...]).astype(BF16)


def head_specs(count, width, keys, group, weights_at):
    rows = group * HEAD_DIM
    per_key = GROUPS // group
    query = pl.BlockSpec((count, rows), lambda j: (0, j))
    heads = [
        pl.BlockSpec((keys, HEAD_DIM), lambda j, i=i: (0, KV_HEADS * i + j // per_key))
        for i in range(2)
    ]
    out = [
        pl.BlockSpec((rows, 512), lambda j, t=t: (j, weights_at // 512 + t))
        for t in range(width // 512)
    ]
    places = [whole(keys // count, count)] * 2 + [whole(1, count)] * 2
    return query, heads, out, places


def attend(query, key_value, weights, places, hidden, gain):
    count, width = hidden.shape
    keys = key_value.shape[0]
    group = 3 if keys <= 1024 else 1
    steps = HEADS // group
    query_spec, head_spec, out_spec, place_spec = head_specs(
        count, width, keys, group, width + 2 * KVW
    )
    return pl.pallas_call(
        functools.partial(attend_kernel, group, steps - 1),
        grid=(steps,),
        out_shape=(
            jax.ShapeDtypeStruct((count, width), BF16),
            jax.ShapeDtypeStruct((count, width), F32),
            jax.ShapeDtypeStruct((count, width), BF16),
        ),
        in_specs=[query_spec, *head_spec, *out_spec, *place_spec]
        + [whole(count, width), whole(1, width)],
        out_specs=(query_spec, whole(count, width), whole(count, width)),
        scratch_shapes=[pltpu.VMEM((count, width), F32), pltpu.VMEM((keys, count), F32)],
        compiler_params=pltpu.CompilerParams(vmem_limit_bytes=56 * 2**20),
        cost_estimate=lasting(10),
        name="attend",
    )(query, key_value, key_value, *[weights] * 3, *places, hidden, gain)


def attend_back_kernel(
    group, per_key, query, keys, values, out_0, out_1, out_2, key_pos, key_doc, own_pos, own_doc,
    attn_out, residual, gain, out_grad, d_normed, cosine, signed_sine, d_query, d_key_value,
    o_grad, d_residual, gain_grad, branch, allowed, key_sum, value_sum,
):
    j = pl.program_id(0)

    @pl.when(j == 0)
    def _():
        rows, grads = residual[...], d_normed[...]
        factor = row_scale(rows)
        scaled = grads * gain[...]
        gain_grad[...] = jnp.sum(grads * rows * factor, axis=0, keepdims=True)
        total = out_grad[...].astype(F32) + (
            factor * scaled
            - rows * (factor * factor * factor) * jnp.mean(scaled * rows, axis=-1, keepdims=True)
        )
        d_residual[...] = total
        branch[...] = total.astype(BF16)
        mark_allowed(key_pos, key_doc, own_pos, own_doc, allowed)

    @pl.when(lax.rem(j, per_key) == 0)
    def _():
        key_sum[...] = jnp.zeros_like(key_sum)
        value_sum[...] = jnp.zeros_like(value_sum)

    o_grad[...] = contract_rows(attn_out[...], branch[...]).astype(BF16)
    d_attn = sum(
        times_transposed(branch[:, t * 512 : (t + 1) * 512], weight[...])
        for t, weight in enumerate((out_0, out_1, out_2))
    ).astype(BF16)
    grads = stack_heads(d_attn, group)
    queries = stack_heads(query[...], group)
    probs = probabilities(keys[...], queries, allowed, group)
    d_probs = times_transposed(values[...], grads)
    delta = jnp.sum(probs * d_probs, axis=0, keepdims=True)
    d_scores = (probs * (d_probs - delta)).astype(BF16)
    key_sum[...] += dot(d_scores, queries)
    value_sum[...] += dot(probs.astype(BF16), grads)
    result = contract_rows(keys[...], d_scores).T * INV_ROOT
    count = result.shape[0] // group
    for i in range(group):
        head = turn_head(
            result[i * count : (i + 1) * count], cosine[...], signed_sine[...], back=True
        )
        d_query[:, i * HEAD_DIM : (i + 1) * HEAD_DIM] = head.astype(BF16)

    @pl.when(lax.rem(j, per_key) == per_key - 1)
    def _():
        at = pl.multiple_of(j // per_key * HEAD_DIM, HEAD_DIM)
        d_key_value[:, pl.ds(at, HEAD_DIM)] = (key_sum[...] * INV_ROOT).astype(BF16)
        d_key_value[:, pl.ds(KVW + at, HEAD_DIM)] = value_sum[...].astype(BF16)


def attend_back(query, key_value, weights, places, attn_out, residual, gain, out_grad, d_normed, tables):
    count, width = query.shape
    keys = key_value.shape[0]
    group = 3 if keys <= 1024 else 1
    steps = HEADS // group
    query_spec, head_spec, out_spec, place_spec = head_specs(
        count, width, keys, group, width + 2 * KVW
    )
    rows, table = whole(count, width), whole(count, HEAD_DIM)
    return pl.pallas_call(
        functools.partial(attend_back_kernel, group, GROUPS // group),
        grid=(steps,),
        out_shape=(
            jax.ShapeDtypeStruct((count, width), BF16),
            jax.ShapeDtypeStruct((keys, 2 * KVW), BF16),
            jax.ShapeDtypeStruct((width, width), BF16),
            jax.ShapeDtypeStruct((count, width), F32),
            jax.ShapeDtypeStruct((1, width), F32),
        ),
        in_specs=[query_spec, *head_spec, *out_spec, *place_spec, query_spec]
        + [rows, whole(1, width), rows, rows, table, table],
        out_specs=(
            query_spec,
            whole(keys, 2 * KVW),
            pl.BlockSpec((group * HEAD_DIM, width), lambda j: (j, 0)),
            rows,
            whole(1, width),
        ),
        scratch_shapes=[
            pltpu.VMEM((count, width), BF16),
            pltpu.VMEM((keys, count), F32),
            pltpu.VMEM((keys, HEAD_DIM), F32),
            pltpu.VMEM((keys, HEAD_DIM), F32),
        ],
        compiler_params=pltpu.CompilerParams(vmem_limit_bytes=60 * 2**20),
        cost_estimate=lasting(17),
        name="attend_back",
    )(
        query, key_value, key_value, *[weights] * 3, *places, attn_out, residual, gain, out_grad,
        d_normed, *tables,
    )


def project_back_kernel(
    d_query, d_key_value, weight, normed, hidden, gain, d_residual, gain_two_grad, cosine,
    signed_sine, grad, hidden_grad, sums, flipped, total, biases,
):
    j = pl.program_id(0)
    wide = weight.shape[1]

    @pl.when(j == 0)
    def _():
        flipped[...] = normed[...].astype(F32).T.astype(BF16)
        total[...] = jnp.zeros_like(total)
        sums[...] = jnp.zeros_like(sums)

    def add(d_lin):
        grad[...] = dot(flipped[...], d_lin).astype(BF16)
        total[...] += times_transposed(d_lin, weight[...])
        return jnp.sum(d_lin.astype(F32), axis=0, keepdims=True)

    for i in range(3):

        @pl.when(j == i)
        def _():
            sums[1:2, i * wide : (i + 1) * wide] = add(d_query[...])

    @pl.when(j == 3)
    def _():
        heads = [
            turn_head(
                d_key_value[:, i * HEAD_DIM : (i + 1) * HEAD_DIM],
                cosine[...],
                signed_sine[...],
                back=True,
            )
            for i in range(KV_HEADS)
        ]
        d_lin = jnp.concatenate(heads + [d_key_value[:, KVW:]], axis=1).astype(BF16)
        sums[2:3, :wide] = add(d_lin)
        rows, grads = hidden[...].astype(F32), total[...]
        factor = row_scale(rows)
        scaled = grads * gain[...]
        sums[0:1] = jnp.sum(grads * rows * factor, axis=0, keepdims=True)
        sums[3:4] = gain_two_grad[...]
        hidden_grad[...] = d_residual[...] + (
            factor * scaled
            - rows * (factor * factor * factor) * jnp.mean(scaled * rows, axis=-1, keepdims=True)
        )


def project_back(d_query, d_key_value, weights, normed, hidden, gain, d_residual, gain_two_grad, tables):
    count, width = hidden.shape
    wide = 2 * KVW
    rows, table = whole(count, width), whole(count, HEAD_DIM)
    return pl.pallas_call(
        project_back_kernel,
        grid=(4,),
        out_shape=(
            jax.ShapeDtypeStruct((width, width + wide), BF16),
            jax.ShapeDtypeStruct((count, width), F32),
            jax.ShapeDtypeStruct((8, width), F32),
        ),
        in_specs=[
            pl.BlockSpec((count, wide), lambda j: (0, jnp.minimum(j, 2))),
            whole(count, wide),
            pl.BlockSpec((width, wide), lambda j: (0, j)),
            rows,
            rows,
            whole(1, width),
            rows,
            whole(1, width),
            table,
            table,
        ],
        out_specs=(
            pl.BlockSpec((width, wide), lambda j: (0, j)),
            rows,
            whole(8, width),
        ),
        scratch_shapes=[
            pltpu.VMEM((width, count), BF16),
            pltpu.VMEM((count, width), F32),
            pltpu.VMEM((8, wide), F32),
        ],
        compiler_params=pltpu.CompilerParams(vmem_limit_bytes=48 * 2**20),
        cost_estimate=lasting(9),
        name="project_back",
    )(
        d_query, d_key_value, weights, normed, hidden, gain, d_residual, gain_two_grad, *tables
    )


def unpack_kernel(n_batch, piece, packed, gate, up):
    n_ctx, _, both = packed.shape
    for out, first in ((gate, 0), (up, both // 2)):
        for k in range(n_batch):
            for i in range(n_ctx):
                at = first + k * piece
                to = (k * n_ctx + i) * piece
                out[:, to : to + piece] = packed[i, :, at : at + piece].astype(F32)


def finish_kernel(
    n_batch, piece, packed, hidden_grad, o_grad, q_grad, kv_grad, residual, ff_rows, down_grad, sums,
    gate, up, hidden_grad_out, o_out, q_out, k_out, v_out, hidden_out, down_out, own_sums,
):
    unpack_kernel(n_batch, piece, packed, gate, up)
    hidden_grad_out[...] = hidden_grad[...]
    o_out[...] = o_grad[...]
    q_out[...] = q_grad[...]
    k_out[...] = kv_grad[:, :KVW]
    v_out[...] = kv_grad[:, KVW:]
    hidden_out[...] = (residual[...] + ff_rows[...]).astype(BF16)
    down_out[...] = down_grad[...]
    n_ctx, rows, _ = packed.shape
    width = sums.shape[1]
    own = lax.axis_index("batch") * n_ctx + lax.axis_index("ctx")
    small = KVW // (n_batch * n_ctx)
    for row, first in ((0, own * rows), (1, own * small), (2, KVW + own * small)):
        rolled = pltpu.roll(sums[...], lax.rem(width - first, width), 1)
        own_sums[8 * row : 8 * row + 8] = rolled[:, :128]


def finish(packed, hidden_grad, o_grad, q_grad, kv_grad, residual, ff_rows, down_grad, sums, n_batch, width):
    n_ctx, rows, _ = packed.shape
    wide = jax.ShapeDtypeStruct((rows, width), F32)
    half = jax.ShapeDtypeStruct((rows, KVW), F32)

    def like(array, dtype=F32):
        return jax.ShapeDtypeStruct(array.shape, dtype)

    return pl.pallas_call(
        functools.partial(finish_kernel, n_batch, width // (n_batch * n_ctx)),
        out_shape=(
            wide, wide, like(hidden_grad), like(o_grad), like(q_grad), half, half,
            like(residual, BF16), like(down_grad), jax.ShapeDtypeStruct((24, 128), F32),
        ),
        in_specs=[IN_VMEM] * 9,
        out_specs=(IN_VMEM,) * 10,
        compiler_params=pltpu.CompilerParams(vmem_limit_bytes=56 * 2**20),
        cost_estimate=lasting(5),
        name="finish",
    )(packed, hidden_grad, o_grad, q_grad, kv_grad, residual, ff_rows, down_grad, sums)


def unpack(packed, n_batch, width):
    n_ctx, rows, _ = packed.shape
    out = jax.ShapeDtypeStruct((rows, width), F32)
    return pl.pallas_call(
        functools.partial(unpack_kernel, n_batch, width // (n_batch * n_ctx)),
        out_shape=(out, out),
        in_specs=[IN_VMEM],
        out_specs=(IN_VMEM, IN_VMEM),
        compiler_params=pltpu.CompilerParams(vmem_limit_bytes=40 * 2**20),
        cost_estimate=lasting(3),
        name="unpack",
    )(packed)


def mlp_kernel(line_len, tile, span, own_rows, *refs):
    n_batch, n_ctx = 4, 2 * line_len
    weights, (down, grads_in) = refs[:n_batch], refs[n_batch : n_batch + 2]
    d_rows_out, ff_out, down_out, gate_up_out = refs[n_batch + 2 : n_batch + 6]
    (
        tokens, flipped, gate_up, down_in, grads, mixed, mixed_flipped, d_gate_up, d_parts, ff_parts,
        d_pair, d_line, ff_pair, ff_line, core_wide, chip_wide, down_terms,
        core_down, chip_down, own, lin, d_mixed_rows, load_sems, store_sems,
        line_sems, pair_sems, back_pair, back_line, batch_sems,
    ) = refs[n_batch + 6 :]
    b, c = lax.axis_index("batch"), lax.axis_index("ctx")
    line, pair = c // 2, c % 2
    ahead = (b, 2 * lax.rem(line + 1, line_len) + pair)
    behind = (b, 2 * lax.rem(line + line_len - 1, line_len) + pair)
    across, chip, core = (b, c ^ 1), (b ^ 2, c), (b ^ 1, c)
    count, width = own.shape
    half = gate_up.shape[1] // 2
    own_ff = down.shape[0]
    piece = own_ff // n_batch
    depth = width // n_batch
    for k in range(n_batch):
        source = pl.ds(pl.multiple_of((b ^ k) * depth, 128), depth)
        own[:, k * depth : (k + 1) * depth] = own_rows[:, source]
    greet((ahead, behind, across, chip, core))

    def at(step):
        return 2 * lax.rem(line - step + line_len, line_len)

    sent = []

    def send(source, target, sems, device):
        copy = remote(source, target, sems[0], sems[1], device)
        copy.start()
        sent.append(copy)
        return copy

    on_line, on_pair = [], []

    def forward(step):
        block = own if step == 0 else tokens.at[at(step) + pair]
        target = tokens.at[at(step) + pair]
        if step > 0:
            on_line[step - 1].wait_recv()
        if step < line_len - 1:
            sems = line_sems.at[0, step], line_sems.at[1, step]
            on_line.append(send(block, target, sems, ahead))
        sems = pair_sems.at[0, step], pair_sems.at[1, step]
        on_pair.append(send(block, target, sems, across))

    forward(0)
    loads = [pltpu.make_async_copy(own, tokens.at[c], load_sems.at[0])]
    for k, weight in enumerate(weights):
        loads.append(
            pltpu.make_async_copy(
                weight, gate_up.at[pl.ds(k * depth, depth)], load_sems.at[1 + k]
            )
        )
    loads.append(
        pltpu.make_async_copy(down, down_in.at[pl.ds(0, own_ff)], load_sems.at[1 + n_batch])
    )
    loads.append(pltpu.make_async_copy(grads_in, grads, load_sems.at[2 + n_batch]))
    for copy in loads:
        copy.start()
    if own_ff < half:
        down_in[own_ff:half] = jnp.zeros((half - own_ff, width), BF16)
    for copy in loads:
        copy.wait()

    def chunk(step):
        first = pl.multiple_of(at(step) * count, 2 * count)
        rows, pair_rows = pl.ds(first, 2 * count), pl.ds(at(step), 2)
        block = tokens[pair_rows].reshape(2 * count, width)
        grad_block = grads[pair_rows].reshape(2 * count, width)

        for low in range(0, 2 * half, span):
            lin[:, low : low + span] = dot(block, gate_up[:, low : low + span])
        d_mixed_rows[...] = times_transposed(grad_block, down_in[...])

        def columns(index, _):
            low = pl.multiple_of(index * tile, 128)
            high = pl.multiple_of(half + index * tile, 128)
            gate_lin, up_lin = lin[:, pl.ds(low, tile)], lin[:, pl.ds(high, tile)]
            d_mixed = d_mixed_rows[:, pl.ds(low, tile)]
            sigmoid = 1.0 / (1.0 + jnp.exp(-gate_lin))
            silu = gate_lin * sigmoid
            product = silu * up_lin
            mixed[:, pl.ds(low, tile)] = product.astype(BF16)
            mixed_flipped[pl.ds(low, tile), rows] = product.T.astype(BF16)
            d_gate = d_mixed * up_lin * sigmoid * (1.0 + gate_lin * (1.0 - sigmoid))
            d_gate_up[rows, pl.ds(low, tile)] = d_gate.astype(BF16)
            d_gate_up[rows, pl.ds(high, tile)] = (d_mixed * silu).astype(BF16)
            return 0

        lax.fori_loop(0, half // tile, columns, 0)
        for low in range(0, width, width // 2):
            part = slice(low, low + width // 2)
            back = times_transposed(d_gate_up[rows], gate_up[part])
            d_parts[pair_rows, :, part] = back.astype(BF16).reshape(2, count, width // 2)
        for low in range(0, width, width // 2):
            part = slice(low, low + width // 2)
            out = dot(mixed[...], down_in[:, part])
            ff_parts[pair_rows, :, part] = out.astype(BF16).reshape(2, count, width // 2)
            flipped[part, rows] = (
                tokens[pair_rows, :, part].reshape(2 * count, width // 2).astype(F32).T.astype(BF16)
            )

    moves = (
        (d_parts, d_pair, d_line, d_rows_out),
        (ff_parts, ff_pair, ff_line, ff_out),
    )
    given = {}

    def give(index, which=0):
        parts, pairs = moves[which][:2]
        sems = back_pair.at[0, which, index], back_pair.at[1, which, index]
        source = parts.at[at(index + 1) + 1 - pair]
        given[index, which] = send(source, pairs.at[index], sems, across)

    for step in range(line_len):
        if step + 1 < line_len:
            forward(step + 1)
        on_pair[step].wait_recv()
        chunk(step)
        if step == line_len - 2:
            for index in range(line_len - 2):
                give(index)
    give(line_len - 2)
    give(line_len - 1)
    stores = []

    def store(source, target):
        copy = pltpu.make_async_copy(source, target, store_sems.at[len(stores)])
        copy.start()
        stores.append(copy)

    passed = {}

    def passing(index, which=0):
        parts, pairs, lines, out = moves[which]
        place = at(index + 1) + pair
        given[index, which].wait_recv()
        total = parts[place].astype(F32) + pairs[index].astype(F32)
        if index > 0:
            passed[index - 1, which].wait_recv()
            total = total + lines[index - 1].astype(F32)
        if index < line_len - 1:
            parts[place] = total.astype(BF16)
            sems = back_line.at[0, which, index], back_line.at[1, which, index]
            passed[index, which] = send(parts.at[place], lines.at[index], sems, ahead)
        elif which:
            out[...] = total
        else:
            for k in range(n_batch):
                target = pl.ds(pl.multiple_of((b ^ k) * depth, 128), depth)
                out[:, target] = total[:, k * depth : (k + 1) * depth]

    def batch_send(source, target, index, device):
        sems = batch_sems.at[0, index], batch_sems.at[1, index]
        return send(source, target, sems, device)

    def wide(k, side):
        return gate_up.at[pl.ds(k * depth, depth), pl.ds(side * half, half)]

    def weight_grad(k, side):
        part = slice(k * depth, (k + 1) * depth), slice(side * half, (side + 1) * half)
        gate_up[part] = dot(flipped[part[0]], d_gate_up[:, part[1]]).astype(BF16)

    def down_grads():
        for k in range(n_batch):
            grad = dot(
                mixed_flipped[k * piece : (k + 1) * piece],
                grads[...].reshape(n_ctx * count, width),
            )
            down_terms[k] = grad.astype(BF16)
        for slot, row in ((1, b ^ 3), (0, b ^ 1)):
            to_core["down", slot] = batch_send(
                down_terms.at[row], core_down.at[slot], 6 + slot, core
            )

    def pass_down():
        to_core["down", 1].wait_recv()
        total = down_terms[b ^ 2].astype(F32) + core_down[1].astype(F32)
        down_terms[b ^ 2] = total.astype(BF16)
        to_chip.append(batch_send(down_terms.at[b ^ 2], chip_down, 8, chip))

    def add_wide(k, side, terms):
        def columns(index, _):
            low = pl.multiple_of(index * tile, 128)
            at_low = pl.ds(pl.multiple_of(side * half + low, 128), tile)
            rows = slice(k * depth, (k + 1) * depth)
            total = gate_up[rows, at_low].astype(F32)
            for term in terms:
                total = total + term[:, pl.ds(low, tile)].astype(F32)
            gate_up[rows, at_low] = total.astype(BF16)
            return 0

        lax.fori_loop(0, half // tile, columns, 0)

    to_core, to_chip = {}, []

    def compute_and_send(k, side):
        weight_grad(k, side)
        slot = k // 2
        target = core_wide.at[slot, side]
        to_core[k, side] = batch_send(wide(k, side), target, 2 * slot + side, core)

    def compute_and_pass(side):
        weight_grad(2, side)
        to_core[3, side].wait_recv()
        add_wide(2, side, [core_wide.at[1, side]])
        to_chip.append(batch_send(wide(2, side), chip_wide.at[side], 4 + side, chip))

    compute_and_send(3, 0)
    compute_and_pass(0)
    compute_and_send(3, 1)
    compute_and_pass(1)
    work = [
        down_grads,
        lambda: (pass_down(), compute_and_send(1, 0)),
        lambda: compute_and_send(1, 1),
        lambda: (weight_grad(0, 0), weight_grad(0, 1)),
    ]
    for index in range(max(line_len, len(work))):
        if index < line_len:
            passing(index)
            give(index, 1)
        if index < len(work):
            work[index]()
    for index in range(line_len - 1):
        passing(index, 1)
    for side in range(2):
        to_core[1, side].wait_recv()
        to_chip[side].wait_recv()
        add_wide(0, side, [core_wide.at[0, side], chip_wide.at[side]])
        store(wide(0, side), gate_up_out.at[:, pl.ds(side * half, half)])
    to_core["down", 0].wait_recv()
    to_chip[2].wait_recv()
    down_out[...] = (
        down_terms[b].astype(F32) + core_down[0].astype(F32) + chip_down[...].astype(F32)
    )
    passing(line_len - 1, 1)
    for copy in sent:
        copy.wait_send()
    for copy in stores:
        copy.wait()


def mlp_scratch(n_ctx, n_batch, count, width, hidden_own):
    line_len, half = n_ctx // 2, lanes(hidden_own)
    tokens, piece = n_ctx * count, hidden_own // n_batch

    def room(*shape):
        return pltpu.VMEM(shape, BF16)

    return [
        room(n_ctx, count, width),
        room(width, tokens),
        room(width, 2 * half),
        room(half, width),
        room(n_ctx, count, width),
        room(2 * count, half),
        room(half, tokens),
        room(tokens, 2 * half),
        room(n_ctx, count, width),
        room(n_ctx, count, width),
        *[room(line_len, count, width), room(line_len - 1, count, width)] * 2,
        room(2, 2, width // n_batch, half),
        room(2, width // n_batch, half),
        room(n_batch, piece, width),
        room(2, piece, width),
        room(piece, width),
        room(count, width),
        pltpu.VMEM((2 * count, 2 * half), F32),
        pltpu.VMEM((2 * count, half), F32),
    ]


def mlp(own, weights, down, grads, collective_id, name):
    n_batch, n_ctx = lax.axis_size("batch"), lax.axis_size("ctx")
    line_len = n_ctx // 2
    count, width = own.shape
    half = weights[0].shape[1] // 2
    tile = 384 if half % 384 == 0 else 128
    span = 768 if 2 * half % 768 == 0 else tile
    return pl.pallas_call(
        functools.partial(mlp_kernel, line_len, tile, span),
        out_shape=(
            jax.ShapeDtypeStruct((count, width), F32),
            jax.ShapeDtypeStruct((count, width), F32),
            jax.ShapeDtypeStruct((down.shape[0] // n_batch, width), F32),
            jax.ShapeDtypeStruct(weights[0].shape, BF16),
        ),
        in_specs=[IN_VMEM] + [ANYWHERE] * (n_batch + 2),
        out_specs=(IN_VMEM, IN_VMEM, IN_VMEM, ANYWHERE),
        scratch_shapes=mlp_scratch(n_ctx, n_batch, count, width, down.shape[0])
        + [
            DMA((3 + n_batch,)),
            DMA((2,)),
            DMA((2, line_len)),
            DMA((2, line_len)),
            DMA((2, 2, line_len)),
            DMA((2, 2, line_len)),
            DMA((2, 9)),
        ],
        compiler_params=pltpu.CompilerParams(
            collective_id=collective_id, has_side_effects=True, vmem_limit_bytes=62 * 2**20
        ),
        cost_estimate=lasting(100),
        name=name,
    )(own, *weights, down, grads.reshape(n_ctx, count, width))


def front_kernel(line_len, group, *refs):
    (
        q_weight, k_weight, v_weight, o_weight, gate, up, hidden, cosine, signed_sine, own_pos,
        own_doc, down, out_grad,
    ) = refs[:13]
    own_vectors = refs[13:18]
    (
        normed_out, query, attn_out, residual, normed_two, gain_one, gain_two, key_pos, key_doc,
        key_value_out, w_in_out, w_out_out, columns_out, near, far, farther, down_out, grads_out,
    ) = refs[18:36]
    own_in, w_in, w_out, columns, key_own, key_value, allowed, vectors, bias, small = refs[36:46]
    (
        load_sems, line_sems, first_sems, second_sems, core_sems, column_sems, near_sems, far_sems,
        farther_sems, keys_line_sems, keys_pair_sems, grads_line_sems, grads_pair_sems, down_sems,
    ) = refs[46:]
    b, c = lax.axis_index("batch"), lax.axis_index("ctx")
    n_batch, n_ctx = 4, 2 * line_len
    line, pair = c // 2, c % 2
    ahead = (b, 2 * lax.rem(line + 1, line_len) + pair)
    across, chip, core = (b, c ^ 1), (b ^ 2, c), (b ^ 1, c)
    others = [(b, lax.rem(c + k, n_ctx)) for k in range(1, n_ctx)]
    count, width = hidden.shape
    rows = q_weight.shape[0]
    wide = width + 2 * KVW
    at = 0
    for part in (q_weight, k_weight, v_weight):
        own_in[:, at : at + part.shape[1]] = part[...]
        at += part.shape[1]
    small[...] = jnp.zeros_like(small)
    for row, vector in enumerate(own_vectors):
        small[row : row + 1, : vector.shape[1]] = vector[...].astype(F32)
    small[5:6] = jnp.right_shift(own_pos[...], 6).astype(F32)
    small[6:7] = jnp.bitwise_and(own_pos[...], 63).astype(F32)
    small[7:8] = own_doc[...].astype(F32)
    own_in[:, at:] = jnp.zeros((rows, 128), BF16)
    own_in[:8, at:] = small[...].astype(BF16)
    greet([chip, core] + others)
    sent, local = [], []

    def send(source, target, sems, index, device):
        copy = remote(source, target, sems.at[(0, *index)], sems.at[(1, *index)], device)
        copy.start()
        sent.append(copy)
        return copy

    def store(source, target):
        copy = pltpu.make_async_copy(source, target, load_sems.at[len(local)])
        copy.start()
        local.append(copy)

    owns, wholes = (own_in, o_weight), (w_in, w_out)
    first_to, second_to = (across, chip), (chip, across)
    on_line, on_first, on_second, on_core = {}, {}, {}, {}

    def place(step, side):
        return 2 * lax.rem(line - step + line_len, line_len) + side

    def block(p, row, column):
        first = pl.multiple_of((row * n_ctx + column) * rows, rows)
        return wholes[p].at[pl.ds(first, rows)]

    def line_step(p, step):
        target = block(p, b, place(step, pair))
        source = owns[p] if step == 0 else target
        if step > 0:
            on_line[p, step - 1].wait_recv()
        if step < line_len - 1:
            on_line[p, step] = send(source, target, line_sems, (p, step), ahead)
        on_first[p, step] = send(source, target, first_sems, (p, step), first_to[p])
        on_second[p, step] = send(source, target, second_sems, (p, step), second_to[p])
        on_core[p, step] = send(source, target, core_sems, (p, step), core)

    def first_step(p, step):
        on_first[p, step].wait_recv()
        row, side = ((b, 1 - pair), (b ^ 2, pair))[p]
        landed = block(p, row, place(step, side))
        index = line_len + step
        on_second[p, index] = send(landed, landed, second_sems, (p, index), second_to[p])
        on_core[p, index] = send(landed, landed, core_sems, (p, index), core)

    def second_step(p, index):
        on_second[p, index].wait_recv()
        late = index >= line_len
        row = b ^ 2 if p == 0 or late else b
        side = 1 - pair if p == 1 or late else pair
        landed = block(p, row, place(index % line_len, side))
        on_core[p, n_ctx + index] = send(landed, landed, core_sems, (p, n_ctx + index), core)

    def complete(p):
        for index in range(2 * n_ctx):
            on_core[p, index].wait_recv()

    on_down = []

    def down_step(step):
        if step == 0:
            store(down, down_out.at[b])
            on_down.append(send(down, down_out.at[b], down_sems, (0,), chip))
            on_down.append(send(down, down_out.at[b], down_sems, (1,), core))
        else:
            on_down[0].wait_recv()
            landed = down_out.at[b ^ 2]
            on_down.append(send(landed, landed, down_sems, (2,), core))

    def pack():
        half = columns.shape[2] // 2
        piece = gate.shape[1] // (n_batch * n_ctx)
        for first, weight in ((0, gate), (half, up)):
            if n_batch * piece < half:
                columns[:, :, first + half - 128 : first + half] = jnp.zeros(
                    (n_ctx, columns.shape[1], 128), BF16
                )
            for k in range(n_batch):
                for i in range(n_ctx):
                    to = (k * n_ctx + i) * piece
                    low = first + k * piece
                    columns[i, :, low : low + piece] = weight[:, to : to + piece]
        store(columns.at[c], columns_out.at[c])

    on_columns, on_near, on_far, on_farther = [], [], [], []

    def exchange_columns(first, last):
        for k in range(first, last):
            source = columns.at[others[k][1]]
            on_columns.append(send(source, columns_out.at[c], column_sems, (k,), others[k]))

    def spread_columns(k):
        slot = lax.rem(c - k + n_ctx, n_ctx)
        if k > 0:
            on_columns[k - 1].wait_recv()
        source = columns_out.at[slot] if k > 0 else columns.at[c]
        on_far.append(send(source, far.at[slot], far_sems, (k,), chip))
        on_near.append(send(source, near.at[slot], near_sems, (k,), core))

    def spread_farther(k):
        slot = lax.rem(c - k + n_ctx, n_ctx)
        on_far[k].wait_recv()
        on_farther.append(send(far.at[slot], farther.at[slot], farther_sems, (k,), core))

    keys_line, keys_pair = [], []

    def keys_step(step):
        column = place(step, pair)
        source = key_own if step == 0 else key_value.at[column]
        if step > 0:
            keys_line[step - 1].wait_recv()
        if step < line_len - 1:
            keys_line.append(send(source, key_value.at[column], keys_line_sems, (step,), ahead))
        keys_pair.append(send(source, key_value.at[column], keys_pair_sems, (step,), across))

    grads_line, grads_pair = [], []

    def grads_step(step):
        target = grads_out.at[place(step, pair)]
        source = out_grad if step == 0 else target
        if step > 0:
            grads_line[step - 1].wait_recv()
        if step < line_len - 1:
            grads_line.append(send(source, target, grads_line_sems, (step,), ahead))
        grads_pair.append(send(source, target, grads_pair_sems, (step,), across))

    line_step(0, 0)
    mine = pl.ds(pl.multiple_of((b * n_ctx + c) * rows, rows), rows)
    w_in[mine] = own_in[...]
    w_out[mine] = o_weight[...]
    pack()
    for step in range(1, line_len):
        line_step(0, step)
    exchange_columns(0, 2)
    line_step(1, 0)
    for step in range(line_len):
        first_step(0, step)
    between = [functools.partial(line_step, 1, step) for step in range(1, line_len)]
    between += [functools.partial(first_step, 1, step) for step in range(line_len)]
    between += [functools.partial(down_step, 0)]
    for index in range(n_ctx):
        second_step(0, index)
        between[index]()
        if index in (1, 3, 4, 5, 6):
            exchange_columns(len(on_columns), len(on_columns) + 1)
    store(out_grad, grads_out.at[c])
    complete(0)
    for k in range(3):
        spread_columns(k)

    values = hidden[...].astype(F32)
    for d in range(n_batch * n_ctx):
        piece = w_in[d * rows : d * rows + 16, wide:].astype(F32)
        vectors[0:3, d * rows : (d + 1) * rows] = piece[0:3, :rows]
        part = KVW // (n_batch * n_ctx)
        for i in range(2):
            bias[0:1, i * KVW + d * part : i * KVW + (d + 1) * part] = piece[3 + i : 4 + i, :part]
    for k in range(n_ctx):
        first = pl.multiple_of((b * n_ctx + k) * rows, rows)
        piece = w_in[pl.ds(first, 16), wide:].astype(F32)
        key_pos[k : k + 1] = piece[5:6] * 64.0 + piece[6:7]
        key_doc[k : k + 1] = piece[7:8]
    gain_one[...] = vectors[0:1]
    gain_two[...] = vectors[1:2]
    normed_out[...] = (values * row_scale(values) * vectors[0:1]).astype(BF16)
    tables = cosine[...], signed_sine[...]
    lin = dot(normed_out[...], w_in[:, width:wide]) + bias[...]
    for i in range(2 * KV_HEADS):
        head = lin[:, i * HEAD_DIM : (i + 1) * HEAD_DIM]
        head = turn_head(head, *tables) if i < KV_HEADS else head
        key_own[:, i * HEAD_DIM : (i + 1) * HEAD_DIM] = head.astype(BF16)
    keys_step(0)
    key_value[c] = key_own[...]
    for k in range(3):
        step = width // 3
        part = slice(k * step, (k + 1) * step)
        lin = dot(normed_out[...], w_in[:, part]) + vectors[2:3, part]
        for i in range(step // HEAD_DIM):
            head = turn_head(lin[:, i * HEAD_DIM : (i + 1) * HEAD_DIM], *tables)
            low = k * step + i * HEAD_DIM
            query[:, low : low + HEAD_DIM] = head.astype(BF16)
    store(w_in, w_in_out)
    mark_allowed(key_pos, key_doc, own_pos, own_doc, allowed)
    for step in range(1, line_len):
        second_step(1, step - 1)
        keys_step(step)
        spread_columns(len(on_near))
    grads_step(0)
    for step in range(line_len):
        keys_pair[step].wait_recv()
    store(key_value, key_value_out)

    def attention(i):
        wide_part = group * HEAD_DIM
        part = slice(i * wide_part, (i + 1) * wide_part)
        head = i * group // GROUPS * HEAD_DIM
        keys = key_value[:, :, head : head + HEAD_DIM].reshape(n_ctx * count, HEAD_DIM)
        low = KVW + head
        values = key_value[:, :, low : low + HEAD_DIM].reshape(n_ctx * count, HEAD_DIM)
        probs = probabilities(keys, stack_heads(query[:, part], group), allowed, group)
        result = contract_rows(values, probs.astype(BF16)).T
        attn_out[:, part] = lay_heads(result, group).astype(BF16)

    steps = HEADS // group
    for i in range(steps):
        attention(i)
        if i + 1 < line_len:
            grads_step(i + 1)
        for index in range(line_len - 1 + i, n_ctx, steps):
            second_step(1, index)
        if len(on_near) < n_ctx:
            spread_columns(len(on_near))
    down_step(1)
    complete(1)
    store(w_out, w_out_out)
    total = hidden[...].astype(F32) + dot(attn_out[...], w_out[...])
    residual[...] = total
    normed_two[...] = (total * row_scale(total) * vectors[1:2]).astype(BF16)
    for k in range(n_ctx // 2):
        spread_farther(k)
    for k in range(n_ctx // 2, n_ctx):
        spread_farther(k)
    for copy in on_near + on_farther + grads_pair + on_down[1:]:
        copy.wait_recv()
    for copy in sent:
        copy.wait_send()
    for copy in local:
        copy.wait()


def front(matrices, gate, up, hidden, tables, own_places, down, out_grad, vectors, collective_id, name):
    n_batch, n_ctx = lax.axis_size("batch"), lax.axis_size("ctx")
    line_len = n_ctx // 2
    rows = gate.shape[0]
    count, width = hidden.shape
    wide = width + 2 * KVW
    columns = (n_ctx, rows, 2 * lanes(gate.shape[1] // n_ctx))

    def shaped(dtype, *shape):
        return jax.ShapeDtypeStruct(shape, dtype)

    def room(*shape, dtype=BF16):
        return pltpu.VMEM(shape, dtype)

    return pl.pallas_call(
        functools.partial(front_kernel, line_len, 3),
        out_shape=(
            shaped(BF16, count, width),
            shaped(BF16, count, width),
            shaped(BF16, count, width),
            shaped(F32, count, width),
            shaped(BF16, count, width),
            shaped(F32, 1, width),
            shaped(F32, 1, width),
            shaped(F32, n_ctx, count),
            shaped(F32, n_ctx, count),
            shaped(BF16, n_ctx, count, 2 * KVW),
            shaped(BF16, width, wide + 128),
            shaped(BF16, width, width),
            *[shaped(BF16, *columns)] * 4,
            shaped(BF16, n_batch, *down.shape),
            shaped(BF16, n_ctx, count, width),
        ),
        in_specs=[IN_VMEM] * 11 + [ANYWHERE] * 2 + [IN_VMEM] * 5,
        out_specs=(IN_VMEM,) * 9 + (ANYWHERE,) * 9,
        scratch_shapes=[
            room(rows, wide + 128),
            room(width, wide + 128),
            room(width, width),
            room(*columns),
            room(count, 2 * KVW),
            room(n_ctx, count, 2 * KVW),
            room(n_ctx * count, count, dtype=F32),
            room(8, width, dtype=F32),
            room(1, 2 * KVW, dtype=F32),
            room(8, 128, dtype=F32),
            DMA((6,)),
            DMA((2, 2, line_len)),
            DMA((2, 2, line_len)),
            DMA((2, 2, n_ctx)),
            DMA((2, 2, 2 * n_ctx)),
            DMA((2, n_ctx)),
            DMA((2, n_ctx)),
            DMA((2, n_ctx)),
            DMA((2, n_ctx)),
            DMA((2, line_len)),
            DMA((2, line_len)),
            DMA((2, line_len)),
            DMA((2, line_len)),
            DMA((2, 3)),
        ],
        compiler_params=pltpu.CompilerParams(
            collective_id=collective_id, has_side_effects=True, vmem_limit_bytes=58 * 2**20
        ),
        cost_estimate=lasting(100),
        name=name,
    )(*matrices, gate, up, hidden, *tables, *own_places, down, out_grad, *vectors)


def back_kernel(line_len, group, *refs):
    (
        query, key_value, key_pos, key_doc, own_pos, own_doc, attn_out, residual, gain_two, out_grad,
        d_normed, cosine, signed_sine, normed, hidden, gain_one, in_weights, out_weights, columns,
    ) = refs[:19]
    hidden_grad, o_out, q_out, kv_out, sums_out, columns_out = refs[19:25]
    w_out, w_in, branch, allowed, key_sum, value_sum, d_query, flipped, d_residual = refs[25:34]
    d_key_value, keys_pair, keys_line, keys_pass, sums_got, sums_mine = refs[34:40]
    grads = refs[40:43]
    core_in, chip_in, pair_in, line_in, chip_out, pair_out, line_out = [
        refs[43 + 3 * i : 46 + 3 * i] for i in range(7)
    ]
    (
        load_sems, column_sems, keys_pair_sems, keys_line_sems, sums_sems, core_sems, chip_sems,
        pair_sems, line_sems,
    ) = refs[64:]
    outs = o_out, q_out, kv_out
    b, c = lax.axis_index("batch"), lax.axis_index("ctx")
    n_ctx = 2 * line_len
    line, pair = c // 2, c % 2
    ahead = (b, 2 * lax.rem(line + 1, line_len) + pair)
    across, chip, core = (b, c ^ 1), (b ^ 2, c), (b ^ 1, c)
    others = [(b, lax.rem(c + k, n_ctx)) for k in range(1, n_ctx)]
    on_same_line = others[1::2]
    count, width = query.shape
    wide = group * HEAD_DIM
    rows = q_out.shape[0]
    greet([chip, core] + others)
    sent = []

    def send(source, target, sems, index, device):
        copy = remote(source, target, sems.at[(0, *index)], sems.at[(1, *index)], device)
        copy.start()
        sent.append(copy)
        return copy

    loads = [
        pltpu.make_async_copy(out_weights, w_out, load_sems.at[0]),
        pltpu.make_async_copy(in_weights.at[:, pl.ds(0, width + 2 * KVW)], w_in, load_sems.at[1]),
        pltpu.make_async_copy(columns.at[c], columns_out.at[c], load_sems.at[2]),
    ]
    for copy in loads:
        copy.start()
    on_columns = []

    def exchange_columns(first, last):
        for k in range(first, last):
            source = columns.at[others[k][1]]
            on_columns.append(send(source, columns_out.at[c], column_sems, (k,), others[k]))

    exchange_columns(0, n_ctx - 1)

    def to(step):
        return 2 * lax.rem(line - 1 - step + line_len, line_len)

    def place(index):
        return to(index // 2) + (1 - pair if index % 2 == 0 else pair)

    def block(row, index):
        at = (row * n_ctx + place(index)) * rows
        return pl.ds(pl.multiple_of(at, rows), rows)

    to_core, to_chip, to_pair, to_line = {}, {}, {}, {}

    def core_stage(p):
        for index in range(2 * n_ctx):
            row = b ^ 3 if index < n_ctx else b ^ 1
            source = grads[p].at[block(row, index % n_ctx)]
            to_core[p, index] = send(source, core_in[p].at[index], core_sems, (p, index), core)

    def chip_stage(p):
        for index in range(n_ctx):
            to_core[p, index].wait_recv()
            total = grads[p][block(b ^ 2, index)].astype(F32) + core_in[p][index].astype(F32)
            chip_out[p][index] = total.astype(BF16)
            to_chip[p, index] = send(
                chip_out[p].at[index], chip_in[p].at[index], chip_sems, (p, index), chip
            )

    def mine(p, index):
        to_core[p, n_ctx + index].wait_recv()
        to_chip[p, index].wait_recv()
        return (
            grads[p][block(b, index)].astype(F32)
            + core_in[p][n_ctx + index].astype(F32)
            + chip_in[p][index].astype(F32)
        )

    def pair_stage(p, step):
        pair_out[p][step] = mine(p, 2 * step).astype(BF16)
        to_pair[p, step] = send(
            pair_out[p].at[step], pair_in[p].at[step], pair_sems, (p, step), across
        )

    def line_stage(p, step):
        total = mine(p, 2 * step + 1)
        to_pair[p, step].wait_recv()
        total = total + pair_in[p][step].astype(F32)
        if step > 0:
            to_line[p, step - 1].wait_recv()
            total = total + line_in[p][step - 1].astype(F32)
        if step < line_len - 1:
            line_out[p][step] = total.astype(BF16)
            to_line[p, step] = send(
                line_out[p].at[step], line_in[p].at[step], line_sems, (p, step), ahead
            )
        else:
            outs[p][...] = total

    values, gradient = residual[...], d_normed[...]
    factor = row_scale(values)
    scaled = gradient * gain_two[...]
    sums_mine[...] = jnp.zeros_like(sums_mine)
    sums_mine[3:4] = jnp.sum(gradient * values * factor, axis=0, keepdims=True)
    total = out_grad[...].astype(F32) + (
        factor * scaled
        - values * (factor * factor * factor) * jnp.mean(scaled * values, axis=-1, keepdims=True)
    )
    d_residual[...] = total
    branch[...] = total.astype(BF16)
    for i in range(HEADS // group):
        part = slice(i * wide, (i + 1) * wide)
        grads[0][part] = contract_rows(attn_out[:, part], branch[...]).astype(BF16)
    core_stage(0)
    mark_allowed(key_pos, key_doc, own_pos, own_doc, allowed)
    flipped[...] = normed[...].astype(F32).T.astype(BF16)
    tables = cosine[...], signed_sine[...]

    def attention(i):
        part = slice(i * wide, (i + 1) * wide)
        head = i * group // GROUPS
        key_part = slice(head * HEAD_DIM, (head + 1) * HEAD_DIM)
        value_part = slice(KVW + head * HEAD_DIM, KVW + (head + 1) * HEAD_DIM)
        keys, values = key_value[:, key_part], key_value[:, value_part]
        d_attn = times_transposed(branch[...], w_out[part]).astype(BF16)
        head_grads, queries = stack_heads(d_attn, group), stack_heads(query[:, part], group)
        probs = probabilities(keys, queries, allowed, group)
        d_probs = times_transposed(values, head_grads)
        delta = jnp.sum(probs * d_probs, axis=0, keepdims=True)
        d_scores = (probs * (d_probs - delta)).astype(BF16)
        key_term = dot(d_scores, queries)
        value_term = dot(probs.astype(BF16), head_grads)
        first = i * group % GROUPS == 0
        key_sum[...] = key_term if first else key_sum[...] + key_term
        value_sum[...] = value_term if first else value_sum[...] + value_term
        result = contract_rows(keys, d_scores).T * INV_ROOT
        for k in range(group):
            turned = turn_head(result[k * count : (k + 1) * count], *tables, back=True)
            at = (i * group + k) * HEAD_DIM
            d_query[:, at : at + HEAD_DIM] = turned.astype(BF16)
        if (i + 1) * group % GROUPS == 0:
            shape = d_key_value.shape[:2] + (HEAD_DIM,)
            d_key_value[:, :, key_part] = (key_sum[...] * INV_ROOT).astype(BF16).reshape(shape)
            d_key_value[:, :, value_part] = value_sum[...].astype(BF16).reshape(shape)

    loads[0].wait()
    attention(0)
    chip_stage(0)
    for i in range(1, HEADS // group):
        attention(i)

    given, passed = [], []
    for step in range(line_len):
        source = d_key_value.at[to(step) + 1 - pair]
        given.append(send(source, keys_pair.at[step], keys_pair_sems, (step,), across))
    key_total = None

    def keys_stage(step):
        given[step].wait_recv()
        total = d_key_value[to(step) + pair].astype(F32) + keys_pair[step].astype(F32)
        if step > 0:
            passed[step - 1].wait_recv()
            total = total + keys_line[step - 1].astype(F32)
        if step < line_len - 1:
            keys_pass[step] = total.astype(BF16)
            passed.append(
                send(keys_pass.at[step], keys_line.at[step], keys_line_sems, (step,), ahead)
            )
        return total

    last = line_len - 1
    for step in range(line_len // 2):
        pair_stage(0, step)
    half = width // 2
    for i in range(2):
        part = slice(i * half, (i + 1) * half)
        grads[1][:, part] = dot(flipped[...], d_query[:, part]).astype(BF16)
        if i == 0:
            keys_stage(0)
    core_stage(1)
    loads[1].wait()
    d_one = times_transposed(d_query[...], w_in[:, :width])
    for step in range(1, line_len):
        if step == 1:
            chip_stage(1)
        key_total = keys_stage(step)
        if line_len // 2 + step - 1 < line_len:
            pair_stage(0, line_len // 2 + step - 1)
        if step < last:
            line_stage(0, step - 1)
    heads = [
        turn_head(key_total[:, i * HEAD_DIM : (i + 1) * HEAD_DIM], *tables, back=True)
        for i in range(KV_HEADS)
    ]
    d_lin = jnp.concatenate(heads + [key_total[:, KVW:]], axis=1).astype(BF16)
    grads[2][...] = dot(flipped[...], d_lin).astype(BF16)
    core_stage(2)
    line_stage(0, last - 1)
    d_one = d_one + times_transposed(d_lin, w_in[:, width:])
    sums_mine[1:2] = jnp.sum(d_query[...].astype(F32), axis=0, keepdims=True)
    sums_mine[2:3, : 2 * KVW] = jnp.sum(d_lin.astype(F32), axis=0, keepdims=True)
    values = hidden[...].astype(F32)
    factor = row_scale(values)
    scaled = d_one * gain_one[...]
    sums_mine[0:1] = jnp.sum(d_one * values * factor, axis=0, keepdims=True)

    def start_sums(index, device):
        copy = remote(
            sums_mine, sums_got.at[index], sums_sems.at[0, index], sums_sems.at[1, index], device
        )
        copy.start()
        return copy

    def add_sums(index, copy):
        copy.wait()
        sums_mine[...] += sums_got[index]

    by_core = start_sums(0, core)
    pair_stage(1, 0)
    line_stage(0, last)
    add_sums(0, by_core)
    by_chip = start_sums(1, chip)
    chip_stage(2)
    hidden_grad[...] = d_residual[...] + (
        factor * scaled
        - values * (factor * factor * factor) * jnp.mean(scaled * values, axis=-1, keepdims=True)
    )
    for step in range(1, line_len):
        pair_stage(1, step)
        line_stage(1, step - 1)
    add_sums(1, by_chip)
    by_pair = start_sums(2, across)
    pair_stage(2, 0)
    line_stage(1, last)
    for step in range(1, line_len):
        pair_stage(2, step)
        line_stage(2, step - 1)
        if step == 1:
            add_sums(2, by_pair)
            by_line = [start_sums(3 + k, device) for k, device in enumerate(on_same_line)]
    line_stage(2, last)
    total = sums_mine[...]
    for k, copy in enumerate(by_line):
        copy.wait()
        total = total + sums_got[3 + k]
    sums_out[...] = total
    for copy in on_columns:
        copy.wait_recv()
    for copy in sent:
        copy.wait_send()
    loads[2].wait()


def back(query, key_value, weights, places, attn_out, residual, gain_two, out_grad, d_normed, tables, normed, hidden, gain_one, columns, collective_id, name):
    n_ctx = columns.shape[0]
    line_len, rows = n_ctx // 2, columns.shape[1]
    count, width = query.shape
    keys = key_value.shape[0]
    widths = width, width, 2 * KVW

    def room(*shape, dtype=BF16):
        return pltpu.VMEM(shape, dtype)

    def rooms(size):
        return [room(size, rows, part) for part in widths]

    outs = [(count, width)] + [(rows, part) for part in widths] + [(8, width)]
    return pl.pallas_call(
        functools.partial(back_kernel, line_len, 3),
        out_shape=(
            *[jax.ShapeDtypeStruct(shape, F32) for shape in outs],
            jax.ShapeDtypeStruct(columns.shape, BF16),
        ),
        in_specs=[IN_VMEM] * 16 + [ANYWHERE] * 3,
        out_specs=(IN_VMEM,) * 5 + (ANYWHERE,),
        scratch_shapes=[
            room(width, width),
            room(width, width + 2 * KVW),
            room(count, width),
            room(keys, count, dtype=F32),
            room(keys, HEAD_DIM, dtype=F32),
            room(keys, HEAD_DIM, dtype=F32),
            room(count, width),
            room(width, count),
            room(count, width, dtype=F32),
            room(n_ctx, count, 2 * KVW),
            room(line_len, count, 2 * KVW),
            room(line_len - 1, count, 2 * KVW),
            room(line_len - 1, count, 2 * KVW),
            room(2 + line_len, 8, width, dtype=F32),
            room(8, width, dtype=F32),
            *[room(width, part) for part in widths],
            *rooms(2 * n_ctx),
            *rooms(n_ctx),
            *rooms(line_len),
            *rooms(line_len - 1),
            *rooms(n_ctx),
            *rooms(line_len),
            *rooms(line_len - 1),
            DMA((3,)),
            DMA((2, n_ctx)),
            DMA((2, line_len)),
            DMA((2, line_len)),
            DMA((2, 2 + line_len)),
            DMA((2, 3, 2 * n_ctx)),
            DMA((2, 3, n_ctx)),
            DMA((2, 3, line_len)),
            DMA((2, 3, line_len)),
        ],
        compiler_params=pltpu.CompilerParams(
            collective_id=collective_id, has_side_effects=True, vmem_limit_bytes=60 * 2**20
        ),
        cost_estimate=lasting(90),
        name=name,
    )(
        query, key_value, *places, attn_out, residual, gain_two, out_grad, d_normed, *tables, normed,
        hidden, gain_one, *weights, columns,
    )


def swap(values, bit):
    size = lax.axis_size("batch")
    return lax.ppermute(values, "batch", [(i, i ^ bit) for i in range(size)])


def by_batch(values, b, n_batch):
    step = values.shape[1] // n_batch
    blocks = [lax.dynamic_slice_in_dim(values, (b ^ k) * step, step, 1) for k in range(n_batch)]
    return jnp.concatenate(blocks, axis=1)


def batch_terms(terms):
    passed = swap((terms[2].astype(F32) + swap(terms[3], 1).astype(F32)).astype(BF16), 2)
    return [term.astype(F32) for term in (terms[0], swap(terms[1], 1), passed)]


def mlp_room(*sizes):
    rooms = mlp_scratch(*sizes)
    return sum(math.prod(room.shape) * jnp.dtype(room.dtype).itemsize for room in rooms)


def mlp_in_steps(normed_two, w_gate_up, w_down, out_grad_all):
    n_batch, b = lax.axis_size("batch"), lax.axis_index("batch")
    normed_two = by_batch(normed_two, b, n_batch)
    w_gate_up = jnp.concatenate(w_gate_up, axis=0)
    half, width = w_gate_up.shape[1] // 2, normed_two.shape[1]
    own_ff = w_down.shape[0]
    w_down = jnp.pad(w_down, ((0, half - own_ff), (0, 0)))
    normed_two = gather_ctx(normed_two, 3, "gather_tokens").reshape(-1, width)
    gate_up = dot(normed_two, w_gate_up)
    gate_lin, up_lin = gate_up[:, :half], gate_up[:, half:]
    sigmoid_gate = jax.nn.sigmoid(gate_lin)
    mixed_rows = (gate_lin * sigmoid_gate * up_lin).astype(BF16)
    d_mixed = times_transposed(out_grad_all, w_down)
    d_gate = d_mixed * up_lin * sigmoid_gate * (1.0 + gate_lin * (1.0 - sigmoid_gate))
    d_up = d_mixed * (gate_lin * sigmoid_gate)
    d_gate_up = jnp.concatenate([d_gate.astype(BF16), d_up.astype(BF16)], axis=1)
    (d_normed_two,) = scatter_ctx(
        [times_transposed(d_gate_up, w_gate_up).astype(BF16)], 4, "scatter_tokens"
    )
    (ff_out,) = scatter_ctx([dot(mixed_rows, w_down).astype(BF16)], 8, "scatter_outputs")
    gate_up_grad = contract_rows(normed_two, d_gate_up).astype(BF16).reshape(n_batch, -1, 2 * half)
    down_grad = contract_rows(mixed_rows, out_grad_all).astype(BF16)[:own_ff]
    return (
        by_batch(d_normed_two, b, n_batch),
        ff_out,
        sum(
            batch_terms(
                [
                    lax.dynamic_index_in_dim(
                        down_grad.reshape(n_batch, -1, width), b ^ k, 0, keepdims=False
                    )
                    for k in range(n_batch)
                ]
            )
        ),
        sum(batch_terms(gate_up_grad)).astype(BF16),
    )


def vector_rows(vectors):
    pieces = []
    for vector in vectors:
        pieces += [vector, jnp.zeros((128 - vector.shape[0],), vector.dtype)]
    pieces.append(jnp.zeros((128 * (8 - len(vectors)),), vectors[0].dtype))
    return jnp.concatenate(pieces).reshape(8, 128)


def local(
    hidden_in,
    positions,
    doc_ids,
    attn_gain,
    q_weight,
    q_bias,
    k_weight,
    k_bias,
    v_weight,
    v_bias,
    o_weight,
    mlp_gain,
    gate_weight,
    up_weight,
    down_weight,
    out_grad,
):
    n_batch, n_ctx = lax.axis_size("batch"), lax.axis_size("ctx")
    n_all = n_batch * n_ctx
    count, width = hidden_in.shape
    hidden_ff = gate_weight.shape[1]

    b = lax.axis_index("batch")
    rows = q_weight.shape[0]
    vectors = (attn_gain, mlp_gain, q_bias, k_bias, v_bias)
    weights = (q_weight, k_weight, v_weight, o_weight)
    cosine, sine_table = rope_tables(positions)
    half_lane = jnp.arange(HEAD_DIM) < HEAD_DIM // 2
    tables = cosine, jnp.where(half_lane[None], -sine_table, sine_table)
    own_places = positions[None], doc_ids[None]
    together = rows % 16 == 0
    if together:
        (
            normed_one, query, attn_out, residual, normed_two, gain_one, gain_two, key_pos, key_doc,
            key_value, *weights, packed, near, far, farther, w_down, out_grad_all,
        ) = front(
            weights, gate_weight, up_weight, hidden_in, tables, own_places, down_weight, out_grad,
            [vector[None] for vector in vectors], 1, "front",
        )
        w_down = w_down.reshape(-1, width)
        half = packed.shape[2] // 2
        key_value = key_value.reshape(-1, 2 * KVW)
        w_gate_up = [columns.reshape(-1, 2 * half) for columns in (packed, near, far, farther)]
        places = (key_pos, key_doc, *own_places)
    else:
        w_down = lax.all_gather(down_weight, "batch", axis=0, tiled=True)
        out_grad_all = lax.all_gather(out_grad, "ctx", axis=0, tiled=True)
        marks = (positions // 64, positions % 64, doc_ids)
        small = vector_rows(vectors + tuple(mark.astype(BF16) for mark in marks))
        small = jnp.pad(small, ((0, rows - 8), (0, 0)))
        attn_all, packed = spread(
            (*weights, small), gate_weight, up_weight, 1, "spread_weights"
        )
        half = packed.shape[2] // 2
        own_rows = packed.reshape(-1, 2 * half)
        near, far = swap(own_rows, 1), swap(own_rows, 2)
        small = attn_all[:, :, :8, attn_all.shape[3] - 128 :].astype(F32)
        gain_one, gain_two, b_query, b_key, b_value = (
            small[:, :, i, : part.shape[0]].reshape(-1)
            for i, part in enumerate((attn_gain, mlp_gain, q_bias, k_bias, v_bias))
        )
        places = lax.dynamic_index_in_dim(small, b, 0, keepdims=False)[:, 5:8, :count]
        key_pos, key_doc = places[:, 0] * 64 + places[:, 1], places[:, 2]
        attn_all = attn_all.reshape(width, -1)
        b_qkv = jnp.concatenate([b_query, b_key, b_value])
        gain_one, gain_two = gain_one[None], gain_two[None]

        normed_one, query, key_value = project(hidden_in, gain_one, attn_all, b_qkv[None], tables)
        key_value = gather_ctx(key_value, 2, "gather_keys").reshape(-1, 2 * KVW)
        far, key_value = lax.optimization_barrier((far, key_value))
        w_gate_up = (own_rows, near, far, swap(far, 1))
        places = (key_pos, key_doc, *own_places)
        attn_out, residual, normed_two = attend(
            query, key_value, attn_all, places, hidden_in, gain_two
        )

    fits = mlp_room(n_ctx, n_batch, count, width, w_down.shape[0]) < 60 * 2**20
    feed_forward = functools.partial(mlp, collective_id=3, name="mlp") if fits else mlp_in_steps
    d_normed_two, ff_out, down_grad, gate_up_grad = feed_forward(
        normed_two, w_gate_up, w_down, out_grad_all.reshape(-1, width)
    )

    columns = gate_up_grad.reshape(n_ctx, rows, 2 * half)
    if together:
        hidden_grad, o_grad, q_grad, kv_grad, sums, gate_up_grad = back(
            query, key_value, weights, places, attn_out, residual, gain_two, out_grad,
            d_normed_two, tables, normed_one, hidden_in, gain_one, columns, 7, "back"
        )
        (
            gate_grad, up_grad, hidden_grad, o_grad, q_grad, k_grad, v_grad, hidden_out, down_grad, sums,
        ) = finish(
            gate_up_grad, hidden_grad, o_grad, q_grad, kv_grad, residual, ff_out, down_grad, sums,
            n_batch, hidden_ff,
        )
        gain_one_grad, q_bias_grad, gain_two_grad = (sums[i, :rows] for i in (0, 1, 3))
        k_bias_grad, v_bias_grad = (sums[i, : KVW // n_all] for i in (10, 18))
    else:
        d_query, d_key_value, o_grad, d_residual, gain_two_grad = attend_back(
            query, key_value, attn_all, places, attn_out, residual, gain_two, out_grad,
            d_normed_two, tables,
        )
        (d_key_value,) = scatter_ctx([d_key_value], 5, "scatter_keys")
        qkv_grad, hidden_grad, sums = project_back(
            d_query, d_key_value, attn_all, normed_one, hidden_in, gain_one, d_residual,
            gain_two_grad, tables,
        )
        grads = [grad.reshape(n_batch, n_ctx, rows, -1) for grad in (qkv_grad, o_grad)]
        qkv_grad, o_grad, sums, gate_up_grad = collect(grads, sums, columns, 6, "collect")
        q_grad, k_grad = qkv_grad[:, :width], qkv_grad[:, width : width + KVW]
        v_grad = qkv_grad[:, width + KVW :]
        gate_grad, up_grad = unpack(gate_up_grad, n_batch, hidden_ff)
        hidden_out = (residual + ff_out).astype(BF16)

        def own_part(row, first, total):
            size = total // n_all
            at = first + (b * n_ctx + lax.axis_index("ctx")) * size
            return lax.dynamic_slice(sums, (row, at), (1, size))[0]

        gain_one_grad, q_bias_grad = own_part(0, 0, width), own_part(1, 0, width)
        k_bias_grad, v_bias_grad = own_part(2, 0, KVW), own_part(2, KVW, KVW)
        gain_two_grad = own_part(3, 0, width)
    return (
        hidden_out,
        hidden_grad,
        gain_one_grad,
        q_grad,
        q_bias_grad,
        k_grad,
        k_bias_grad,
        v_grad,
        v_bias_grad,
        o_grad,
        gain_two_grad,
        gate_grad,
        up_grad,
        down_grad,
    )


def solution(mesh):
    matrix, vector = P(ALL, None), P(ALL)
    placed = (
        (matrix, vector, vector, vector, matrix, vector, matrix, vector)
        + (matrix, vector, matrix, vector, matrix, matrix, matrix, matrix)
    )
    results = (matrix, matrix) + (vector, matrix) * 4 + (vector, matrix, matrix, matrix)
    return jax.shard_map(local, mesh=mesh, in_specs=placed, out_specs=results, check_vma=False)
```
